32 devices in a mesh: clip: 2 (over x), seq: 16 (over z, y, core).
Axes of the slice: x: 2, y: 2, z: 4, core: 2. Of those that a mesh axis runs over, the one named last changes fastest.
Arguments:
- video_query: bfloat16 [512, 4096], P(('clip', 'seq')), parts along dimension 0, may hold values from -6 to 6
- video_keys: bfloat16 [512, 4096], P(('clip', 'seq')), parts along dimension 0, may hold values from -6 to 6
- video_values: bfloat16 [512, 4096], P(('clip', 'seq')), parts along dimension 0, may hold values from -6 to 6
- audio_query: bfloat16 [256, 2048], P(('clip', 'seq')), parts along dimension 0, may hold values from -6 to 6
- audio_keys: bfloat16 [256, 2048], P(('clip', 'seq')), parts along dimension 0, may hold values from -6 to 6
- audio_values: bfloat16 [256, 2048], P(('clip', 'seq')), parts along dimension 0, may hold values from -6 to 6
- cross_video_query: bfloat16 [512, 2048], P(('clip', 'seq')), parts along dimension 0, may hold values from -6 to 6
- cross_video_keys: bfloat16 [512, 2048], P(('clip', 'seq')), parts along dimension 0, may hold values from -6 to 6
- cross_video_values: bfloat16 [512, 2048], P(('clip', 'seq')), parts along dimension 0, may hold values from -6 to 6
- cross_audio_query: bfloat16 [256, 2048], P(('clip', 'seq')), parts along dimension 0, may hold values from -6 to 6
- cross_audio_keys: bfloat16 [256, 2048], P(('clip', 'seq')), parts along dimension 0, may hold values from -6 to 6
- cross_audio_values: bfloat16 [256, 2048], P(('clip', 'seq')), parts along dimension 0, may hold values from -6 to 6
- video_length: int32 [2], P('clip'), parts along dimension 0, may hold values from 128 to 256
- audio_length: int32 [2], P('clip'), parts along dimension 0, may hold values from 64 to 128
- align_offset: int32 [2], P('clip'), parts along dimension 0, may hold values from -8 to 8
Outputs:
- video_mixed: bfloat16 [512, 4096], P(('clip', 'seq')), parts along dimension 0
- audio_mixed: bfloat16 [256, 2048], P(('clip', 'seq')), parts along dimension 0
- video_cross: bfloat16 [512, 2048], P(('clip', 'seq')), parts along dimension 0
- audio_cross: bfloat16 [256, 2048], P(('clip', 'seq')), parts along dimension 0
The draws below stay inside these ranges and needn't reach their ends.
There are 2 independent parts, one for each index of `clip`. The reference program is written for one: setup_inputs(seed, part) draws one part's arguments, and reference() takes and returns one part's arrays. A program takes and returns all parts, laid end to end along the dimension named above; each array names one. Nothing has to cross between parts.
All inputs are finite; a program needn't handle non-finite values.
Results may differ from the reference program's by a relative error of at most 0.006.
Values may be sent and summed in bfloat16 or wider, within the bound.
No kernel may reach another device: no remote copies, remote signals or barrier semaphores. Data moves between devices by JAX's collectives and lax.ppermute only.
A program may use at most 128 MiB of HBM per device.

```python
import math
import jax
import jax.numpy as jnp
from jax import lax

HV = 32
HDV = 128
HA = 32
HDA = 64
DV = 4096
DA = 2048
TV = 256
TA = 128
AWIN = 80
VWIN = 32


def base_field(key, rows, width):
    values = jnp.clip(jax.random.normal(key, (rows, width), dtype=jnp.float32), -6.0, 6.0)
    return values


def plant_queries(values, key):
    return values.astype(jnp.bfloat16)


def plant_keys(values, key):
    return values.astype(jnp.bfloat16)


def draw_video_query(key, part):
    return plant_queries(base_field(jax.random.fold_in(key, 101), TV, DV), key)


def draw_video_keys(key, part):
    return plant_keys(base_field(jax.random.fold_in(key, 102), TV, DV), key)


def draw_audio_query(key, part):
    return plant_queries(base_field(jax.random.fold_in(key, 103), TA, DA), key)


def draw_audio_keys(key, part):
    return plant_keys(base_field(jax.random.fold_in(key, 104), TA, DA), key)


def draw_cross_video_query(key, part):
    return plant_queries(base_field(jax.random.fold_in(key, 105), TV, DA), key)


def draw_cross_audio_keys(key, part):
    return plant_keys(base_field(jax.random.fold_in(key, 106), TA, DA), key)


def draw_cross_audio_query(key, part):
    return plant_queries(base_field(jax.random.fold_in(key, 107), TA, DA), key)


def draw_cross_video_keys(key, part):
    return plant_keys(base_field(jax.random.fold_in(key, 108), TV, DA), key)


def level_of(key, extent, pieces, least, largest):
    def one(axis_at, parts):
        heights = jax.random.uniform(jax.random.fold_in(jax.random.fold_in(key, 6), axis_at), (parts,), jnp.float32, least / len(pieces), largest / len(pieces))
        return jnp.repeat(jnp.exp(heights), extent[axis_at] // parts).reshape((-1,) + (1,) * (len(extent) - axis_at - 1))

    factor_of = one(*pieces[0])
    for cut in pieces[1:]:
        factor_of = factor_of * one(*cut)
    return factor_of


def gaussian(rng, shape, scale, reach, shards=(), kind=jnp.bfloat16):
    level = level_of(rng, shape, shards, -0.22, 0.18) if shards else 1.0
    values = jax.random.normal(rng, shape, jnp.float32) * scale * level
    return jnp.minimum(jnp.maximum(values, -reach), reach).astype(kind)


def setup_inputs(seed: int = 0, part: int = 0) -> dict:
    splits = jax.random.split(jax.random.key(seed), 16)
    part_splits = jax.random.split(jax.random.fold_in(splits[15], part), 16)
    return {
        "video_query": draw_video_query(jax.random.fold_in(jax.random.fold_in(splits[15], part), 71), part),
        "video_keys": draw_video_keys(jax.random.fold_in(jax.random.fold_in(splits[15], part), 71), part),
        "video_values": gaussian(part_splits[2], (TV, DV), 1.0, 6.0, ((0, 16),)),
        "audio_query": draw_audio_query(jax.random.fold_in(jax.random.fold_in(splits[15], part), 71), part),
        "audio_keys": draw_audio_keys(jax.random.fold_in(jax.random.fold_in(splits[15], part), 71), part),
        "audio_values": gaussian(part_splits[5], (TA, DA), 1.0, 6.0, ((0, 16),)),
        "cross_video_query": draw_cross_video_query(jax.random.fold_in(jax.random.fold_in(splits[15], part), 71), part),
        "cross_video_keys": draw_cross_video_keys(jax.random.fold_in(jax.random.fold_in(splits[15], part), 71), part),
        "cross_video_values": gaussian(part_splits[8], (TV, DA), 1.0, 6.0, ((0, 16),)),
        "cross_audio_query": draw_cross_audio_query(jax.random.fold_in(jax.random.fold_in(splits[15], part), 71), part),
        "cross_audio_keys": draw_cross_audio_keys(jax.random.fold_in(jax.random.fold_in(splits[15], part), 71), part),
        "cross_audio_values": gaussian(part_splits[11], (TA, DA), 1.0, 6.0, ((0, 16),)),
        "video_length": jax.random.randint(part_splits[12], (1,), TV // 2, TV + 1).astype(jnp.int32),
        "audio_length": jax.random.randint(part_splits[13], (1,), TA // 2, TA + 1).astype(jnp.int32),
        "align_offset": jax.random.randint(part_splits[14], (1,), -(TA // 16), TA // 16 + 1).astype(jnp.int32),
    }


def block_size(total, limit):
    chosen = min(total, limit)
    while total % chosen:
        chosen -= 1
    return chosen

def exact_attention(queries, keys, values, heads, depth, query_pos, key_pos, allowed):
    count = queries.shape[0]
    key_count = keys.shape[0]
    head_queries = queries.reshape(count, heads, depth).transpose(1, 0, 2)
    head_keys = keys.reshape(key_count, heads, depth).transpose(1, 0, 2)
    head_values = values.reshape(key_count, heads, depth).transpose(1, 0, 2)
    q_block = block_size(count, 512)
    scale = 1.0 / math.sqrt(depth)
    places = query_pos.reshape(count // q_block, q_block)

    def one_head(packed):
        one_query, one_key, one_value = packed
        tiles = one_query.reshape(count // q_block, q_block, depth)

        def one_tile(tile_pack):
            tile, tile_pos = tile_pack
            scores = jnp.dot(tile, one_key.T, preferred_element_type=jnp.float32) * scale
            permit = allowed(tile_pos[:, None], key_pos[None, :])
            scores = jnp.where(permit, scores, -jnp.inf)
            peak = lax.optimization_barrier(jnp.max(scores, axis=1, keepdims=True))
            weights = jnp.exp(scores - peak)
            total = lax.optimization_barrier(jnp.sum(weights, axis=1, keepdims=True))
            mixed = jnp.dot(weights.astype(jnp.bfloat16), one_value, preferred_element_type=jnp.float32)
            return (mixed / total).astype(jnp.bfloat16)
        return lax.map(one_tile, (tiles, places)).reshape(count, depth)
    result = lax.map(one_head, (head_queries, head_keys, head_values))
    return result.transpose(1, 0, 2).reshape(count, heads * depth)

def reference(video_query, video_keys, video_values, audio_query, audio_keys, audio_values, cross_video_query, cross_video_keys, cross_video_values, cross_audio_query, cross_audio_keys, cross_audio_values, video_length, audio_length, align_offset):
    video_valid = video_length[0]
    audio_valid = audio_length[0]
    align_shift = align_offset[0]
    video_places = jnp.arange(TV, dtype=jnp.int32)
    audio_places = jnp.arange(TA, dtype=jnp.int32)

    def video_open(q_where, k_where):
        return k_where < video_valid

    def audio_open(q_where, k_where):
        return k_where < audio_valid

    def toward_video(q_where, k_where):
        center = jnp.clip(q_where * TA // TV + align_shift, 0, audio_valid - 1)
        return (k_where < audio_valid) & (jnp.abs(k_where - center) <= AWIN)

    def toward_audio(q_where, k_where):
        center = jnp.clip((q_where - align_shift) * TV // TA, 0, video_valid - 1)
        return (k_where < video_valid) & (jnp.abs(k_where - center) <= VWIN)
    video_mixed = exact_attention(video_query, video_keys, video_values, HV, HDV, video_places, video_places, video_open)
    audio_mixed = exact_attention(audio_query, audio_keys, audio_values, HA, HDA, audio_places, audio_places, audio_open)
    video_cross = exact_attention(cross_video_query, cross_audio_keys, cross_audio_values, HA, HDA, video_places, audio_places, toward_video)
    audio_cross = exact_attention(cross_audio_query, cross_video_keys, cross_video_values, HA, HDA, audio_places, video_places, toward_audio)
    return (video_mixed, audio_mixed, video_cross, audio_cross)
```

```python
import functools
import math

import jax
import jax.numpy as jnp
from jax import lax
from jax.experimental import pallas as pl
from jax.experimental.pallas import tpu as pltpu
from jax.sharding import PartitionSpec as P

HV = 32
HDV = 128
HA = 32
HDA = 64


def block_size(total, limit):
    chosen = min(total, limit)
    while total % chosen:
        chosen -= 1
    return chosen


def split_heads(tokens, heads, depth, copies):
    rows = tokens.shape[0]
    shaped = tokens.reshape(copies, rows // copies, heads, depth).transpose(2, 0, 1, 3)
    return shaped.reshape(heads * copies, rows // copies, depth)


def spread_heads(tokens, heads, depth, copies):
    rows = tokens.shape[0]
    shaped = tokens.reshape(rows, heads, depth).transpose(1, 0, 2)
    shaped = jnp.broadcast_to(shaped[:, None], (heads, copies, rows, depth))
    return shaped.reshape(heads * copies, rows, depth)


def join_heads(owned, heads, depth, copies):
    part_rows = owned.shape[1]
    shaped = owned.reshape(heads, copies, part_rows, depth).transpose(1, 2, 0, 3)
    return shaped.reshape(copies * part_rows, heads * depth)


def owned_positions(rows, copies, devices, index):
    part_rows = rows // copies
    flat = jnp.arange(devices * part_rows, dtype=jnp.int32)
    return flat // part_rows * rows + index % copies * part_rows + flat % part_rows


def online_update(carry, scores, permit, value_tile, value_form):
    running, total, accum = carry
    scores = jnp.where(permit, scores, -1e30)
    newmax = jnp.maximum(running, jnp.max(scores, axis=2))
    weights = jnp.where(permit, jnp.exp(scores - newmax[:, :, None]), 0.0)
    factor = jnp.exp(running - newmax)
    total = total * factor + jnp.sum(weights, axis=2)
    mixed = jnp.einsum(
        value_form, weights.astype(jnp.bfloat16), value_tile, preferred_element_type=jnp.float32
    )
    accum = accum * factor[:, :, None] + mixed
    return (newmax, total, accum)


def fold_initial(rows, heads, depth):
    return (
        jnp.full((heads, rows), -1e30, jnp.float32),
        jnp.zeros((heads, rows), jnp.float32),
        jnp.zeros((heads, rows, depth), jnp.float32),
    )


def fold_piece(carry, local_query, key_rows, value_rows, permit, heads, depth):
    keyed = key_rows.reshape(key_rows.shape[0], heads, depth)
    valued = value_rows.reshape(value_rows.shape[0], heads, depth)
    scores = jnp.einsum("qhd,khd->hqk", local_query, keyed, preferred_element_type=jnp.float32) * (
        1.0 / math.sqrt(depth)
    )
    return online_update(carry, scores, permit[None], valued, "hqk,khd->hqd")


def fold_finish(carry, heads, depth):
    running, total, accum = carry
    result = (accum / total[:, :, None]).astype(jnp.bfloat16)
    return result.transpose(1, 0, 2).reshape(result.shape[1], heads * depth)


def attend_local(queries, keys, values, query_pos, key_pos, allowed):
    heads, q_count, depth = queries.shape
    k_count = keys.shape[1]
    q_block = block_size(q_count, 512)
    k_block = block_size(k_count, 2048)
    scale = 1.0 / math.sqrt(depth)
    q_tiles = queries.reshape(heads, q_count // q_block, q_block, depth).transpose(1, 0, 2, 3)
    k_tiles = keys.reshape(heads, k_count // k_block, k_block, depth).transpose(1, 0, 2, 3)
    v_tiles = values.reshape(heads, k_count // k_block, k_block, depth).transpose(1, 0, 2, 3)
    q_places = query_pos.reshape(q_count // q_block, q_block)
    k_places = key_pos.reshape(k_count // k_block, k_block)

    def one_tile(packed):
        q_tile, q_where = packed

        def absorb(carry, piece):
            k_tile, v_tile, k_where = piece
            scores = (
                jnp.einsum("hqd,hkd->hqk", q_tile, k_tile, preferred_element_type=jnp.float32)
                * scale
            )
            permit = allowed(q_where[:, None], k_where[None, :])[None]
            return (online_update(carry, scores, permit, v_tile, "hqk,hkd->hqd"), None)

        initial = fold_initial(q_block, heads, depth)
        final_state, unused = lax.scan(absorb, initial, (k_tiles, v_tiles, k_places))
        running, total, accum = final_state
        return (accum / total[:, :, None]).astype(jnp.bfloat16)

    tiles = lax.map(one_tile, (q_tiles, q_places))
    return tiles.transpose(1, 0, 2, 3).reshape(heads, q_count, depth)


def shards_general(
    video_query,
    video_keys,
    video_values,
    audio_query,
    audio_keys,
    audio_values,
    cross_video_query,
    cross_video_keys,
    cross_video_values,
    cross_audio_query,
    cross_audio_keys,
    cross_audio_values,
    video_length,
    audio_length,
    align_offset,
):
    devices = lax.axis_size("seq")
    index = lax.axis_index("seq")
    video_rows = video_query.shape[0]
    audio_rows = audio_query.shape[0]
    video_total = video_rows * devices
    audio_total = audio_rows * devices
    video_reach = video_total // 8
    audio_reach = 5 * audio_total // 8
    video_valid = video_length[0]
    audio_valid = audio_length[0]
    align_shift = align_offset[0]
    copies = max(devices // HV, 1)
    video_places = jnp.arange(video_total, dtype=jnp.int32)
    audio_places = jnp.arange(audio_total, dtype=jnp.int32)

    def video_open(q_where, k_where):
        return k_where < video_valid

    def toward_video(q_where, k_where):
        center = jnp.clip(q_where * audio_total // video_total + align_shift, 0, audio_valid - 1)
        return (k_where < audio_valid) & (jnp.abs(k_where - center) <= audio_reach)

    def toward_audio(q_where, k_where):
        center = jnp.clip((q_where - align_shift) * video_total // audio_total, 0, video_valid - 1)
        return (k_where < video_valid) & (jnp.abs(k_where - center) <= video_reach)

    video_owned = (
        lax.all_to_all(
            split_heads(video_query, HV, HDV, copies),
            "seq",
            split_axis=0,
            concat_axis=1,
            tiled=True,
        ),
        lax.all_to_all(
            spread_heads(video_keys, HV, HDV, copies),
            "seq",
            split_axis=0,
            concat_axis=1,
            tiled=True,
        ),
        lax.all_to_all(
            spread_heads(video_values, HV, HDV, copies),
            "seq",
            split_axis=0,
            concat_axis=1,
            tiled=True,
        ),
    )
    video_done = attend_local(
        video_owned[0],
        video_owned[1],
        video_owned[2],
        owned_positions(video_rows, copies, devices, index),
        video_places,
        video_open,
    )
    video_mixed = join_heads(
        lax.all_to_all(video_done, "seq", split_axis=1, concat_axis=0, tiled=True), HV, HDV, copies
    )
    audio_local = audio_query.reshape(audio_rows, HA, HDA)
    piece = (
        lax.all_gather(audio_keys, "seq", axis=0, tiled=True),
        lax.all_gather(audio_values, "seq", axis=0, tiled=True),
    )
    k_where = jnp.arange(piece[0].shape[0], dtype=jnp.int32)
    audio_k_where = k_where[None, :]
    permit = audio_k_where < audio_valid
    audio_state = fold_piece(
        fold_initial(audio_rows, HA, HDA), audio_local, piece[0], piece[1], permit, HA, HDA
    )
    audio_mixed = fold_finish(audio_state, HA, HDA)
    cross_owned = (
        lax.all_to_all(
            split_heads(cross_video_query, HA, HDA, copies),
            "seq",
            split_axis=0,
            concat_axis=1,
            tiled=True,
        ),
        lax.all_to_all(
            spread_heads(cross_audio_keys, HA, HDA, copies),
            "seq",
            split_axis=0,
            concat_axis=1,
            tiled=True,
        ),
        lax.all_to_all(
            spread_heads(cross_audio_values, HA, HDA, copies),
            "seq",
            split_axis=0,
            concat_axis=1,
            tiled=True,
        ),
    )
    cross_done = attend_local(
        cross_owned[0],
        cross_owned[1],
        cross_owned[2],
        owned_positions(video_rows, copies, devices, index),
        audio_places,
        toward_video,
    )
    video_cross = join_heads(
        lax.all_to_all(cross_done, "seq", split_axis=1, concat_axis=0, tiled=True), HA, HDA, copies
    )
    listen_owned = (
        lax.all_to_all(
            split_heads(cross_audio_query, HA, HDA, copies),
            "seq",
            split_axis=0,
            concat_axis=1,
            tiled=True,
        ),
        lax.all_to_all(
            spread_heads(cross_video_keys, HA, HDA, copies),
            "seq",
            split_axis=0,
            concat_axis=1,
            tiled=True,
        ),
        lax.all_to_all(
            spread_heads(cross_video_values, HA, HDA, copies),
            "seq",
            split_axis=0,
            concat_axis=1,
            tiled=True,
        ),
    )
    listen_done = attend_local(
        listen_owned[0],
        listen_owned[1],
        listen_owned[2],
        owned_positions(audio_rows, copies, devices, index),
        video_places,
        toward_audio,
    )
    audio_cross = join_heads(
        lax.all_to_all(listen_done, "seq", split_axis=1, concat_axis=0, tiled=True), HA, HDA, copies
    )
    return (video_mixed, audio_mixed, video_cross, audio_cross)


LANES = 128


def pack_kernel(n, *refs):
    video, cross, audio, packed = refs[0:3], refs[3:6], refs[6:12], refs[12]
    parts = video[0].shape[1] // n // LANES
    rows = cross[0].shape[0]
    for d in range(n):
        at = 0
        for ref in video:
            for part in range(parts):
                packed[d, at : at + rows, :] = ref[:, (d * parts + part) * LANES : (d * parts + part + 1) * LANES]
                at += rows
        for ref in cross:
            packed[d, at : at + rows, :] = ref[:, d * LANES : (d + 1) * LANES]
            at += rows
        for first, second in zip(audio[0::2], audio[1::2]):
            pair = jnp.concatenate(
                [first[:, d * LANES : (d + 1) * LANES], second[:, d * LANES : (d + 1) * LANES]], axis=0
            )
            packed[d, at : at + pair.shape[0], :] = pair
            at += pair.shape[0]


def softmax_mix(query, key, value, scale, permit):
    scores = lax.dot_general(
        query, key, (((1,), (1,)), ((), ())), preferred_element_type=jnp.float32
    )
    scores = jnp.where(permit, scores * scale, -1e30)
    peak = jnp.max(scores, axis=1, keepdims=True)
    weights = jnp.exp(scores - peak)
    total = jnp.sum(weights, axis=1, keepdims=True)
    mixed = jnp.dot(weights.astype(jnp.bfloat16), value, preferred_element_type=jnp.float32)
    return mixed / total


def paired_mix(query, key, value, depth, permit):
    scale = 1.0 / math.sqrt(depth)
    lane = lax.broadcasted_iota(jnp.int32, query.shape, 1) // depth
    zero = jnp.zeros_like(query)
    result = None
    for h in range(LANES // depth):
        one = softmax_mix(jnp.where(lane == h, query, zero), key, value, scale, permit)
        result = one if h == 0 else jnp.where(lane == h, one, result)
    return result


def attend_kernel(n, rows, parts, video_len, audio_len, shift, got, done):
    half = rows // 2
    tv, ta = n * rows, n * half
    ratio = tv // ta
    bits = ratio.bit_length() - 1
    video_valid, audio_valid, offset = video_len[0], audio_len[0], shift[0]

    def slab(at):
        return got[:, at : at + rows, :].reshape(tv, LANES)

    def halves(at):
        both = got[:, at : at + rows, :].astype(jnp.float32)
        first = both[:, :half, :].reshape(ta, LANES).astype(jnp.bfloat16)
        second = both[:, half:, :].reshape(ta, LANES).astype(jnp.bfloat16)
        return first, second

    def places(q_count, k_count):
        return (
            lax.broadcasted_iota(jnp.int32, (q_count, k_count), 0),
            lax.broadcasted_iota(jnp.int32, (q_count, k_count), 1),
        )

    q_at, k_at = places(tv, tv)
    permit = k_at < video_valid
    for h in range(parts):
        mixed = softmax_mix(
            slab(h * rows),
            slab((parts + h) * rows),
            slab((2 * parts + h) * rows),
            1.0 / math.sqrt(HDV),
            permit,
        )
        done[:, h * rows : (h + 1) * rows, :] = mixed.astype(jnp.bfloat16).reshape(n, rows, LANES)
    at = 3 * parts * rows
    cross_query, cross_keys, cross_values = slab(at), slab(at + rows), slab(at + 2 * rows)
    at += 3 * rows
    audio_query, audio_keys = halves(at)
    audio_values, listen_query = halves(at + rows)
    sound_keys, sound_values = halves(at + 2 * rows)

    q_at, k_at = places(tv, ta)
    center = jnp.clip((q_at >> bits) + offset, 0, audio_valid - 1)
    permit = (k_at < audio_valid) & (jnp.abs(k_at - center) <= 5 * ta // 8)
    mixed = paired_mix(cross_query, sound_keys, sound_values, HDA, permit)
    out = parts * rows
    done[:, out : out + rows, :] = mixed.astype(jnp.bfloat16).reshape(n, rows, LANES)

    q_at, k_at = places(ta, ta)
    heard = paired_mix(audio_query, audio_keys, audio_values, HDA, k_at < audio_valid)
    q_at, k_at = places(ta, tv)
    center = jnp.clip((q_at - offset) * ratio, 0, video_valid - 1)
    permit = (k_at < video_valid) & (jnp.abs(k_at - center) <= tv // 8)
    listened = paired_mix(listen_query, cross_keys, cross_values, HDA, permit)
    both = jnp.concatenate(
        [heard.reshape(n, half, LANES), listened.reshape(n, half, LANES)], axis=1
    )
    out += rows
    done[:, out : out + rows, :] = both.astype(jnp.bfloat16)


def unpack_kernel(n, back, video_mixed, audio_mixed, video_cross, audio_cross):
    rows = video_mixed.shape[0]
    half = audio_mixed.shape[0]
    parts = video_mixed.shape[1] // n // LANES
    for s in range(n):
        for h in range(parts):
            at = (s * parts + h) * LANES
            video_mixed[:, at : at + LANES] = back[s, h * rows : (h + 1) * rows, :]
        at = s * LANES
        out = parts * rows
        video_cross[:, at : at + LANES] = back[s, out : out + rows, :]
        both = back[s, out + rows : out + 2 * rows, :]
        audio_mixed[:, at : at + LANES] = both[:half, :]
        audio_cross[:, at : at + LANES] = both[half:, :]


def shards_packed(*arrays):
    (
        video_query, video_keys, video_values,
        audio_query, audio_keys, audio_values,
        cross_video_query, cross_video_keys, cross_video_values,
        cross_audio_query, cross_audio_keys, cross_audio_values,
        video_length, audio_length, align_offset,
    ) = arrays
    n = lax.axis_size("seq")
    rows, half = video_query.shape[0], audio_query.shape[0]
    parts = video_query.shape[1] // n // LANES
    vmem = pl.BlockSpec(memory_space=pltpu.VMEM)
    smem = pl.BlockSpec(memory_space=pltpu.SMEM)
    params = pltpu.CompilerParams(vmem_limit_bytes=32 * 1024 * 1024)
    in_rows = (3 * parts + 6) * rows
    out_rows = (parts + 2) * rows
    packed = pl.pallas_call(
        functools.partial(pack_kernel, n),
        out_shape=jax.ShapeDtypeStruct((n, in_rows, LANES), jnp.bfloat16),
        in_specs=[vmem] * 12,
        out_specs=vmem,
        compiler_params=params,
    )(
        video_query, video_keys, video_values,
        cross_video_query, cross_video_keys, cross_video_values,
        audio_query, audio_keys, audio_values,
        cross_audio_query, cross_audio_keys, cross_audio_values,
    )
    got = lax.all_to_all(packed, "seq", split_axis=0, concat_axis=0, tiled=True)
    done = pl.pallas_call(
        functools.partial(attend_kernel, n, rows, parts),
        out_shape=jax.ShapeDtypeStruct((n, out_rows, LANES), jnp.bfloat16),
        in_specs=[smem] * 3 + [vmem],
        out_specs=vmem,
        compiler_params=params,
    )(video_length, audio_length, align_offset, got)
    back = lax.all_to_all(done, "seq", split_axis=0, concat_axis=0, tiled=True)
    return pl.pallas_call(
        functools.partial(unpack_kernel, n),
        out_shape=(
            jax.ShapeDtypeStruct(video_query.shape, jnp.bfloat16),
            jax.ShapeDtypeStruct(audio_query.shape, jnp.bfloat16),
            jax.ShapeDtypeStruct(cross_video_query.shape, jnp.bfloat16),
            jax.ShapeDtypeStruct(cross_audio_query.shape, jnp.bfloat16),
        ),
        in_specs=[vmem],
        out_specs=(vmem,) * 4,
        compiler_params=params,
    )(back)


def shards(*arrays):
    n = lax.axis_size("seq")
    rows, half = arrays[0].shape[0], arrays[3].shape[0]
    fits = (
        arrays[0].shape[1] % (n * LANES) == 0
        and arrays[3].shape[1] == n * LANES
        and HDV == LANES
        and LANES % HDA == 0
        and rows == 2 * half
        and half % 8 == 0
    )
    return shards_packed(*arrays) if fits else shards_general(*arrays)


def solution(mesh):
    placed = (
        P(("clip", "seq"), None),
        P(("clip", "seq"), None),
        P(("clip", "seq"), None),
        P(("clip", "seq"), None),
        P(("clip", "seq"), None),
        P(("clip", "seq"), None),
        P(("clip", "seq"), None),
        P(("clip", "seq"), None),
        P(("clip", "seq"), None),
        P(("clip", "seq"), None),
        P(("clip", "seq"), None),
        P(("clip", "seq"), None),
        P("clip"),
        P("clip"),
        P("clip"),
    )
    return jax.shard_map(
        shards,
        mesh=mesh,
        in_specs=placed,
        out_specs=(
            P(("clip", "seq"), None),
            P(("clip", "seq"), None),
            P(("clip", "seq"), None),
            P(("clip", "seq"), None),
        ),
        check_vma=False,
    )
```

```python
import functools
import math

import jax
import jax.numpy as jnp
from jax import lax
from jax.experimental import pallas as pl
from jax.experimental.pallas import tpu as pltpu
from jax.sharding import PartitionSpec as P

HV = 32
HDV = 128
HA = 32
HDA = 64


def block_size(total, limit):
    chosen = min(total, limit)
    while total % chosen:
        chosen -= 1
    return chosen


def split_heads(tokens, heads, depth, copies):
    rows = tokens.shape[0]
    shaped = tokens.reshape(copies, rows // copies, heads, depth).transpose(2, 0, 1, 3)
    return shaped.reshape(heads * copies, rows // copies, depth)


def spread_heads(tokens, heads, depth, copies):
    rows = tokens.shape[0]
    shaped = tokens.reshape(rows, heads, depth).transpose(1, 0, 2)
    shaped = jnp.broadcast_to(shaped[:, None], (heads, copies, rows, depth))
    return shaped.reshape(heads * copies, rows, depth)


def join_heads(owned, heads, depth, copies):
    part_rows = owned.shape[1]
    shaped = owned.reshape(heads, copies, part_rows, depth).transpose(1, 2, 0, 3)
    return shaped.reshape(copies * part_rows, heads * depth)


def owned_positions(rows, copies, devices, index):
    part_rows = rows // copies
    flat = jnp.arange(devices * part_rows, dtype=jnp.int32)
    return flat // part_rows * rows + index % copies * part_rows + flat % part_rows


def online_update(carry, scores, permit, value_tile, value_form):
    running, total, accum = carry
    scores = jnp.where(permit, scores, -1e30)
    newmax = jnp.maximum(running, jnp.max(scores, axis=2))
    weights = jnp.where(permit, jnp.exp(scores - newmax[:, :, None]), 0.0)
    factor = jnp.exp(running - newmax)
    total = total * factor + jnp.sum(weights, axis=2)
    mixed = jnp.einsum(
        value_form, weights.astype(jnp.bfloat16), value_tile, preferred_element_type=jnp.float32
    )
    accum = accum * factor[:, :, None] + mixed
    return (newmax, total, accum)


def fold_initial(rows, heads, depth):
    return (
        jnp.full((heads, rows), -1e30, jnp.float32),
        jnp.zeros((heads, rows), jnp.float32),
        jnp.zeros((heads, rows, depth), jnp.float32),
    )


def fold_piece(carry, local_query, key_rows, value_rows, permit, heads, depth):
    keyed = key_rows.reshape(key_rows.shape[0], heads, depth)
    valued = value_rows.reshape(value_rows.shape[0], heads, depth)
    scores = jnp.einsum("qhd,khd->hqk", local_query, keyed, preferred_element_type=jnp.float32) * (
        1.0 / math.sqrt(depth)
    )
    return online_update(carry, scores, permit[None], valued, "hqk,khd->hqd")


def fold_finish(carry, heads, depth):
    running, total, accum = carry
    result = (accum / total[:, :, None]).astype(jnp.bfloat16)
    return result.transpose(1, 0, 2).reshape(result.shape[1], heads * depth)


def attend_local(queries, keys, values, query_pos, key_pos, allowed):
    heads, q_count, depth = queries.shape
    k_count = keys.shape[1]
    q_block = block_size(q_count, 512)
    k_block = block_size(k_count, 2048)
    scale = 1.0 / math.sqrt(depth)
    q_tiles = queries.reshape(heads, q_count // q_block, q_block, depth).transpose(1, 0, 2, 3)
    k_tiles = keys.reshape(heads, k_count // k_block, k_block, depth).transpose(1, 0, 2, 3)
    v_tiles = values.reshape(heads, k_count // k_block, k_block, depth).transpose(1, 0, 2, 3)
    q_places = query_pos.reshape(q_count // q_block, q_block)
    k_places = key_pos.reshape(k_count // k_block, k_block)

    def one_tile(packed):
        q_tile, q_where = packed

        def absorb(carry, piece):
            k_tile, v_tile, k_where = piece
            scores = (
                jnp.einsum("hqd,hkd->hqk", q_tile, k_tile, preferred_element_type=jnp.float32)
                * scale
            )
            permit = allowed(q_where[:, None], k_where[None, :])[None]
            return (online_update(carry, scores, permit, v_tile, "hqk,hkd->hqd"), None)

        initial = fold_initial(q_block, heads, depth)
        final_state, unused = lax.scan(absorb, initial, (k_tiles, v_tiles, k_places))
        running, total, accum = final_state
        return (accum / total[:, :, None]).astype(jnp.bfloat16)

    tiles = lax.map(one_tile, (q_tiles, q_places))
    return tiles.transpose(1, 0, 2, 3).reshape(heads, q_count, depth)


def shards_general(
    video_query,
    video_keys,
    video_values,
    audio_query,
    audio_keys,
    audio_values,
    cross_video_query,
    cross_video_keys,
    cross_video_values,
    cross_audio_query,
    cross_audio_keys,
    cross_audio_values,
    video_length,
    audio_length,
    align_offset,
):
    devices = lax.axis_size("seq")
    index = lax.axis_index("seq")
    video_rows = video_query.shape[0]
    audio_rows = audio_query.shape[0]
    video_total = video_rows * devices
    audio_total = audio_rows * devices
    video_reach = video_total // 8
    audio_reach = 5 * audio_total // 8
    video_valid = video_length[0]
    audio_valid = audio_length[0]
    align_shift = align_offset[0]
    copies = max(devices // HV, 1)
    video_places = jnp.arange(video_total, dtype=jnp.int32)
    audio_places = jnp.arange(audio_total, dtype=jnp.int32)

    def video_open(q_where, k_where):
        return k_where < video_valid

    def toward_video(q_where, k_where):
        center = jnp.clip(q_where * audio_total // video_total + align_shift, 0, audio_valid - 1)
        return (k_where < audio_valid) & (jnp.abs(k_where - center) <= audio_reach)

    def toward_audio(q_where, k_where):
        center = jnp.clip((q_where - align_shift) * video_total // audio_total, 0, video_valid - 1)
        return (k_where < video_valid) & (jnp.abs(k_where - center) <= video_reach)

    video_owned = (
        lax.all_to_all(
            split_heads(video_query, HV, HDV, copies),
            "seq",
            split_axis=0,
            concat_axis=1,
            tiled=True,
        ),
        lax.all_to_all(
            spread_heads(video_keys, HV, HDV, copies),
            "seq",
            split_axis=0,
            concat_axis=1,
            tiled=True,
        ),
        lax.all_to_all(
            spread_heads(video_values, HV, HDV, copies),
            "seq",
            split_axis=0,
            concat_axis=1,
            tiled=True,
        ),
    )
    video_done = attend_local(
        video_owned[0],
        video_owned[1],
        video_owned[2],
        owned_positions(video_rows, copies, devices, index),
        video_places,
        video_open,
    )
    video_mixed = join_heads(
        lax.all_to_all(video_done, "seq", split_axis=1, concat_axis=0, tiled=True), HV, HDV, copies
    )
    audio_local = audio_query.reshape(audio_rows, HA, HDA)
    piece = (
        lax.all_gather(audio_keys, "seq", axis=0, tiled=True),
        lax.all_gather(audio_values, "seq", axis=0, tiled=True),
    )
    k_where = jnp.arange(piece[0].shape[0], dtype=jnp.int32)
    audio_k_where = k_where[None, :]
    permit = audio_k_where < audio_valid
    audio_state = fold_piece(
        fold_initial(audio_rows, HA, HDA), audio_local, piece[0], piece[1], permit, HA, HDA
    )
    audio_mixed = fold_finish(audio_state, HA, HDA)
    cross_owned = (
        lax.all_to_all(
            split_heads(cross_video_query, HA, HDA, copies),
            "seq",
            split_axis=0,
            concat_axis=1,
            tiled=True,
        ),
        lax.all_to_all(
            spread_heads(cross_audio_keys, HA, HDA, copies),
            "seq",
            split_axis=0,
            concat_axis=1,
            tiled=True,
        ),
        lax.all_to_all(
            spread_heads(cross_audio_values, HA, HDA, copies),
            "seq",
            split_axis=0,
            concat_axis=1,
            tiled=True,
        ),
    )
    cross_done = attend_local(
        cross_owned[0],
        cross_owned[1],
        cross_owned[2],
        owned_positions(video_rows, copies, devices, index),
        audio_places,
        toward_video,
    )
    video_cross = join_heads(
        lax.all_to_all(cross_done, "seq", split_axis=1, concat_axis=0, tiled=True), HA, HDA, copies
    )
    listen_owned = (
        lax.all_to_all(
            split_heads(cross_audio_query, HA, HDA, copies),
            "seq",
            split_axis=0,
            concat_axis=1,
            tiled=True,
        ),
        lax.all_to_all(
            spread_heads(cross_video_keys, HA, HDA, copies),
            "seq",
            split_axis=0,
            concat_axis=1,
            tiled=True,
        ),
        lax.all_to_all(
            spread_heads(cross_video_values, HA, HDA, copies),
            "seq",
            split_axis=0,
            concat_axis=1,
            tiled=True,
        ),
    )
    listen_done = attend_local(
        listen_owned[0],
        listen_owned[1],
        listen_owned[2],
        owned_positions(audio_rows, copies, devices, index),
        video_places,
        toward_audio,
    )
    audio_cross = join_heads(
        lax.all_to_all(listen_done, "seq", split_axis=1, concat_axis=0, tiled=True), HA, HDA, copies
    )
    return (video_mixed, audio_mixed, video_cross, audio_cross)


LANES = 128


def pack_kernel(n, *refs):
    sources, packed, held, arrived = refs[0:12], refs[12], refs[13:25], refs[25]
    copies = [
        pltpu.make_async_copy(source, slot, arrived.at[i])
        for i, (source, slot) in enumerate(zip(sources, held))
    ]
    for copy in copies:
        copy.start()
    video, cross, audio = held[0:3], held[3:6], held[6:12]
    parts = video[0].shape[1] // n // LANES
    rows = cross[0].shape[0]
    at = 0
    for i, ref in enumerate(video):
        copies[i].wait()
        for part in range(parts):
            for d in range(n):
                packed[d, at : at + rows, :] = ref[:, (d * parts + part) * LANES : (d * parts + part + 1) * LANES]
            at += rows
    for i, ref in enumerate(cross):
        copies[3 + i].wait()
        for d in range(n):
            packed[d, at : at + rows, :] = ref[:, d * LANES : (d + 1) * LANES]
        at += rows
    for i in range(0, 6, 2):
        copies[6 + i].wait()
        copies[7 + i].wait()
        for d in range(n):
            pair = jnp.concatenate(
                [
                    audio[i][:, d * LANES : (d + 1) * LANES],
                    audio[i + 1][:, d * LANES : (d + 1) * LANES],
                ],
                axis=0,
            )
            packed[d, at : at + pair.shape[0], :] = pair
        at += rows


def softmax_mix(query, key, value, scale, permit):
    scores = lax.dot_general(
        query, key, (((1,), (1,)), ((), ())), preferred_element_type=jnp.float32
    )
    scores = jnp.where(permit, scores * scale, -1e30)
    peak = jnp.max(scores, axis=1, keepdims=True)
    weights = jnp.exp(scores - peak)
    total = jnp.sum(weights, axis=1, keepdims=True)
    mixed = jnp.dot(weights.astype(jnp.bfloat16), value, preferred_element_type=jnp.float32)
    return mixed / total


def paired_mix(query, key, value, depth, permit):
    scale = 1.0 / math.sqrt(depth)
    lane = lax.broadcasted_iota(jnp.int32, query.shape, 1) // depth
    zero = jnp.zeros_like(query)
    result = None
    for h in range(LANES // depth):
        one = softmax_mix(jnp.where(lane == h, query, zero), key, value, scale, permit)
        result = one if h == 0 else jnp.where(lane == h, one, result)
    return result


def attend_kernel(n, rows, parts, video_len, audio_len, shift, got, done):
    half = rows // 2
    tv, ta = n * rows, n * half
    ratio = tv // ta
    bits = ratio.bit_length() - 1
    video_valid, audio_valid, offset = video_len[0], audio_len[0], shift[0]

    def slab(at):
        return got[:, at : at + rows, :].reshape(tv, LANES)

    def halves(at):
        both = got[:, at : at + rows, :].astype(jnp.float32)
        first = both[:, :half, :].reshape(ta, LANES).astype(jnp.bfloat16)
        second = both[:, half:, :].reshape(ta, LANES).astype(jnp.bfloat16)
        return first, second

    def places(q_count, k_count):
        return (
            lax.broadcasted_iota(jnp.int32, (q_count, k_count), 0),
            lax.broadcasted_iota(jnp.int32, (q_count, k_count), 1),
        )

    q_at, k_at = places(tv, tv)
    permit = k_at < video_valid
    for h in range(parts):
        mixed = softmax_mix(
            slab(h * rows),
            slab((parts + h) * rows),
            slab((2 * parts + h) * rows),
            1.0 / math.sqrt(HDV),
            permit,
        )
        done[:, h * rows : (h + 1) * rows, :] = mixed.astype(jnp.bfloat16).reshape(n, rows, LANES)
    at = 3 * parts * rows
    cross_query, cross_keys, cross_values = slab(at), slab(at + rows), slab(at + 2 * rows)
    at += 3 * rows
    audio_query, audio_keys = halves(at)
    audio_values, listen_query = halves(at + rows)
    sound_keys, sound_values = halves(at + 2 * rows)

    q_at, k_at = places(tv, ta)
    center = jnp.clip((q_at >> bits) + offset, 0, audio_valid - 1)
    permit = (k_at < audio_valid) & (jnp.abs(k_at - center) <= 5 * ta // 8)
    mixed = paired_mix(cross_query, sound_keys, sound_values, HDA, permit)
    out = parts * rows
    done[:, out : out + rows, :] = mixed.astype(jnp.bfloat16).reshape(n, rows, LANES)

    q_at, k_at = places(ta, ta)
    heard = paired_mix(audio_query, audio_keys, audio_values, HDA, k_at < audio_valid)
    q_at, k_at = places(ta, tv)
    center = jnp.clip((q_at - offset) * ratio, 0, video_valid - 1)
    permit = (k_at < video_valid) & (jnp.abs(k_at - center) <= tv // 8)
    listened = paired_mix(listen_query, cross_keys, cross_values, HDA, permit)
    both = jnp.concatenate(
        [heard.reshape(n, half, LANES), listened.reshape(n, half, LANES)], axis=1
    )
    out += rows
    done[:, out : out + rows, :] = both.astype(jnp.bfloat16)


def unpack_kernel(n, back, video_mixed, audio_mixed, video_cross, audio_cross):
    rows = video_mixed.shape[0]
    half = audio_mixed.shape[0]
    parts = video_mixed.shape[1] // n // LANES
    for s in range(n):
        for h in range(parts):
            at = (s * parts + h) * LANES
            video_mixed[:, at : at + LANES] = back[s, h * rows : (h + 1) * rows, :]
        at = s * LANES
        out = parts * rows
        video_cross[:, at : at + LANES] = back[s, out : out + rows, :]
        both = back[s, out + rows : out + 2 * rows, :]
        audio_mixed[:, at : at + LANES] = both[:half, :]
        audio_cross[:, at : at + LANES] = both[half:, :]


def shards_packed(*arrays):
    (
        video_query, video_keys, video_values,
        audio_query, audio_keys, audio_values,
        cross_video_query, cross_video_keys, cross_video_values,
        cross_audio_query, cross_audio_keys, cross_audio_values,
        video_length, audio_length, align_offset,
    ) = arrays
    n = lax.axis_size("seq")
    rows, half = video_query.shape[0], audio_query.shape[0]
    parts = video_query.shape[1] // n // LANES
    vmem = pl.BlockSpec(memory_space=pltpu.VMEM)
    smem = pl.BlockSpec(memory_space=pltpu.SMEM)
    params = pltpu.CompilerParams(vmem_limit_bytes=32 * 1024 * 1024)
    in_rows = (3 * parts + 6) * rows
    out_rows = (parts + 2) * rows
    sources = (
        video_query, video_keys, video_values,
        cross_video_query, cross_video_keys, cross_video_values,
        audio_query, audio_keys, audio_values,
        cross_audio_query, cross_audio_keys, cross_audio_values,
    )
    packed = pl.pallas_call(
        functools.partial(pack_kernel, n),
        out_shape=jax.ShapeDtypeStruct((n, in_rows, LANES), jnp.bfloat16),
        in_specs=[pl.BlockSpec(memory_space=pltpu.HBM)] * 12,
        out_specs=vmem,
        scratch_shapes=[pltpu.VMEM(source.shape, source.dtype) for source in sources]
        + [pltpu.SemaphoreType.DMA((12,))],
        compiler_params=pltpu.CompilerParams(vmem_limit_bytes=60 * 1024 * 1024),
    )(*sources)
    got = lax.all_to_all(packed, "seq", split_axis=0, concat_axis=0, tiled=True)
    done = pl.pallas_call(
        functools.partial(attend_kernel, n, rows, parts),
        out_shape=jax.ShapeDtypeStruct((n, out_rows, LANES), jnp.bfloat16),
        in_specs=[smem] * 3 + [vmem],
        out_specs=vmem,
        compiler_params=params,
    )(video_length, audio_length, align_offset, got)
    back = lax.all_to_all(done, "seq", split_axis=0, concat_axis=0, tiled=True)
    return pl.pallas_call(
        functools.partial(unpack_kernel, n),
        out_shape=(
            jax.ShapeDtypeStruct(video_query.shape, jnp.bfloat16),
            jax.ShapeDtypeStruct(audio_query.shape, jnp.bfloat16),
            jax.ShapeDtypeStruct(cross_video_query.shape, jnp.bfloat16),
            jax.ShapeDtypeStruct(cross_audio_query.shape, jnp.bfloat16),
        ),
        in_specs=[vmem],
        out_specs=(vmem,) * 4,
        compiler_params=params,
    )(back)


def shards(*arrays):
    n = lax.axis_size("seq")
    rows, half = arrays[0].shape[0], arrays[3].shape[0]
    fits = (
        arrays[0].shape[1] % (n * LANES) == 0
        and arrays[3].shape[1] == n * LANES
        and HDV == LANES
        and LANES % HDA == 0
        and rows == 2 * half
        and half % 8 == 0
    )
    return shards_packed(*arrays) if fits else shards_general(*arrays)


def solution(mesh):
    placed = (
        P(("clip", "seq"), None),
        P(("clip", "seq"), None),
        P(("clip", "seq"), None),
        P(("clip", "seq"), None),
        P(("clip", "seq"), None),
        P(("clip", "seq"), None),
        P(("clip", "seq"), None),
        P(("clip", "seq"), None),
        P(("clip", "seq"), None),
        P(("clip", "seq"), None),
        P(("clip", "seq"), None),
        P(("clip", "seq"), None),
        P("clip"),
        P("clip"),
        P("clip"),
    )
    return jax.shard_map(
        shards,
        mesh=mesh,
        in_specs=placed,
        out_specs=(
            P(("clip", "seq"), None),
            P(("clip", "seq"), None),
            P(("clip", "seq"), None),
            P(("clip", "seq"), None),
        ),
        check_vma=False,
    )
```

```python
import functools
import math

import jax
import jax.numpy as jnp
from jax import lax
from jax.experimental import pallas as pl
from jax.experimental.pallas import tpu as pltpu
from jax.sharding import PartitionSpec as P

HV = 32
HDV = 128
HA = 32
HDA = 64


def block_size(total, limit):
    chosen = min(total, limit)
    while total % chosen:
        chosen -= 1
    return chosen


def split_heads(tokens, heads, depth, copies):
    rows = tokens.shape[0]
    shaped = tokens.reshape(copies, rows // copies, heads, depth).transpose(2, 0, 1, 3)
    return shaped.reshape(heads * copies, rows // copies, depth)


def spread_heads(tokens, heads, depth, copies):
    rows = tokens.shape[0]
    shaped = tokens.reshape(rows, heads, depth).transpose(1, 0, 2)
    shaped = jnp.broadcast_to(shaped[:, None], (heads, copies, rows, depth))
    return shaped.reshape(heads * copies, rows, depth)


def join_heads(owned, heads, depth, copies):
    part_rows = owned.shape[1]
    shaped = owned.reshape(heads, copies, part_rows, depth).transpose(1, 2, 0, 3)
    return shaped.reshape(copies * part_rows, heads * depth)


def owned_positions(rows, copies, devices, index):
    part_rows = rows // copies
    flat = jnp.arange(devices * part_rows, dtype=jnp.int32)
    return flat // part_rows * rows + index % copies * part_rows + flat % part_rows


def online_update(carry, scores, permit, value_tile, value_form):
    running, total, accum = carry
    scores = jnp.where(permit, scores, -1e30)
    newmax = jnp.maximum(running, jnp.max(scores, axis=2))
    weights = jnp.where(permit, jnp.exp(scores - newmax[:, :, None]), 0.0)
    factor = jnp.exp(running - newmax)
    total = total * factor + jnp.sum(weights, axis=2)
    mixed = jnp.einsum(
        value_form, weights.astype(jnp.bfloat16), value_tile, preferred_element_type=jnp.float32
    )
    accum = accum * factor[:, :, None] + mixed
    return (newmax, total, accum)


def fold_initial(rows, heads, depth):
    return (
        jnp.full((heads, rows), -1e30, jnp.float32),
        jnp.zeros((heads, rows), jnp.float32),
        jnp.zeros((heads, rows, depth), jnp.float32),
    )


def fold_piece(carry, local_query, key_rows, value_rows, permit, heads, depth):
    keyed = key_rows.reshape(key_rows.shape[0], heads, depth)
    valued = value_rows.reshape(value_rows.shape[0], heads, depth)
    scores = jnp.einsum("qhd,khd->hqk", local_query, keyed, preferred_element_type=jnp.float32) * (
        1.0 / math.sqrt(depth)
    )
    return online_update(carry, scores, permit[None], valued, "hqk,khd->hqd")


def fold_finish(carry, heads, depth):
    running, total, accum = carry
    result = (accum / total[:, :, None]).astype(jnp.bfloat16)
    return result.transpose(1, 0, 2).reshape(result.shape[1], heads * depth)


def attend_local(queries, keys, values, query_pos, key_pos, allowed):
    heads, q_count, depth = queries.shape
    k_count = keys.shape[1]
    q_block = block_size(q_count, 512)
    k_block = block_size(k_count, 2048)
    scale = 1.0 / math.sqrt(depth)
    q_tiles = queries.reshape(heads, q_count // q_block, q_block, depth).transpose(1, 0, 2, 3)
    k_tiles = keys.reshape(heads, k_count // k_block, k_block, depth).transpose(1, 0, 2, 3)
    v_tiles = values.reshape(heads, k_count // k_block, k_block, depth).transpose(1, 0, 2, 3)
    q_places = query_pos.reshape(q_count // q_block, q_block)
    k_places = key_pos.reshape(k_count // k_block, k_block)

    def one_tile(packed):
        q_tile, q_where = packed

        def absorb(carry, piece):
            k_tile, v_tile, k_where = piece
            scores = (
                jnp.einsum("hqd,hkd->hqk", q_tile, k_tile, preferred_element_type=jnp.float32)
                * scale
            )
            permit = allowed(q_where[:, None], k_where[None, :])[None]
            return (online_update(carry, scores, permit, v_tile, "hqk,hkd->hqd"), None)

        initial = fold_initial(q_block, heads, depth)
        final_state, unused = lax.scan(absorb, initial, (k_tiles, v_tiles, k_places))
        running, total, accum = final_state
        return (accum / total[:, :, None]).astype(jnp.bfloat16)

    tiles = lax.map(one_tile, (q_tiles, q_places))
    return tiles.transpose(1, 0, 2, 3).reshape(heads, q_count, depth)


def shards_general(
    video_query,
    video_keys,
    video_values,
    audio_query,
    audio_keys,
    audio_values,
    cross_video_query,
    cross_video_keys,
    cross_video_values,
    cross_audio_query,
    cross_audio_keys,
    cross_audio_values,
    video_length,
    audio_length,
    align_offset,
):
    devices = lax.axis_size("seq")
    index = lax.axis_index("seq")
    video_rows = video_query.shape[0]
    audio_rows = audio_query.shape[0]
    video_total = video_rows * devices
    audio_total = audio_rows * devices
    video_reach = video_total // 8
    audio_reach = 5 * audio_total // 8
    video_valid = video_length[0]
    audio_valid = audio_length[0]
    align_shift = align_offset[0]
    copies = max(devices // HV, 1)
    video_places = jnp.arange(video_total, dtype=jnp.int32)
    audio_places = jnp.arange(audio_total, dtype=jnp.int32)

    def video_open(q_where, k_where):
        return k_where < video_valid

    def toward_video(q_where, k_where):
        center = jnp.clip(q_where * audio_total // video_total + align_shift, 0, audio_valid - 1)
        return (k_where < audio_valid) & (jnp.abs(k_where - center) <= audio_reach)

    def toward_audio(q_where, k_where):
        center = jnp.clip((q_where - align_shift) * video_total // audio_total, 0, video_valid - 1)
        return (k_where < video_valid) & (jnp.abs(k_where - center) <= video_reach)

    video_owned = (
        lax.all_to_all(
            split_heads(video_query, HV, HDV, copies),
            "seq",
            split_axis=0,
            concat_axis=1,
            tiled=True,
        ),
        lax.all_to_all(
            spread_heads(video_keys, HV, HDV, copies),
            "seq",
            split_axis=0,
            concat_axis=1,
            tiled=True,
        ),
        lax.all_to_all(
            spread_heads(video_values, HV, HDV, copies),
            "seq",
            split_axis=0,
            concat_axis=1,
            tiled=True,
        ),
    )
    video_done = attend_local(
        video_owned[0],
        video_owned[1],
        video_owned[2],
        owned_positions(video_rows, copies, devices, index),
        video_places,
        video_open,
    )
    video_mixed = join_heads(
        lax.all_to_all(video_done, "seq", split_axis=1, concat_axis=0, tiled=True), HV, HDV, copies
    )
    audio_local = audio_query.reshape(audio_rows, HA, HDA)
    piece = (
        lax.all_gather(audio_keys, "seq", axis=0, tiled=True),
        lax.all_gather(audio_values, "seq", axis=0, tiled=True),
    )
    k_where = jnp.arange(piece[0].shape[0], dtype=jnp.int32)
    audio_k_where = k_where[None, :]
    permit = audio_k_where < audio_valid
    audio_state = fold_piece(
        fold_initial(audio_rows, HA, HDA), audio_local, piece[0], piece[1], permit, HA, HDA
    )
    audio_mixed = fold_finish(audio_state, HA, HDA)
    cross_owned = (
        lax.all_to_all(
            split_heads(cross_video_query, HA, HDA, copies),
            "seq",
            split_axis=0,
            concat_axis=1,
            tiled=True,
        ),
        lax.all_to_all(
            spread_heads(cross_audio_keys, HA, HDA, copies),
            "seq",
            split_axis=0,
            concat_axis=1,
            tiled=True,
        ),
        lax.all_to_all(
            spread_heads(cross_audio_values, HA, HDA, copies),
            "seq",
            split_axis=0,
            concat_axis=1,
            tiled=True,
        ),
    )
    cross_done = attend_local(
        cross_owned[0],
        cross_owned[1],
        cross_owned[2],
        owned_positions(video_rows, copies, devices, index),
        audio_places,
        toward_video,
    )
    video_cross = join_heads(
        lax.all_to_all(cross_done, "seq", split_axis=1, concat_axis=0, tiled=True), HA, HDA, copies
    )
    listen_owned = (
        lax.all_to_all(
            split_heads(cross_audio_query, HA, HDA, copies),
            "seq",
            split_axis=0,
            concat_axis=1,
            tiled=True,
        ),
        lax.all_to_all(
            spread_heads(cross_video_keys, HA, HDA, copies),
            "seq",
            split_axis=0,
            concat_axis=1,
            tiled=True,
        ),
        lax.all_to_all(
            spread_heads(cross_video_values, HA, HDA, copies),
            "seq",
            split_axis=0,
            concat_axis=1,
            tiled=True,
        ),
    )
    listen_done = attend_local(
        listen_owned[0],
        listen_owned[1],
        listen_owned[2],
        owned_positions(audio_rows, copies, devices, index),
        video_places,
        toward_audio,
    )
    audio_cross = join_heads(
        lax.all_to_all(listen_done, "seq", split_axis=1, concat_axis=0, tiled=True), HA, HDA, copies
    )
    return (video_mixed, audio_mixed, video_cross, audio_cross)


LANES = 128


def pack_kernel(n, *refs):
    sources, packed, held, arrived = refs[0:12], refs[12 : 12 + n], refs[12 + n : 24 + n], refs[24 + n]
    copies = [
        pltpu.make_async_copy(source, slot, arrived.at[i])
        for i, (source, slot) in enumerate(zip(sources, held))
    ]
    for copy in copies:
        copy.start()
    me = lax.axis_index("seq")
    video, cross, audio = held[0:3], held[3:6], held[6:12]
    parts = video[0].shape[1] // n // LANES
    rows = cross[0].shape[0]

    def group(ref, k, count, part):
        at = pl.multiple_of(((me ^ k) * count + part) * LANES, LANES)
        return ref[:, pl.ds(at, LANES)]

    at = 0
    for i, ref in enumerate(video):
        copies[i].wait()
        for part in range(parts):
            for k in range(n):
                packed[k][at : at + rows, :] = group(ref, k, parts, part)
            at += rows
    for i, ref in enumerate(cross):
        copies[3 + i].wait()
        for k in range(n):
            packed[k][at : at + rows, :] = group(ref, k, 1, 0)
        at += rows
    for i in range(0, 6, 2):
        copies[6 + i].wait()
        copies[7 + i].wait()
        for k in range(n):
            pair = jnp.concatenate(
                [group(audio[i], k, 1, 0), group(audio[i + 1], k, 1, 0)], axis=0
            )
            packed[k][at : at + rows, :] = pair
        at += rows


def softmax_mix(query, key, value, scale, permit):
    scores = lax.dot_general(
        query, key, (((1,), (1,)), ((), ())), preferred_element_type=jnp.float32
    )
    scores = jnp.where(permit, scores * scale, -1e30)
    peak = jnp.max(scores, axis=1, keepdims=True)
    weights = jnp.exp(scores - peak)
    total = jnp.sum(weights, axis=1, keepdims=True)
    mixed = jnp.dot(weights.astype(jnp.bfloat16), value, preferred_element_type=jnp.float32)
    return mixed / total


def paired_mix(query, key, value, depth, permit):
    scale = 1.0 / math.sqrt(depth)
    lane = lax.broadcasted_iota(jnp.int32, query.shape, 1) // depth
    zero = jnp.zeros_like(query)
    result = None
    for h in range(LANES // depth):
        one = softmax_mix(jnp.where(lane == h, query, zero), key, value, scale, permit)
        result = one if h == 0 else jnp.where(lane == h, one, result)
    return result


def attend_kernel(n, rows, parts, video_len, audio_len, shift, *refs):
    got, done = refs[:n], refs[n:]
    half = rows // 2
    tv, ta = n * rows, n * half
    ratio = tv // ta
    bits = ratio.bit_length() - 1
    me = lax.axis_index("seq")
    video_valid, audio_valid, offset = video_len[0], audio_len[0], shift[0]

    def slab(at):
        return jnp.concatenate([ref[at : at + rows, :] for ref in got], axis=0)

    def halves(at):
        both = [ref[at : at + rows, :].astype(jnp.float32) for ref in got]
        first = jnp.concatenate([piece[:half] for piece in both], axis=0)
        second = jnp.concatenate([piece[half:] for piece in both], axis=0)
        return first.astype(jnp.bfloat16), second.astype(jnp.bfloat16)

    def places(q_count, k_count):
        return tuple(
            lax.broadcasted_iota(jnp.int32, (q_count, k_count), axis) ^ (me * (count // n))
            for axis, count in enumerate((q_count, k_count))
        )

    def put(at, mixed):
        for k in range(n):
            done[k][at : at + rows, :] = mixed[k * rows : (k + 1) * rows].astype(jnp.bfloat16)

    q_at, k_at = places(tv, tv)
    permit = k_at < video_valid
    for h in range(parts):
        mixed = softmax_mix(
            slab(h * rows),
            slab((parts + h) * rows),
            slab((2 * parts + h) * rows),
            1.0 / math.sqrt(HDV),
            permit,
        )
        put(h * rows, mixed)
    at = 3 * parts * rows
    cross_query, cross_keys, cross_values = slab(at), slab(at + rows), slab(at + 2 * rows)
    at += 3 * rows
    audio_query, audio_keys = halves(at)
    audio_values, listen_query = halves(at + rows)
    sound_keys, sound_values = halves(at + 2 * rows)

    q_at, k_at = places(tv, ta)
    center = jnp.clip((q_at >> bits) + offset, 0, audio_valid - 1)
    permit = (k_at < audio_valid) & (jnp.abs(k_at - center) <= 5 * ta // 8)
    put(parts * rows, paired_mix(cross_query, sound_keys, sound_values, HDA, permit))

    q_at, k_at = places(ta, ta)
    heard = paired_mix(audio_query, audio_keys, audio_values, HDA, k_at < audio_valid)
    q_at, k_at = places(ta, tv)
    center = jnp.clip((q_at - offset) * ratio, 0, video_valid - 1)
    permit = (k_at < video_valid) & (jnp.abs(k_at - center) <= tv // 8)
    listened = paired_mix(listen_query, cross_keys, cross_values, HDA, permit)
    for k in range(n):
        both = jnp.concatenate(
            [heard[k * half : (k + 1) * half], listened[k * half : (k + 1) * half]], axis=0
        )
        done[k][(parts + 1) * rows :, :] = both.astype(jnp.bfloat16)


def unpack_kernel(n, *refs):
    back, (video_mixed, audio_mixed, video_cross, audio_cross) = refs[:n], refs[n:]
    rows = video_mixed.shape[0]
    half = audio_mixed.shape[0]
    parts = video_mixed.shape[1] // n // LANES
    me = lax.axis_index("seq")
    for k in range(n):
        for h in range(parts):
            at = pl.multiple_of(((me ^ k) * parts + h) * LANES, LANES)
            video_mixed[:, pl.ds(at, LANES)] = back[k][h * rows : (h + 1) * rows, :]
        at = pl.multiple_of((me ^ k) * LANES, LANES)
        out = parts * rows
        video_cross[:, pl.ds(at, LANES)] = back[k][out : out + rows, :]
        both = back[k][out + rows : out + 2 * rows, :]
        audio_mixed[:, pl.ds(at, LANES)] = both[:half, :]
        audio_cross[:, pl.ds(at, LANES)] = both[half:, :]


def swap_pieces(pieces):
    n = len(pieces)
    order = sorted(range(1, n), key=lambda k: (k < n // 2, k))
    moved = {0: pieces[0]}
    for k in order:
        moved[k] = lax.ppermute(pieces[k], "seq", [(i, i ^ k) for i in range(n)])
    return [moved[k] for k in range(n)]


def shards_packed(*arrays):
    (
        video_query, video_keys, video_values,
        audio_query, audio_keys, audio_values,
        cross_video_query, cross_video_keys, cross_video_values,
        cross_audio_query, cross_audio_keys, cross_audio_values,
        video_length, audio_length, align_offset,
    ) = arrays
    n = lax.axis_size("seq")
    rows = video_query.shape[0]
    parts = video_query.shape[1] // n // LANES
    vmem = pl.BlockSpec(memory_space=pltpu.VMEM)
    smem = pl.BlockSpec(memory_space=pltpu.SMEM)
    params = pltpu.CompilerParams(vmem_limit_bytes=32 * 1024 * 1024)
    in_rows = (3 * parts + 6) * rows
    out_rows = (parts + 2) * rows
    sources = (
        video_query, video_keys, video_values,
        cross_video_query, cross_video_keys, cross_video_values,
        audio_query, audio_keys, audio_values,
        cross_audio_query, cross_audio_keys, cross_audio_values,
    )
    packed = pl.pallas_call(
        functools.partial(pack_kernel, n),
        out_shape=(jax.ShapeDtypeStruct((in_rows, LANES), jnp.bfloat16),) * n,
        in_specs=[pl.BlockSpec(memory_space=pltpu.HBM)] * 12,
        out_specs=(vmem,) * n,
        scratch_shapes=[pltpu.VMEM(source.shape, source.dtype) for source in sources]
        + [pltpu.SemaphoreType.DMA((12,))],
        compiler_params=pltpu.CompilerParams(vmem_limit_bytes=60 * 1024 * 1024),
    )(*sources)
    got = swap_pieces(packed)
    done = pl.pallas_call(
        functools.partial(attend_kernel, n, rows, parts),
        out_shape=(jax.ShapeDtypeStruct((out_rows, LANES), jnp.bfloat16),) * n,
        in_specs=[smem] * 3 + [vmem] * n,
        out_specs=(vmem,) * n,
        compiler_params=params,
    )(video_length, audio_length, align_offset, *got)
    back = swap_pieces(done)
    return pl.pallas_call(
        functools.partial(unpack_kernel, n),
        out_shape=(
            jax.ShapeDtypeStruct(video_query.shape, jnp.bfloat16),
            jax.ShapeDtypeStruct(audio_query.shape, jnp.bfloat16),
            jax.ShapeDtypeStruct(cross_video_query.shape, jnp.bfloat16),
            jax.ShapeDtypeStruct(cross_audio_query.shape, jnp.bfloat16),
        ),
        in_specs=[vmem] * n,
        out_specs=(vmem,) * 4,
        compiler_params=params,
    )(*back)


def shards(*arrays):
    n = lax.axis_size("seq")
    rows, half = arrays[0].shape[0], arrays[3].shape[0]
    fits = (
        arrays[0].shape[1] % (n * LANES) == 0
        and arrays[3].shape[1] == n * LANES
        and HDV == LANES
        and LANES % HDA == 0
        and rows == 2 * half
        and half % 8 == 0
        and n & (n - 1) == 0
        and half & (half - 1) == 0
    )
    return shards_packed(*arrays) if fits else shards_general(*arrays)


def solution(mesh):
    placed = (
        P(("clip", "seq"), None),
        P(("clip", "seq"), None),
        P(("clip", "seq"), None),
        P(("clip", "seq"), None),
        P(("clip", "seq"), None),
        P(("clip", "seq"), None),
        P(("clip", "seq"), None),
        P(("clip", "seq"), None),
        P(("clip", "seq"), None),
        P(("clip", "seq"), None),
        P(("clip", "seq"), None),
        P(("clip", "seq"), None),
        P("clip"),
        P("clip"),
        P("clip"),
    )
    return jax.shard_map(
        shards,
        mesh=mesh,
        in_specs=placed,
        out_specs=(
            P(("clip", "seq"), None),
            P(("clip", "seq"), None),
            P(("clip", "seq"), None),
            P(("clip", "seq"), None),
        ),
        check_vma=False,
    )
```

```python
import functools
import math

import jax
import jax.numpy as jnp
from jax import lax
from jax.experimental import pallas as pl
from jax.experimental.pallas import tpu as pltpu
from jax.sharding import PartitionSpec as P

HV = 32
HDV = 128
HA = 32
HDA = 64


def block_size(total, limit):
    chosen = min(total, limit)
    while total % chosen:
        chosen -= 1
    return chosen


def split_heads(tokens, heads, depth, copies):
    rows = tokens.shape[0]
    shaped = tokens.reshape(copies, rows // copies, heads, depth).transpose(2, 0, 1, 3)
    return shaped.reshape(heads * copies, rows // copies, depth)


def spread_heads(tokens, heads, depth, copies):
    rows = tokens.shape[0]
    shaped = tokens.reshape(rows, heads, depth).transpose(1, 0, 2)
    shaped = jnp.broadcast_to(shaped[:, None], (heads, copies, rows, depth))
    return shaped.reshape(heads * copies, rows, depth)


def join_heads(owned, heads, depth, copies):
    part_rows = owned.shape[1]
    shaped = owned.reshape(heads, copies, part_rows, depth).transpose(1, 2, 0, 3)
    return shaped.reshape(copies * part_rows, heads * depth)


def owned_positions(rows, copies, devices, index):
    part_rows = rows // copies
    flat = jnp.arange(devices * part_rows, dtype=jnp.int32)
    return flat // part_rows * rows + index % copies * part_rows + flat % part_rows


def online_update(carry, scores, permit, value_tile, value_form):
    running, total, accum = carry
    scores = jnp.where(permit, scores, -1e30)
    newmax = jnp.maximum(running, jnp.max(scores, axis=2))
    weights = jnp.where(permit, jnp.exp(scores - newmax[:, :, None]), 0.0)
    factor = jnp.exp(running - newmax)
    total = total * factor + jnp.sum(weights, axis=2)
    mixed = jnp.einsum(
        value_form, weights.astype(jnp.bfloat16), value_tile, preferred_element_type=jnp.float32
    )
    accum = accum * factor[:, :, None] + mixed
    return (newmax, total, accum)


def fold_initial(rows, heads, depth):
    return (
        jnp.full((heads, rows), -1e30, jnp.float32),
        jnp.zeros((heads, rows), jnp.float32),
        jnp.zeros((heads, rows, depth), jnp.float32),
    )


def fold_piece(carry, local_query, key_rows, value_rows, permit, heads, depth):
    keyed = key_rows.reshape(key_rows.shape[0], heads, depth)
    valued = value_rows.reshape(value_rows.shape[0], heads, depth)
    scores = jnp.einsum("qhd,khd->hqk", local_query, keyed, preferred_element_type=jnp.float32) * (
        1.0 / math.sqrt(depth)
    )
    return online_update(carry, scores, permit[None], valued, "hqk,khd->hqd")


def fold_finish(carry, heads, depth):
    running, total, accum = carry
    result = (accum / total[:, :, None]).astype(jnp.bfloat16)
    return result.transpose(1, 0, 2).reshape(result.shape[1], heads * depth)


def attend_local(queries, keys, values, query_pos, key_pos, allowed):
    heads, q_count, depth = queries.shape
    k_count = keys.shape[1]
    q_block = block_size(q_count, 512)
    k_block = block_size(k_count, 2048)
    scale = 1.0 / math.sqrt(depth)
    q_tiles = queries.reshape(heads, q_count // q_block, q_block, depth).transpose(1, 0, 2, 3)
    k_tiles = keys.reshape(heads, k_count // k_block, k_block, depth).transpose(1, 0, 2, 3)
    v_tiles = values.reshape(heads, k_count // k_block, k_block, depth).transpose(1, 0, 2, 3)
    q_places = query_pos.reshape(q_count // q_block, q_block)
    k_places = key_pos.reshape(k_count // k_block, k_block)

    def one_tile(packed):
        q_tile, q_where = packed

        def absorb(carry, piece):
            k_tile, v_tile, k_where = piece
            scores = (
                jnp.einsum("hqd,hkd->hqk", q_tile, k_tile, preferred_element_type=jnp.float32)
                * scale
            )
            permit = allowed(q_where[:, None], k_where[None, :])[None]
            return (online_update(carry, scores, permit, v_tile, "hqk,hkd->hqd"), None)

        initial = fold_initial(q_block, heads, depth)
        final_state, unused = lax.scan(absorb, initial, (k_tiles, v_tiles, k_places))
        running, total, accum = final_state
        return (accum / total[:, :, None]).astype(jnp.bfloat16)

    tiles = lax.map(one_tile, (q_tiles, q_places))
    return tiles.transpose(1, 0, 2, 3).reshape(heads, q_count, depth)


def shards_general(
    video_query,
    video_keys,
    video_values,
    audio_query,
    audio_keys,
    audio_values,
    cross_video_query,
    cross_video_keys,
    cross_video_values,
    cross_audio_query,
    cross_audio_keys,
    cross_audio_values,
    video_length,
    audio_length,
    align_offset,
):
    devices = lax.axis_size("seq")
    index = lax.axis_index("seq")
    video_rows = video_query.shape[0]
    audio_rows = audio_query.shape[0]
    video_total = video_rows * devices
    audio_total = audio_rows * devices
    video_reach = video_total // 8
    audio_reach = 5 * audio_total // 8
    video_valid = video_length[0]
    audio_valid = audio_length[0]
    align_shift = align_offset[0]
    copies = max(devices // HV, 1)
    video_places = jnp.arange(video_total, dtype=jnp.int32)
    audio_places = jnp.arange(audio_total, dtype=jnp.int32)

    def video_open(q_where, k_where):
        return k_where < video_valid

    def toward_video(q_where, k_where):
        center = jnp.clip(q_where * audio_total // video_total + align_shift, 0, audio_valid - 1)
        return (k_where < audio_valid) & (jnp.abs(k_where - center) <= audio_reach)

    def toward_audio(q_where, k_where):
        center = jnp.clip((q_where - align_shift) * video_total // audio_total, 0, video_valid - 1)
        return (k_where < video_valid) & (jnp.abs(k_where - center) <= video_reach)

    video_owned = (
        lax.all_to_all(
            split_heads(video_query, HV, HDV, copies),
            "seq",
            split_axis=0,
            concat_axis=1,
            tiled=True,
        ),
        lax.all_to_all(
            spread_heads(video_keys, HV, HDV, copies),
            "seq",
            split_axis=0,
            concat_axis=1,
            tiled=True,
        ),
        lax.all_to_all(
            spread_heads(video_values, HV, HDV, copies),
            "seq",
            split_axis=0,
            concat_axis=1,
            tiled=True,
        ),
    )
    video_done = attend_local(
        video_owned[0],
        video_owned[1],
        video_owned[2],
        owned_positions(video_rows, copies, devices, index),
        video_places,
        video_open,
    )
    video_mixed = join_heads(
        lax.all_to_all(video_done, "seq", split_axis=1, concat_axis=0, tiled=True), HV, HDV, copies
    )
    audio_local = audio_query.reshape(audio_rows, HA, HDA)
    piece = (
        lax.all_gather(audio_keys, "seq", axis=0, tiled=True),
        lax.all_gather(audio_values, "seq", axis=0, tiled=True),
    )
    k_where = jnp.arange(piece[0].shape[0], dtype=jnp.int32)
    audio_k_where = k_where[None, :]
    permit = audio_k_where < audio_valid
    audio_state = fold_piece(
        fold_initial(audio_rows, HA, HDA), audio_local, piece[0], piece[1], permit, HA, HDA
    )
    audio_mixed = fold_finish(audio_state, HA, HDA)
    cross_owned = (
        lax.all_to_all(
            split_heads(cross_video_query, HA, HDA, copies),
            "seq",
            split_axis=0,
            concat_axis=1,
            tiled=True,
        ),
        lax.all_to_all(
            spread_heads(cross_audio_keys, HA, HDA, copies),
            "seq",
            split_axis=0,
            concat_axis=1,
            tiled=True,
        ),
        lax.all_to_all(
            spread_heads(cross_audio_values, HA, HDA, copies),
            "seq",
            split_axis=0,
            concat_axis=1,
            tiled=True,
        ),
    )
    cross_done = attend_local(
        cross_owned[0],
        cross_owned[1],
        cross_owned[2],
        owned_positions(video_rows, copies, devices, index),
        audio_places,
        toward_video,
    )
    video_cross = join_heads(
        lax.all_to_all(cross_done, "seq", split_axis=1, concat_axis=0, tiled=True), HA, HDA, copies
    )
    listen_owned = (
        lax.all_to_all(
            split_heads(cross_audio_query, HA, HDA, copies),
            "seq",
            split_axis=0,
            concat_axis=1,
            tiled=True,
        ),
        lax.all_to_all(
            spread_heads(cross_video_keys, HA, HDA, copies),
            "seq",
            split_axis=0,
            concat_axis=1,
            tiled=True,
        ),
        lax.all_to_all(
            spread_heads(cross_video_values, HA, HDA, copies),
            "seq",
            split_axis=0,
            concat_axis=1,
            tiled=True,
        ),
    )
    listen_done = attend_local(
        listen_owned[0],
        listen_owned[1],
        listen_owned[2],
        owned_positions(audio_rows, copies, devices, index),
        video_places,
        toward_audio,
    )
    audio_cross = join_heads(
        lax.all_to_all(listen_done, "seq", split_axis=1, concat_axis=0, tiled=True), HA, HDA, copies
    )
    return (video_mixed, audio_mixed, video_cross, audio_cross)


LANES = 128


def by_step(items):
    return [items[-j % len(items)] for j in range(len(items))]


def pack_kernel(chips, *refs):
    sources, refs = refs[:12], refs[12:]
    packed, held, arrived = by_step(refs[:chips]), refs[chips : chips + 12], refs[chips + 12]
    copies = [
        pltpu.make_async_copy(source, slot, arrived.at[i])
        for i, (source, slot) in enumerate(zip(sources, held))
    ]
    for copy in copies:
        copy.start()
    chip = lax.axis_index("seq") // 2
    video, cross, audio = held[0:3], held[3:6], held[6:12]
    rows = video[0].shape[0]

    def group(ref, j, part):
        width = ref.shape[1] // chips
        at = pl.multiple_of((chip ^ j) * width + part * LANES, LANES)
        return ref[:, pl.ds(at, LANES)]

    at = 0
    for i, ref in enumerate(video + cross):
        copies[i].wait()
        for part in range(ref.shape[1] // chips // LANES):
            for j in range(chips):
                packed[j][at : at + rows, :] = group(ref, j, part)
            at += rows
    for i in range(0, 6, 2):
        copies[6 + i].wait()
        copies[7 + i].wait()
        for part in range(audio[i].shape[1] // chips // LANES):
            for j in range(chips):
                pair = jnp.concatenate(
                    [group(audio[i], j, part), group(audio[i + 1], j, part)], axis=0
                )
                packed[j][at : at + rows, :] = pair
            at += rows


def softmax_mix(query, key, value, scale, permit):
    scores = lax.dot_general(
        query, key, (((1,), (1,)), ((), ())), preferred_element_type=jnp.float32
    )
    scores = jnp.where(permit, scores * scale, -1e30)
    peak = jnp.max(scores, axis=1, keepdims=True)
    weights = jnp.exp(scores - peak)
    total = jnp.sum(weights, axis=1, keepdims=True)
    mixed = jnp.dot(weights.astype(jnp.bfloat16), value, preferred_element_type=jnp.float32)
    return mixed / total


def paired_mix(query, key, value, depth, permit):
    scale = 1.0 / math.sqrt(depth)
    lane = lax.broadcasted_iota(jnp.int32, query.shape, 1) // depth
    zero = jnp.zeros_like(query)
    result = None
    for h in range(LANES // depth):
        one = softmax_mix(jnp.where(lane == h, query, zero), key, value, scale, permit)
        result = one if h == 0 else jnp.where(lane == h, one, result)
    return result


def attend_kernel(chips, rows, parts, pairs, video_len, audio_len, shift, *refs):
    own, other, done = (by_step(refs[i * chips : (i + 1) * chips]) for i in range(3))
    every = [ref for both in zip(own, other) for ref in both]
    half = rows // 2
    tv, ta = 2 * chips * rows, 2 * chips * half
    ratio = tv // ta
    bits = ratio.bit_length() - 1
    me = lax.axis_index("seq")
    video_valid, audio_valid, offset = video_len[0], audio_len[0], shift[0]

    def slab(refs, at):
        return jnp.concatenate([ref[at : at + rows, :] for ref in refs], axis=0)

    def side(refs, at, second):
        wide = [ref[at : at + rows, :].astype(jnp.float32) for ref in refs]
        taken = [piece[half:] if second else piece[:half] for piece in wide]
        return jnp.concatenate(taken, axis=0).astype(jnp.bfloat16)

    def places(q_step, k_step):
        q_at = lax.broadcasted_iota(jnp.int32, (chips * q_step, 2 * chips * k_step), 0)
        q_at = (q_at // q_step * (2 * q_step) + q_at % q_step) ^ (me * q_step)
        k_at = lax.broadcasted_iota(jnp.int32, (chips * q_step, 2 * chips * k_step), 1)
        return q_at, k_at ^ (me * k_step)

    def put(at, mixed):
        for j in range(chips):
            done[j][at : at + rows, :] = mixed[j * rows : (j + 1) * rows].astype(jnp.bfloat16)

    q_at, k_at = places(rows, rows)
    permit = k_at < video_valid
    for h in range(parts):
        mixed = softmax_mix(
            slab(own, h * rows),
            slab(every, (parts + h) * rows),
            slab(every, (2 * parts + h) * rows),
            1.0 / math.sqrt(HDV),
            permit,
        )
        put(h * rows, mixed)

    cross = 3 * parts * rows
    audio = cross + 3 * pairs * rows
    q_at, k_at = places(rows, half)
    center = jnp.clip((q_at >> bits) + offset, 0, audio_valid - 1)
    toward_video = (k_at < audio_valid) & (jnp.abs(k_at - center) <= 5 * ta // 8)
    q_at, k_at = places(half, half)
    within_audio = k_at < audio_valid
    q_at, k_at = places(half, rows)
    center = jnp.clip((q_at - offset) * ratio, 0, video_valid - 1)
    toward_audio = (k_at < video_valid) & (jnp.abs(k_at - center) <= tv // 8)
    for p in range(pairs):
        at = cross + p * rows
        cross_query = slab(own, at)
        cross_keys = slab(every, at + pairs * rows)
        cross_values = slab(every, at + 2 * pairs * rows)
        at = audio + p * rows
        audio_query, audio_keys = side(own, at, False), side(every, at, True)
        at += pairs * rows
        audio_values, listen_query = side(every, at, False), side(own, at, True)
        at += pairs * rows
        sound_keys, sound_values = side(every, at, False), side(every, at, True)
        out = (parts + p) * rows
        put(out, paired_mix(cross_query, sound_keys, sound_values, HDA, toward_video))
        heard = paired_mix(audio_query, audio_keys, audio_values, HDA, within_audio)
        listened = paired_mix(listen_query, cross_keys, cross_values, HDA, toward_audio)
        out += pairs * rows
        for j in range(chips):
            both = jnp.concatenate(
                [heard[j * half : (j + 1) * half], listened[j * half : (j + 1) * half]], axis=0
            )
            done[j][out : out + rows, :] = both.astype(jnp.bfloat16)


def unpack_kernel(chips, *refs):
    back, (video_mixed, audio_mixed, video_cross, audio_cross) = by_step(refs[:chips]), refs[chips:]
    rows = video_mixed.shape[0]
    half = audio_mixed.shape[0]
    parts = video_mixed.shape[1] // chips // LANES
    pairs = audio_mixed.shape[1] // chips // LANES
    chip = lax.axis_index("seq") // 2
    for j in range(chips):
        for h in range(parts):
            at = pl.multiple_of(((chip ^ j) * parts + h) * LANES, LANES)
            video_mixed[:, pl.ds(at, LANES)] = back[j][h * rows : (h + 1) * rows, :]
        for p in range(pairs):
            at = pl.multiple_of(((chip ^ j) * pairs + p) * LANES, LANES)
            out = (parts + p) * rows
            video_cross[:, pl.ds(at, LANES)] = back[j][out : out + rows, :]
            out += pairs * rows
            both = back[j][out : out + rows, :]
            audio_mixed[:, pl.ds(at, LANES)] = both[:half, :]
            audio_cross[:, pl.ds(at, LANES)] = both[half:, :]


def swap(piece, n, step):
    return lax.ppermute(piece, "seq", [(i, i ^ step) for i in range(n)])


def shards_packed(*arrays):
    (
        video_query, video_keys, video_values,
        audio_query, audio_keys, audio_values,
        cross_video_query, cross_video_keys, cross_video_values,
        cross_audio_query, cross_audio_keys, cross_audio_values,
        video_length, audio_length, align_offset,
    ) = arrays
    n = lax.axis_size("seq")
    chips = n // 2
    rows = video_query.shape[0]
    parts = video_query.shape[1] // chips // LANES
    pairs = audio_query.shape[1] // chips // LANES
    vmem = pl.BlockSpec(memory_space=pltpu.VMEM)
    smem = pl.BlockSpec(memory_space=pltpu.SMEM)
    params = pltpu.CompilerParams(vmem_limit_bytes=32 * 1024 * 1024)
    in_rows = (3 * parts + 6 * pairs) * rows
    out_rows = (parts + 2 * pairs) * rows
    sources = (
        video_query, video_keys, video_values,
        cross_video_query, cross_video_keys, cross_video_values,
        audio_query, audio_keys, audio_values,
        cross_audio_query, cross_audio_keys, cross_audio_values,
    )
    packed = pl.pallas_call(
        functools.partial(pack_kernel, chips),
        out_shape=(jax.ShapeDtypeStruct((in_rows, LANES), jnp.bfloat16),) * chips,
        in_specs=[pl.BlockSpec(memory_space=pltpu.HBM)] * 12,
        out_specs=(vmem,) * chips,
        scratch_shapes=[pltpu.VMEM(source.shape, source.dtype) for source in sources]
        + [pltpu.SemaphoreType.DMA((12,))],
        compiler_params=pltpu.CompilerParams(vmem_limit_bytes=60 * 1024 * 1024),
    )(*sources)
    packed = by_step(packed)
    own = packed[:1] + [swap(packed[j], n, 2 * j) for j in range(1, chips)]
    other = [swap(piece, n, 1) for piece in own]
    done = pl.pallas_call(
        functools.partial(attend_kernel, chips, rows, parts, pairs),
        out_shape=(jax.ShapeDtypeStruct((out_rows, LANES), jnp.bfloat16),) * chips,
        in_specs=[smem] * 3 + [vmem] * (2 * chips),
        out_specs=(vmem,) * chips,
        compiler_params=params,
    )(
        video_length, audio_length, align_offset,
        *by_step(own), *by_step(other),
    )
    done = by_step(done)
    back = done[:1] + [swap(done[j], n, 2 * j) for j in range(1, chips)]
    return pl.pallas_call(
        functools.partial(unpack_kernel, chips),
        out_shape=(
            jax.ShapeDtypeStruct(video_query.shape, jnp.bfloat16),
            jax.ShapeDtypeStruct(audio_query.shape, jnp.bfloat16),
            jax.ShapeDtypeStruct(cross_video_query.shape, jnp.bfloat16),
            jax.ShapeDtypeStruct(cross_audio_query.shape, jnp.bfloat16),
        ),
        in_specs=[vmem] * chips,
        out_specs=(vmem,) * 4,
        compiler_params=params,
    )(*by_step(back))


def shards(*arrays):
    n = lax.axis_size("seq")
    rows, half = arrays[0].shape[0], arrays[3].shape[0]
    chips = max(n // 2, 1)
    fits = (
        n % 2 == 0
        and n & (n - 1) == 0
        and arrays[0].shape[1] % (chips * LANES) == 0
        and arrays[3].shape[1] % (chips * LANES) == 0
        and HDV == LANES
        and LANES % HDA == 0
        and rows == 2 * half
        and half % 8 == 0
        and half & (half - 1) == 0
    )
    return shards_packed(*arrays) if fits else shards_general(*arrays)


def solution(mesh):
    placed = (
        P(("clip", "seq"), None),
        P(("clip", "seq"), None),
        P(("clip", "seq"), None),
        P(("clip", "seq"), None),
        P(("clip", "seq"), None),
        P(("clip", "seq"), None),
        P(("clip", "seq"), None),
        P(("clip", "seq"), None),
        P(("clip", "seq"), None),
        P(("clip", "seq"), None),
        P(("clip", "seq"), None),
        P(("clip", "seq"), None),
        P("clip"),
        P("clip"),
        P("clip"),
    )
    return jax.shard_map(
        shards,
        mesh=mesh,
        in_specs=placed,
        out_specs=(
            P(("clip", "seq"), None),
            P(("clip", "seq"), None),
            P(("clip", "seq"), None),
            P(("clip", "seq"), None),
        ),
        check_vma=False,
    )
```

```python
import functools
import math

import jax
import jax.numpy as jnp
from jax import lax
from jax.experimental import pallas as pl
from jax.experimental.pallas import tpu as pltpu
from jax.sharding import PartitionSpec as P

HV = 32
HDV = 128
HA = 32
HDA = 64


def block_size(total, limit):
    chosen = min(total, limit)
    while total % chosen:
        chosen -= 1
    return chosen


def split_heads(tokens, heads, depth, copies):
    rows = tokens.shape[0]
    shaped = tokens.reshape(copies, rows // copies, heads, depth).transpose(2, 0, 1, 3)
    return shaped.reshape(heads * copies, rows // copies, depth)


def spread_heads(tokens, heads, depth, copies):
    rows = tokens.shape[0]
    shaped = tokens.reshape(rows, heads, depth).transpose(1, 0, 2)
    shaped = jnp.broadcast_to(shaped[:, None], (heads, copies, rows, depth))
    return shaped.reshape(heads * copies, rows, depth)


def join_heads(owned, heads, depth, copies):
    part_rows = owned.shape[1]
    shaped = owned.reshape(heads, copies, part_rows, depth).transpose(1, 2, 0, 3)
    return shaped.reshape(copies * part_rows, heads * depth)


def owned_positions(rows, copies, devices, index):
    part_rows = rows // copies
    flat = jnp.arange(devices * part_rows, dtype=jnp.int32)
    return flat // part_rows * rows + index % copies * part_rows + flat % part_rows


def online_update(carry, scores, permit, value_tile, value_form):
    running, total, accum = carry
    scores = jnp.where(permit, scores, -1e30)
    newmax = jnp.maximum(running, jnp.max(scores, axis=2))
    weights = jnp.where(permit, jnp.exp(scores - newmax[:, :, None]), 0.0)
    factor = jnp.exp(running - newmax)
    total = total * factor + jnp.sum(weights, axis=2)
    mixed = jnp.einsum(
        value_form, weights.astype(jnp.bfloat16), value_tile, preferred_element_type=jnp.float32
    )
    accum = accum * factor[:, :, None] + mixed
    return (newmax, total, accum)


def fold_initial(rows, heads, depth):
    return (
        jnp.full((heads, rows), -1e30, jnp.float32),
        jnp.zeros((heads, rows), jnp.float32),
        jnp.zeros((heads, rows, depth), jnp.float32),
    )


def fold_piece(carry, local_query, key_rows, value_rows, permit, heads, depth):
    keyed = key_rows.reshape(key_rows.shape[0], heads, depth)
    valued = value_rows.reshape(value_rows.shape[0], heads, depth)
    scores = jnp.einsum("qhd,khd->hqk", local_query, keyed, preferred_element_type=jnp.float32) * (
        1.0 / math.sqrt(depth)
    )
    return online_update(carry, scores, permit[None], valued, "hqk,khd->hqd")


def fold_finish(carry, heads, depth):
    running, total, accum = carry
    result = (accum / total[:, :, None]).astype(jnp.bfloat16)
    return result.transpose(1, 0, 2).reshape(result.shape[1], heads * depth)


def attend_local(queries, keys, values, query_pos, key_pos, allowed):
    heads, q_count, depth = queries.shape
    k_count = keys.shape[1]
    q_block = block_size(q_count, 512)
    k_block = block_size(k_count, 2048)
    scale = 1.0 / math.sqrt(depth)
    q_tiles = queries.reshape(heads, q_count // q_block, q_block, depth).transpose(1, 0, 2, 3)
    k_tiles = keys.reshape(heads, k_count // k_block, k_block, depth).transpose(1, 0, 2, 3)
    v_tiles = values.reshape(heads, k_count // k_block, k_block, depth).transpose(1, 0, 2, 3)
    q_places = query_pos.reshape(q_count // q_block, q_block)
    k_places = key_pos.reshape(k_count // k_block, k_block)

    def one_tile(packed):
        q_tile, q_where = packed

        def absorb(carry, piece):
            k_tile, v_tile, k_where = piece
            scores = (
                jnp.einsum("hqd,hkd->hqk", q_tile, k_tile, preferred_element_type=jnp.float32)
                * scale
            )
            permit = allowed(q_where[:, None], k_where[None, :])[None]
            return (online_update(carry, scores, permit, v_tile, "hqk,hkd->hqd"), None)

        initial = fold_initial(q_block, heads, depth)
        final_state, unused = lax.scan(absorb, initial, (k_tiles, v_tiles, k_places))
        running, total, accum = final_state
        return (accum / total[:, :, None]).astype(jnp.bfloat16)

    tiles = lax.map(one_tile, (q_tiles, q_places))
    return tiles.transpose(1, 0, 2, 3).reshape(heads, q_count, depth)


def shards_general(
    video_query,
    video_keys,
    video_values,
    audio_query,
    audio_keys,
    audio_values,
    cross_video_query,
    cross_video_keys,
    cross_video_values,
    cross_audio_query,
    cross_audio_keys,
    cross_audio_values,
    video_length,
    audio_length,
    align_offset,
):
    devices = lax.axis_size("seq")
    index = lax.axis_index("seq")
    video_rows = video_query.shape[0]
    audio_rows = audio_query.shape[0]
    video_total = video_rows * devices
    audio_total = audio_rows * devices
    video_reach = video_total // 8
    audio_reach = 5 * audio_total // 8
    video_valid = video_length[0]
    audio_valid = audio_length[0]
    align_shift = align_offset[0]
    copies = max(devices // HV, 1)
    video_places = jnp.arange(video_total, dtype=jnp.int32)
    audio_places = jnp.arange(audio_total, dtype=jnp.int32)

    def video_open(q_where, k_where):
        return k_where < video_valid

    def toward_video(q_where, k_where):
        center = jnp.clip(q_where * audio_total // video_total + align_shift, 0, audio_valid - 1)
        return (k_where < audio_valid) & (jnp.abs(k_where - center) <= audio_reach)

    def toward_audio(q_where, k_where):
        center = jnp.clip((q_where - align_shift) * video_total // audio_total, 0, video_valid - 1)
        return (k_where < video_valid) & (jnp.abs(k_where - center) <= video_reach)

    video_owned = (
        lax.all_to_all(
            split_heads(video_query, HV, HDV, copies),
            "seq",
            split_axis=0,
            concat_axis=1,
            tiled=True,
        ),
        lax.all_to_all(
            spread_heads(video_keys, HV, HDV, copies),
            "seq",
            split_axis=0,
            concat_axis=1,
            tiled=True,
        ),
        lax.all_to_all(
            spread_heads(video_values, HV, HDV, copies),
            "seq",
            split_axis=0,
            concat_axis=1,
            tiled=True,
        ),
    )
    video_done = attend_local(
        video_owned[0],
        video_owned[1],
        video_owned[2],
        owned_positions(video_rows, copies, devices, index),
        video_places,
        video_open,
    )
    video_mixed = join_heads(
        lax.all_to_all(video_done, "seq", split_axis=1, concat_axis=0, tiled=True), HV, HDV, copies
    )
    audio_local = audio_query.reshape(audio_rows, HA, HDA)
    piece = (
        lax.all_gather(audio_keys, "seq", axis=0, tiled=True),
        lax.all_gather(audio_values, "seq", axis=0, tiled=True),
    )
    k_where = jnp.arange(piece[0].shape[0], dtype=jnp.int32)
    audio_k_where = k_where[None, :]
    permit = audio_k_where < audio_valid
    audio_state = fold_piece(
        fold_initial(audio_rows, HA, HDA), audio_local, piece[0], piece[1], permit, HA, HDA
    )
    audio_mixed = fold_finish(audio_state, HA, HDA)
    cross_owned = (
        lax.all_to_all(
            split_heads(cross_video_query, HA, HDA, copies),
            "seq",
            split_axis=0,
            concat_axis=1,
            tiled=True,
        ),
        lax.all_to_all(
            spread_heads(cross_audio_keys, HA, HDA, copies),
            "seq",
            split_axis=0,
            concat_axis=1,
            tiled=True,
        ),
        lax.all_to_all(
            spread_heads(cross_audio_values, HA, HDA, copies),
            "seq",
            split_axis=0,
            concat_axis=1,
            tiled=True,
        ),
    )
    cross_done = attend_local(
        cross_owned[0],
        cross_owned[1],
        cross_owned[2],
        owned_positions(video_rows, copies, devices, index),
        audio_places,
        toward_video,
    )
    video_cross = join_heads(
        lax.all_to_all(cross_done, "seq", split_axis=1, concat_axis=0, tiled=True), HA, HDA, copies
    )
    listen_owned = (
        lax.all_to_all(
            split_heads(cross_audio_query, HA, HDA, copies),
            "seq",
            split_axis=0,
            concat_axis=1,
            tiled=True,
        ),
        lax.all_to_all(
            spread_heads(cross_video_keys, HA, HDA, copies),
            "seq",
            split_axis=0,
            concat_axis=1,
            tiled=True,
        ),
        lax.all_to_all(
            spread_heads(cross_video_values, HA, HDA, copies),
            "seq",
            split_axis=0,
            concat_axis=1,
            tiled=True,
        ),
    )
    listen_done = attend_local(
        listen_owned[0],
        listen_owned[1],
        listen_owned[2],
        owned_positions(audio_rows, copies, devices, index),
        video_places,
        toward_audio,
    )
    audio_cross = join_heads(
        lax.all_to_all(listen_done, "seq", split_axis=1, concat_axis=0, tiled=True), HA, HDA, copies
    )
    return (video_mixed, audio_mixed, video_cross, audio_cross)


LANES = 128


def fetch(sources, held, arrived):
    copies = [
        pltpu.make_async_copy(source, slot, arrived.at[i])
        for i, (source, slot) in enumerate(zip(sources, held))
    ]
    for copy in copies:
        copy.start()
    return copies


def by_step(items):
    return [items[-j % len(items)] for j in range(len(items))]


def pack_small(n, *refs):
    sources, packed, held, arrived = refs[:9], refs[9], refs[10:19], refs[19]
    copies = fetch(sources, held, arrived)
    cross, audio = held[:3], held[3:]
    rows = cross[0].shape[0]
    at = 0
    for i, ref in enumerate(cross):
        copies[i].wait()
        for d in range(n):
            packed[d, at : at + rows, :] = ref[:, d * LANES : (d + 1) * LANES]
        at += rows
    for i in range(0, 6, 2):
        copies[3 + i].wait()
        copies[4 + i].wait()
        for d in range(n):
            pair = jnp.concatenate(
                [
                    audio[i][:, d * LANES : (d + 1) * LANES],
                    audio[i + 1][:, d * LANES : (d + 1) * LANES],
                ],
                axis=0,
            )
            packed[d, at : at + rows, :] = pair
        at += rows


def pack_video(chips, *refs):
    sources, refs = refs[:3], refs[4:]
    packed, held, arrived = by_step(refs[:chips]), refs[chips : chips + 3], refs[chips + 3]
    copies = fetch(sources, held, arrived)
    chip = lax.axis_index("seq") // 2
    side = chips // 2
    rows, width = held[0].shape[0], held[0].shape[1] // side
    tiles = width // LANES
    for i, ref in enumerate(held):
        copies[i].wait()
        for t in range(tiles):
            for j in range(chips):
                if j >= side and i == 0:
                    continue
                at = ((i if j < side else i - 1) * tiles + t) * rows
                column = pl.multiple_of(((chip ^ j) % side) * width + t * LANES, LANES)
                packed[j][at : at + rows, :] = ref[:, pl.ds(column, LANES)]


def keep_kernel(source, kept, arrived):
    copy = pltpu.make_async_copy(source, kept, arrived)
    copy.start()
    copy.wait()


def softmax_mix(query, key, value, scale, permit):
    scores = lax.dot_general(
        query, key, (((1,), (1,)), ((), ())), preferred_element_type=jnp.float32
    )
    scores = jnp.where(permit, scores * scale, -1e30)
    peak = jnp.max(scores, axis=1, keepdims=True)
    weights = jnp.exp(scores - peak)
    total = jnp.sum(weights, axis=1, keepdims=True)
    mixed = jnp.dot(weights.astype(jnp.bfloat16), value, preferred_element_type=jnp.float32)
    return mixed / total


def paired_mix(query, key, value, depth, permit):
    scale = 1.0 / math.sqrt(depth)
    lane = lax.broadcasted_iota(jnp.int32, query.shape, 1) // depth
    zero = jnp.zeros_like(query)
    result = None
    for h in range(LANES // depth):
        one = softmax_mix(jnp.where(lane == h, query, zero), key, value, scale, permit)
        result = one if h == 0 else jnp.where(lane == h, one, result)
    return result


def attend_video(chips, tiles, video_len, *refs):
    side = chips // 2
    own, other = by_step(refs[:chips]), by_step(refs[chips : 2 * chips])
    done = by_step(refs[2 * chips : 2 * chips + side])
    length, arrived = refs[2 * chips + side :]
    copy = pltpu.make_async_copy(video_len, length, arrived)
    copy.start()
    rows = own[0].shape[0] // (3 * tiles)
    me = lax.axis_index("seq")
    slot = lax.broadcasted_iota(jnp.int32, (side * rows, 2 * chips * rows), 1)
    k_at = slot ^ (me * rows)
    copy.wait()
    permit = k_at < length[0]

    def gather(kind, t):
        pieces = []
        for j in range(chips):
            at = ((kind if j < side else kind - 1) * tiles + t) * rows
            pieces += [own[j][at : at + rows, :], other[j][at : at + rows, :]]
        return jnp.concatenate(pieces, axis=0)

    for t in range(tiles):
        query = jnp.concatenate([own[j][t * rows : (t + 1) * rows, :] for j in range(side)], axis=0)
        mixed = softmax_mix(query, gather(1, t), gather(2, t), 1.0 / math.sqrt(HDV), permit)
        for j in range(side):
            done[j][t * rows : (t + 1) * rows, :] = mixed[j * rows : (j + 1) * rows].astype(
                jnp.bfloat16
            )


def attend_small(n, rows, video_len, audio_len, shift, got, done, *scratch):
    copies = fetch((video_len, audio_len, shift), scratch[:3], scratch[3])
    half = rows // 2
    tv, ta = n * rows, n * half
    ratio = tv // ta
    bits = ratio.bit_length() - 1

    def slab(at):
        return got[:, at : at + rows, :].reshape(tv, LANES)

    def halves(at):
        both = got[:, at : at + rows, :].astype(jnp.float32)
        first = both[:, :half, :].reshape(ta, LANES).astype(jnp.bfloat16)
        second = both[:, half:, :].reshape(ta, LANES).astype(jnp.bfloat16)
        return first, second

    def places(q_count, k_count):
        return (
            lax.broadcasted_iota(jnp.int32, (q_count, k_count), 0),
            lax.broadcasted_iota(jnp.int32, (q_count, k_count), 1),
        )

    cross_query, cross_keys, cross_values = slab(0), slab(rows), slab(2 * rows)
    audio_query, audio_keys = halves(3 * rows)
    audio_values, listen_query = halves(4 * rows)
    sound_keys, sound_values = halves(5 * rows)
    for copy in copies:
        copy.wait()
    video_valid, audio_valid, offset = (ref[0] for ref in scratch[:3])

    q_at, k_at = places(tv, ta)
    center = jnp.clip((q_at >> bits) + offset, 0, audio_valid - 1)
    permit = (k_at < audio_valid) & (jnp.abs(k_at - center) <= 5 * ta // 8)
    mixed = paired_mix(cross_query, sound_keys, sound_values, HDA, permit)
    done[:, :rows, :] = mixed.astype(jnp.bfloat16).reshape(n, rows, LANES)

    q_at, k_at = places(ta, ta)
    heard = paired_mix(audio_query, audio_keys, audio_values, HDA, k_at < audio_valid)
    q_at, k_at = places(ta, tv)
    center = jnp.clip((q_at - offset) * ratio, 0, video_valid - 1)
    permit = (k_at < video_valid) & (jnp.abs(k_at - center) <= tv // 8)
    listened = paired_mix(listen_query, cross_keys, cross_values, HDA, permit)
    both = jnp.concatenate(
        [heard.reshape(n, half, LANES), listened.reshape(n, half, LANES)], axis=1
    )
    done[:, rows:, :] = both.astype(jnp.bfloat16)


def unpack_small(n, back, audio_mixed, video_cross, audio_cross):
    rows, half = video_cross.shape[0], audio_mixed.shape[0]
    for s in range(n):
        at = s * LANES
        video_cross[:, at : at + LANES] = back[s, :rows, :]
        both = back[s, rows:, :]
        audio_mixed[:, at : at + LANES] = both[:half, :]
        audio_cross[:, at : at + LANES] = both[half:, :]


def unpack_video(side, *refs):
    back, video_mixed = by_step(refs[:side]), refs[side]
    rows, width = video_mixed.shape[0], video_mixed.shape[1] // side
    chip = lax.axis_index("seq") // 2
    for j in range(side):
        for t in range(width // LANES):
            column = pl.multiple_of(((chip ^ j) % side) * width + t * LANES, LANES)
            video_mixed[:, pl.ds(column, LANES)] = back[j][t * rows : (t + 1) * rows, :]


def swap(piece, n, step):
    return lax.ppermute(piece, "seq", [(i, i ^ step) for i in range(n)])


def shards_packed(*arrays):
    (
        video_query, video_keys, video_values,
        audio_query, audio_keys, audio_values,
        cross_video_query, cross_video_keys, cross_video_values,
        cross_audio_query, cross_audio_keys, cross_audio_values,
        video_length, audio_length, align_offset,
    ) = arrays
    n = lax.axis_size("seq")
    chips, side = n // 2, n // 4
    rows = video_query.shape[0]
    tiles = video_query.shape[1] // side // LANES
    vmem = pl.BlockSpec(memory_space=pltpu.VMEM)
    hbm = pl.BlockSpec(memory_space=pltpu.HBM)
    params = pltpu.CompilerParams(vmem_limit_bytes=32 * 1024 * 1024)
    first = pltpu.CompilerParams(vmem_limit_bytes=60 * 1024 * 1024)
    one = pltpu.SMEM((1,), jnp.int32)

    def buffer(*shape):
        return jax.ShapeDtypeStruct(shape, jnp.bfloat16)

    def staging(sources):
        return [pltpu.VMEM(source.shape, source.dtype) for source in sources] + [
            pltpu.SemaphoreType.DMA((len(sources),))
        ]

    small = (
        cross_video_query, cross_video_keys, cross_video_values,
        audio_query, audio_keys, audio_values,
        cross_audio_query, cross_audio_keys, cross_audio_values,
    )
    packed_small = pl.pallas_call(
        functools.partial(pack_small, n),
        out_shape=buffer(n, 6 * rows, LANES),
        in_specs=[hbm] * 9,
        out_specs=vmem,
        scratch_shapes=staging(small),
        compiler_params=first,
    )(*small)
    got = lax.all_to_all(packed_small, "seq", split_axis=0, concat_axis=0, tiled=True)

    video = (video_query, video_keys, video_values)
    packed = pl.pallas_call(
        functools.partial(pack_video, chips),
        out_shape=by_step(
            [buffer((3 if j < side else 2) * tiles * rows, LANES) for j in range(chips)]
        ),
        in_specs=[hbm] * 4,
        out_specs=[vmem] * chips,
        scratch_shapes=staging(video),
        compiler_params=first,
    )(*video, packed_small)
    packed = by_step(packed)
    moved = [swap(packed[j], n, 2 * j) for j in range(1, chips)]
    kept = pl.pallas_call(
        keep_kernel,
        out_shape=packed[0],
        in_specs=[hbm],
        out_specs=vmem,
        scratch_shapes=[pltpu.SemaphoreType.DMA],
        compiler_params=params,
    )(packed[0])
    own = [kept] + moved
    other = [swap(piece, n, 1) for piece in packed[:1] + moved]

    done_small = pl.pallas_call(
        functools.partial(attend_small, n, rows),
        out_shape=buffer(n, 2 * rows, LANES),
        in_specs=[hbm] * 3 + [vmem],
        out_specs=vmem,
        scratch_shapes=[one] * 3 + [pltpu.SemaphoreType.DMA((3,))],
        compiler_params=params,
    )(video_length, audio_length, align_offset, got)
    back_small = lax.all_to_all(done_small, "seq", split_axis=0, concat_axis=0, tiled=True)

    done = by_step(
        pl.pallas_call(
            functools.partial(attend_video, chips, tiles),
            out_shape=[buffer(tiles * rows, LANES)] * side,
            in_specs=[hbm] + [vmem] * (2 * chips),
            out_specs=[vmem] * side,
            scratch_shapes=[one, pltpu.SemaphoreType.DMA],
            compiler_params=params,
        )(video_length, *by_step(own), *by_step(other))
    )
    back = done[:1] + [swap(done[j], n, 2 * j) for j in range(1, side)]
    audio_mixed, video_cross, audio_cross = pl.pallas_call(
        functools.partial(unpack_small, n),
        out_shape=(
            buffer(*audio_query.shape),
            buffer(*cross_video_query.shape),
            buffer(*cross_audio_query.shape),
        ),
        in_specs=[vmem],
        out_specs=(vmem,) * 3,
        compiler_params=params,
    )(back_small)
    video_mixed = pl.pallas_call(
        functools.partial(unpack_video, side),
        out_shape=buffer(*video_query.shape),
        in_specs=[vmem] * side,
        out_specs=vmem,
        compiler_params=params,
    )(*by_step(back))
    return (video_mixed, audio_mixed, video_cross, audio_cross)


def shards(*arrays):
    n = lax.axis_size("seq")
    rows, half = arrays[0].shape[0], arrays[3].shape[0]
    fits = (
        n % 4 == 0
        and n & (n - 1) == 0
        and arrays[0].shape[1] % (n // 4 * LANES) == 0
        and arrays[3].shape[1] == n * LANES
        and HDV == LANES
        and LANES % HDA == 0
        and rows == 2 * half
        and half % 8 == 0
        and half & (half - 1) == 0
    )
    return shards_packed(*arrays) if fits else shards_general(*arrays)


def solution(mesh):
    placed = (
        P(("clip", "seq"), None),
        P(("clip", "seq"), None),
        P(("clip", "seq"), None),
        P(("clip", "seq"), None),
        P(("clip", "seq"), None),
        P(("clip", "seq"), None),
        P(("clip", "seq"), None),
        P(("clip", "seq"), None),
        P(("clip", "seq"), None),
        P(("clip", "seq"), None),
        P(("clip", "seq"), None),
        P(("clip", "seq"), None),
        P("clip"),
        P("clip"),
        P("clip"),
    )
    return jax.shard_map(
        shards,
        mesh=mesh,
        in_specs=placed,
        out_specs=(
            P(("clip", "seq"), None),
            P(("clip", "seq"), None),
            P(("clip", "seq"), None),
            P(("clip", "seq"), None),
        ),
        check_vma=False,
    )
```

```python
import functools
import math

import jax
import jax.numpy as jnp
from jax import lax
from jax.experimental import pallas as pl
from jax.experimental.pallas import tpu as pltpu
from jax.sharding import PartitionSpec as P

HV = 32
HDV = 128
HA = 32
HDA = 64


def block_size(total, limit):
    chosen = min(total, limit)
    while total % chosen:
        chosen -= 1
    return chosen


def split_heads(tokens, heads, depth, copies):
    rows = tokens.shape[0]
    shaped = tokens.reshape(copies, rows // copies, heads, depth).transpose(2, 0, 1, 3)
    return shaped.reshape(heads * copies, rows // copies, depth)


def spread_heads(tokens, heads, depth, copies):
    rows = tokens.shape[0]
    shaped = tokens.reshape(rows, heads, depth).transpose(1, 0, 2)
    shaped = jnp.broadcast_to(shaped[:, None], (heads, copies, rows, depth))
    return shaped.reshape(heads * copies, rows, depth)


def join_heads(owned, heads, depth, copies):
    part_rows = owned.shape[1]
    shaped = owned.reshape(heads, copies, part_rows, depth).transpose(1, 2, 0, 3)
    return shaped.reshape(copies * part_rows, heads * depth)


def owned_positions(rows, copies, devices, index):
    part_rows = rows // copies
    flat = jnp.arange(devices * part_rows, dtype=jnp.int32)
    return flat // part_rows * rows + index % copies * part_rows + flat % part_rows


def online_update(carry, scores, permit, value_tile, value_form):
    running, total, accum = carry
    scores = jnp.where(permit, scores, -1e30)
    newmax = jnp.maximum(running, jnp.max(scores, axis=2))
    weights = jnp.where(permit, jnp.exp(scores - newmax[:, :, None]), 0.0)
    factor = jnp.exp(running - newmax)
    total = total * factor + jnp.sum(weights, axis=2)
    mixed = jnp.einsum(
        value_form, weights.astype(jnp.bfloat16), value_tile, preferred_element_type=jnp.float32
    )
    accum = accum * factor[:, :, None] + mixed
    return (newmax, total, accum)


def fold_initial(rows, heads, depth):
    return (
        jnp.full((heads, rows), -1e30, jnp.float32),
        jnp.zeros((heads, rows), jnp.float32),
        jnp.zeros((heads, rows, depth), jnp.float32),
    )


def fold_piece(carry, local_query, key_rows, value_rows, permit, heads, depth):
    keyed = key_rows.reshape(key_rows.shape[0], heads, depth)
    valued = value_rows.reshape(value_rows.shape[0], heads, depth)
    scores = jnp.einsum("qhd,khd->hqk", local_query, keyed, preferred_element_type=jnp.float32) * (
        1.0 / math.sqrt(depth)
    )
    return online_update(carry, scores, permit[None], valued, "hqk,khd->hqd")


def fold_finish(carry, heads, depth):
    running, total, accum = carry
    result = (accum / total[:, :, None]).astype(jnp.bfloat16)
    return result.transpose(1, 0, 2).reshape(result.shape[1], heads * depth)


def attend_local(queries, keys, values, query_pos, key_pos, allowed):
    heads, q_count, depth = queries.shape
    k_count = keys.shape[1]
    q_block = block_size(q_count, 512)
    k_block = block_size(k_count, 2048)
    scale = 1.0 / math.sqrt(depth)
    q_tiles = queries.reshape(heads, q_count // q_block, q_block, depth).transpose(1, 0, 2, 3)
    k_tiles = keys.reshape(heads, k_count // k_block, k_block, depth).transpose(1, 0, 2, 3)
    v_tiles = values.reshape(heads, k_count // k_block, k_block, depth).transpose(1, 0, 2, 3)
    q_places = query_pos.reshape(q_count // q_block, q_block)
    k_places = key_pos.reshape(k_count // k_block, k_block)

    def one_tile(packed):
        q_tile, q_where = packed

        def absorb(carry, piece):
            k_tile, v_tile, k_where = piece
            scores = (
                jnp.einsum("hqd,hkd->hqk", q_tile, k_tile, preferred_element_type=jnp.float32)
                * scale
            )
            permit = allowed(q_where[:, None], k_where[None, :])[None]
            return (online_update(carry, scores, permit, v_tile, "hqk,hkd->hqd"), None)

        initial = fold_initial(q_block, heads, depth)
        final_state, unused = lax.scan(absorb, initial, (k_tiles, v_tiles, k_places))
        running, total, accum = final_state
        return (accum / total[:, :, None]).astype(jnp.bfloat16)

    tiles = lax.map(one_tile, (q_tiles, q_places))
    return tiles.transpose(1, 0, 2, 3).reshape(heads, q_count, depth)


def shards_general(
    video_query,
    video_keys,
    video_values,
    audio_query,
    audio_keys,
    audio_values,
    cross_video_query,
    cross_video_keys,
    cross_video_values,
    cross_audio_query,
    cross_audio_keys,
    cross_audio_values,
    video_length,
    audio_length,
    align_offset,
):
    devices = lax.axis_size("seq")
    index = lax.axis_index("seq")
    video_rows = video_query.shape[0]
    audio_rows = audio_query.shape[0]
    video_total = video_rows * devices
    audio_total = audio_rows * devices
    video_reach = video_total // 8
    audio_reach = 5 * audio_total // 8
    video_valid = video_length[0]
    audio_valid = audio_length[0]
    align_shift = align_offset[0]
    copies = max(devices // HV, 1)
    video_places = jnp.arange(video_total, dtype=jnp.int32)
    audio_places = jnp.arange(audio_total, dtype=jnp.int32)

    def video_open(q_where, k_where):
        return k_where < video_valid

    def toward_video(q_where, k_where):
        center = jnp.clip(q_where * audio_total // video_total + align_shift, 0, audio_valid - 1)
        return (k_where < audio_valid) & (jnp.abs(k_where - center) <= audio_reach)

    def toward_audio(q_where, k_where):
        center = jnp.clip((q_where - align_shift) * video_total // audio_total, 0, video_valid - 1)
        return (k_where < video_valid) & (jnp.abs(k_where - center) <= video_reach)

    video_owned = (
        lax.all_to_all(
            split_heads(video_query, HV, HDV, copies),
            "seq",
            split_axis=0,
            concat_axis=1,
            tiled=True,
        ),
        lax.all_to_all(
            spread_heads(video_keys, HV, HDV, copies),
            "seq",
            split_axis=0,
            concat_axis=1,
            tiled=True,
        ),
        lax.all_to_all(
            spread_heads(video_values, HV, HDV, copies),
            "seq",
            split_axis=0,
            concat_axis=1,
            tiled=True,
        ),
    )
    video_done = attend_local(
        video_owned[0],
        video_owned[1],
        video_owned[2],
        owned_positions(video_rows, copies, devices, index),
        video_places,
        video_open,
    )
    video_mixed = join_heads(
        lax.all_to_all(video_done, "seq", split_axis=1, concat_axis=0, tiled=True), HV, HDV, copies
    )
    audio_local = audio_query.reshape(audio_rows, HA, HDA)
    piece = (
        lax.all_gather(audio_keys, "seq", axis=0, tiled=True),
        lax.all_gather(audio_values, "seq", axis=0, tiled=True),
    )
    k_where = jnp.arange(piece[0].shape[0], dtype=jnp.int32)
    audio_k_where = k_where[None, :]
    permit = audio_k_where < audio_valid
    audio_state = fold_piece(
        fold_initial(audio_rows, HA, HDA), audio_local, piece[0], piece[1], permit, HA, HDA
    )
    audio_mixed = fold_finish(audio_state, HA, HDA)
    cross_owned = (
        lax.all_to_all(
            split_heads(cross_video_query, HA, HDA, copies),
            "seq",
            split_axis=0,
            concat_axis=1,
            tiled=True,
        ),
        lax.all_to_all(
            spread_heads(cross_audio_keys, HA, HDA, copies),
            "seq",
            split_axis=0,
            concat_axis=1,
            tiled=True,
        ),
        lax.all_to_all(
            spread_heads(cross_audio_values, HA, HDA, copies),
            "seq",
            split_axis=0,
            concat_axis=1,
            tiled=True,
        ),
    )
    cross_done = attend_local(
        cross_owned[0],
        cross_owned[1],
        cross_owned[2],
        owned_positions(video_rows, copies, devices, index),
        audio_places,
        toward_video,
    )
    video_cross = join_heads(
        lax.all_to_all(cross_done, "seq", split_axis=1, concat_axis=0, tiled=True), HA, HDA, copies
    )
    listen_owned = (
        lax.all_to_all(
            split_heads(cross_audio_query, HA, HDA, copies),
            "seq",
            split_axis=0,
            concat_axis=1,
            tiled=True,
        ),
        lax.all_to_all(
            spread_heads(cross_video_keys, HA, HDA, copies),
            "seq",
            split_axis=0,
            concat_axis=1,
            tiled=True,
        ),
        lax.all_to_all(
            spread_heads(cross_video_values, HA, HDA, copies),
            "seq",
            split_axis=0,
            concat_axis=1,
            tiled=True,
        ),
    )
    listen_done = attend_local(
        listen_owned[0],
        listen_owned[1],
        listen_owned[2],
        owned_positions(audio_rows, copies, devices, index),
        video_places,
        toward_audio,
    )
    audio_cross = join_heads(
        lax.all_to_all(listen_done, "seq", split_axis=1, concat_axis=0, tiled=True), HA, HDA, copies
    )
    return (video_mixed, audio_mixed, video_cross, audio_cross)


LANES = 128


def fetch(sources, held, arrived):
    copies = [
        pltpu.make_async_copy(source, slot, arrived.at[i])
        for i, (source, slot) in enumerate(zip(sources, held))
    ]
    for copy in copies:
        copy.start()
    return copies


def by_step(items):
    return [items[-j % len(items)] for j in range(len(items))]


def pack_kernel(chips, *refs):
    sources, refs = refs[:12], refs[12:]
    packed, held, arrived = by_step(refs[:chips]), refs[chips : chips + 12], refs[chips + 12]
    copies = fetch(sources, held, arrived)
    chip = lax.axis_index("seq") // 2
    video, cross, audio = held[0:3], held[3:6], held[6:12]
    rows = video[0].shape[0]

    def group(ref, j, part):
        width = ref.shape[1] // chips
        at = pl.multiple_of((chip ^ j) * width + part * LANES, LANES)
        return ref[:, pl.ds(at, LANES)]

    at = 0
    for i, ref in enumerate(video + cross):
        copies[i].wait()
        for part in range(ref.shape[1] // chips // LANES):
            for j in range(chips):
                packed[j][at : at + rows, :] = group(ref, j, part)
            at += rows
    for i in range(0, 6, 2):
        copies[6 + i].wait()
        copies[7 + i].wait()
        for part in range(audio[i].shape[1] // chips // LANES):
            for j in range(chips):
                pair = jnp.concatenate(
                    [group(audio[i], j, part), group(audio[i + 1], j, part)], axis=0
                )
                packed[j][at : at + rows, :] = pair
            at += rows


def keep_kernel(source, video_len, audio_len, shift, after, kept, bounds, *scratch):
    held, arrived = scratch[:3], scratch[3]
    copies = fetch((source, video_len, audio_len, shift), (kept, *held), arrived)
    for copy in copies:
        copy.wait()
    row = lax.broadcasted_iota(jnp.int32, bounds.shape, 0)
    bounds[...] = jnp.where(row == 0, held[0][0], jnp.where(row == 1, held[1][0], held[2][0]))


def softmax_mix(query, key, value, scale, permit):
    scores = lax.dot_general(
        query, key, (((1,), (1,)), ((), ())), preferred_element_type=jnp.float32
    )
    scores = jnp.where(permit, scores * scale, -1e30)
    peak = jnp.max(scores, axis=1, keepdims=True)
    weights = jnp.exp(scores - peak)
    total = jnp.sum(weights, axis=1, keepdims=True)
    mixed = jnp.dot(weights.astype(jnp.bfloat16), value, preferred_element_type=jnp.float32)
    return mixed / total


def paired_mix(query, key, value, depth, permit):
    scale = 1.0 / math.sqrt(depth)
    lane = lax.broadcasted_iota(jnp.int32, query.shape, 1) // depth
    zero = jnp.zeros_like(query)
    result = None
    for h in range(LANES // depth):
        one = softmax_mix(jnp.where(lane == h, query, zero), key, value, scale, permit)
        result = one if h == 0 else jnp.where(lane == h, one, result)
    return result


def shares(chips):
    turn = chips // 4
    first = [j for j in range(chips) if (j // turn ^ j // (2 * turn)) % 2 == 0]
    return [(j, j ^ turn) for j in first]


def attend_kernel(chips, rows, parts, pairs, bounds, *refs):
    own, other = by_step(refs[:chips]), by_step(refs[chips : 2 * chips])
    done = refs[2 * chips :]
    share = shares(chips)
    every = [ref for both in zip(own, other) for ref in both]
    half = rows // 2
    tv, ta = 2 * chips * rows, 2 * chips * half
    bits = (tv // ta).bit_length() - 1
    me = lax.axis_index("seq")
    core, home = me % 2, me // 2 * 2
    video_valid, audio_valid, offset = (bounds[i : i + 1, 0:1] for i in range(3))

    def slab(at):
        return jnp.concatenate([ref[at : at + rows, :] for ref in every], axis=0)

    def asked(at):
        pieces = []
        for zero, one in share:
            for c in range(2):
                low = (own, other)[c][zero][at : at + rows, :]
                high = (other, own)[c][one][at : at + rows, :]
                pieces.append(jnp.where(core == 0, low, high))
        return jnp.concatenate(pieces, axis=0)

    def split(wide):
        wide = wide.astype(jnp.float32).reshape(-1, rows, LANES)
        first = wide[:, :half, :].reshape(-1, LANES).astype(jnp.bfloat16)
        second = wide[:, half:, :].reshape(-1, LANES).astype(jnp.bfloat16)
        return first, second

    def places(q_step, k_step):
        shape = (chips * q_step, 2 * chips * k_step)
        k_at = lax.broadcasted_iota(jnp.int32, shape, 1) ^ (me * k_step)
        starts = []
        for zero, one in share:
            chip = home ^ jnp.where(core == 0, 2 * zero, 2 * one)
            starts.append(lax.broadcasted_iota(jnp.int32, (2 * q_step, 1), 0) + chip * q_step)
        return jnp.concatenate(starts, axis=0), k_at

    def put(at, mixed):
        count = done[0].shape[0] // 2
        for u in range(len(share)):
            for c in range(2):
                piece = mixed[(2 * u + c) * rows : (2 * u + c + 1) * rows]
                done[u][c * count + at : c * count + at + rows, :] = piece.astype(jnp.bfloat16)

    q_at, k_at = places(rows, rows)
    permit = k_at < video_valid
    for h in range(parts):
        mixed = softmax_mix(
            asked(h * rows),
            slab((parts + h) * rows),
            slab((2 * parts + h) * rows),
            1.0 / math.sqrt(HDV),
            permit,
        )
        put(h * rows, mixed)

    cross = 3 * parts * rows
    audio = cross + 3 * pairs * rows
    q_at, k_at = places(rows, half)
    center = jnp.clip((q_at >> bits) + offset, 0, audio_valid - 1)
    toward_video = (k_at < audio_valid) & (jnp.abs(k_at - center) <= 5 * ta // 8)
    q_at, k_at = places(half, half)
    within_audio = k_at < audio_valid
    q_at, k_at = places(half, rows)
    center = jnp.clip((q_at - offset) << bits, 0, video_valid - 1)
    toward_audio = (k_at < video_valid) & (jnp.abs(k_at - center) <= tv // 8)
    for p in range(pairs):
        at = cross + p * rows
        cross_query = asked(at)
        cross_keys = slab(at + pairs * rows)
        cross_values = slab(at + 2 * pairs * rows)
        at = audio + p * rows
        audio_query = split(asked(at))[0]
        audio_keys = split(slab(at))[1]
        at += pairs * rows
        audio_values = split(slab(at))[0]
        listen_query = split(asked(at))[1]
        at += pairs * rows
        sound_keys, sound_values = split(slab(at))
        out = (parts + p) * rows
        put(out, paired_mix(cross_query, sound_keys, sound_values, HDA, toward_video))
        heard = paired_mix(audio_query, audio_keys, audio_values, HDA, within_audio)
        listened = paired_mix(listen_query, cross_keys, cross_values, HDA, toward_audio)
        both = jnp.concatenate(
            [heard.reshape(-1, half, LANES), listened.reshape(-1, half, LANES)], axis=1
        )
        put(out + pairs * rows, both.reshape(-1, LANES))


def unpack_kernel(chips, *refs):
    share = shares(chips)
    back, other = refs[: len(share)], refs[len(share) : 2 * len(share)]
    video_mixed, audio_mixed, video_cross, audio_cross = refs[2 * len(share) :]
    rows = video_mixed.shape[0]
    half = audio_mixed.shape[0]
    parts = video_mixed.shape[1] // chips // LANES
    pairs = audio_mixed.shape[1] // chips // LANES
    me = lax.axis_index("seq")
    core, home = me % 2, me // 2
    for u, (zero, one) in enumerate(share):
        for ref, chip in (
            (back[u], home ^ jnp.where(core == 0, zero, one)),
            (other[u], home ^ jnp.where(core == 0, one, zero)),
        ):
            base = pl.multiple_of(core * (ref.shape[0] // 2), 16)

            def piece(at):
                return ref[pl.ds(base + at, rows), :]

            for h in range(parts):
                at = pl.multiple_of((chip * parts + h) * LANES, LANES)
                video_mixed[:, pl.ds(at, LANES)] = piece(h * rows)
            for p in range(pairs):
                at = pl.multiple_of((chip * pairs + p) * LANES, LANES)
                out = (parts + p) * rows
                video_cross[:, pl.ds(at, LANES)] = piece(out)
                both = piece(out + pairs * rows)
                audio_mixed[:, pl.ds(at, LANES)] = both[:half, :]
                audio_cross[:, pl.ds(at, LANES)] = both[half:, :]


def swap(piece, n, step):
    return lax.ppermute(piece, "seq", [(i, i ^ step) for i in range(n)])


def shards_packed(*arrays):
    (
        video_query, video_keys, video_values,
        audio_query, audio_keys, audio_values,
        cross_video_query, cross_video_keys, cross_video_values,
        cross_audio_query, cross_audio_keys, cross_audio_values,
        video_length, audio_length, align_offset,
    ) = arrays
    n = lax.axis_size("seq")
    chips = n // 2
    rows = video_query.shape[0]
    parts = video_query.shape[1] // chips // LANES
    pairs = audio_query.shape[1] // chips // LANES
    vmem = pl.BlockSpec(memory_space=pltpu.VMEM)
    hbm = pl.BlockSpec(memory_space=pltpu.HBM)
    params = pltpu.CompilerParams(vmem_limit_bytes=32 * 1024 * 1024)

    def buffer(*shape):
        return jax.ShapeDtypeStruct(shape, jnp.bfloat16)

    sources = (
        video_query, video_keys, video_values,
        cross_video_query, cross_video_keys, cross_video_values,
        audio_query, audio_keys, audio_values,
        cross_audio_query, cross_audio_keys, cross_audio_values,
    )
    packed = pl.pallas_call(
        functools.partial(pack_kernel, chips),
        out_shape=[buffer((3 * parts + 6 * pairs) * rows, LANES)] * chips,
        in_specs=[hbm] * 12,
        out_specs=[vmem] * chips,
        scratch_shapes=[pltpu.VMEM(source.shape, source.dtype) for source in sources]
        + [pltpu.SemaphoreType.DMA((12,))],
        compiler_params=pltpu.CompilerParams(vmem_limit_bytes=60 * 1024 * 1024),
    )(*sources)
    packed = by_step(packed)
    moved = [swap(packed[j], n, 2 * j) for j in range(1, chips)]
    kept, bounds = pl.pallas_call(
        keep_kernel,
        out_shape=(packed[0], jax.ShapeDtypeStruct((8, LANES), jnp.int32)),
        in_specs=[hbm] * 4 + [pl.BlockSpec(memory_space=pl.ANY)],
        out_specs=(vmem, vmem),
        scratch_shapes=[pltpu.SMEM((1,), jnp.int32)] * 3 + [pltpu.SemaphoreType.DMA((4,))],
        compiler_params=params,
    )(packed[0], video_length, audio_length, align_offset, moved[-1])
    own = [kept] + moved
    other = [swap(piece, n, 1) for piece in own]
    share = shares(chips)
    done = pl.pallas_call(
        functools.partial(attend_kernel, chips, rows, parts, pairs),
        out_shape=[buffer(2 * (parts + 2 * pairs) * rows, LANES)] * len(share),
        in_specs=[vmem] * (1 + 2 * chips),
        out_specs=[vmem] * len(share),
        compiler_params=params,
    )(bounds, *by_step(own), *by_step(other))
    back = [
        lax.ppermute(piece, "seq", [(i, i ^ 2 * pair[i % 2]) for i in range(n)])
        for piece, pair in zip(done, share)
    ]
    return pl.pallas_call(
        functools.partial(unpack_kernel, chips),
        out_shape=(
            buffer(*video_query.shape),
            buffer(*audio_query.shape),
            buffer(*cross_video_query.shape),
            buffer(*cross_audio_query.shape),
        ),
        in_specs=[vmem] * (2 * len(share)),
        out_specs=(vmem,) * 4,
        compiler_params=params,
    )(*back, *[swap(piece, n, 1) for piece in back])


def shards(*arrays):
    n = lax.axis_size("seq")
    chips = max(n // 2, 1)
    rows, half = arrays[0].shape[0], arrays[3].shape[0]
    fits = (
        n % 8 == 0
        and n & (n - 1) == 0
        and arrays[0].shape[1] % (chips * LANES) == 0
        and arrays[3].shape[1] % (chips * LANES) == 0
        and HDV == LANES
        and LANES % HDA == 0
        and rows == 2 * half
        and half % 8 == 0
        and half & (half - 1) == 0
    )
    return shards_packed(*arrays) if fits else shards_general(*arrays)


def solution(mesh):
    placed = (
        P(("clip", "seq"), None),
        P(("clip", "seq"), None),
        P(("clip", "seq"), None),
        P(("clip", "seq"), None),
        P(("clip", "seq"), None),
        P(("clip", "seq"), None),
        P(("clip", "seq"), None),
        P(("clip", "seq"), None),
        P(("clip", "seq"), None),
        P(("clip", "seq"), None),
        P(("clip", "seq"), None),
        P(("clip", "seq"), None),
        P("clip"),
        P("clip"),
        P("clip"),
    )
    return jax.shard_map(
        shards,
        mesh=mesh,
        in_specs=placed,
        out_specs=(
            P(("clip", "seq"), None),
            P(("clip", "seq"), None),
            P(("clip", "seq"), None),
            P(("clip", "seq"), None),
        ),
        check_vma=False,
    )
```

```python
import functools
import math

import jax
import jax.numpy as jnp
from jax import lax
from jax.experimental import pallas as pl
from jax.experimental.pallas import tpu as pltpu
from jax.sharding import PartitionSpec as P

HV = 32
HDV = 128
HA = 32
HDA = 64


def block_size(total, limit):
    chosen = min(total, limit)
    while total % chosen:
        chosen -= 1
    return chosen


def split_heads(tokens, heads, depth, copies):
    rows = tokens.shape[0]
    shaped = tokens.reshape(copies, rows // copies, heads, depth).transpose(2, 0, 1, 3)
    return shaped.reshape(heads * copies, rows // copies, depth)


def spread_heads(tokens, heads, depth, copies):
    rows = tokens.shape[0]
    shaped = tokens.reshape(rows, heads, depth).transpose(1, 0, 2)
    shaped = jnp.broadcast_to(shaped[:, None], (heads, copies, rows, depth))
    return shaped.reshape(heads * copies, rows, depth)


def join_heads(owned, heads, depth, copies):
    part_rows = owned.shape[1]
    shaped = owned.reshape(heads, copies, part_rows, depth).transpose(1, 2, 0, 3)
    return shaped.reshape(copies * part_rows, heads * depth)


def owned_positions(rows, copies, devices, index):
    part_rows = rows // copies
    flat = jnp.arange(devices * part_rows, dtype=jnp.int32)
    return flat // part_rows * rows + index % copies * part_rows + flat % part_rows


def online_update(carry, scores, permit, value_tile, value_form):
    running, total, accum = carry
    scores = jnp.where(permit, scores, -1e30)
    newmax = jnp.maximum(running, jnp.max(scores, axis=2))
    weights = jnp.where(permit, jnp.exp(scores - newmax[:, :, None]), 0.0)
    factor = jnp.exp(running - newmax)
    total = total * factor + jnp.sum(weights, axis=2)
    mixed = jnp.einsum(
        value_form, weights.astype(jnp.bfloat16), value_tile, preferred_element_type=jnp.float32
    )
    accum = accum * factor[:, :, None] + mixed
    return (newmax, total, accum)


def fold_initial(rows, heads, depth):
    return (
        jnp.full((heads, rows), -1e30, jnp.float32),
        jnp.zeros((heads, rows), jnp.float32),
        jnp.zeros((heads, rows, depth), jnp.float32),
    )


def fold_piece(carry, local_query, key_rows, value_rows, permit, heads, depth):
    keyed = key_rows.reshape(key_rows.shape[0], heads, depth)
    valued = value_rows.reshape(value_rows.shape[0], heads, depth)
    scores = jnp.einsum("qhd,khd->hqk", local_query, keyed, preferred_element_type=jnp.float32) * (
        1.0 / math.sqrt(depth)
    )
    return online_update(carry, scores, permit[None], valued, "hqk,khd->hqd")


def fold_finish(carry, heads, depth):
    running, total, accum = carry
    result = (accum / total[:, :, None]).astype(jnp.bfloat16)
    return result.transpose(1, 0, 2).reshape(result.shape[1], heads * depth)


def attend_local(queries, keys, values, query_pos, key_pos, allowed):
    heads, q_count, depth = queries.shape
    k_count = keys.shape[1]
    q_block = block_size(q_count, 512)
    k_block = block_size(k_count, 2048)
    scale = 1.0 / math.sqrt(depth)
    q_tiles = queries.reshape(heads, q_count // q_block, q_block, depth).transpose(1, 0, 2, 3)
    k_tiles = keys.reshape(heads, k_count // k_block, k_block, depth).transpose(1, 0, 2, 3)
    v_tiles = values.reshape(heads, k_count // k_block, k_block, depth).transpose(1, 0, 2, 3)
    q_places = query_pos.reshape(q_count // q_block, q_block)
    k_places = key_pos.reshape(k_count // k_block, k_block)

    def one_tile(packed):
        q_tile, q_where = packed

        def absorb(carry, piece):
            k_tile, v_tile, k_where = piece
            scores = (
                jnp.einsum("hqd,hkd->hqk", q_tile, k_tile, preferred_element_type=jnp.float32)
                * scale
            )
            permit = allowed(q_where[:, None], k_where[None, :])[None]
            return (online_update(carry, scores, permit, v_tile, "hqk,hkd->hqd"), None)

        initial = fold_initial(q_block, heads, depth)
        final_state, unused = lax.scan(absorb, initial, (k_tiles, v_tiles, k_places))
        running, total, accum = final_state
        return (accum / total[:, :, None]).astype(jnp.bfloat16)

    tiles = lax.map(one_tile, (q_tiles, q_places))
    return tiles.transpose(1, 0, 2, 3).reshape(heads, q_count, depth)


def shards_general(
    video_query,
    video_keys,
    video_values,
    audio_query,
    audio_keys,
    audio_values,
    cross_video_query,
    cross_video_keys,
    cross_video_values,
    cross_audio_query,
    cross_audio_keys,
    cross_audio_values,
    video_length,
    audio_length,
    align_offset,
):
    devices = lax.axis_size("seq")
    index = lax.axis_index("seq")
    video_rows = video_query.shape[0]
    audio_rows = audio_query.shape[0]
    video_total = video_rows * devices
    audio_total = audio_rows * devices
    video_reach = video_total // 8
    audio_reach = 5 * audio_total // 8
    video_valid = video_length[0]
    audio_valid = audio_length[0]
    align_shift = align_offset[0]
    copies = max(devices // HV, 1)
    video_places = jnp.arange(video_total, dtype=jnp.int32)
    audio_places = jnp.arange(audio_total, dtype=jnp.int32)

    def video_open(q_where, k_where):
        return k_where < video_valid

    def toward_video(q_where, k_where):
        center = jnp.clip(q_where * audio_total // video_total + align_shift, 0, audio_valid - 1)
        return (k_where < audio_valid) & (jnp.abs(k_where - center) <= audio_reach)

    def toward_audio(q_where, k_where):
        center = jnp.clip((q_where - align_shift) * video_total // audio_total, 0, video_valid - 1)
        return (k_where < video_valid) & (jnp.abs(k_where - center) <= video_reach)

    video_owned = (
        lax.all_to_all(
            split_heads(video_query, HV, HDV, copies),
            "seq",
            split_axis=0,
            concat_axis=1,
            tiled=True,
        ),
        lax.all_to_all(
            spread_heads(video_keys, HV, HDV, copies),
            "seq",
            split_axis=0,
            concat_axis=1,
            tiled=True,
        ),
        lax.all_to_all(
            spread_heads(video_values, HV, HDV, copies),
            "seq",
            split_axis=0,
            concat_axis=1,
            tiled=True,
        ),
    )
    video_done = attend_local(
        video_owned[0],
        video_owned[1],
        video_owned[2],
        owned_positions(video_rows, copies, devices, index),
        video_places,
        video_open,
    )
    video_mixed = join_heads(
        lax.all_to_all(video_done, "seq", split_axis=1, concat_axis=0, tiled=True), HV, HDV, copies
    )
    audio_local = audio_query.reshape(audio_rows, HA, HDA)
    piece = (
        lax.all_gather(audio_keys, "seq", axis=0, tiled=True),
        lax.all_gather(audio_values, "seq", axis=0, tiled=True),
    )
    k_where = jnp.arange(piece[0].shape[0], dtype=jnp.int32)
    audio_k_where = k_where[None, :]
    permit = audio_k_where < audio_valid
    audio_state = fold_piece(
        fold_initial(audio_rows, HA, HDA), audio_local, piece[0], piece[1], permit, HA, HDA
    )
    audio_mixed = fold_finish(audio_state, HA, HDA)
    cross_owned = (
        lax.all_to_all(
            split_heads(cross_video_query, HA, HDA, copies),
            "seq",
            split_axis=0,
            concat_axis=1,
            tiled=True,
        ),
        lax.all_to_all(
            spread_heads(cross_audio_keys, HA, HDA, copies),
            "seq",
            split_axis=0,
            concat_axis=1,
            tiled=True,
        ),
        lax.all_to_all(
            spread_heads(cross_audio_values, HA, HDA, copies),
            "seq",
            split_axis=0,
            concat_axis=1,
            tiled=True,
        ),
    )
    cross_done = attend_local(
        cross_owned[0],
        cross_owned[1],
        cross_owned[2],
        owned_positions(video_rows, copies, devices, index),
        audio_places,
        toward_video,
    )
    video_cross = join_heads(
        lax.all_to_all(cross_done, "seq", split_axis=1, concat_axis=0, tiled=True), HA, HDA, copies
    )
    listen_owned = (
        lax.all_to_all(
            split_heads(cross_audio_query, HA, HDA, copies),
            "seq",
            split_axis=0,
            concat_axis=1,
            tiled=True,
        ),
        lax.all_to_all(
            spread_heads(cross_video_keys, HA, HDA, copies),
            "seq",
            split_axis=0,
            concat_axis=1,
            tiled=True,
        ),
        lax.all_to_all(
            spread_heads(cross_video_values, HA, HDA, copies),
            "seq",
            split_axis=0,
            concat_axis=1,
            tiled=True,
        ),
    )
    listen_done = attend_local(
        listen_owned[0],
        listen_owned[1],
        listen_owned[2],
        owned_positions(audio_rows, copies, devices, index),
        video_places,
        toward_audio,
    )
    audio_cross = join_heads(
        lax.all_to_all(listen_done, "seq", split_axis=1, concat_axis=0, tiled=True), HA, HDA, copies
    )
    return (video_mixed, audio_mixed, video_cross, audio_cross)


LANES = 128


def fetch(sources, held, arrived):
    copies = [
        pltpu.make_async_copy(source, slot, arrived.at[i])
        for i, (source, slot) in enumerate(zip(sources, held))
    ]
    for copy in copies:
        copy.start()
    return copies


def step_order(chips):
    far, near = list(range(chips - 1, chips // 2 - 1, -1)), list(range(1, chips // 2))
    return [0] + far[:2] + near[:2] + far[2:] + near[2:]


def by_step(items):
    order = step_order(len(items))
    return [items[order.index(j)] for j in range(len(items))]


def in_order(items):
    return [items[j] for j in step_order(len(items))]


def pack_kernel(chips, *refs):
    sources, refs = refs[:12], refs[12:]
    packed, held, arrived = by_step(refs[:chips]), refs[chips : chips + 12], refs[chips + 12]
    copies = fetch(sources, held, arrived)
    chip = lax.axis_index("seq") // 2
    video, cross, audio = held[0:3], held[3:6], held[6:12]
    rows = video[0].shape[0]

    def group(ref, j, part):
        width = ref.shape[1] // chips
        at = pl.multiple_of((chip ^ j) * width + part * LANES, LANES)
        return ref[:, pl.ds(at, LANES)]

    at = 0
    for i, ref in enumerate(video + cross):
        copies[i].wait()
        for part in range(ref.shape[1] // chips // LANES):
            for j in range(chips):
                packed[j][at : at + rows, :] = group(ref, j, part)
            at += rows
    for i in range(0, 6, 2):
        copies[6 + i].wait()
        copies[7 + i].wait()
        for part in range(audio[i].shape[1] // chips // LANES):
            for j in range(chips):
                pair = jnp.concatenate(
                    [group(audio[i], j, part), group(audio[i + 1], j, part)], axis=0
                )
                packed[j][at : at + rows, :] = pair
            at += rows


def keep_kernel(source, video_len, audio_len, shift, after, kept, bounds, *scratch):
    held, arrived = scratch[:3], scratch[3]
    copies = fetch((source, video_len, audio_len, shift), (kept, *held), arrived)
    for copy in copies:
        copy.wait()
    row = lax.broadcasted_iota(jnp.int32, bounds.shape, 0)
    bounds[...] = jnp.where(row == 0, held[0][0], jnp.where(row == 1, held[1][0], held[2][0]))


def mix_all(units):
    scores = [
        lax.dot_general(query, key, (((1,), (1,)), ((), ())), preferred_element_type=jnp.float32)
        for query, key, value, depth, permit in units
    ]
    weights, totals = [], []
    for score, (query, key, value, depth, permit) in zip(scores, units):
        score = jnp.where(permit, score, -1e30)
        peak = jnp.max(score, axis=1, keepdims=True)
        weight = jnp.exp2((score - peak) * (math.log2(math.e) / math.sqrt(depth)))
        totals.append(jnp.sum(weight, axis=1, keepdims=True))
        weights.append(weight.astype(jnp.bfloat16))
    return [
        jnp.dot(weight, unit[2], preferred_element_type=jnp.float32) / total
        for weight, total, unit in zip(weights, totals, units)
    ]


def pair_units(query, key, value, permit):
    lane = lax.broadcasted_iota(jnp.int32, query.shape, 1) // HDA
    zero = jnp.zeros_like(query)
    return [
        (jnp.where(lane == h, query, zero), key, value, HDA, permit) for h in range(LANES // HDA)
    ]


def pair_join(mixed):
    lane = lax.broadcasted_iota(jnp.int32, mixed[0].shape, 1) // HDA
    result = mixed[0]
    for h in range(1, len(mixed)):
        result = jnp.where(lane == h, mixed[h], result)
    return result


def shares(chips):
    zero = list(range(chips - 1, 3 * chips // 4 - 1, -1)) + list(range(chips // 4 - 1, -1, -1))
    one = list(range(3 * chips // 4 - 1, chips // 4 - 1, -1))
    return list(zip(zero, one))


def attend_kernel(chips, rows, parts, pairs, bounds, *refs):
    own, other = by_step(refs[:chips]), by_step(refs[chips : 2 * chips])
    done = refs[2 * chips :]
    share = shares(chips)
    every = [ref for both in zip(own, other) for ref in both]
    half = rows // 2
    tv, ta = 2 * chips * rows, 2 * chips * half
    bits = (tv // ta).bit_length() - 1
    me = lax.axis_index("seq")
    core, home = me % 2, me // 2 * 2
    video_valid, audio_valid, offset = (bounds[i : i + 1, 0:1] for i in range(3))

    def slab(at):
        return jnp.concatenate([ref[at : at + rows, :] for ref in every], axis=0)

    def asked(at):
        pieces = []
        for zero, one in share:
            for c in range(2):
                low = (own, other)[c][zero][at : at + rows, :]
                high = (other, own)[c][one][at : at + rows, :]
                pieces.append(jnp.where(core == 0, low, high))
        return jnp.concatenate(pieces, axis=0)

    def split(wide):
        wide = wide.astype(jnp.float32).reshape(-1, rows, LANES)
        first = wide[:, :half, :].reshape(-1, LANES).astype(jnp.bfloat16)
        second = wide[:, half:, :].reshape(-1, LANES).astype(jnp.bfloat16)
        return first, second

    def places(q_step, k_step):
        shape = (chips * q_step, 2 * chips * k_step)
        k_at = lax.broadcasted_iota(jnp.int32, shape, 1) ^ (me * k_step)
        starts = []
        for zero, one in share:
            chip = home ^ jnp.where(core == 0, 2 * zero, 2 * one)
            starts.append(lax.broadcasted_iota(jnp.int32, (2 * q_step, 1), 0) + chip * q_step)
        return jnp.concatenate(starts, axis=0), k_at

    def put(at, mixed):
        count = done[0].shape[0] // 2
        for u in range(len(share)):
            for c in range(2):
                piece = mixed[(2 * u + c) * rows : (2 * u + c + 1) * rows]
                done[u][c * count + at : c * count + at + rows, :] = piece.astype(jnp.bfloat16)

    q_at, k_at = places(rows, rows)
    permit = k_at < video_valid
    units = [
        (
            asked(h * rows),
            slab((parts + h) * rows),
            slab((2 * parts + h) * rows),
            HDV,
            permit,
        )
        for h in range(parts)
    ]
    for h, mixed in enumerate(mix_all(units)):
        put(h * rows, mixed)

    cross = 3 * parts * rows
    audio = cross + 3 * pairs * rows
    q_at, k_at = places(rows, half)
    center = jnp.clip((q_at >> bits) + offset, 0, audio_valid - 1)
    toward_video = (k_at < audio_valid) & (jnp.abs(k_at - center) <= 5 * ta // 8)
    q_at, k_at = places(half, half)
    within_audio = k_at < audio_valid
    q_at, k_at = places(half, rows)
    center = jnp.clip((q_at - offset) << bits, 0, video_valid - 1)
    toward_audio = (k_at < video_valid) & (jnp.abs(k_at - center) <= tv // 8)
    units = []
    for p in range(pairs):
        at = cross + p * rows
        cross_query = asked(at)
        cross_keys = slab(at + pairs * rows)
        cross_values = slab(at + 2 * pairs * rows)
        at = audio + p * rows
        audio_query = split(asked(at))[0]
        audio_keys = split(slab(at))[1]
        at += pairs * rows
        audio_values = split(slab(at))[0]
        listen_query = split(asked(at))[1]
        at += pairs * rows
        sound_keys, sound_values = split(slab(at))
        units += pair_units(cross_query, sound_keys, sound_values, toward_video)
        units += pair_units(audio_query, audio_keys, audio_values, within_audio)
        units += pair_units(listen_query, cross_keys, cross_values, toward_audio)
    mixed = mix_all(units)
    heads = LANES // HDA
    for p in range(pairs):
        seen, heard, listened = (
            pair_join(mixed[(3 * p + i) * heads : (3 * p + i + 1) * heads]) for i in range(3)
        )
        out = (parts + p) * rows
        put(out, seen)
        both = jnp.concatenate(
            [heard.reshape(-1, half, LANES), listened.reshape(-1, half, LANES)], axis=1
        )
        put(out + pairs * rows, both.reshape(-1, LANES))


def unpack_kernel(chips, *refs):
    share = shares(chips)
    back, other = refs[: len(share)], refs[len(share) : 2 * len(share)]
    video_mixed, audio_mixed, video_cross, audio_cross = refs[2 * len(share) :]
    rows = video_mixed.shape[0]
    half = audio_mixed.shape[0]
    parts = video_mixed.shape[1] // chips // LANES
    pairs = audio_mixed.shape[1] // chips // LANES
    me = lax.axis_index("seq")
    core, home = me % 2, me // 2
    for u, (zero, one) in enumerate(share):
        for ref, chip in (
            (back[u], home ^ jnp.where(core == 0, zero, one)),
            (other[u], home ^ jnp.where(core == 0, one, zero)),
        ):
            base = pl.multiple_of(core * (ref.shape[0] // 2), 16)

            def piece(at):
                return ref[pl.ds(base + at, rows), :]

            for h in range(parts):
                at = pl.multiple_of((chip * parts + h) * LANES, LANES)
                video_mixed[:, pl.ds(at, LANES)] = piece(h * rows)
            for p in range(pairs):
                at = pl.multiple_of((chip * pairs + p) * LANES, LANES)
                out = (parts + p) * rows
                video_cross[:, pl.ds(at, LANES)] = piece(out)
                both = piece(out + pairs * rows)
                audio_mixed[:, pl.ds(at, LANES)] = both[:half, :]
                audio_cross[:, pl.ds(at, LANES)] = both[half:, :]


def swap(piece, n, step):
    return lax.ppermute(piece, "seq", [(i, i ^ step) for i in range(n)])


def shards_packed(*arrays):
    (
        video_query, video_keys, video_values,
        audio_query, audio_keys, audio_values,
        cross_video_query, cross_video_keys, cross_video_values,
        cross_audio_query, cross_audio_keys, cross_audio_values,
        video_length, audio_length, align_offset,
    ) = arrays
    n = lax.axis_size("seq")
    chips = n // 2
    rows = video_query.shape[0]
    parts = video_query.shape[1] // chips // LANES
    pairs = audio_query.shape[1] // chips // LANES
    vmem = pl.BlockSpec(memory_space=pltpu.VMEM)
    hbm = pl.BlockSpec(memory_space=pltpu.HBM)
    params = pltpu.CompilerParams(vmem_limit_bytes=32 * 1024 * 1024)

    def buffer(*shape):
        return jax.ShapeDtypeStruct(shape, jnp.bfloat16)

    sources = (
        video_query, video_keys, video_values,
        cross_video_query, cross_video_keys, cross_video_values,
        audio_query, audio_keys, audio_values,
        cross_audio_query, cross_audio_keys, cross_audio_values,
    )
    packed = pl.pallas_call(
        functools.partial(pack_kernel, chips),
        out_shape=[buffer((3 * parts + 6 * pairs) * rows, LANES)] * chips,
        in_specs=[hbm] * 12,
        out_specs=[vmem] * chips,
        scratch_shapes=[pltpu.VMEM(source.shape, source.dtype) for source in sources]
        + [pltpu.SemaphoreType.DMA((12,))],
        compiler_params=pltpu.CompilerParams(vmem_limit_bytes=60 * 1024 * 1024),
    )(*sources)
    packed = by_step(packed)
    moved = [swap(packed[j], n, 2 * j) for j in range(1, chips)]
    kept, bounds = pl.pallas_call(
        keep_kernel,
        out_shape=(packed[0], jax.ShapeDtypeStruct((8, LANES), jnp.int32)),
        in_specs=[hbm] * 4 + [pl.BlockSpec(memory_space=pl.ANY)],
        out_specs=(vmem, vmem),
        scratch_shapes=[pltpu.SMEM((1,), jnp.int32)] * 3 + [pltpu.SemaphoreType.DMA((4,))],
        compiler_params=params,
    )(packed[0], video_length, audio_length, align_offset, moved[-1])
    own = [kept] + moved
    other = [swap(piece, n, 1) for piece in own]
    share = shares(chips)
    done = pl.pallas_call(
        functools.partial(attend_kernel, chips, rows, parts, pairs),
        out_shape=[buffer(2 * (parts + 2 * pairs) * rows, LANES)] * len(share),
        in_specs=[vmem] * (1 + 2 * chips),
        out_specs=[vmem] * len(share),
        compiler_params=params,
    )(bounds, *in_order(own), *in_order(other))
    back = [
        lax.ppermute(piece, "seq", [(i, i ^ 2 * pair[i % 2]) for i in range(n)])
        for piece, pair in zip(done, share)
    ]
    return pl.pallas_call(
        functools.partial(unpack_kernel, chips),
        out_shape=(
            buffer(*video_query.shape),
            buffer(*audio_query.shape),
            buffer(*cross_video_query.shape),
            buffer(*cross_audio_query.shape),
        ),
        in_specs=[vmem] * (2 * len(share)),
        out_specs=(vmem,) * 4,
        compiler_params=params,
    )(*back, *[swap(piece, n, 1) for piece in back])


def shards(*arrays):
    n = lax.axis_size("seq")
    chips = max(n // 2, 1)
    rows, half = arrays[0].shape[0], arrays[3].shape[0]
    fits = (
        n % 8 == 0
        and n & (n - 1) == 0
        and arrays[0].shape[1] % (chips * LANES) == 0
        and arrays[3].shape[1] % (chips * LANES) == 0
        and HDV == LANES
        and LANES % HDA == 0
        and rows == 2 * half
        and half % 8 == 0
        and half & (half - 1) == 0
    )
    return shards_packed(*arrays) if fits else shards_general(*arrays)


def solution(mesh):
    placed = (
        P(("clip", "seq"), None),
        P(("clip", "seq"), None),
        P(("clip", "seq"), None),
        P(("clip", "seq"), None),
        P(("clip", "seq"), None),
        P(("clip", "seq"), None),
        P(("clip", "seq"), None),
        P(("clip", "seq"), None),
        P(("clip", "seq"), None),
        P(("clip", "seq"), None),
        P(("clip", "seq"), None),
        P(("clip", "seq"), None),
        P("clip"),
        P("clip"),
        P("clip"),
    )
    return jax.shard_map(
        shards,
        mesh=mesh,
        in_specs=placed,
        out_specs=(
            P(("clip", "seq"), None),
            P(("clip", "seq"), None),
            P(("clip", "seq"), None),
            P(("clip", "seq"), None),
        ),
        check_vma=False,
    )
```

```python
import functools
import math

import jax
import jax.numpy as jnp
from jax import lax
from jax.experimental import pallas as pl
from jax.experimental.pallas import tpu as pltpu
from jax.sharding import PartitionSpec as P

HV = 32
HDV = 128
HA = 32
HDA = 64


def block_size(total, limit):
    chosen = min(total, limit)
    while total % chosen:
        chosen -= 1
    return chosen


def split_heads(tokens, heads, depth, copies):
    rows = tokens.shape[0]
    shaped = tokens.reshape(copies, rows // copies, heads, depth).transpose(2, 0, 1, 3)
    return shaped.reshape(heads * copies, rows // copies, depth)


def spread_heads(tokens, heads, depth, copies):
    rows = tokens.shape[0]
    shaped = tokens.reshape(rows, heads, depth).transpose(1, 0, 2)
    shaped = jnp.broadcast_to(shaped[:, None], (heads, copies, rows, depth))
    return shaped.reshape(heads * copies, rows, depth)


def join_heads(owned, heads, depth, copies):
    part_rows = owned.shape[1]
    shaped = owned.reshape(heads, copies, part_rows, depth).transpose(1, 2, 0, 3)
    return shaped.reshape(copies * part_rows, heads * depth)


def owned_positions(rows, copies, devices, index):
    part_rows = rows // copies
    flat = jnp.arange(devices * part_rows, dtype=jnp.int32)
    return flat // part_rows * rows + index % copies * part_rows + flat % part_rows


def online_update(carry, scores, permit, value_tile, value_form):
    running, total, accum = carry
    scores = jnp.where(permit, scores, -1e30)
    newmax = jnp.maximum(running, jnp.max(scores, axis=2))
    weights = jnp.where(permit, jnp.exp(scores - newmax[:, :, None]), 0.0)
    factor = jnp.exp(running - newmax)
    total = total * factor + jnp.sum(weights, axis=2)
    mixed = jnp.einsum(
        value_form, weights.astype(jnp.bfloat16), value_tile, preferred_element_type=jnp.float32
    )
    accum = accum * factor[:, :, None] + mixed
    return (newmax, total, accum)


def fold_initial(rows, heads, depth):
    return (
        jnp.full((heads, rows), -1e30, jnp.float32),
        jnp.zeros((heads, rows), jnp.float32),
        jnp.zeros((heads, rows, depth), jnp.float32),
    )


def fold_piece(carry, local_query, key_rows, value_rows, permit, heads, depth):
    keyed = key_rows.reshape(key_rows.shape[0], heads, depth)
    valued = value_rows.reshape(value_rows.shape[0], heads, depth)
    scores = jnp.einsum("qhd,khd->hqk", local_query, keyed, preferred_element_type=jnp.float32) * (
        1.0 / math.sqrt(depth)
    )
    return online_update(carry, scores, permit[None], valued, "hqk,khd->hqd")


def fold_finish(carry, heads, depth):
    running, total, accum = carry
    result = (accum / total[:, :, None]).astype(jnp.bfloat16)
    return result.transpose(1, 0, 2).reshape(result.shape[1], heads * depth)


def attend_local(queries, keys, values, query_pos, key_pos, allowed):
    heads, q_count, depth = queries.shape
    k_count = keys.shape[1]
    q_block = block_size(q_count, 512)
    k_block = block_size(k_count, 2048)
    scale = 1.0 / math.sqrt(depth)
    q_tiles = queries.reshape(heads, q_count // q_block, q_block, depth).transpose(1, 0, 2, 3)
    k_tiles = keys.reshape(heads, k_count // k_block, k_block, depth).transpose(1, 0, 2, 3)
    v_tiles = values.reshape(heads, k_count // k_block, k_block, depth).transpose(1, 0, 2, 3)
    q_places = query_pos.reshape(q_count // q_block, q_block)
    k_places = key_pos.reshape(k_count // k_block, k_block)

    def one_tile(packed):
        q_tile, q_where = packed

        def absorb(carry, piece):
            k_tile, v_tile, k_where = piece
            scores = (
                jnp.einsum("hqd,hkd->hqk", q_tile, k_tile, preferred_element_type=jnp.float32)
                * scale
            )
            permit = allowed(q_where[:, None], k_where[None, :])[None]
            return (online_update(carry, scores, permit, v_tile, "hqk,hkd->hqd"), None)

        initial = fold_initial(q_block, heads, depth)
        final_state, unused = lax.scan(absorb, initial, (k_tiles, v_tiles, k_places))
        running, total, accum = final_state
        return (accum / total[:, :, None]).astype(jnp.bfloat16)

    tiles = lax.map(one_tile, (q_tiles, q_places))
    return tiles.transpose(1, 0, 2, 3).reshape(heads, q_count, depth)


def shards_general(
    video_query,
    video_keys,
    video_values,
    audio_query,
    audio_keys,
    audio_values,
    cross_video_query,
    cross_video_keys,
    cross_video_values,
    cross_audio_query,
    cross_audio_keys,
    cross_audio_values,
    video_length,
    audio_length,
    align_offset,
):
    devices = lax.axis_size("seq")
    index = lax.axis_index("seq")
    video_rows = video_query.shape[0]
    audio_rows = audio_query.shape[0]
    video_total = video_rows * devices
    audio_total = audio_rows * devices
    video_reach = video_total // 8
    audio_reach = 5 * audio_total // 8
    video_valid = video_length[0]
    audio_valid = audio_length[0]
    align_shift = align_offset[0]
    copies = max(devices // HV, 1)
    video_places = jnp.arange(video_total, dtype=jnp.int32)
    audio_places = jnp.arange(audio_total, dtype=jnp.int32)

    def video_open(q_where, k_where):
        return k_where < video_valid

    def toward_video(q_where, k_where):
        center = jnp.clip(q_where * audio_total // video_total + align_shift, 0, audio_valid - 1)
        return (k_where < audio_valid) & (jnp.abs(k_where - center) <= audio_reach)

    def toward_audio(q_where, k_where):
        center = jnp.clip((q_where - align_shift) * video_total // audio_total, 0, video_valid - 1)
        return (k_where < video_valid) & (jnp.abs(k_where - center) <= video_reach)

    video_owned = (
        lax.all_to_all(
            split_heads(video_query, HV, HDV, copies),
            "seq",
            split_axis=0,
            concat_axis=1,
            tiled=True,
        ),
        lax.all_to_all(
            spread_heads(video_keys, HV, HDV, copies),
            "seq",
            split_axis=0,
            concat_axis=1,
            tiled=True,
        ),
        lax.all_to_all(
            spread_heads(video_values, HV, HDV, copies),
            "seq",
            split_axis=0,
            concat_axis=1,
            tiled=True,
        ),
    )
    video_done = attend_local(
        video_owned[0],
        video_owned[1],
        video_owned[2],
        owned_positions(video_rows, copies, devices, index),
        video_places,
        video_open,
    )
    video_mixed = join_heads(
        lax.all_to_all(video_done, "seq", split_axis=1, concat_axis=0, tiled=True), HV, HDV, copies
    )
    audio_local = audio_query.reshape(audio_rows, HA, HDA)
    piece = (
        lax.all_gather(audio_keys, "seq", axis=0, tiled=True),
        lax.all_gather(audio_values, "seq", axis=0, tiled=True),
    )
    k_where = jnp.arange(piece[0].shape[0], dtype=jnp.int32)
    audio_k_where = k_where[None, :]
    permit = audio_k_where < audio_valid
    audio_state = fold_piece(
        fold_initial(audio_rows, HA, HDA), audio_local, piece[0], piece[1], permit, HA, HDA
    )
    audio_mixed = fold_finish(audio_state, HA, HDA)
    cross_owned = (
        lax.all_to_all(
            split_heads(cross_video_query, HA, HDA, copies),
            "seq",
            split_axis=0,
            concat_axis=1,
            tiled=True,
        ),
        lax.all_to_all(
            spread_heads(cross_audio_keys, HA, HDA, copies),
            "seq",
            split_axis=0,
            concat_axis=1,
            tiled=True,
        ),
        lax.all_to_all(
            spread_heads(cross_audio_values, HA, HDA, copies),
            "seq",
            split_axis=0,
            concat_axis=1,
            tiled=True,
        ),
    )
    cross_done = attend_local(
        cross_owned[0],
        cross_owned[1],
        cross_owned[2],
        owned_positions(video_rows, copies, devices, index),
        audio_places,
        toward_video,
    )
    video_cross = join_heads(
        lax.all_to_all(cross_done, "seq", split_axis=1, concat_axis=0, tiled=True), HA, HDA, copies
    )
    listen_owned = (
        lax.all_to_all(
            split_heads(cross_audio_query, HA, HDA, copies),
            "seq",
            split_axis=0,
            concat_axis=1,
            tiled=True,
        ),
        lax.all_to_all(
            spread_heads(cross_video_keys, HA, HDA, copies),
            "seq",
            split_axis=0,
            concat_axis=1,
            tiled=True,
        ),
        lax.all_to_all(
            spread_heads(cross_video_values, HA, HDA, copies),
            "seq",
            split_axis=0,
            concat_axis=1,
            tiled=True,
        ),
    )
    listen_done = attend_local(
        listen_owned[0],
        listen_owned[1],
        listen_owned[2],
        owned_positions(audio_rows, copies, devices, index),
        video_places,
        toward_audio,
    )
    audio_cross = join_heads(
        lax.all_to_all(listen_done, "seq", split_axis=1, concat_axis=0, tiled=True), HA, HDA, copies
    )
    return (video_mixed, audio_mixed, video_cross, audio_cross)


LANES = 128


def fetch(sources, held, arrived):
    copies = [
        pltpu.make_async_copy(source, slot, arrived.at[i])
        for i, (source, slot) in enumerate(zip(sources, held))
    ]
    for copy in copies:
        copy.start()
    return copies


def step_order(chips):
    far, near = list(range(chips - 1, chips // 2 - 1, -1)), list(range(1, chips // 2))
    return [0] + near[:1] + far[:2] + near[1:2] + far[2:] + near[2:]


def by_step(items):
    order = step_order(len(items))
    return [items[order.index(j)] for j in range(len(items))]


def in_order(items):
    return [items[j] for j in step_order(len(items))]


def pack_kernel(chips, *refs):
    sources, refs = refs[:12], refs[12:]
    packed, held, arrived = by_step(refs[:chips]), refs[chips : chips + 12], refs[chips + 12]
    copies = fetch(sources, held, arrived)
    chip = lax.axis_index("seq") // 2
    video, cross, audio = held[0:3], held[3:6], held[6:12]
    rows = video[0].shape[0]

    def group(ref, j, part):
        width = ref.shape[1] // chips
        at = pl.multiple_of((chip ^ j) * width + part * LANES, LANES)
        return ref[:, pl.ds(at, LANES)]

    at = 0
    for i, ref in enumerate(video + cross):
        copies[i].wait()
        for part in range(ref.shape[1] // chips // LANES):
            for j in range(chips):
                packed[j][at : at + rows, :] = group(ref, j, part)
            at += rows
    for i in range(0, 6, 2):
        copies[6 + i].wait()
        copies[7 + i].wait()
        for part in range(audio[i].shape[1] // chips // LANES):
            for j in range(chips):
                pair = jnp.concatenate(
                    [group(audio[i], j, part), group(audio[i + 1], j, part)], axis=0
                )
                packed[j][at : at + rows, :] = pair
            at += rows


def bounds_kernel(video_len, audio_len, shift, after, slab, bounds, same):
    row = lax.broadcasted_iota(jnp.int32, bounds.shape, 0)
    bounds[...] = jnp.where(row == 0, video_len[0], jnp.where(row == 1, audio_len[0], shift[0]))


def mix_all(units):
    scores = [
        lax.dot_general(query, key, (((1,), (1,)), ((), ())), preferred_element_type=jnp.float32)
        for query, key, value, depth, permit in units
    ]
    weights, totals = [], []
    for score, (query, key, value, depth, permit) in zip(scores, units):
        score = jnp.where(permit, score, -1e30)
        peak = jnp.max(score, axis=1, keepdims=True)
        weight = jnp.exp2((score - peak) * (math.log2(math.e) / math.sqrt(depth)))
        totals.append(jnp.sum(weight, axis=1, keepdims=True))
        weights.append(weight.astype(jnp.bfloat16))
    return [
        jnp.dot(weight, unit[2], preferred_element_type=jnp.float32) / total
        for weight, total, unit in zip(weights, totals, units)
    ]


def pair_units(query, key, value, permit):
    lane = lax.broadcasted_iota(jnp.int32, query.shape, 1) // HDA
    zero = jnp.zeros_like(query)
    return [
        (jnp.where(lane == h, query, zero), key, value, HDA, permit) for h in range(LANES // HDA)
    ]


def pair_join(mixed):
    lane = lax.broadcasted_iota(jnp.int32, mixed[0].shape, 1) // HDA
    result = mixed[0]
    for h in range(1, len(mixed)):
        result = jnp.where(lane == h, mixed[h], result)
    return result


def shares(chips):
    zero = list(range(chips - 1, 3 * chips // 4 - 1, -1)) + list(range(chips // 4 - 1, -1, -1))
    one = list(range(3 * chips // 4 - 1, chips // 4 - 1, -1))
    return list(zip(zero, one))


def attend_kernel(chips, rows, parts, pairs, bounds, *refs):
    own, other = by_step(refs[:chips]), by_step(refs[chips : 2 * chips])
    done = refs[2 * chips :]
    share = shares(chips)
    every = [ref for both in zip(own, other) for ref in both]
    half = rows // 2
    tv, ta = 2 * chips * rows, 2 * chips * half
    bits = (tv // ta).bit_length() - 1
    me = lax.axis_index("seq")
    core, home = me % 2, me // 2 * 2
    video_valid, audio_valid, offset = (bounds[i : i + 1, 0:1] for i in range(3))

    def slab(at):
        return jnp.concatenate([ref[at : at + rows, :] for ref in every], axis=0)

    def asked(at):
        pieces = []
        for zero, one in share:
            for c in range(2):
                low = (own, other)[c][zero][at : at + rows, :]
                high = (other, own)[c][one][at : at + rows, :]
                pieces.append(jnp.where(core == 0, low, high))
        return jnp.concatenate(pieces, axis=0)

    def split(wide):
        wide = wide.astype(jnp.float32).reshape(-1, rows, LANES)
        first = wide[:, :half, :].reshape(-1, LANES).astype(jnp.bfloat16)
        second = wide[:, half:, :].reshape(-1, LANES).astype(jnp.bfloat16)
        return first, second

    def places(q_step, k_step):
        shape = (chips * q_step, 2 * chips * k_step)
        k_at = lax.broadcasted_iota(jnp.int32, shape, 1) ^ (me * k_step)
        starts = []
        for zero, one in share:
            chip = home ^ jnp.where(core == 0, 2 * zero, 2 * one)
            starts.append(lax.broadcasted_iota(jnp.int32, (2 * q_step, 1), 0) + chip * q_step)
        return jnp.concatenate(starts, axis=0), k_at

    def put(at, mixed):
        count = done[0].shape[0] // 2
        for u in range(len(share)):
            for c in range(2):
                piece = mixed[(2 * u + c) * rows : (2 * u + c + 1) * rows]
                done[u][c * count + at : c * count + at + rows, :] = piece.astype(jnp.bfloat16)

    q_at, k_at = places(rows, rows)
    permit = k_at < video_valid
    units = [
        (
            asked(h * rows),
            slab((parts + h) * rows),
            slab((2 * parts + h) * rows),
            HDV,
            permit,
        )
        for h in range(parts)
    ]
    for h, mixed in enumerate(mix_all(units)):
        put(h * rows, mixed)

    cross = 3 * parts * rows
    audio = cross + 3 * pairs * rows
    q_at, k_at = places(rows, half)
    center = jnp.clip((q_at >> bits) + offset, 0, audio_valid - 1)
    toward_video = (k_at < audio_valid) & (jnp.abs(k_at - center) <= 5 * ta // 8)
    q_at, k_at = places(half, half)
    within_audio = k_at < audio_valid
    q_at, k_at = places(half, rows)
    center = jnp.clip((q_at - offset) << bits, 0, video_valid - 1)
    toward_audio = (k_at < video_valid) & (jnp.abs(k_at - center) <= tv // 8)
    units = []
    for p in range(pairs):
        at = cross + p * rows
        cross_query = asked(at)
        cross_keys = slab(at + pairs * rows)
        cross_values = slab(at + 2 * pairs * rows)
        at = audio + p * rows
        audio_query = split(asked(at))[0]
        audio_keys = split(slab(at))[1]
        at += pairs * rows
        audio_values = split(slab(at))[0]
        listen_query = split(asked(at))[1]
        at += pairs * rows
        sound_keys, sound_values = split(slab(at))
        units += pair_units(cross_query, sound_keys, sound_values, toward_video)
        units += pair_units(audio_query, audio_keys, audio_values, within_audio)
        units += pair_units(listen_query, cross_keys, cross_values, toward_audio)
    mixed = mix_all(units)
    heads = LANES // HDA
    for p in range(pairs):
        seen, heard, listened = (
            pair_join(mixed[(3 * p + i) * heads : (3 * p + i + 1) * heads]) for i in range(3)
        )
        out = (parts + p) * rows
        put(out, seen)
        both = jnp.concatenate(
            [heard.reshape(-1, half, LANES), listened.reshape(-1, half, LANES)], axis=1
        )
        put(out + pairs * rows, both.reshape(-1, LANES))


def unpack_kernel(chips, *refs):
    share = shares(chips)
    back, other = refs[: len(share)], refs[len(share) : 2 * len(share)]
    video_mixed, audio_mixed, video_cross, audio_cross = refs[2 * len(share) :]
    rows = video_mixed.shape[0]
    half = audio_mixed.shape[0]
    parts = video_mixed.shape[1] // chips // LANES
    pairs = audio_mixed.shape[1] // chips // LANES
    me = lax.axis_index("seq")
    core, home = me % 2, me // 2
    for u, (zero, one) in enumerate(share):
        for ref, chip in (
            (back[u], home ^ jnp.where(core == 0, zero, one)),
            (other[u], home ^ jnp.where(core == 0, one, zero)),
        ):
            base = pl.multiple_of(core * (ref.shape[0] // 2), 16)

            def piece(at):
                return ref[pl.ds(base + at, rows), :]

            for h in range(parts):
                at = pl.multiple_of((chip * parts + h) * LANES, LANES)
                video_mixed[:, pl.ds(at, LANES)] = piece(h * rows)
            for p in range(pairs):
                at = pl.multiple_of((chip * pairs + p) * LANES, LANES)
                out = (parts + p) * rows
                video_cross[:, pl.ds(at, LANES)] = piece(out)
                both = piece(out + pairs * rows)
                audio_mixed[:, pl.ds(at, LANES)] = both[:half, :]
                audio_cross[:, pl.ds(at, LANES)] = both[half:, :]


def swap(piece, n, step):
    return lax.ppermute(piece, "seq", [(i, i ^ step) for i in range(n)])


def shards_packed(*arrays):
    (
        video_query, video_keys, video_values,
        audio_query, audio_keys, audio_values,
        cross_video_query, cross_video_keys, cross_video_values,
        cross_audio_query, cross_audio_keys, cross_audio_values,
        video_length, audio_length, align_offset,
    ) = arrays
    n = lax.axis_size("seq")
    chips = n // 2
    rows = video_query.shape[0]
    parts = video_query.shape[1] // chips // LANES
    pairs = audio_query.shape[1] // chips // LANES
    vmem = pl.BlockSpec(memory_space=pltpu.VMEM)
    hbm = pl.BlockSpec(memory_space=pltpu.HBM)
    smem = pl.BlockSpec(memory_space=pltpu.SMEM)
    params = pltpu.CompilerParams(vmem_limit_bytes=32 * 1024 * 1024)

    def buffer(*shape):
        return jax.ShapeDtypeStruct(shape, jnp.bfloat16)

    sources = (
        video_query, video_keys, video_values,
        cross_video_query, cross_video_keys, cross_video_values,
        audio_query, audio_keys, audio_values,
        cross_audio_query, cross_audio_keys, cross_audio_values,
    )
    packed = pl.pallas_call(
        functools.partial(pack_kernel, chips),
        out_shape=[pltpu.VMEM(((3 * parts + 6 * pairs) * rows, LANES), jnp.bfloat16)] * chips,
        in_specs=[hbm] * 12,
        out_specs=[vmem] * chips,
        scratch_shapes=[pltpu.VMEM(source.shape, source.dtype) for source in sources]
        + [pltpu.SemaphoreType.DMA((12,))],
        compiler_params=params,
    )(*[pltpu.with_memory_space_constraint(source, pltpu.HBM) for source in sources])
    packed = by_step(packed)
    moved = [swap(packed[j], n, 2 * j) for j in range(1, chips)]
    anywhere = pl.BlockSpec(memory_space=pl.ANY)
    bounds, kept = pl.pallas_call(
        bounds_kernel,
        out_shape=(
            pltpu.VMEM((8, LANES), jnp.int32),
            pltpu.VMEM(packed[0].shape, packed[0].dtype),
        ),
        in_specs=[smem] * 3 + [anywhere] * 2,
        out_specs=(vmem, anywhere),
        input_output_aliases={4: 1},
        compiler_params=params,
    )(video_length, audio_length, align_offset, moved[0], packed[0])
    own = [kept] + moved
    other = [swap(piece, n, 1) for piece in own]
    share = shares(chips)
    done = pl.pallas_call(
        functools.partial(attend_kernel, chips, rows, parts, pairs),
        out_shape=[buffer(2 * (parts + 2 * pairs) * rows, LANES)] * len(share),
        in_specs=[vmem] * (1 + 2 * chips),
        out_specs=[vmem] * len(share),
        compiler_params=params,
    )(bounds, *in_order(own), *in_order(other))
    back = [
        lax.ppermute(piece, "seq", [(i, i ^ 2 * pair[i % 2]) for i in range(n)])
        for piece, pair in zip(done, share)
    ]
    return pl.pallas_call(
        functools.partial(unpack_kernel, chips),
        out_shape=(
            buffer(*video_query.shape),
            buffer(*audio_query.shape),
            buffer(*cross_video_query.shape),
            buffer(*cross_audio_query.shape),
        ),
        in_specs=[vmem] * (2 * len(share)),
        out_specs=(vmem,) * 4,
        compiler_params=params,
    )(*back, *[swap(piece, n, 1) for piece in back])


def shards(*arrays):
    n = lax.axis_size("seq")
    chips = max(n // 2, 1)
    rows, half = arrays[0].shape[0], arrays[3].shape[0]
    fits = (
        n % 8 == 0
        and n & (n - 1) == 0
        and arrays[0].shape[1] % (chips * LANES) == 0
        and arrays[3].shape[1] % (chips * LANES) == 0
        and HDV == LANES
        and LANES % HDA == 0
        and rows == 2 * half
        and half % 8 == 0
        and half & (half - 1) == 0
    )
    return shards_packed(*arrays) if fits else shards_general(*arrays)


def solution(mesh):
    placed = (
        P(("clip", "seq"), None),
        P(("clip", "seq"), None),
        P(("clip", "seq"), None),
        P(("clip", "seq"), None),
        P(("clip", "seq"), None),
        P(("clip", "seq"), None),
        P(("clip", "seq"), None),
        P(("clip", "seq"), None),
        P(("clip", "seq"), None),
        P(("clip", "seq"), None),
        P(("clip", "seq"), None),
        P(("clip", "seq"), None),
        P("clip"),
        P("clip"),
        P("clip"),
    )
    return jax.shard_map(
        shards,
        mesh=mesh,
        in_specs=placed,
        out_specs=(
            P(("clip", "seq"), None),
            P(("clip", "seq"), None),
            P(("clip", "seq"), None),
            P(("clip", "seq"), None),
        ),
        check_vma=False,
    )
```

```python
import functools
import math

import jax
import jax.numpy as jnp
from jax import lax
from jax.experimental import pallas as pl
from jax.experimental.pallas import tpu as pltpu
from jax.sharding import PartitionSpec as P

HV = 32
HDV = 128
HA = 32
HDA = 64


def block_size(total, limit):
    chosen = min(total, limit)
    while total % chosen:
        chosen -= 1
    return chosen


def split_heads(tokens, heads, depth, copies):
    rows = tokens.shape[0]
    shaped = tokens.reshape(copies, rows // copies, heads, depth).transpose(2, 0, 1, 3)
    return shaped.reshape(heads * copies, rows // copies, depth)


def spread_heads(tokens, heads, depth, copies):
    rows = tokens.shape[0]
    shaped = tokens.reshape(rows, heads, depth).transpose(1, 0, 2)
    shaped = jnp.broadcast_to(shaped[:, None], (heads, copies, rows, depth))
    return shaped.reshape(heads * copies, rows, depth)


def join_heads(owned, heads, depth, copies):
    part_rows = owned.shape[1]
    shaped = owned.reshape(heads, copies, part_rows, depth).transpose(1, 2, 0, 3)
    return shaped.reshape(copies * part_rows, heads * depth)


def owned_positions(rows, copies, devices, index):
    part_rows = rows // copies
    flat = jnp.arange(devices * part_rows, dtype=jnp.int32)
    return flat // part_rows * rows + index % copies * part_rows + flat % part_rows


def online_update(carry, scores, permit, value_tile, value_form):
    running, total, accum = carry
    scores = jnp.where(permit, scores, -1e30)
    newmax = jnp.maximum(running, jnp.max(scores, axis=2))
    weights = jnp.where(permit, jnp.exp(scores - newmax[:, :, None]), 0.0)
    factor = jnp.exp(running - newmax)
    total = total * factor + jnp.sum(weights, axis=2)
    mixed = jnp.einsum(
        value_form, weights.astype(jnp.bfloat16), value_tile, preferred_element_type=jnp.float32
    )
    accum = accum * factor[:, :, None] + mixed
    return (newmax, total, accum)


def fold_initial(rows, heads, depth):
    return (
        jnp.full((heads, rows), -1e30, jnp.float32),
        jnp.zeros((heads, rows), jnp.float32),
        jnp.zeros((heads, rows, depth), jnp.float32),
    )


def fold_piece(carry, local_query, key_rows, value_rows, permit, heads, depth):
    keyed = key_rows.reshape(key_rows.shape[0], heads, depth)
    valued = value_rows.reshape(value_rows.shape[0], heads, depth)
    scores = jnp.einsum("qhd,khd->hqk", local_query, keyed, preferred_element_type=jnp.float32) * (
        1.0 / math.sqrt(depth)
    )
    return online_update(carry, scores, permit[None], valued, "hqk,khd->hqd")


def fold_finish(carry, heads, depth):
    running, total, accum = carry
    result = (accum / total[:, :, None]).astype(jnp.bfloat16)
    return result.transpose(1, 0, 2).reshape(result.shape[1], heads * depth)


def attend_local(queries, keys, values, query_pos, key_pos, allowed):
    heads, q_count, depth = queries.shape
    k_count = keys.shape[1]
    q_block = block_size(q_count, 512)
    k_block = block_size(k_count, 2048)
    scale = 1.0 / math.sqrt(depth)
    q_tiles = queries.reshape(heads, q_count // q_block, q_block, depth).transpose(1, 0, 2, 3)
    k_tiles = keys.reshape(heads, k_count // k_block, k_block, depth).transpose(1, 0, 2, 3)
    v_tiles = values.reshape(heads, k_count // k_block, k_block, depth).transpose(1, 0, 2, 3)
    q_places = query_pos.reshape(q_count // q_block, q_block)
    k_places = key_pos.reshape(k_count // k_block, k_block)

    def one_tile(packed):
        q_tile, q_where = packed

        def absorb(carry, piece):
            k_tile, v_tile, k_where = piece
            scores = (
                jnp.einsum("hqd,hkd->hqk", q_tile, k_tile, preferred_element_type=jnp.float32)
                * scale
            )
            permit = allowed(q_where[:, None], k_where[None, :])[None]
            return (online_update(carry, scores, permit, v_tile, "hqk,hkd->hqd"), None)

        initial = fold_initial(q_block, heads, depth)
        final_state, unused = lax.scan(absorb, initial, (k_tiles, v_tiles, k_places))
        running, total, accum = final_state
        return (accum / total[:, :, None]).astype(jnp.bfloat16)

    tiles = lax.map(one_tile, (q_tiles, q_places))
    return tiles.transpose(1, 0, 2, 3).reshape(heads, q_count, depth)


def shards_general(
    video_query,
    video_keys,
    video_values,
    audio_query,
    audio_keys,
    audio_values,
    cross_video_query,
    cross_video_keys,
    cross_video_values,
    cross_audio_query,
    cross_audio_keys,
    cross_audio_values,
    video_length,
    audio_length,
    align_offset,
):
    devices = lax.axis_size("seq")
    index = lax.axis_index("seq")
    video_rows = video_query.shape[0]
    audio_rows = audio_query.shape[0]
    video_total = video_rows * devices
    audio_total = audio_rows * devices
    video_reach = video_total // 8
    audio_reach = 5 * audio_total // 8
    video_valid = video_length[0]
    audio_valid = audio_length[0]
    align_shift = align_offset[0]
    copies = max(devices // HV, 1)
    video_places = jnp.arange(video_total, dtype=jnp.int32)
    audio_places = jnp.arange(audio_total, dtype=jnp.int32)

    def video_open(q_where, k_where):
        return k_where < video_valid

    def toward_video(q_where, k_where):
        center = jnp.clip(q_where * audio_total // video_total + align_shift, 0, audio_valid - 1)
        return (k_where < audio_valid) & (jnp.abs(k_where - center) <= audio_reach)

    def toward_audio(q_where, k_where):
        center = jnp.clip((q_where - align_shift) * video_total // audio_total, 0, video_valid - 1)
        return (k_where < video_valid) & (jnp.abs(k_where - center) <= video_reach)

    video_owned = (
        lax.all_to_all(
            split_heads(video_query, HV, HDV, copies),
            "seq",
            split_axis=0,
            concat_axis=1,
            tiled=True,
        ),
        lax.all_to_all(
            spread_heads(video_keys, HV, HDV, copies),
            "seq",
            split_axis=0,
            concat_axis=1,
            tiled=True,
        ),
        lax.all_to_all(
            spread_heads(video_values, HV, HDV, copies),
            "seq",
            split_axis=0,
            concat_axis=1,
            tiled=True,
        ),
    )
    video_done = attend_local(
        video_owned[0],
        video_owned[1],
        video_owned[2],
        owned_positions(video_rows, copies, devices, index),
        video_places,
        video_open,
    )
    video_mixed = join_heads(
        lax.all_to_all(video_done, "seq", split_axis=1, concat_axis=0, tiled=True), HV, HDV, copies
    )
    audio_local = audio_query.reshape(audio_rows, HA, HDA)
    piece = (
        lax.all_gather(audio_keys, "seq", axis=0, tiled=True),
        lax.all_gather(audio_values, "seq", axis=0, tiled=True),
    )
    k_where = jnp.arange(piece[0].shape[0], dtype=jnp.int32)
    audio_k_where = k_where[None, :]
    permit = audio_k_where < audio_valid
    audio_state = fold_piece(
        fold_initial(audio_rows, HA, HDA), audio_local, piece[0], piece[1], permit, HA, HDA
    )
    audio_mixed = fold_finish(audio_state, HA, HDA)
    cross_owned = (
        lax.all_to_all(
            split_heads(cross_video_query, HA, HDA, copies),
            "seq",
            split_axis=0,
            concat_axis=1,
            tiled=True,
        ),
        lax.all_to_all(
            spread_heads(cross_audio_keys, HA, HDA, copies),
            "seq",
            split_axis=0,
            concat_axis=1,
            tiled=True,
        ),
        lax.all_to_all(
            spread_heads(cross_audio_values, HA, HDA, copies),
            "seq",
            split_axis=0,
            concat_axis=1,
            tiled=True,
        ),
    )
    cross_done = attend_local(
        cross_owned[0],
        cross_owned[1],
        cross_owned[2],
        owned_positions(video_rows, copies, devices, index),
        audio_places,
        toward_video,
    )
    video_cross = join_heads(
        lax.all_to_all(cross_done, "seq", split_axis=1, concat_axis=0, tiled=True), HA, HDA, copies
    )
    listen_owned = (
        lax.all_to_all(
            split_heads(cross_audio_query, HA, HDA, copies),
            "seq",
            split_axis=0,
            concat_axis=1,
            tiled=True,
        ),
        lax.all_to_all(
            spread_heads(cross_video_keys, HA, HDA, copies),
            "seq",
            split_axis=0,
            concat_axis=1,
            tiled=True,
        ),
        lax.all_to_all(
            spread_heads(cross_video_values, HA, HDA, copies),
            "seq",
            split_axis=0,
            concat_axis=1,
            tiled=True,
        ),
    )
    listen_done = attend_local(
        listen_owned[0],
        listen_owned[1],
        listen_owned[2],
        owned_positions(audio_rows, copies, devices, index),
        video_places,
        toward_audio,
    )
    audio_cross = join_heads(
        lax.all_to_all(listen_done, "seq", split_axis=1, concat_axis=0, tiled=True), HA, HDA, copies
    )
    return (video_mixed, audio_mixed, video_cross, audio_cross)


LANES = 128


def fetch(sources, held, arrived):
    copies = [
        pltpu.make_async_copy(source, slot, arrived.at[i])
        for i, (source, slot) in enumerate(zip(sources, held))
    ]
    for copy in copies:
        copy.start()
    return copies


def step_order(chips):
    far, near = list(range(chips - 1, chips // 2 - 1, -1)), list(range(1, chips // 2))
    return [0] + far[:1] + near[:1] + far[1:2] + near[1:2] + far[2:] + near[2:]


def by_step(items):
    order = step_order(len(items))
    return [items[order.index(j)] for j in range(len(items))]


def in_order(items):
    return [items[j] for j in step_order(len(items))]


def pack_kernel(chips, *refs):
    sources, refs = refs[:12], refs[12:]
    packed, held, arrived = by_step(refs[:chips]), refs[chips : chips + 12], refs[chips + 12]
    copies = fetch(sources, held, arrived)
    chip = lax.axis_index("seq") // 2
    video, cross, audio = held[0:3], held[3:6], held[6:12]
    rows = video[0].shape[0]

    def group(ref, j, part):
        width = ref.shape[1] // chips
        at = pl.multiple_of((chip ^ j) * width + part * LANES, LANES)
        return ref[:, pl.ds(at, LANES)]

    at = 0
    for i, ref in enumerate(video + cross):
        copies[i].wait()
        for part in range(ref.shape[1] // chips // LANES):
            for j in range(chips):
                packed[j][at : at + rows, :] = group(ref, j, part)
            at += rows
    for i in range(0, 6, 2):
        copies[6 + i].wait()
        copies[7 + i].wait()
        for part in range(audio[i].shape[1] // chips // LANES):
            for j in range(chips):
                pair = jnp.concatenate(
                    [group(audio[i], j, part), group(audio[i + 1], j, part)], axis=0
                )
                packed[j][at : at + rows, :] = pair
            at += rows


def bounds_kernel(video_len, audio_len, shift, after, slab, bounds, same):
    row = lax.broadcasted_iota(jnp.int32, bounds.shape, 0)
    bounds[...] = jnp.where(row == 0, video_len[0], jnp.where(row == 1, audio_len[0], shift[0]))


def mix_all(units):
    scores = [
        lax.dot_general(query, key, (((1,), (1,)), ((), ())), preferred_element_type=jnp.float32)
        for query, key, value, depth, permit in units
    ]
    weights, totals = [], []
    for score, (query, key, value, depth, permit) in zip(scores, units):
        score = jnp.where(permit, score, -1e30)
        peak = jnp.max(score, axis=1, keepdims=True)
        weight = jnp.exp2((score - peak) * (math.log2(math.e) / math.sqrt(depth)))
        totals.append(jnp.sum(weight, axis=1, keepdims=True))
        weights.append(weight.astype(jnp.bfloat16))
    return [
        jnp.dot(weight, unit[2], preferred_element_type=jnp.float32) / total
        for weight, total, unit in zip(weights, totals, units)
    ]


def pair_units(query, key, value, permit):
    lane = lax.broadcasted_iota(jnp.int32, query.shape, 1) // HDA
    zero = jnp.zeros_like(query)
    return [
        (jnp.where(lane == h, query, zero), key, value, HDA, permit) for h in range(LANES // HDA)
    ]


def pair_join(mixed):
    lane = lax.broadcasted_iota(jnp.int32, mixed[0].shape, 1) // HDA
    result = mixed[0]
    for h in range(1, len(mixed)):
        result = jnp.where(lane == h, mixed[h], result)
    return result


def shares(chips):
    quarter = chips // 4
    far = list(zip(range(chips - 1, 3 * quarter - 1, -1), range(3 * quarter - 1, 2 * quarter - 1, -1)))
    near = list(zip(range(quarter - 1, -1, -1), range(2 * quarter - 1, quarter - 1, -1)))
    return [pair for both in zip(far, near) for pair in both]


def attend_kernel(chips, rows, parts, pairs, bounds, *refs):
    own, other = by_step(refs[:chips]), by_step(refs[chips : 2 * chips])
    done = refs[2 * chips :]
    share = shares(chips)
    every = [ref for both in zip(own, other) for ref in both]
    half = rows // 2
    tv, ta = 2 * chips * rows, 2 * chips * half
    bits = (tv // ta).bit_length() - 1
    me = lax.axis_index("seq")
    core, home = me % 2, me // 2 * 2
    video_valid, audio_valid, offset = (bounds[i : i + 1, 0:1] for i in range(3))

    def slab(at):
        return jnp.concatenate([ref[at : at + rows, :] for ref in every], axis=0)

    def asked(at):
        pieces = []
        for zero, one in share:
            for c in range(2):
                low = (own, other)[c][zero][at : at + rows, :]
                high = (other, own)[c][one][at : at + rows, :]
                pieces.append(jnp.where(core == 0, low, high))
        return jnp.concatenate(pieces, axis=0)

    def split(wide):
        wide = wide.astype(jnp.float32).reshape(-1, rows, LANES)
        first = wide[:, :half, :].reshape(-1, LANES).astype(jnp.bfloat16)
        second = wide[:, half:, :].reshape(-1, LANES).astype(jnp.bfloat16)
        return first, second

    def places(q_step, k_step):
        shape = (chips * q_step, 2 * chips * k_step)
        k_at = lax.broadcasted_iota(jnp.int32, shape, 1) ^ (me * k_step)
        starts = []
        for zero, one in share:
            chip = home ^ jnp.where(core == 0, 2 * zero, 2 * one)
            starts.append(lax.broadcasted_iota(jnp.int32, (2 * q_step, 1), 0) + chip * q_step)
        return jnp.concatenate(starts, axis=0), k_at

    def put(at, mixed):
        count = done[0].shape[0] // 2
        for u in range(len(share)):
            for c in range(2):
                piece = mixed[(2 * u + c) * rows : (2 * u + c + 1) * rows]
                done[u][c * count + at : c * count + at + rows, :] = piece.astype(jnp.bfloat16)

    q_at, k_at = places(rows, rows)
    permit = k_at < video_valid
    units = [
        (
            asked(h * rows),
            slab((parts + h) * rows),
            slab((2 * parts + h) * rows),
            HDV,
            permit,
        )
        for h in range(parts)
    ]
    for h, mixed in enumerate(mix_all(units)):
        put(h * rows, mixed)

    cross = 3 * parts * rows
    audio = cross + 3 * pairs * rows
    q_at, k_at = places(rows, half)
    center = jnp.clip((q_at >> bits) + offset, 0, audio_valid - 1)
    toward_video = (k_at < audio_valid) & (jnp.abs(k_at - center) <= 5 * ta // 8)
    q_at, k_at = places(half, half)
    within_audio = k_at < audio_valid
    q_at, k_at = places(half, rows)
    center = jnp.clip((q_at - offset) << bits, 0, video_valid - 1)
    toward_audio = (k_at < video_valid) & (jnp.abs(k_at - center) <= tv // 8)
    units = []
    for p in range(pairs):
        at = cross + p * rows
        cross_query = asked(at)
        cross_keys = slab(at + pairs * rows)
        cross_values = slab(at + 2 * pairs * rows)
        at = audio + p * rows
        audio_query = split(asked(at))[0]
        audio_keys = split(slab(at))[1]
        at += pairs * rows
        audio_values = split(slab(at))[0]
        listen_query = split(asked(at))[1]
        at += pairs * rows
        sound_keys, sound_values = split(slab(at))
        units += pair_units(cross_query, sound_keys, sound_values, toward_video)
        units += pair_units(audio_query, audio_keys, audio_values, within_audio)
        units += pair_units(listen_query, cross_keys, cross_values, toward_audio)
    mixed = mix_all(units)
    heads = LANES // HDA
    for p in range(pairs):
        seen, heard, listened = (
            pair_join(mixed[(3 * p + i) * heads : (3 * p + i + 1) * heads]) for i in range(3)
        )
        out = (parts + p) * rows
        put(out, seen)
        both = jnp.concatenate(
            [heard.reshape(-1, half, LANES), listened.reshape(-1, half, LANES)], axis=1
        )
        put(out + pairs * rows, both.reshape(-1, LANES))


def unpack_kernel(chips, *refs):
    share = shares(chips)
    back, other = refs[: len(share)], refs[len(share) : 2 * len(share)]
    video_mixed, audio_mixed, video_cross, audio_cross = refs[2 * len(share) :]
    rows = video_mixed.shape[0]
    half = audio_mixed.shape[0]
    parts = video_mixed.shape[1] // chips // LANES
    pairs = audio_mixed.shape[1] // chips // LANES
    me = lax.axis_index("seq")
    core, home = me % 2, me // 2
    for u, (zero, one) in enumerate(share):
        for ref, chip in (
            (back[u], home ^ jnp.where(core == 0, zero, one)),
            (other[u], home ^ jnp.where(core == 0, one, zero)),
        ):
            base = pl.multiple_of(core * (ref.shape[0] // 2), 16)

            def piece(at):
                return ref[pl.ds(base + at, rows), :]

            for h in range(parts):
                at = pl.multiple_of((chip * parts + h) * LANES, LANES)
                video_mixed[:, pl.ds(at, LANES)] = piece(h * rows)
            for p in range(pairs):
                at = pl.multiple_of((chip * pairs + p) * LANES, LANES)
                out = (parts + p) * rows
                video_cross[:, pl.ds(at, LANES)] = piece(out)
                both = piece(out + pairs * rows)
                audio_mixed[:, pl.ds(at, LANES)] = both[:half, :]
                audio_cross[:, pl.ds(at, LANES)] = both[half:, :]


def swap(piece, n, step):
    return lax.ppermute(piece, "seq", [(i, i ^ step) for i in range(n)])


def shards_packed(*arrays):
    (
        video_query, video_keys, video_values,
        audio_query, audio_keys, audio_values,
        cross_video_query, cross_video_keys, cross_video_values,
        cross_audio_query, cross_audio_keys, cross_audio_values,
        video_length, audio_length, align_offset,
    ) = arrays
    n = lax.axis_size("seq")
    chips = n // 2
    rows = video_query.shape[0]
    parts = video_query.shape[1] // chips // LANES
    pairs = audio_query.shape[1] // chips // LANES
    vmem = pl.BlockSpec(memory_space=pltpu.VMEM)
    hbm = pl.BlockSpec(memory_space=pltpu.HBM)
    smem = pl.BlockSpec(memory_space=pltpu.SMEM)
    params = pltpu.CompilerParams(vmem_limit_bytes=32 * 1024 * 1024)

    def buffer(*shape):
        return jax.ShapeDtypeStruct(shape, jnp.bfloat16)

    sources = (
        video_query, video_keys, video_values,
        cross_video_query, cross_video_keys, cross_video_values,
        audio_query, audio_keys, audio_values,
        cross_audio_query, cross_audio_keys, cross_audio_values,
    )
    packed = pl.pallas_call(
        functools.partial(pack_kernel, chips),
        out_shape=[pltpu.VMEM(((3 * parts + 6 * pairs) * rows, LANES), jnp.bfloat16)] * chips,
        in_specs=[hbm] * 12,
        out_specs=[vmem] * chips,
        scratch_shapes=[pltpu.VMEM(source.shape, source.dtype) for source in sources]
        + [pltpu.SemaphoreType.DMA((12,))],
        compiler_params=params,
    )(*[pltpu.with_memory_space_constraint(source, pltpu.HBM) for source in sources])
    packed = by_step(packed)
    moved = [swap(packed[j], n, 2 * j) for j in range(1, chips)]
    anywhere = pl.BlockSpec(memory_space=pl.ANY)
    bounds, kept = pl.pallas_call(
        bounds_kernel,
        out_shape=(
            pltpu.VMEM((8, LANES), jnp.int32),
            pltpu.VMEM(packed[0].shape, packed[0].dtype),
        ),
        in_specs=[smem] * 3 + [anywhere] * 2,
        out_specs=(vmem, anywhere),
        input_output_aliases={4: 1},
        compiler_params=params,
    )(video_length, audio_length, align_offset, moved[-1], packed[0])
    own = [kept] + moved
    other = [swap(piece, n, 1) for piece in own]
    share = shares(chips)
    done = pl.pallas_call(
        functools.partial(attend_kernel, chips, rows, parts, pairs),
        out_shape=[buffer(2 * (parts + 2 * pairs) * rows, LANES)] * len(share),
        in_specs=[vmem] * (1 + 2 * chips),
        out_specs=[vmem] * len(share),
        compiler_params=params,
    )(bounds, *in_order(own), *in_order(other))
    back = [
        lax.ppermute(piece, "seq", [(i, i ^ 2 * pair[i % 2]) for i in range(n)])
        for piece, pair in zip(done, share)
    ]
    return pl.pallas_call(
        functools.partial(unpack_kernel, chips),
        out_shape=(
            buffer(*video_query.shape),
            buffer(*audio_query.shape),
            buffer(*cross_video_query.shape),
            buffer(*cross_audio_query.shape),
        ),
        in_specs=[vmem] * (2 * len(share)),
        out_specs=(vmem,) * 4,
        compiler_params=params,
    )(*back, *[swap(piece, n, 1) for piece in back])


def shards(*arrays):
    n = lax.axis_size("seq")
    chips = max(n // 2, 1)
    rows, half = arrays[0].shape[0], arrays[3].shape[0]
    fits = (
        n % 8 == 0
        and n & (n - 1) == 0
        and arrays[0].shape[1] % (chips * LANES) == 0
        and arrays[3].shape[1] % (chips * LANES) == 0
        and HDV == LANES
        and LANES % HDA == 0
        and rows == 2 * half
        and half % 8 == 0
        and half & (half - 1) == 0
    )
    return shards_packed(*arrays) if fits else shards_general(*arrays)


def solution(mesh):
    placed = (
        P(("clip", "seq"), None),
        P(("clip", "seq"), None),
        P(("clip", "seq"), None),
        P(("clip", "seq"), None),
        P(("clip", "seq"), None),
        P(("clip", "seq"), None),
        P(("clip", "seq"), None),
        P(("clip", "seq"), None),
        P(("clip", "seq"), None),
        P(("clip", "seq"), None),
        P(("clip", "seq"), None),
        P(("clip", "seq"), None),
        P("clip"),
        P("clip"),
        P("clip"),
    )
    return jax.shard_map(
        shards,
        mesh=mesh,
        in_specs=placed,
        out_specs=(
            P(("clip", "seq"), None),
            P(("clip", "seq"), None),
            P(("clip", "seq"), None),
            P(("clip", "seq"), None),
        ),
        check_vma=False,
    )
```

```python
import functools
import math

import jax
import jax.numpy as jnp
from jax import lax
from jax.experimental import pallas as pl
from jax.experimental.pallas import tpu as pltpu
from jax.sharding import PartitionSpec as P

HV = 32
HDV = 128
HA = 32
HDA = 64


def block_size(total, limit):
    chosen = min(total, limit)
    while total % chosen:
        chosen -= 1
    return chosen


def split_heads(tokens, heads, depth, copies):
    rows = tokens.shape[0]
    shaped = tokens.reshape(copies, rows // copies, heads, depth).transpose(2, 0, 1, 3)
    return shaped.reshape(heads * copies, rows // copies, depth)


def spread_heads(tokens, heads, depth, copies):
    rows = tokens.shape[0]
    shaped = tokens.reshape(rows, heads, depth).transpose(1, 0, 2)
    shaped = jnp.broadcast_to(shaped[:, None], (heads, copies, rows, depth))
    return shaped.reshape(heads * copies, rows, depth)


def join_heads(owned, heads, depth, copies):
    part_rows = owned.shape[1]
    shaped = owned.reshape(heads, copies, part_rows, depth).transpose(1, 2, 0, 3)
    return shaped.reshape(copies * part_rows, heads * depth)


def owned_positions(rows, copies, devices, index):
    part_rows = rows // copies
    flat = jnp.arange(devices * part_rows, dtype=jnp.int32)
    return flat // part_rows * rows + index % copies * part_rows + flat % part_rows


def online_update(carry, scores, permit, value_tile, value_form):
    running, total, accum = carry
    scores = jnp.where(permit, scores, -1e30)
    newmax = jnp.maximum(running, jnp.max(scores, axis=2))
    weights = jnp.where(permit, jnp.exp(scores - newmax[:, :, None]), 0.0)
    factor = jnp.exp(running - newmax)
    total = total * factor + jnp.sum(weights, axis=2)
    mixed = jnp.einsum(
        value_form, weights.astype(jnp.bfloat16), value_tile, preferred_element_type=jnp.float32
    )
    accum = accum * factor[:, :, None] + mixed
    return (newmax, total, accum)


def fold_initial(rows, heads, depth):
    return (
        jnp.full((heads, rows), -1e30, jnp.float32),
        jnp.zeros((heads, rows), jnp.float32),
        jnp.zeros((heads, rows, depth), jnp.float32),
    )


def fold_piece(carry, local_query, key_rows, value_rows, permit, heads, depth):
    keyed = key_rows.reshape(key_rows.shape[0], heads, depth)
    valued = value_rows.reshape(value_rows.shape[0], heads, depth)
    scores = jnp.einsum("qhd,khd->hqk", local_query, keyed, preferred_element_type=jnp.float32) * (
        1.0 / math.sqrt(depth)
    )
    return online_update(carry, scores, permit[None], valued, "hqk,khd->hqd")


def fold_finish(carry, heads, depth):
    running, total, accum = carry
    result = (accum / total[:, :, None]).astype(jnp.bfloat16)
    return result.transpose(1, 0, 2).reshape(result.shape[1], heads * depth)


def attend_local(queries, keys, values, query_pos, key_pos, allowed):
    heads, q_count, depth = queries.shape
    k_count = keys.shape[1]
    q_block = block_size(q_count, 512)
    k_block = block_size(k_count, 2048)
    scale = 1.0 / math.sqrt(depth)
    q_tiles = queries.reshape(heads, q_count // q_block, q_block, depth).transpose(1, 0, 2, 3)
    k_tiles = keys.reshape(heads, k_count // k_block, k_block, depth).transpose(1, 0, 2, 3)
    v_tiles = values.reshape(heads, k_count // k_block, k_block, depth).transpose(1, 0, 2, 3)
    q_places = query_pos.reshape(q_count // q_block, q_block)
    k_places = key_pos.reshape(k_count // k_block, k_block)

    def one_tile(packed):
        q_tile, q_where = packed

        def absorb(carry, piece):
            k_tile, v_tile, k_where = piece
            scores = (
                jnp.einsum("hqd,hkd->hqk", q_tile, k_tile, preferred_element_type=jnp.float32)
                * scale
            )
            permit = allowed(q_where[:, None], k_where[None, :])[None]
            return (online_update(carry, scores, permit, v_tile, "hqk,hkd->hqd"), None)

        initial = fold_initial(q_block, heads, depth)
        final_state, unused = lax.scan(absorb, initial, (k_tiles, v_tiles, k_places))
        running, total, accum = final_state
        return (accum / total[:, :, None]).astype(jnp.bfloat16)

    tiles = lax.map(one_tile, (q_tiles, q_places))
    return tiles.transpose(1, 0, 2, 3).reshape(heads, q_count, depth)


def shards_general(
    video_query,
    video_keys,
    video_values,
    audio_query,
    audio_keys,
    audio_values,
    cross_video_query,
    cross_video_keys,
    cross_video_values,
    cross_audio_query,
    cross_audio_keys,
    cross_audio_values,
    video_length,
    audio_length,
    align_offset,
):
    devices = lax.axis_size("seq")
    index = lax.axis_index("seq")
    video_rows = video_query.shape[0]
    audio_rows = audio_query.shape[0]
    video_total = video_rows * devices
    audio_total = audio_rows * devices
    video_reach = video_total // 8
    audio_reach = 5 * audio_total // 8
    video_valid = video_length[0]
    audio_valid = audio_length[0]
    align_shift = align_offset[0]
    copies = max(devices // HV, 1)
    video_places = jnp.arange(video_total, dtype=jnp.int32)
    audio_places = jnp.arange(audio_total, dtype=jnp.int32)

    def video_open(q_where, k_where):
        return k_where < video_valid

    def toward_video(q_where, k_where):
        center = jnp.clip(q_where * audio_total // video_total + align_shift, 0, audio_valid - 1)
        return (k_where < audio_valid) & (jnp.abs(k_where - center) <= audio_reach)

    def toward_audio(q_where, k_where):
        center = jnp.clip((q_where - align_shift) * video_total // audio_total, 0, video_valid - 1)
        return (k_where < video_valid) & (jnp.abs(k_where - center) <= video_reach)

    video_owned = (
        lax.all_to_all(
            split_heads(video_query, HV, HDV, copies),
            "seq",
            split_axis=0,
            concat_axis=1,
            tiled=True,
        ),
        lax.all_to_all(
            spread_heads(video_keys, HV, HDV, copies),
            "seq",
            split_axis=0,
            concat_axis=1,
            tiled=True,
        ),
        lax.all_to_all(
            spread_heads(video_values, HV, HDV, copies),
            "seq",
            split_axis=0,
            concat_axis=1,
            tiled=True,
        ),
    )
    video_done = attend_local(
        video_owned[0],
        video_owned[1],
        video_owned[2],
        owned_positions(video_rows, copies, devices, index),
        video_places,
        video_open,
    )
    video_mixed = join_heads(
        lax.all_to_all(video_done, "seq", split_axis=1, concat_axis=0, tiled=True), HV, HDV, copies
    )
    audio_local = audio_query.reshape(audio_rows, HA, HDA)
    piece = (
        lax.all_gather(audio_keys, "seq", axis=0, tiled=True),
        lax.all_gather(audio_values, "seq", axis=0, tiled=True),
    )
    k_where = jnp.arange(piece[0].shape[0], dtype=jnp.int32)
    audio_k_where = k_where[None, :]
    permit = audio_k_where < audio_valid
    audio_state = fold_piece(
        fold_initial(audio_rows, HA, HDA), audio_local, piece[0], piece[1], permit, HA, HDA
    )
    audio_mixed = fold_finish(audio_state, HA, HDA)
    cross_owned = (
        lax.all_to_all(
            split_heads(cross_video_query, HA, HDA, copies),
            "seq",
            split_axis=0,
            concat_axis=1,
            tiled=True,
        ),
        lax.all_to_all(
            spread_heads(cross_audio_keys, HA, HDA, copies),
            "seq",
            split_axis=0,
            concat_axis=1,
            tiled=True,
        ),
        lax.all_to_all(
            spread_heads(cross_audio_values, HA, HDA, copies),
            "seq",
            split_axis=0,
            concat_axis=1,
            tiled=True,
        ),
    )
    cross_done = attend_local(
        cross_owned[0],
        cross_owned[1],
        cross_owned[2],
        owned_positions(video_rows, copies, devices, index),
        audio_places,
        toward_video,
    )
    video_cross = join_heads(
        lax.all_to_all(cross_done, "seq", split_axis=1, concat_axis=0, tiled=True), HA, HDA, copies
    )
    listen_owned = (
        lax.all_to_all(
            split_heads(cross_audio_query, HA, HDA, copies),
            "seq",
            split_axis=0,
            concat_axis=1,
            tiled=True,
        ),
        lax.all_to_all(
            spread_heads(cross_video_keys, HA, HDA, copies),
            "seq",
            split_axis=0,
            concat_axis=1,
            tiled=True,
        ),
        lax.all_to_all(
            spread_heads(cross_video_values, HA, HDA, copies),
            "seq",
            split_axis=0,
            concat_axis=1,
            tiled=True,
        ),
    )
    listen_done = attend_local(
        listen_owned[0],
        listen_owned[1],
        listen_owned[2],
        owned_positions(audio_rows, copies, devices, index),
        video_places,
        toward_audio,
    )
    audio_cross = join_heads(
        lax.all_to_all(listen_done, "seq", split_axis=1, concat_axis=0, tiled=True), HA, HDA, copies
    )
    return (video_mixed, audio_mixed, video_cross, audio_cross)


LANES = 128


def fetch(sources, held, arrived):
    copies = [
        pltpu.make_async_copy(source, slot, arrived.at[i])
        for i, (source, slot) in enumerate(zip(sources, held))
    ]
    for copy in copies:
        copy.start()
    return copies


def step_order(chips):
    far, near = list(range(chips - 1, chips // 2 - 1, -1)), list(range(1, chips // 2))
    return [0] + far[:1] + near[:1] + far[1:2] + near[1:2] + far[2:] + near[2:]


def by_step(items):
    order = step_order(len(items))
    return [items[order.index(j)] for j in range(len(items))]


def in_order(items):
    return [items[j] for j in step_order(len(items))]


def pack_kernel(chips, *refs):
    sources, refs = refs[:12], refs[12:]
    packed, held, arrived = by_step(refs[:chips]), refs[chips : chips + 12], refs[chips + 12]
    copies = fetch(sources, held, arrived)
    chip = lax.axis_index("seq") // 2
    video, cross, audio = held[0:3], held[3:6], held[6:12]
    rows = video[0].shape[0]

    def group(ref, j, part):
        width = ref.shape[1] // chips
        at = pl.multiple_of((chip ^ j) * width + part * LANES, LANES)
        return ref[:, pl.ds(at, LANES)]

    at = 0
    for i, ref in enumerate(video + cross):
        copies[i].wait()
        for part in range(ref.shape[1] // chips // LANES):
            for j in range(chips):
                packed[j][at : at + rows, :] = group(ref, j, part)
            at += rows
    for i in range(0, 6, 2):
        copies[6 + i].wait()
        copies[7 + i].wait()
        for part in range(audio[i].shape[1] // chips // LANES):
            for j in range(chips):
                pair = jnp.concatenate(
                    [group(audio[i], j, part), group(audio[i + 1], j, part)], axis=0
                )
                packed[j][at : at + rows, :] = pair
            at += rows


def bounds_kernel(video_len, audio_len, shift, after, slab, bounds, same):
    row = lax.broadcasted_iota(jnp.int32, bounds.shape, 0)
    bounds[...] = jnp.where(row == 0, video_len[0], jnp.where(row == 1, audio_len[0], shift[0]))


def mix_all(units):
    scores = [
        lax.dot_general(query, key, (((1,), (1,)), ((), ())), preferred_element_type=jnp.float32)
        for query, key, value, depth, permit in units
    ]
    weights, totals = [], []
    for score, (query, key, value, depth, permit) in zip(scores, units):
        score = jnp.where(permit, score, -1e30)
        peak = jnp.max(score, axis=1, keepdims=True)
        weight = jnp.exp2((score - peak) * (math.log2(math.e) / math.sqrt(depth)))
        totals.append(jnp.sum(weight, axis=1, keepdims=True))
        weights.append(weight.astype(jnp.bfloat16))
    return [
        jnp.dot(weight, unit[2], preferred_element_type=jnp.float32) / total
        for weight, total, unit in zip(weights, totals, units)
    ]


def pair_units(query, key, value, permit):
    lane = lax.broadcasted_iota(jnp.int32, query.shape, 1) // HDA
    zero = jnp.zeros_like(query)
    return [
        (jnp.where(lane == h, query, zero), key, value, HDA, permit) for h in range(LANES // HDA)
    ]


def pair_join(mixed):
    lane = lax.broadcasted_iota(jnp.int32, mixed[0].shape, 1) // HDA
    result = mixed[0]
    for h in range(1, len(mixed)):
        result = jnp.where(lane == h, mixed[h], result)
    return result


def shares(chips):
    quarter = chips // 4
    far = list(zip(range(chips - 1, 3 * quarter - 1, -1), range(3 * quarter - 1, 2 * quarter - 1, -1)))
    near = list(zip(range(quarter - 1, -1, -1), range(2 * quarter - 1, quarter - 1, -1)))
    return far + near


def attend_kernel(chips, rows, parts, pairs, bounds, *refs):
    own, other = by_step(refs[:chips]), by_step(refs[chips : 2 * chips])
    done = refs[2 * chips :]
    share = shares(chips)
    every = [ref for both in zip(own, other) for ref in both]
    half = rows // 2
    tv, ta = 2 * chips * rows, 2 * chips * half
    bits = (tv // ta).bit_length() - 1
    me = lax.axis_index("seq")
    core, home = me % 2, me // 2 * 2
    video_valid, audio_valid, offset = (bounds[i : i + 1, 0:1] for i in range(3))

    def slab(at):
        return jnp.concatenate([ref[at : at + rows, :] for ref in every], axis=0)

    def asked(at):
        pieces = []
        for zero, one in share:
            for c in range(2):
                low = (own, other)[c][zero][at : at + rows, :]
                high = (other, own)[c][one][at : at + rows, :]
                pieces.append(jnp.where(core == 0, low, high))
        return jnp.concatenate(pieces, axis=0)

    def split(wide):
        wide = wide.astype(jnp.float32).reshape(-1, rows, LANES)
        first = wide[:, :half, :].reshape(-1, LANES).astype(jnp.bfloat16)
        second = wide[:, half:, :].reshape(-1, LANES).astype(jnp.bfloat16)
        return first, second

    def places(q_step, k_step):
        shape = (chips * q_step, 2 * chips * k_step)
        k_at = lax.broadcasted_iota(jnp.int32, shape, 1) ^ (me * k_step)
        starts = []
        for zero, one in share:
            chip = home ^ jnp.where(core == 0, 2 * zero, 2 * one)
            starts.append(lax.broadcasted_iota(jnp.int32, (2 * q_step, 1), 0) + chip * q_step)
        return jnp.concatenate(starts, axis=0), k_at

    def put(at, mixed):
        count = done[0].shape[0] // 2
        for u in range(len(share)):
            for c in range(2):
                piece = mixed[(2 * u + c) * rows : (2 * u + c + 1) * rows]
                done[u][c * count + at : c * count + at + rows, :] = piece.astype(jnp.bfloat16)

    q_at, k_at = places(rows, rows)
    permit = k_at < video_valid
    units = [
        (
            asked(h * rows),
            slab((parts + h) * rows),
            slab((2 * parts + h) * rows),
            HDV,
            permit,
        )
        for h in range(parts)
    ]
    for h, mixed in enumerate(mix_all(units)):
        put(h * rows, mixed)

    cross = 3 * parts * rows
    audio = cross + 3 * pairs * rows
    q_at, k_at = places(rows, half)
    center = jnp.clip((q_at >> bits) + offset, 0, audio_valid - 1)
    toward_video = (k_at < audio_valid) & (jnp.abs(k_at - center) <= 5 * ta // 8)
    q_at, k_at = places(half, half)
    within_audio = k_at < audio_valid
    q_at, k_at = places(half, rows)
    center = jnp.clip((q_at - offset) << bits, 0, video_valid - 1)
    toward_audio = (k_at < video_valid) & (jnp.abs(k_at - center) <= tv // 8)
    units = []
    for p in range(pairs):
        at = cross + p * rows
        cross_query = asked(at)
        cross_keys = slab(at + pairs * rows)
        cross_values = slab(at + 2 * pairs * rows)
        at = audio + p * rows
        audio_query = split(asked(at))[0]
        audio_keys = split(slab(at))[1]
        at += pairs * rows
        audio_values = split(slab(at))[0]
        listen_query = split(asked(at))[1]
        at += pairs * rows
        sound_keys, sound_values = split(slab(at))
        units += pair_units(cross_query, sound_keys, sound_values, toward_video)
        units += pair_units(audio_query, audio_keys, audio_values, within_audio)
        units += pair_units(listen_query, cross_keys, cross_values, toward_audio)
    mixed = mix_all(units)
    heads = LANES // HDA
    for p in range(pairs):
        seen, heard, listened = (
            pair_join(mixed[(3 * p + i) * heads : (3 * p + i + 1) * heads]) for i in range(3)
        )
        out = (parts + p) * rows
        put(out, seen)
        both = jnp.concatenate(
            [heard.reshape(-1, half, LANES), listened.reshape(-1, half, LANES)], axis=1
        )
        put(out + pairs * rows, both.reshape(-1, LANES))


def unpack_kernel(chips, *refs):
    share = shares(chips)
    back, other = refs[: len(share)], refs[len(share) : 2 * len(share)]
    video_mixed, audio_mixed, video_cross, audio_cross = refs[2 * len(share) :]
    rows = video_mixed.shape[0]
    half = audio_mixed.shape[0]
    parts = video_mixed.shape[1] // chips // LANES
    pairs = audio_mixed.shape[1] // chips // LANES
    me = lax.axis_index("seq")
    core, home = me % 2, me // 2
    for u, (zero, one) in enumerate(share):
        for ref, chip in (
            (back[u], home ^ jnp.where(core == 0, zero, one)),
            (other[u], home ^ jnp.where(core == 0, one, zero)),
        ):
            base = pl.multiple_of(core * (ref.shape[0] // 2), 16)

            def piece(at):
                return ref[pl.ds(base + at, rows), :]

            for h in range(parts):
                at = pl.multiple_of((chip * parts + h) * LANES, LANES)
                video_mixed[:, pl.ds(at, LANES)] = piece(h * rows)
            for p in range(pairs):
                at = pl.multiple_of((chip * pairs + p) * LANES, LANES)
                out = (parts + p) * rows
                video_cross[:, pl.ds(at, LANES)] = piece(out)
                both = piece(out + pairs * rows)
                audio_mixed[:, pl.ds(at, LANES)] = both[:half, :]
                audio_cross[:, pl.ds(at, LANES)] = both[half:, :]


def swap(piece, n, step):
    return lax.ppermute(piece, "seq", [(i, i ^ step) for i in range(n)])


def shards_packed(*arrays):
    (
        video_query, video_keys, video_values,
        audio_query, audio_keys, audio_values,
        cross_video_query, cross_video_keys, cross_video_values,
        cross_audio_query, cross_audio_keys, cross_audio_values,
        video_length, audio_length, align_offset,
    ) = arrays
    n = lax.axis_size("seq")
    chips = n // 2
    rows = video_query.shape[0]
    parts = video_query.shape[1] // chips // LANES
    pairs = audio_query.shape[1] // chips // LANES
    vmem = pl.BlockSpec(memory_space=pltpu.VMEM)
    hbm = pl.BlockSpec(memory_space=pltpu.HBM)
    smem = pl.BlockSpec(memory_space=pltpu.SMEM)
    params = pltpu.CompilerParams(vmem_limit_bytes=32 * 1024 * 1024)

    def buffer(*shape):
        return jax.ShapeDtypeStruct(shape, jnp.bfloat16)

    sources = (
        video_query, video_keys, video_values,
        cross_video_query, cross_video_keys, cross_video_values,
        audio_query, audio_keys, audio_values,
        cross_audio_query, cross_audio_keys, cross_audio_values,
    )
    packed = pl.pallas_call(
        functools.partial(pack_kernel, chips),
        out_shape=[pltpu.VMEM(((3 * parts + 6 * pairs) * rows, LANES), jnp.bfloat16)] * chips,
        in_specs=[hbm] * 12,
        out_specs=[vmem] * chips,
        scratch_shapes=[pltpu.VMEM(source.shape, source.dtype) for source in sources]
        + [pltpu.SemaphoreType.DMA((12,))],
        compiler_params=params,
    )(*[pltpu.with_memory_space_constraint(source, pltpu.HBM) for source in sources])
    packed = by_step(packed)
    moved = [swap(packed[j], n, 2 * j) for j in range(1, chips)]
    anywhere = pl.BlockSpec(memory_space=pl.ANY)
    bounds, kept = pl.pallas_call(
        bounds_kernel,
        out_shape=(
            pltpu.VMEM((8, LANES), jnp.int32),
            pltpu.VMEM(packed[0].shape, packed[0].dtype),
        ),
        in_specs=[smem] * 3 + [anywhere] * 2,
        out_specs=(vmem, anywhere),
        input_output_aliases={4: 1},
        compiler_params=params,
    )(video_length, audio_length, align_offset, moved[-1], packed[0])
    own = [kept] + moved
    other = [swap(piece, n, 1) for piece in own]
    share = shares(chips)
    done = pl.pallas_call(
        functools.partial(attend_kernel, chips, rows, parts, pairs),
        out_shape=[buffer(2 * (parts + 2 * pairs) * rows, LANES)] * len(share),
        in_specs=[vmem] * (1 + 2 * chips),
        out_specs=[vmem] * len(share),
        compiler_params=params,
    )(bounds, *in_order(own), *in_order(other))
    back = [
        lax.ppermute(piece, "seq", [(i, i ^ 2 * pair[i % 2]) for i in range(n)])
        for piece, pair in zip(done, share)
    ]
    return pl.pallas_call(
        functools.partial(unpack_kernel, chips),
        out_shape=(
            buffer(*video_query.shape),
            buffer(*audio_query.shape),
            buffer(*cross_video_query.shape),
            buffer(*cross_audio_query.shape),
        ),
        in_specs=[vmem] * (2 * len(share)),
        out_specs=(vmem,) * 4,
        compiler_params=params,
    )(*back, *[swap(piece, n, 1) for piece in back])


def shards(*arrays):
    n = lax.axis_size("seq")
    chips = max(n // 2, 1)
    rows, half = arrays[0].shape[0], arrays[3].shape[0]
    fits = (
        n % 8 == 0
        and n & (n - 1) == 0
        and arrays[0].shape[1] % (chips * LANES) == 0
        and arrays[3].shape[1] % (chips * LANES) == 0
        and HDV == LANES
        and LANES % HDA == 0
        and rows == 2 * half
        and half % 8 == 0
        and half & (half - 1) == 0
    )
    return shards_packed(*arrays) if fits else shards_general(*arrays)


def solution(mesh):
    placed = (
        P(("clip", "seq"), None),
        P(("clip", "seq"), None),
        P(("clip", "seq"), None),
        P(("clip", "seq"), None),
        P(("clip", "seq"), None),
        P(("clip", "seq"), None),
        P(("clip", "seq"), None),
        P(("clip", "seq"), None),
        P(("clip", "seq"), None),
        P(("clip", "seq"), None),
        P(("clip", "seq"), None),
        P(("clip", "seq"), None),
        P("clip"),
        P("clip"),
        P("clip"),
    )
    return jax.shard_map(
        shards,
        mesh=mesh,
        in_specs=placed,
        out_specs=(
            P(("clip", "seq"), None),
            P(("clip", "seq"), None),
            P(("clip", "seq"), None),
            P(("clip", "seq"), None),
        ),
        check_vma=False,
    )
```

```python
import functools
import math

import jax
import jax.numpy as jnp
from jax import lax
from jax.experimental import pallas as pl
from jax.experimental.pallas import tpu as pltpu
from jax.sharding import PartitionSpec as P

HV = 32
HDV = 128
HA = 32
HDA = 64


def block_size(total, limit):
    chosen = min(total, limit)
    while total % chosen:
        chosen -= 1
    return chosen


def split_heads(tokens, heads, depth, copies):
    rows = tokens.shape[0]
    shaped = tokens.reshape(copies, rows // copies, heads, depth).transpose(2, 0, 1, 3)
    return shaped.reshape(heads * copies, rows // copies, depth)


def spread_heads(tokens, heads, depth, copies):
    rows = tokens.shape[0]
    shaped = tokens.reshape(rows, heads, depth).transpose(1, 0, 2)
    shaped = jnp.broadcast_to(shaped[:, None], (heads, copies, rows, depth))
    return shaped.reshape(heads * copies, rows, depth)


def join_heads(owned, heads, depth, copies):
    part_rows = owned.shape[1]
    shaped = owned.reshape(heads, copies, part_rows, depth).transpose(1, 2, 0, 3)
    return shaped.reshape(copies * part_rows, heads * depth)


def owned_positions(rows, copies, devices, index):
    part_rows = rows // copies
    flat = jnp.arange(devices * part_rows, dtype=jnp.int32)
    return flat // part_rows * rows + index % copies * part_rows + flat % part_rows


def online_update(carry, scores, permit, value_tile, value_form):
    running, total, accum = carry
    scores = jnp.where(permit, scores, -1e30)
    newmax = jnp.maximum(running, jnp.max(scores, axis=2))
    weights = jnp.where(permit, jnp.exp(scores - newmax[:, :, None]), 0.0)
    factor = jnp.exp(running - newmax)
    total = total * factor + jnp.sum(weights, axis=2)
    mixed = jnp.einsum(
        value_form, weights.astype(jnp.bfloat16), value_tile, preferred_element_type=jnp.float32
    )
    accum = accum * factor[:, :, None] + mixed
    return (newmax, total, accum)


def fold_initial(rows, heads, depth):
    return (
        jnp.full((heads, rows), -1e30, jnp.float32),
        jnp.zeros((heads, rows), jnp.float32),
        jnp.zeros((heads, rows, depth), jnp.float32),
    )


def fold_piece(carry, local_query, key_rows, value_rows, permit, heads, depth):
    keyed = key_rows.reshape(key_rows.shape[0], heads, depth)
    valued = value_rows.reshape(value_rows.shape[0], heads, depth)
    scores = jnp.einsum("qhd,khd->hqk", local_query, keyed, preferred_element_type=jnp.float32) * (
        1.0 / math.sqrt(depth)
    )
    return online_update(carry, scores, permit[None], valued, "hqk,khd->hqd")


def fold_finish(carry, heads, depth):
    running, total, accum = carry
    result = (accum / total[:, :, None]).astype(jnp.bfloat16)
    return result.transpose(1, 0, 2).reshape(result.shape[1], heads * depth)


def attend_local(queries, keys, values, query_pos, key_pos, allowed):
    heads, q_count, depth = queries.shape
    k_count = keys.shape[1]
    q_block = block_size(q_count, 512)
    k_block = block_size(k_count, 2048)
    scale = 1.0 / math.sqrt(depth)
    q_tiles = queries.reshape(heads, q_count // q_block, q_block, depth).transpose(1, 0, 2, 3)
    k_tiles = keys.reshape(heads, k_count // k_block, k_block, depth).transpose(1, 0, 2, 3)
    v_tiles = values.reshape(heads, k_count // k_block, k_block, depth).transpose(1, 0, 2, 3)
    q_places = query_pos.reshape(q_count // q_block, q_block)
    k_places = key_pos.reshape(k_count // k_block, k_block)

    def one_tile(packed):
        q_tile, q_where = packed

        def absorb(carry, piece):
            k_tile, v_tile, k_where = piece
            scores = (
                jnp.einsum("hqd,hkd->hqk", q_tile, k_tile, preferred_element_type=jnp.float32)
                * scale
            )
            permit = allowed(q_where[:, None], k_where[None, :])[None]
            return (online_update(carry, scores, permit, v_tile, "hqk,hkd->hqd"), None)

        initial = fold_initial(q_block, heads, depth)
        final_state, unused = lax.scan(absorb, initial, (k_tiles, v_tiles, k_places))
        running, total, accum = final_state
        return (accum / total[:, :, None]).astype(jnp.bfloat16)

    tiles = lax.map(one_tile, (q_tiles, q_places))
    return tiles.transpose(1, 0, 2, 3).reshape(heads, q_count, depth)


def shards_general(
    video_query,
    video_keys,
    video_values,
    audio_query,
    audio_keys,
    audio_values,
    cross_video_query,
    cross_video_keys,
    cross_video_values,
    cross_audio_query,
    cross_audio_keys,
    cross_audio_values,
    video_length,
    audio_length,
    align_offset,
):
    devices = lax.axis_size("seq")
    index = lax.axis_index("seq")
    video_rows = video_query.shape[0]
    audio_rows = audio_query.shape[0]
    video_total = video_rows * devices
    audio_total = audio_rows * devices
    video_reach = video_total // 8
    audio_reach = 5 * audio_total // 8
    video_valid = video_length[0]
    audio_valid = audio_length[0]
    align_shift = align_offset[0]
    copies = max(devices // HV, 1)
    video_places = jnp.arange(video_total, dtype=jnp.int32)
    audio_places = jnp.arange(audio_total, dtype=jnp.int32)

    def video_open(q_where, k_where):
        return k_where < video_valid

    def toward_video(q_where, k_where):
        center = jnp.clip(q_where * audio_total // video_total + align_shift, 0, audio_valid - 1)
        return (k_where < audio_valid) & (jnp.abs(k_where - center) <= audio_reach)

    def toward_audio(q_where, k_where):
        center = jnp.clip((q_where - align_shift) * video_total // audio_total, 0, video_valid - 1)
        return (k_where < video_valid) & (jnp.abs(k_where - center) <= video_reach)

    video_owned = (
        lax.all_to_all(
            split_heads(video_query, HV, HDV, copies),
            "seq",
            split_axis=0,
            concat_axis=1,
            tiled=True,
        ),
        lax.all_to_all(
            spread_heads(video_keys, HV, HDV, copies),
            "seq",
            split_axis=0,
            concat_axis=1,
            tiled=True,
        ),
        lax.all_to_all(
            spread_heads(video_values, HV, HDV, copies),
            "seq",
            split_axis=0,
            concat_axis=1,
            tiled=True,
        ),
    )
    video_done = attend_local(
        video_owned[0],
        video_owned[1],
        video_owned[2],
        owned_positions(video_rows, copies, devices, index),
        video_places,
        video_open,
    )
    video_mixed = join_heads(
        lax.all_to_all(video_done, "seq", split_axis=1, concat_axis=0, tiled=True), HV, HDV, copies
    )
    audio_local = audio_query.reshape(audio_rows, HA, HDA)
    piece = (
        lax.all_gather(audio_keys, "seq", axis=0, tiled=True),
        lax.all_gather(audio_values, "seq", axis=0, tiled=True),
    )
    k_where = jnp.arange(piece[0].shape[0], dtype=jnp.int32)
    audio_k_where = k_where[None, :]
    permit = audio_k_where < audio_valid
    audio_state = fold_piece(
        fold_initial(audio_rows, HA, HDA), audio_local, piece[0], piece[1], permit, HA, HDA
    )
    audio_mixed = fold_finish(audio_state, HA, HDA)
    cross_owned = (
        lax.all_to_all(
            split_heads(cross_video_query, HA, HDA, copies),
            "seq",
            split_axis=0,
            concat_axis=1,
            tiled=True,
        ),
        lax.all_to_all(
            spread_heads(cross_audio_keys, HA, HDA, copies),
            "seq",
            split_axis=0,
            concat_axis=1,
            tiled=True,
        ),
        lax.all_to_all(
            spread_heads(cross_audio_values, HA, HDA, copies),
            "seq",
            split_axis=0,
            concat_axis=1,
            tiled=True,
        ),
    )
    cross_done = attend_local(
        cross_owned[0],
        cross_owned[1],
        cross_owned[2],
        owned_positions(video_rows, copies, devices, index),
        audio_places,
        toward_video,
    )
    video_cross = join_heads(
        lax.all_to_all(cross_done, "seq", split_axis=1, concat_axis=0, tiled=True), HA, HDA, copies
    )
    listen_owned = (
        lax.all_to_all(
            split_heads(cross_audio_query, HA, HDA, copies),
            "seq",
            split_axis=0,
            concat_axis=1,
            tiled=True,
        ),
        lax.all_to_all(
            spread_heads(cross_video_keys, HA, HDA, copies),
            "seq",
            split_axis=0,
            concat_axis=1,
            tiled=True,
        ),
        lax.all_to_all(
            spread_heads(cross_video_values, HA, HDA, copies),
            "seq",
            split_axis=0,
            concat_axis=1,
            tiled=True,
        ),
    )
    listen_done = attend_local(
        listen_owned[0],
        listen_owned[1],
        listen_owned[2],
        owned_positions(audio_rows, copies, devices, index),
        video_places,
        toward_audio,
    )
    audio_cross = join_heads(
        lax.all_to_all(listen_done, "seq", split_axis=1, concat_axis=0, tiled=True), HA, HDA, copies
    )
    return (video_mixed, audio_mixed, video_cross, audio_cross)


LANES = 128


def fetch(sources, held, arrived):
    copies = [
        pltpu.make_async_copy(source, slot, arrived.at[i])
        for i, (source, slot) in enumerate(zip(sources, held))
    ]
    for copy in copies:
        copy.start()
    return copies


def step_order(chips):
    far, near = list(range(chips - 1, chips // 2 - 1, -1)), list(range(1, chips // 2))
    return [0] + far[:1] + near[:1] + far[1:2] + near[1:2] + far[2:] + near[2:]


def by_step(items):
    order = step_order(len(items))
    return [items[order.index(j)] for j in range(len(items))]


def in_order(items):
    return [items[j] for j in step_order(len(items))]


def pack_kernel(chips, *refs):
    sources, refs = refs[:12], refs[12:]
    packed, held, arrived = by_step(refs[:chips]), refs[chips : chips + 12], refs[chips + 12]
    copies = fetch(sources, held, arrived)
    chip = lax.axis_index("seq") // 2
    video, cross, audio = held[0:3], held[3:6], held[6:12]
    rows = video[0].shape[0]

    def group(ref, j, part):
        width = ref.shape[1] // chips
        at = pl.multiple_of((chip ^ j) * width + part * LANES, LANES)
        return ref[:, pl.ds(at, LANES)]

    at = 0
    for i, ref in enumerate(video + cross):
        copies[i].wait()
        for part in range(ref.shape[1] // chips // LANES):
            for j in range(chips):
                packed[j][at : at + rows, :] = group(ref, j, part)
            at += rows
    for i in range(0, 6, 2):
        copies[6 + i].wait()
        copies[7 + i].wait()
        for part in range(audio[i].shape[1] // chips // LANES):
            for j in range(chips):
                pair = jnp.concatenate(
                    [group(audio[i], j, part), group(audio[i + 1], j, part)], axis=0
                )
                packed[j][at : at + rows, :] = pair
            at += rows


def bounds_kernel(video_len, audio_len, shift, after, slab, bounds, same):
    row = lax.broadcasted_iota(jnp.int32, bounds.shape, 0)
    bounds[...] = jnp.where(row == 0, video_len[0], jnp.where(row == 1, audio_len[0], shift[0]))


def mix_all(units):
    scores = [
        lax.dot_general(query, key, (((1,), (1,)), ((), ())), preferred_element_type=jnp.float32)
        for query, key, value, depth, permit in units
    ]
    weights, totals = [], []
    for score, (query, key, value, depth, permit) in zip(scores, units):
        score = jnp.where(permit, score, -1e30)
        peak = jnp.max(score, axis=1, keepdims=True)
        weight = jnp.exp2((score - peak) * (math.log2(math.e) / math.sqrt(depth)))
        totals.append(jnp.sum(weight, axis=1, keepdims=True))
        weights.append(weight.astype(jnp.bfloat16))
    return [
        jnp.dot(weight, unit[2], preferred_element_type=jnp.float32) / total
        for weight, total, unit in zip(weights, totals, units)
    ]


def pair_units(query, key, value, permit):
    lane = lax.broadcasted_iota(jnp.int32, query.shape, 1) // HDA
    zero = jnp.zeros_like(query)
    return [
        (jnp.where(lane == h, query, zero), key, value, HDA, permit) for h in range(LANES // HDA)
    ]


def pair_join(mixed):
    lane = lax.broadcasted_iota(jnp.int32, mixed[0].shape, 1) // HDA
    result = mixed[0]
    for h in range(1, len(mixed)):
        result = jnp.where(lane == h, mixed[h], result)
    return result


def shares(chips):
    quarter = chips // 4
    far = [(chips - 1 - 2 * i - i % 2, chips - 2 - 2 * i + i % 2) for i in range(quarter)]
    near = list(zip(range(quarter - 1, -1, -1), range(2 * quarter - 1, quarter - 1, -1)))
    return far + near


def attend_kernel(chips, rows, parts, pairs, bounds, *refs):
    own, other = by_step(refs[:chips]), by_step(refs[chips : 2 * chips])
    done = refs[2 * chips :]
    share = shares(chips)
    every = [ref for both in zip(own, other) for ref in both]
    half = rows // 2
    tv, ta = 2 * chips * rows, 2 * chips * half
    bits = (tv // ta).bit_length() - 1
    me = lax.axis_index("seq")
    core, home = me % 2, me // 2 * 2
    video_valid, audio_valid, offset = (bounds[i : i + 1, 0:1] for i in range(3))

    def slab(at):
        return jnp.concatenate([ref[at : at + rows, :] for ref in every], axis=0)

    def asked(at):
        pieces = []
        for zero, one in share:
            for c in range(2):
                low = (own, other)[c][zero][at : at + rows, :]
                high = (other, own)[c][one][at : at + rows, :]
                pieces.append(jnp.where(core == 0, low, high))
        return jnp.concatenate(pieces, axis=0)

    def split(wide):
        wide = wide.astype(jnp.float32).reshape(-1, rows, LANES)
        first = wide[:, :half, :].reshape(-1, LANES).astype(jnp.bfloat16)
        second = wide[:, half:, :].reshape(-1, LANES).astype(jnp.bfloat16)
        return first, second

    def places(q_step, k_step):
        shape = (chips * q_step, 2 * chips * k_step)
        k_at = lax.broadcasted_iota(jnp.int32, shape, 1) ^ (me * k_step)
        starts = []
        for zero, one in share:
            chip = home ^ jnp.where(core == 0, 2 * zero, 2 * one)
            starts.append(lax.broadcasted_iota(jnp.int32, (2 * q_step, 1), 0) + chip * q_step)
        return jnp.concatenate(starts, axis=0), k_at

    def put(at, mixed):
        count = done[0].shape[0] // 2
        for u in range(len(share)):
            for c in range(2):
                piece = mixed[(2 * u + c) * rows : (2 * u + c + 1) * rows]
                done[u][c * count + at : c * count + at + rows, :] = piece.astype(jnp.bfloat16)

    q_at, k_at = places(rows, rows)
    permit = k_at < video_valid
    units = [
        (
            asked(h * rows),
            slab((parts + h) * rows),
            slab((2 * parts + h) * rows),
            HDV,
            permit,
        )
        for h in range(parts)
    ]
    for h, mixed in enumerate(mix_all(units)):
        put(h * rows, mixed)

    cross = 3 * parts * rows
    audio = cross + 3 * pairs * rows
    q_at, k_at = places(rows, half)
    center = jnp.clip((q_at >> bits) + offset, 0, audio_valid - 1)
    toward_video = (k_at < audio_valid) & (jnp.abs(k_at - center) <= 5 * ta // 8)
    q_at, k_at = places(half, half)
    within_audio = k_at < audio_valid
    q_at, k_at = places(half, rows)
    center = jnp.clip((q_at - offset) << bits, 0, video_valid - 1)
    toward_audio = (k_at < video_valid) & (jnp.abs(k_at - center) <= tv // 8)
    units = []
    for p in range(pairs):
        at = cross + p * rows
        cross_query = asked(at)
        cross_keys = slab(at + pairs * rows)
        cross_values = slab(at + 2 * pairs * rows)
        at = audio + p * rows
        audio_query = split(asked(at))[0]
        audio_keys = split(slab(at))[1]
        at += pairs * rows
        audio_values = split(slab(at))[0]
        listen_query = split(asked(at))[1]
        at += pairs * rows
        sound_keys, sound_values = split(slab(at))
        units += pair_units(cross_query, sound_keys, sound_values, toward_video)
        units += pair_units(audio_query, audio_keys, audio_values, within_audio)
        units += pair_units(listen_query, cross_keys, cross_values, toward_audio)
    mixed = mix_all(units)
    heads = LANES // HDA
    for p in range(pairs):
        seen, heard, listened = (
            pair_join(mixed[(3 * p + i) * heads : (3 * p + i + 1) * heads]) for i in range(3)
        )
        out = (parts + p) * rows
        put(out, seen)
        both = jnp.concatenate(
            [heard.reshape(-1, half, LANES), listened.reshape(-1, half, LANES)], axis=1
        )
        put(out + pairs * rows, both.reshape(-1, LANES))


def unpack_kernel(chips, *refs):
    share = shares(chips)
    back, other = refs[: len(share)], refs[len(share) : 2 * len(share)]
    video_mixed, audio_mixed, video_cross, audio_cross = refs[2 * len(share) :]
    rows = video_mixed.shape[0]
    half = audio_mixed.shape[0]
    parts = video_mixed.shape[1] // chips // LANES
    pairs = audio_mixed.shape[1] // chips // LANES
    me = lax.axis_index("seq")
    core, home = me % 2, me // 2
    for u, (zero, one) in enumerate(share):
        for ref, chip in (
            (back[u], home ^ jnp.where(core == 0, zero, one)),
            (other[u], home ^ jnp.where(core == 0, one, zero)),
        ):
            base = pl.multiple_of(core * (ref.shape[0] // 2), 16)

            def piece(at):
                return ref[pl.ds(base + at, rows), :]

            for h in range(parts):
                at = pl.multiple_of((chip * parts + h) * LANES, LANES)
                video_mixed[:, pl.ds(at, LANES)] = piece(h * rows)
            for p in range(pairs):
                at = pl.multiple_of((chip * pairs + p) * LANES, LANES)
                out = (parts + p) * rows
                video_cross[:, pl.ds(at, LANES)] = piece(out)
                both = piece(out + pairs * rows)
                audio_mixed[:, pl.ds(at, LANES)] = both[:half, :]
                audio_cross[:, pl.ds(at, LANES)] = both[half:, :]


def swap(piece, n, step):
    return lax.ppermute(piece, "seq", [(i, i ^ step) for i in range(n)])


def shards_packed(*arrays):
    (
        video_query, video_keys, video_values,
        audio_query, audio_keys, audio_values,
        cross_video_query, cross_video_keys, cross_video_values,
        cross_audio_query, cross_audio_keys, cross_audio_values,
        video_length, audio_length, align_offset,
    ) = arrays
    n = lax.axis_size("seq")
    chips = n // 2
    rows = video_query.shape[0]
    parts = video_query.shape[1] // chips // LANES
    pairs = audio_query.shape[1] // chips // LANES
    vmem = pl.BlockSpec(memory_space=pltpu.VMEM)
    hbm = pl.BlockSpec(memory_space=pltpu.HBM)
    smem = pl.BlockSpec(memory_space=pltpu.SMEM)
    params = pltpu.CompilerParams(vmem_limit_bytes=32 * 1024 * 1024)

    def buffer(*shape):
        return jax.ShapeDtypeStruct(shape, jnp.bfloat16)

    sources = (
        video_query, video_keys, video_values,
        cross_video_query, cross_video_keys, cross_video_values,
        audio_query, audio_keys, audio_values,
        cross_audio_query, cross_audio_keys, cross_audio_values,
    )
    packed = pl.pallas_call(
        functools.partial(pack_kernel, chips),
        out_shape=[pltpu.VMEM(((3 * parts + 6 * pairs) * rows, LANES), jnp.bfloat16)] * chips,
        in_specs=[hbm] * 12,
        out_specs=[vmem] * chips,
        scratch_shapes=[pltpu.VMEM(source.shape, source.dtype) for source in sources]
        + [pltpu.SemaphoreType.DMA((12,))],
        compiler_params=params,
    )(*[pltpu.with_memory_space_constraint(source, pltpu.HBM) for source in sources])
    packed = by_step(packed)
    moved = [swap(packed[j], n, 2 * j) for j in range(1, chips)]
    anywhere = pl.BlockSpec(memory_space=pl.ANY)
    bounds, kept = pl.pallas_call(
        bounds_kernel,
        out_shape=(
            pltpu.VMEM((8, LANES), jnp.int32),
            pltpu.VMEM(packed[0].shape, packed[0].dtype),
        ),
        in_specs=[smem] * 3 + [anywhere] * 2,
        out_specs=(vmem, anywhere),
        input_output_aliases={4: 1},
        compiler_params=params,
    )(video_length, audio_length, align_offset, moved[-1], packed[0])
    own = [kept] + moved
    other = [swap(piece, n, 1) for piece in own]
    share = shares(chips)
    done = pl.pallas_call(
        functools.partial(attend_kernel, chips, rows, parts, pairs),
        out_shape=[buffer(2 * (parts + 2 * pairs) * rows, LANES)] * len(share),
        in_specs=[vmem] * (1 + 2 * chips),
        out_specs=[vmem] * len(share),
        compiler_params=params,
    )(bounds, *in_order(own), *in_order(other))
    back = [
        lax.ppermute(piece, "seq", [(i, i ^ 2 * pair[i % 2]) for i in range(n)])
        for piece, pair in zip(done, share)
    ]
    return pl.pallas_call(
        functools.partial(unpack_kernel, chips),
        out_shape=(
            buffer(*video_query.shape),
            buffer(*audio_query.shape),
            buffer(*cross_video_query.shape),
            buffer(*cross_audio_query.shape),
        ),
        in_specs=[vmem] * (2 * len(share)),
        out_specs=(vmem,) * 4,
        compiler_params=params,
    )(*back, *[swap(piece, n, 1) for piece in back])


def shards(*arrays):
    n = lax.axis_size("seq")
    chips = max(n // 2, 1)
    rows, half = arrays[0].shape[0], arrays[3].shape[0]
    fits = (
        n % 8 == 0
        and n & (n - 1) == 0
        and arrays[0].shape[1] % (chips * LANES) == 0
        and arrays[3].shape[1] % (chips * LANES) == 0
        and HDV == LANES
        and LANES % HDA == 0
        and rows == 2 * half
        and half % 8 == 0
        and half & (half - 1) == 0
    )
    return shards_packed(*arrays) if fits else shards_general(*arrays)


def solution(mesh):
    placed = (
        P(("clip", "seq"), None),
        P(("clip", "seq"), None),
        P(("clip", "seq"), None),
        P(("clip", "seq"), None),
        P(("clip", "seq"), None),
        P(("clip", "seq"), None),
        P(("clip", "seq"), None),
        P(("clip", "seq"), None),
        P(("clip", "seq"), None),
        P(("clip", "seq"), None),
        P(("clip", "seq"), None),
        P(("clip", "seq"), None),
        P("clip"),
        P("clip"),
        P("clip"),
    )
    return jax.shard_map(
        shards,
        mesh=mesh,
        in_specs=placed,
        out_specs=(
            P(("clip", "seq"), None),
            P(("clip", "seq"), None),
            P(("clip", "seq"), None),
            P(("clip", "seq"), None),
        ),
        check_vma=False,
    )
```

```python
import functools
import math

import jax
import jax.numpy as jnp
from jax import lax
from jax.experimental import pallas as pl
from jax.experimental.pallas import tpu as pltpu
from jax.sharding import PartitionSpec as P

HV = 32
HDV = 128
HA = 32
HDA = 64


def block_size(total, limit):
    chosen = min(total, limit)
    while total % chosen:
        chosen -= 1
    return chosen


def split_heads(tokens, heads, depth, copies):
    rows = tokens.shape[0]
    shaped = tokens.reshape(copies, rows // copies, heads, depth).transpose(2, 0, 1, 3)
    return shaped.reshape(heads * copies, rows // copies, depth)


def spread_heads(tokens, heads, depth, copies):
    rows = tokens.shape[0]
    shaped = tokens.reshape(rows, heads, depth).transpose(1, 0, 2)
    shaped = jnp.broadcast_to(shaped[:, None], (heads, copies, rows, depth))
    return shaped.reshape(heads * copies, rows, depth)


def join_heads(owned, heads, depth, copies):
    part_rows = owned.shape[1]
    shaped = owned.reshape(heads, copies, part_rows, depth).transpose(1, 2, 0, 3)
    return shaped.reshape(copies * part_rows, heads * depth)


def owned_positions(rows, copies, devices, index):
    part_rows = rows // copies
    flat = jnp.arange(devices * part_rows, dtype=jnp.int32)
    return flat // part_rows * rows + index % copies * part_rows + flat % part_rows


def online_update(carry, scores, permit, value_tile, value_form):
    running, total, accum = carry
    scores = jnp.where(permit, scores, -1e30)
    newmax = jnp.maximum(running, jnp.max(scores, axis=2))
    weights = jnp.where(permit, jnp.exp(scores - newmax[:, :, None]), 0.0)
    factor = jnp.exp(running - newmax)
    total = total * factor + jnp.sum(weights, axis=2)
    mixed = jnp.einsum(
        value_form, weights.astype(jnp.bfloat16), value_tile, preferred_element_type=jnp.float32
    )
    accum = accum * factor[:, :, None] + mixed
    return (newmax, total, accum)


def fold_initial(rows, heads, depth):
    return (
        jnp.full((heads, rows), -1e30, jnp.float32),
        jnp.zeros((heads, rows), jnp.float32),
        jnp.zeros((heads, rows, depth), jnp.float32),
    )


def fold_piece(carry, local_query, key_rows, value_rows, permit, heads, depth):
    keyed = key_rows.reshape(key_rows.shape[0], heads, depth)
    valued = value_rows.reshape(value_rows.shape[0], heads, depth)
    scores = jnp.einsum("qhd,khd->hqk", local_query, keyed, preferred_element_type=jnp.float32) * (
        1.0 / math.sqrt(depth)
    )
    return online_update(carry, scores, permit[None], valued, "hqk,khd->hqd")


def fold_finish(carry, heads, depth):
    running, total, accum = carry
    result = (accum / total[:, :, None]).astype(jnp.bfloat16)
    return result.transpose(1, 0, 2).reshape(result.shape[1], heads * depth)


def attend_local(queries, keys, values, query_pos, key_pos, allowed):
    heads, q_count, depth = queries.shape
    k_count = keys.shape[1]
    q_block = block_size(q_count, 512)
    k_block = block_size(k_count, 2048)
    scale = 1.0 / math.sqrt(depth)
    q_tiles = queries.reshape(heads, q_count // q_block, q_block, depth).transpose(1, 0, 2, 3)
    k_tiles = keys.reshape(heads, k_count // k_block, k_block, depth).transpose(1, 0, 2, 3)
    v_tiles = values.reshape(heads, k_count // k_block, k_block, depth).transpose(1, 0, 2, 3)
    q_places = query_pos.reshape(q_count // q_block, q_block)
    k_places = key_pos.reshape(k_count // k_block, k_block)

    def one_tile(packed):
        q_tile, q_where = packed

        def absorb(carry, piece):
            k_tile, v_tile, k_where = piece
            scores = (
                jnp.einsum("hqd,hkd->hqk", q_tile, k_tile, preferred_element_type=jnp.float32)
                * scale
            )
            permit = allowed(q_where[:, None], k_where[None, :])[None]
            return (online_update(carry, scores, permit, v_tile, "hqk,hkd->hqd"), None)

        initial = fold_initial(q_block, heads, depth)
        final_state, unused = lax.scan(absorb, initial, (k_tiles, v_tiles, k_places))
        running, total, accum = final_state
        return (accum / total[:, :, None]).astype(jnp.bfloat16)

    tiles = lax.map(one_tile, (q_tiles, q_places))
    return tiles.transpose(1, 0, 2, 3).reshape(heads, q_count, depth)


def shards_general(
    video_query,
    video_keys,
    video_values,
    audio_query,
    audio_keys,
    audio_values,
    cross_video_query,
    cross_video_keys,
    cross_video_values,
    cross_audio_query,
    cross_audio_keys,
    cross_audio_values,
    video_length,
    audio_length,
    align_offset,
):
    devices = lax.axis_size("seq")
    index = lax.axis_index("seq")
    video_rows = video_query.shape[0]
    audio_rows = audio_query.shape[0]
    video_total = video_rows * devices
    audio_total = audio_rows * devices
    video_reach = video_total // 8
    audio_reach = 5 * audio_total // 8
    video_valid = video_length[0]
    audio_valid = audio_length[0]
    align_shift = align_offset[0]
    copies = max(devices // HV, 1)
    video_places = jnp.arange(video_total, dtype=jnp.int32)
    audio_places = jnp.arange(audio_total, dtype=jnp.int32)

    def video_open(q_where, k_where):
        return k_where < video_valid

    def toward_video(q_where, k_where):
        center = jnp.clip(q_where * audio_total // video_total + align_shift, 0, audio_valid - 1)
        return (k_where < audio_valid) & (jnp.abs(k_where - center) <= audio_reach)

    def toward_audio(q_where, k_where):
        center = jnp.clip((q_where - align_shift) * video_total // audio_total, 0, video_valid - 1)
        return (k_where < video_valid) & (jnp.abs(k_where - center) <= video_reach)

    video_owned = (
        lax.all_to_all(
            split_heads(video_query, HV, HDV, copies),
            "seq",
            split_axis=0,
            concat_axis=1,
            tiled=True,
        ),
        lax.all_to_all(
            spread_heads(video_keys, HV, HDV, copies),
            "seq",
            split_axis=0,
            concat_axis=1,
            tiled=True,
        ),
        lax.all_to_all(
            spread_heads(video_values, HV, HDV, copies),
            "seq",
            split_axis=0,
            concat_axis=1,
            tiled=True,
        ),
    )
    video_done = attend_local(
        video_owned[0],
        video_owned[1],
        video_owned[2],
        owned_positions(video_rows, copies, devices, index),
        video_places,
        video_open,
    )
    video_mixed = join_heads(
        lax.all_to_all(video_done, "seq", split_axis=1, concat_axis=0, tiled=True), HV, HDV, copies
    )
    audio_local = audio_query.reshape(audio_rows, HA, HDA)
    piece = (
        lax.all_gather(audio_keys, "seq", axis=0, tiled=True),
        lax.all_gather(audio_values, "seq", axis=0, tiled=True),
    )
    k_where = jnp.arange(piece[0].shape[0], dtype=jnp.int32)
    audio_k_where = k_where[None, :]
    permit = audio_k_where < audio_valid
    audio_state = fold_piece(
        fold_initial(audio_rows, HA, HDA), audio_local, piece[0], piece[1], permit, HA, HDA
    )
    audio_mixed = fold_finish(audio_state, HA, HDA)
    cross_owned = (
        lax.all_to_all(
            split_heads(cross_video_query, HA, HDA, copies),
            "seq",
            split_axis=0,
            concat_axis=1,
            tiled=True,
        ),
        lax.all_to_all(
            spread_heads(cross_audio_keys, HA, HDA, copies),
            "seq",
            split_axis=0,
            concat_axis=1,
            tiled=True,
        ),
        lax.all_to_all(
            spread_heads(cross_audio_values, HA, HDA, copies),
            "seq",
            split_axis=0,
            concat_axis=1,
            tiled=True,
        ),
    )
    cross_done = attend_local(
        cross_owned[0],
        cross_owned[1],
        cross_owned[2],
        owned_positions(video_rows, copies, devices, index),
        audio_places,
        toward_video,
    )
    video_cross = join_heads(
        lax.all_to_all(cross_done, "seq", split_axis=1, concat_axis=0, tiled=True), HA, HDA, copies
    )
    listen_owned = (
        lax.all_to_all(
            split_heads(cross_audio_query, HA, HDA, copies),
            "seq",
            split_axis=0,
            concat_axis=1,
            tiled=True,
        ),
        lax.all_to_all(
            spread_heads(cross_video_keys, HA, HDA, copies),
            "seq",
            split_axis=0,
            concat_axis=1,
            tiled=True,
        ),
        lax.all_to_all(
            spread_heads(cross_video_values, HA, HDA, copies),
            "seq",
            split_axis=0,
            concat_axis=1,
            tiled=True,
        ),
    )
    listen_done = attend_local(
        listen_owned[0],
        listen_owned[1],
        listen_owned[2],
        owned_positions(audio_rows, copies, devices, index),
        video_places,
        toward_audio,
    )
    audio_cross = join_heads(
        lax.all_to_all(listen_done, "seq", split_axis=1, concat_axis=0, tiled=True), HA, HDA, copies
    )
    return (video_mixed, audio_mixed, video_cross, audio_cross)


LANES = 128


def fetch(sources, held, arrived):
    copies = [
        pltpu.make_async_copy(source, slot, arrived.at[i])
        for i, (source, slot) in enumerate(zip(sources, held))
    ]
    for copy in copies:
        copy.start()
    return copies


def step_order(chips):
    far, near = list(range(chips - 1, chips // 2 - 1, -1)), list(range(1, chips // 2))
    return [0] + far[:1] + near[:1] + far[1:2] + near[1:2] + far[2:] + near[2:]


def by_step(items):
    order = step_order(len(items))
    return [items[order.index(j)] for j in range(len(items))]


def in_order(items):
    return [items[j] for j in step_order(len(items))]


def pack_kernel(chips, *refs):
    sources, refs = refs[:12], refs[12:]
    packed, held, arrived = by_step(refs[:chips]), refs[chips : chips + 12], refs[chips + 12]
    copies = fetch(sources, held, arrived)
    chip = lax.axis_index("seq") // 2
    video, cross, audio = held[0:3], held[3:6], held[6:12]
    rows = video[0].shape[0]

    def group(ref, j, part):
        width = ref.shape[1] // chips
        at = pl.multiple_of((chip ^ j) * width + part * LANES, LANES)
        return ref[:, pl.ds(at, LANES)]

    at = 0
    for i, ref in enumerate(video + cross):
        copies[i].wait()
        for part in range(ref.shape[1] // chips // LANES):
            for j in range(chips):
                packed[j][at : at + rows, :] = group(ref, j, part)
            at += rows
    for i in range(0, 6, 2):
        copies[6 + i].wait()
        copies[7 + i].wait()
        for part in range(audio[i].shape[1] // chips // LANES):
            for j in range(chips):
                pair = jnp.concatenate(
                    [group(audio[i], j, part), group(audio[i + 1], j, part)], axis=0
                )
                packed[j][at : at + rows, :] = pair
            at += rows


def bounds_kernel(video_len, audio_len, shift, after, slab, bounds, same):
    row = lax.broadcasted_iota(jnp.int32, bounds.shape, 0)
    bounds[...] = jnp.where(row == 0, video_len[0], jnp.where(row == 1, audio_len[0], shift[0]))


def mix_all(units):
    scores = [
        lax.dot_general(query, key, (((1,), (1,)), ((), ())), preferred_element_type=jnp.float32)
        for query, key, value, depth, permit in units
    ]
    weights, totals = [], []
    for score, (query, key, value, depth, permit) in zip(scores, units):
        score = jnp.where(permit, score, -1e30)
        peak = jnp.max(score, axis=1, keepdims=True)
        weight = jnp.exp2((score - peak) * (math.log2(math.e) / math.sqrt(depth)))
        totals.append(jnp.sum(weight, axis=1, keepdims=True))
        weights.append(weight.astype(jnp.bfloat16))
    return [
        jnp.dot(weight, unit[2], preferred_element_type=jnp.float32) / total
        for weight, total, unit in zip(weights, totals, units)
    ]


def pair_units(query, key, value, permit):
    lane = lax.broadcasted_iota(jnp.int32, query.shape, 1) // HDA
    zero = jnp.zeros_like(query)
    return [
        (jnp.where(lane == h, query, zero), key, value, HDA, permit) for h in range(LANES // HDA)
    ]


def pair_join(mixed):
    lane = lax.broadcasted_iota(jnp.int32, mixed[0].shape, 1) // HDA
    result = mixed[0]
    for h in range(1, len(mixed)):
        result = jnp.where(lane == h, mixed[h], result)
    return result


def shares(chips):
    quarter = chips // 4
    return [(chips - 1 - i, 3 * quarter - 1 - i) for i in range(quarter)]


def attend_kernel(chips, rows, parts, pairs, bounds, *refs):
    own, other = by_step(refs[:chips]), by_step(refs[chips : 2 * chips])
    share = shares(chips)
    side = chips // 2
    done, near_done = refs[2 * chips : 2 * chips + len(share)], refs[2 * chips + len(share) :]
    every = [ref for both in zip(own, other) for ref in both]
    half = rows // 2
    tv, ta = 2 * chips * rows, 2 * chips * half
    bits = (tv // ta).bit_length() - 1
    me = lax.axis_index("seq")
    core, home = me % 2, me // 2 * 2
    video_valid, audio_valid, offset = (bounds[i : i + 1, 0:1] for i in range(3))

    def slab(at):
        return jnp.concatenate([ref[at : at + rows, :] for ref in every], axis=0)

    def asked(at):
        pieces = [own[j][at : at + rows, :] for j in range(side)]
        for zero, one in share:
            for c in range(2):
                low = (own, other)[c][zero][at : at + rows, :]
                high = (other, own)[c][one][at : at + rows, :]
                pieces.append(jnp.where(core == 0, low, high))
        return jnp.concatenate(pieces, axis=0)

    def split(wide):
        wide = wide.astype(jnp.float32).reshape(-1, rows, LANES)
        first = wide[:, :half, :].reshape(-1, LANES).astype(jnp.bfloat16)
        second = wide[:, half:, :].reshape(-1, LANES).astype(jnp.bfloat16)
        return first, second

    def places(q_step, k_step):
        shape = (chips * q_step, 2 * chips * k_step)
        k_at = lax.broadcasted_iota(jnp.int32, shape, 1) ^ (me * k_step)
        within = lax.broadcasted_iota(jnp.int32, (q_step, 1), 0)
        starts = [within + (me ^ (2 * j)) * q_step for j in range(side)]
        for zero, one in share:
            chip = home ^ jnp.where(core == 0, 2 * zero, 2 * one)
            starts += [within + (chip + c) * q_step for c in range(2)]
        return jnp.concatenate(starts, axis=0), k_at

    def put(at, mixed):
        count = near_done[0].shape[0]
        for i in range(chips):
            piece = mixed[i * rows : (i + 1) * rows].astype(jnp.bfloat16)
            if i < side:
                near_done[i][at : at + rows, :] = piece
            else:
                u, c = divmod(i - side, 2)
                done[u][c * count + at : c * count + at + rows, :] = piece

    q_at, k_at = places(rows, rows)
    permit = k_at < video_valid
    units = [
        (
            asked(h * rows),
            slab((parts + h) * rows),
            slab((2 * parts + h) * rows),
            HDV,
            permit,
        )
        for h in range(parts)
    ]
    for h, mixed in enumerate(mix_all(units)):
        put(h * rows, mixed)

    cross = 3 * parts * rows
    audio = cross + 3 * pairs * rows
    q_at, k_at = places(rows, half)
    center = jnp.clip((q_at >> bits) + offset, 0, audio_valid - 1)
    toward_video = (k_at < audio_valid) & (jnp.abs(k_at - center) <= 5 * ta // 8)
    q_at, k_at = places(half, half)
    within_audio = k_at < audio_valid
    q_at, k_at = places(half, rows)
    center = jnp.clip((q_at - offset) << bits, 0, video_valid - 1)
    toward_audio = (k_at < video_valid) & (jnp.abs(k_at - center) <= tv // 8)
    units = []
    for p in range(pairs):
        at = cross + p * rows
        cross_query = asked(at)
        cross_keys = slab(at + pairs * rows)
        cross_values = slab(at + 2 * pairs * rows)
        at = audio + p * rows
        audio_query = split(asked(at))[0]
        audio_keys = split(slab(at))[1]
        at += pairs * rows
        audio_values = split(slab(at))[0]
        listen_query = split(asked(at))[1]
        at += pairs * rows
        sound_keys, sound_values = split(slab(at))
        units += pair_units(cross_query, sound_keys, sound_values, toward_video)
        units += pair_units(audio_query, audio_keys, audio_values, within_audio)
        units += pair_units(listen_query, cross_keys, cross_values, toward_audio)
    mixed = mix_all(units)
    heads = LANES // HDA
    for p in range(pairs):
        seen, heard, listened = (
            pair_join(mixed[(3 * p + i) * heads : (3 * p + i + 1) * heads]) for i in range(3)
        )
        out = (parts + p) * rows
        put(out, seen)
        both = jnp.concatenate(
            [heard.reshape(-1, half, LANES), listened.reshape(-1, half, LANES)], axis=1
        )
        put(out + pairs * rows, both.reshape(-1, LANES))


def unpack_kernel(chips, *refs):
    share = shares(chips)
    count, side = len(share), chips // 2
    back, other, near = refs[:count], refs[count : 2 * count], refs[2 * count : 2 * count + side]
    video_mixed, audio_mixed, video_cross, audio_cross = refs[2 * count + side :]
    rows = video_mixed.shape[0]
    half = audio_mixed.shape[0]
    parts = video_mixed.shape[1] // chips // LANES
    pairs = audio_mixed.shape[1] // chips // LANES
    me = lax.axis_index("seq")
    core, home = me % 2, me // 2

    def place(ref, base, chip):
        for h in range(parts):
            at = pl.multiple_of((chip * parts + h) * LANES, LANES)
            video_mixed[:, pl.ds(at, LANES)] = ref[pl.ds(base + h * rows, rows), :]
        for p in range(pairs):
            at = pl.multiple_of((chip * pairs + p) * LANES, LANES)
            out = (parts + p) * rows
            video_cross[:, pl.ds(at, LANES)] = ref[pl.ds(base + out, rows), :]
            both = ref[pl.ds(base + out + pairs * rows, rows), :]
            audio_mixed[:, pl.ds(at, LANES)] = both[:half, :]
            audio_cross[:, pl.ds(at, LANES)] = both[half:, :]

    for j in range(side):
        place(near[j], 0, home ^ j)
    for u, (zero, one) in enumerate(share):
        base = pl.multiple_of(core * near[0].shape[0], 16)
        place(back[u], base, home ^ jnp.where(core == 0, zero, one))
        place(other[u], base, home ^ jnp.where(core == 0, one, zero))


def tie_kernel(*refs):
    pass


def swap(piece, n, step):
    return lax.ppermute(piece, "seq", [(i, i ^ step) for i in range(n)])


def shards_packed(*arrays):
    (
        video_query, video_keys, video_values,
        audio_query, audio_keys, audio_values,
        cross_video_query, cross_video_keys, cross_video_values,
        cross_audio_query, cross_audio_keys, cross_audio_values,
        video_length, audio_length, align_offset,
    ) = arrays
    n = lax.axis_size("seq")
    chips = n // 2
    rows = video_query.shape[0]
    parts = video_query.shape[1] // chips // LANES
    pairs = audio_query.shape[1] // chips // LANES
    vmem = pl.BlockSpec(memory_space=pltpu.VMEM)
    hbm = pl.BlockSpec(memory_space=pltpu.HBM)
    smem = pl.BlockSpec(memory_space=pltpu.SMEM)
    params = pltpu.CompilerParams(vmem_limit_bytes=32 * 1024 * 1024)

    def buffer(*shape):
        return jax.ShapeDtypeStruct(shape, jnp.bfloat16)

    sources = (
        video_query, video_keys, video_values,
        cross_video_query, cross_video_keys, cross_video_values,
        audio_query, audio_keys, audio_values,
        cross_audio_query, cross_audio_keys, cross_audio_values,
    )
    packed = pl.pallas_call(
        functools.partial(pack_kernel, chips),
        out_shape=[pltpu.VMEM(((3 * parts + 6 * pairs) * rows, LANES), jnp.bfloat16)] * chips,
        in_specs=[hbm] * 12,
        out_specs=[vmem] * chips,
        scratch_shapes=[pltpu.VMEM(source.shape, source.dtype) for source in sources]
        + [pltpu.SemaphoreType.DMA((12,))],
        compiler_params=params,
    )(*[pltpu.with_memory_space_constraint(source, pltpu.HBM) for source in sources])
    packed = by_step(packed)
    moved = [swap(packed[j], n, 2 * j) for j in range(1, chips)]
    anywhere = pl.BlockSpec(memory_space=pl.ANY)
    bounds, kept = pl.pallas_call(
        bounds_kernel,
        out_shape=(
            pltpu.VMEM((8, LANES), jnp.int32),
            pltpu.VMEM(packed[0].shape, packed[0].dtype),
        ),
        in_specs=[smem] * 3 + [anywhere] * 2,
        out_specs=(vmem, anywhere),
        input_output_aliases={4: 1},
        compiler_params=params,
    )(video_length, audio_length, align_offset, moved[-1], packed[0])
    own = [kept] + moved
    other = [swap(piece, n, 1) for piece in own]
    share = shares(chips)
    side = chips // 2
    out_rows = (parts + 2 * pairs) * rows
    results = pl.pallas_call(
        functools.partial(attend_kernel, chips, rows, parts, pairs),
        out_shape=[buffer(2 * out_rows, LANES)] * len(share) + [buffer(out_rows, LANES)] * side,
        in_specs=[vmem] * (1 + 2 * chips),
        out_specs=[vmem] * (len(share) + side),
        compiler_params=params,
    )(bounds, *in_order(own), *in_order(other))
    back = [
        lax.ppermute(piece, "seq", [(i, i ^ 2 * pair[i % 2]) for i in range(n)])
        for piece, pair in zip(results, share)
    ]
    near = list(results[len(share) :])
    near = near[:1] + [swap(near[j], n, 2 * j) for j in range(1, side)]
    back = pl.pallas_call(
        tie_kernel,
        out_shape=[buffer(*piece.shape) for piece in back],
        in_specs=[anywhere] * (len(share) + side - 1),
        out_specs=[anywhere] * len(share),
        input_output_aliases={u: u for u in range(len(share))},
        compiler_params=params,
    )(*back, *near[1:])
    return pl.pallas_call(
        functools.partial(unpack_kernel, chips),
        out_shape=(
            buffer(*video_query.shape),
            buffer(*audio_query.shape),
            buffer(*cross_video_query.shape),
            buffer(*cross_audio_query.shape),
        ),
        in_specs=[vmem] * (2 * len(share) + side),
        out_specs=(vmem,) * 4,
        compiler_params=params,
    )(*back, *[swap(piece, n, 1) for piece in back], *near)


def shards(*arrays):
    n = lax.axis_size("seq")
    chips = max(n // 2, 1)
    rows, half = arrays[0].shape[0], arrays[3].shape[0]
    fits = (
        n % 8 == 0
        and n & (n - 1) == 0
        and arrays[0].shape[1] % (chips * LANES) == 0
        and arrays[3].shape[1] % (chips * LANES) == 0
        and HDV == LANES
        and LANES % HDA == 0
        and rows == 2 * half
        and half % 8 == 0
        and half & (half - 1) == 0
    )
    return shards_packed(*arrays) if fits else shards_general(*arrays)


def solution(mesh):
    placed = (
        P(("clip", "seq"), None),
        P(("clip", "seq"), None),
        P(("clip", "seq"), None),
        P(("clip", "seq"), None),
        P(("clip", "seq"), None),
        P(("clip", "seq"), None),
        P(("clip", "seq"), None),
        P(("clip", "seq"), None),
        P(("clip", "seq"), None),
        P(("clip", "seq"), None),
        P(("clip", "seq"), None),
        P(("clip", "seq"), None),
        P("clip"),
        P("clip"),
        P("clip"),
    )
    return jax.shard_map(
        shards,
        mesh=mesh,
        in_specs=placed,
        out_specs=(
            P(("clip", "seq"), None),
            P(("clip", "seq"), None),
            P(("clip", "seq"), None),
            P(("clip", "seq"), None),
        ),
        check_vma=False,
    )
```

```python
import functools
import math

import jax
import jax.numpy as jnp
from jax import lax
from jax.experimental import pallas as pl
from jax.experimental.pallas import tpu as pltpu
from jax.sharding import PartitionSpec as P

HV = 32
HDV = 128
HA = 32
HDA = 64


def block_size(total, limit):
    chosen = min(total, limit)
    while total % chosen:
        chosen -= 1
    return chosen


def split_heads(tokens, heads, depth, copies):
    rows = tokens.shape[0]
    shaped = tokens.reshape(copies, rows // copies, heads, depth).transpose(2, 0, 1, 3)
    return shaped.reshape(heads * copies, rows // copies, depth)


def spread_heads(tokens, heads, depth, copies):
    rows = tokens.shape[0]
    shaped = tokens.reshape(rows, heads, depth).transpose(1, 0, 2)
    shaped = jnp.broadcast_to(shaped[:, None], (heads, copies, rows, depth))
    return shaped.reshape(heads * copies, rows, depth)


def join_heads(owned, heads, depth, copies):
    part_rows = owned.shape[1]
    shaped = owned.reshape(heads, copies, part_rows, depth).transpose(1, 2, 0, 3)
    return shaped.reshape(copies * part_rows, heads * depth)


def owned_positions(rows, copies, devices, index):
    part_rows = rows // copies
    flat = jnp.arange(devices * part_rows, dtype=jnp.int32)
    return flat // part_rows * rows + index % copies * part_rows + flat % part_rows


def online_update(carry, scores, permit, value_tile, value_form):
    running, total, accum = carry
    scores = jnp.where(permit, scores, -1e30)
    newmax = jnp.maximum(running, jnp.max(scores, axis=2))
    weights = jnp.where(permit, jnp.exp(scores - newmax[:, :, None]), 0.0)
    factor = jnp.exp(running - newmax)
    total = total * factor + jnp.sum(weights, axis=2)
    mixed = jnp.einsum(
        value_form, weights.astype(jnp.bfloat16), value_tile, preferred_element_type=jnp.float32
    )
    accum = accum * factor[:, :, None] + mixed
    return (newmax, total, accum)


def fold_initial(rows, heads, depth):
    return (
        jnp.full((heads, rows), -1e30, jnp.float32),
        jnp.zeros((heads, rows), jnp.float32),
        jnp.zeros((heads, rows, depth), jnp.float32),
    )


def fold_piece(carry, local_query, key_rows, value_rows, permit, heads, depth):
    keyed = key_rows.reshape(key_rows.shape[0], heads, depth)
    valued = value_rows.reshape(value_rows.shape[0], heads, depth)
    scores = jnp.einsum("qhd,khd->hqk", local_query, keyed, preferred_element_type=jnp.float32) * (
        1.0 / math.sqrt(depth)
    )
    return online_update(carry, scores, permit[None], valued, "hqk,khd->hqd")


def fold_finish(carry, heads, depth):
    running, total, accum = carry
    result = (accum / total[:, :, None]).astype(jnp.bfloat16)
    return result.transpose(1, 0, 2).reshape(result.shape[1], heads * depth)


def attend_local(queries, keys, values, query_pos, key_pos, allowed):
    heads, q_count, depth = queries.shape
    k_count = keys.shape[1]
    q_block = block_size(q_count, 512)
    k_block = block_size(k_count, 2048)
    scale = 1.0 / math.sqrt(depth)
    q_tiles = queries.reshape(heads, q_count // q_block, q_block, depth).transpose(1, 0, 2, 3)
    k_tiles = keys.reshape(heads, k_count // k_block, k_block, depth).transpose(1, 0, 2, 3)
    v_tiles = values.reshape(heads, k_count // k_block, k_block, depth).transpose(1, 0, 2, 3)
    q_places = query_pos.reshape(q_count // q_block, q_block)
    k_places = key_pos.reshape(k_count // k_block, k_block)

    def one_tile(packed):
        q_tile, q_where = packed

        def absorb(carry, piece):
            k_tile, v_tile, k_where = piece
            scores = (
                jnp.einsum("hqd,hkd->hqk", q_tile, k_tile, preferred_element_type=jnp.float32)
                * scale
            )
            permit = allowed(q_where[:, None], k_where[None, :])[None]
            return (online_update(carry, scores, permit, v_tile, "hqk,hkd->hqd"), None)

        initial = fold_initial(q_block, heads, depth)
        final_state, unused = lax.scan(absorb, initial, (k_tiles, v_tiles, k_places))
        running, total, accum = final_state
        return (accum / total[:, :, None]).astype(jnp.bfloat16)

    tiles = lax.map(one_tile, (q_tiles, q_places))
    return tiles.transpose(1, 0, 2, 3).reshape(heads, q_count, depth)


def shards_general(
    video_query,
    video_keys,
    video_values,
    audio_query,
    audio_keys,
    audio_values,
    cross_video_query,
    cross_video_keys,
    cross_video_values,
    cross_audio_query,
    cross_audio_keys,
    cross_audio_values,
    video_length,
    audio_length,
    align_offset,
):
    devices = lax.axis_size("seq")
    index = lax.axis_index("seq")
    video_rows = video_query.shape[0]
    audio_rows = audio_query.shape[0]
    video_total = video_rows * devices
    audio_total = audio_rows * devices
    video_reach = video_total // 8
    audio_reach = 5 * audio_total // 8
    video_valid = video_length[0]
    audio_valid = audio_length[0]
    align_shift = align_offset[0]
    copies = max(devices // HV, 1)
    video_places = jnp.arange(video_total, dtype=jnp.int32)
    audio_places = jnp.arange(audio_total, dtype=jnp.int32)

    def video_open(q_where, k_where):
        return k_where < video_valid

    def toward_video(q_where, k_where):
        center = jnp.clip(q_where * audio_total // video_total + align_shift, 0, audio_valid - 1)
        return (k_where < audio_valid) & (jnp.abs(k_where - center) <= audio_reach)

    def toward_audio(q_where, k_where):
        center = jnp.clip((q_where - align_shift) * video_total // audio_total, 0, video_valid - 1)
        return (k_where < video_valid) & (jnp.abs(k_where - center) <= video_reach)

    video_owned = (
        lax.all_to_all(
            split_heads(video_query, HV, HDV, copies),
            "seq",
            split_axis=0,
            concat_axis=1,
            tiled=True,
        ),
        lax.all_to_all(
            spread_heads(video_keys, HV, HDV, copies),
            "seq",
            split_axis=0,
            concat_axis=1,
            tiled=True,
        ),
        lax.all_to_all(
            spread_heads(video_values, HV, HDV, copies),
            "seq",
            split_axis=0,
            concat_axis=1,
            tiled=True,
        ),
    )
    video_done = attend_local(
        video_owned[0],
        video_owned[1],
        video_owned[2],
        owned_positions(video_rows, copies, devices, index),
        video_places,
        video_open,
    )
    video_mixed = join_heads(
        lax.all_to_all(video_done, "seq", split_axis=1, concat_axis=0, tiled=True), HV, HDV, copies
    )
    audio_local = audio_query.reshape(audio_rows, HA, HDA)
    piece = (
        lax.all_gather(audio_keys, "seq", axis=0, tiled=True),
        lax.all_gather(audio_values, "seq", axis=0, tiled=True),
    )
    k_where = jnp.arange(piece[0].shape[0], dtype=jnp.int32)
    audio_k_where = k_where[None, :]
    permit = audio_k_where < audio_valid
    audio_state = fold_piece(
        fold_initial(audio_rows, HA, HDA), audio_local, piece[0], piece[1], permit, HA, HDA
    )
    audio_mixed = fold_finish(audio_state, HA, HDA)
    cross_owned = (
        lax.all_to_all(
            split_heads(cross_video_query, HA, HDA, copies),
            "seq",
            split_axis=0,
            concat_axis=1,
            tiled=True,
        ),
        lax.all_to_all(
            spread_heads(cross_audio_keys, HA, HDA, copies),
            "seq",
            split_axis=0,
            concat_axis=1,
            tiled=True,
        ),
        lax.all_to_all(
            spread_heads(cross_audio_values, HA, HDA, copies),
            "seq",
            split_axis=0,
            concat_axis=1,
            tiled=True,
        ),
    )
    cross_done = attend_local(
        cross_owned[0],
        cross_owned[1],
        cross_owned[2],
        owned_positions(video_rows, copies, devices, index),
        audio_places,
        toward_video,
    )
    video_cross = join_heads(
        lax.all_to_all(cross_done, "seq", split_axis=1, concat_axis=0, tiled=True), HA, HDA, copies
    )
    listen_owned = (
        lax.all_to_all(
            split_heads(cross_audio_query, HA, HDA, copies),
            "seq",
            split_axis=0,
            concat_axis=1,
            tiled=True,
        ),
        lax.all_to_all(
            spread_heads(cross_video_keys, HA, HDA, copies),
            "seq",
            split_axis=0,
            concat_axis=1,
            tiled=True,
        ),
        lax.all_to_all(
            spread_heads(cross_video_values, HA, HDA, copies),
            "seq",
            split_axis=0,
            concat_axis=1,
            tiled=True,
        ),
    )
    listen_done = attend_local(
        listen_owned[0],
        listen_owned[1],
        listen_owned[2],
        owned_positions(audio_rows, copies, devices, index),
        video_places,
        toward_audio,
    )
    audio_cross = join_heads(
        lax.all_to_all(listen_done, "seq", split_axis=1, concat_axis=0, tiled=True), HA, HDA, copies
    )
    return (video_mixed, audio_mixed, video_cross, audio_cross)


LANES = 128


def fetch(sources, held, arrived):
    copies = [
        pltpu.make_async_copy(source, slot, arrived.at[i])
        for i, (source, slot) in enumerate(zip(sources, held))
    ]
    for copy in copies:
        copy.start()
    return copies


def step_order(chips):
    far, near = list(range(chips - 1, chips // 2 - 1, -1)), list(range(1, chips // 2))
    return [0] + far[:1] + near[:1] + far[1:2] + near[1:2] + far[2:] + near[2:]


def by_step(items):
    order = step_order(len(items))
    return [items[order.index(j)] for j in range(len(items))]


def in_order(items):
    return [items[j] for j in step_order(len(items))]


def pack_kernel(chips, *refs):
    sources, refs = refs[:12], refs[12:]
    packed, held, arrived = by_step(refs[:chips]), refs[chips : chips + 12], refs[chips + 12]
    copies = fetch(sources, held, arrived)
    chip = lax.axis_index("seq") // 2
    video, cross, audio = held[0:3], held[3:6], held[6:12]
    rows = video[0].shape[0]

    def group(ref, j, part):
        width = ref.shape[1] // chips
        at = pl.multiple_of((chip ^ j) * width + part * LANES, LANES)
        return ref[:, pl.ds(at, LANES)]

    at = 0
    for i, ref in enumerate(video + cross):
        copies[i].wait()
        for part in range(ref.shape[1] // chips // LANES):
            for j in range(chips):
                packed[j][at : at + rows, :] = group(ref, j, part)
            at += rows
    for i in range(0, 6, 2):
        copies[6 + i].wait()
        copies[7 + i].wait()
        for part in range(audio[i].shape[1] // chips // LANES):
            for j in range(chips):
                pair = jnp.concatenate(
                    [group(audio[i], j, part), group(audio[i + 1], j, part)], axis=0
                )
                packed[j][at : at + rows, :] = pair
            at += rows


def gather_kernel(video_len, audio_len, shift, *refs):
    slabs, bounds, merged = refs[:-2], refs[-2], refs[-1]
    row = lax.broadcasted_iota(jnp.int32, bounds.shape, 0)
    bounds[...] = jnp.where(row == 0, video_len[0], jnp.where(row == 1, audio_len[0], shift[0]))
    for i, slab in enumerate(slabs):
        merged[i] = slab[...]


def merge_kernel(*refs):
    for i, slab in enumerate(refs[:-1]):
        refs[-1][i] = slab[...]


def mix_all(units):
    scores = [
        lax.dot_general(query, key, (((1,), (1,)), ((), ())), preferred_element_type=jnp.float32)
        for query, key, value, depth, permit in units
    ]
    weights, totals = [], []
    for score, (query, key, value, depth, permit) in zip(scores, units):
        score = jnp.where(permit, score, -1e30)
        peak = jnp.max(score, axis=1, keepdims=True)
        weight = jnp.exp2((score - peak) * (math.log2(math.e) / math.sqrt(depth)))
        totals.append(jnp.sum(weight, axis=1, keepdims=True))
        weights.append(weight.astype(jnp.bfloat16))
    return [
        jnp.dot(weight, unit[2], preferred_element_type=jnp.float32) / total
        for weight, total, unit in zip(weights, totals, units)
    ]


def pair_units(query, key, value, permit):
    lane = lax.broadcasted_iota(jnp.int32, query.shape, 1) // HDA
    zero = jnp.zeros_like(query)
    return [
        (jnp.where(lane == h, query, zero), key, value, HDA, permit) for h in range(LANES // HDA)
    ]


def pair_join(mixed):
    lane = lax.broadcasted_iota(jnp.int32, mixed[0].shape, 1) // HDA
    result = mixed[0]
    for h in range(1, len(mixed)):
        result = jnp.where(lane == h, mixed[h], result)
    return result


def shares(chips):
    quarter = chips // 4
    far = list(zip(range(chips - 1, 3 * quarter - 1, -1), range(3 * quarter - 1, 2 * quarter - 1, -1)))
    near = list(zip(range(quarter - 1, -1, -1), range(2 * quarter - 1, quarter - 1, -1)))
    return far + near


def attend_kernel(chips, rows, parts, pairs, bounds, *refs):
    own, early, late, done = by_step(refs[:chips]), refs[chips], refs[chips + 1], refs[chips + 2 :]
    other = by_step([ref.at[i] for ref in (early, late) for i in range(ref.shape[0])])
    share = shares(chips)
    every = [ref for both in zip(own, other) for ref in both]
    half = rows // 2
    tv, ta = 2 * chips * rows, 2 * chips * half
    bits = (tv // ta).bit_length() - 1
    me = lax.axis_index("seq")
    core, home = me % 2, me // 2 * 2
    video_valid, audio_valid, offset = (bounds[i : i + 1, 0:1] for i in range(3))

    def slab(at):
        return jnp.concatenate([ref[at : at + rows, :] for ref in every], axis=0)

    def asked(at):
        pieces = []
        for zero, one in share:
            for c in range(2):
                low = (own, other)[c][zero][at : at + rows, :]
                high = (other, own)[c][one][at : at + rows, :]
                pieces.append(jnp.where(core == 0, low, high))
        return jnp.concatenate(pieces, axis=0)

    def split(wide):
        wide = wide.astype(jnp.float32).reshape(-1, rows, LANES)
        first = wide[:, :half, :].reshape(-1, LANES).astype(jnp.bfloat16)
        second = wide[:, half:, :].reshape(-1, LANES).astype(jnp.bfloat16)
        return first, second

    def places(q_step, k_step):
        shape = (chips * q_step, 2 * chips * k_step)
        k_at = lax.broadcasted_iota(jnp.int32, shape, 1) ^ (me * k_step)
        starts = []
        for zero, one in share:
            chip = home ^ jnp.where(core == 0, 2 * zero, 2 * one)
            starts.append(lax.broadcasted_iota(jnp.int32, (2 * q_step, 1), 0) + chip * q_step)
        return jnp.concatenate(starts, axis=0), k_at

    def put(at, mixed):
        count = done[0].shape[0] // 2
        for u in range(len(share)):
            for c in range(2):
                piece = mixed[(2 * u + c) * rows : (2 * u + c + 1) * rows]
                done[u][c * count + at : c * count + at + rows, :] = piece.astype(jnp.bfloat16)

    q_at, k_at = places(rows, rows)
    permit = k_at < video_valid
    units = [
        (
            asked(h * rows),
            slab((parts + h) * rows),
            slab((2 * parts + h) * rows),
            HDV,
            permit,
        )
        for h in range(parts)
    ]
    for h, mixed in enumerate(mix_all(units)):
        put(h * rows, mixed)

    cross = 3 * parts * rows
    audio = cross + 3 * pairs * rows
    q_at, k_at = places(rows, half)
    center = jnp.clip((q_at >> bits) + offset, 0, audio_valid - 1)
    toward_video = (k_at < audio_valid) & (jnp.abs(k_at - center) <= 5 * ta // 8)
    q_at, k_at = places(half, half)
    within_audio = k_at < audio_valid
    q_at, k_at = places(half, rows)
    center = jnp.clip((q_at - offset) << bits, 0, video_valid - 1)
    toward_audio = (k_at < video_valid) & (jnp.abs(k_at - center) <= tv // 8)
    units = []
    for p in range(pairs):
        at = cross + p * rows
        cross_query = asked(at)
        cross_keys = slab(at + pairs * rows)
        cross_values = slab(at + 2 * pairs * rows)
        at = audio + p * rows
        audio_query = split(asked(at))[0]
        audio_keys = split(slab(at))[1]
        at += pairs * rows
        audio_values = split(slab(at))[0]
        listen_query = split(asked(at))[1]
        at += pairs * rows
        sound_keys, sound_values = split(slab(at))
        units += pair_units(cross_query, sound_keys, sound_values, toward_video)
        units += pair_units(audio_query, audio_keys, audio_values, within_audio)
        units += pair_units(listen_query, cross_keys, cross_values, toward_audio)
    mixed = mix_all(units)
    heads = LANES // HDA
    for p in range(pairs):
        seen, heard, listened = (
            pair_join(mixed[(3 * p + i) * heads : (3 * p + i + 1) * heads]) for i in range(3)
        )
        out = (parts + p) * rows
        put(out, seen)
        both = jnp.concatenate(
            [heard.reshape(-1, half, LANES), listened.reshape(-1, half, LANES)], axis=1
        )
        put(out + pairs * rows, both.reshape(-1, LANES))


def unpack_kernel(chips, *refs):
    share = shares(chips)
    back, other = refs[: len(share)], refs[len(share) : 2 * len(share)]
    video_mixed, audio_mixed, video_cross, audio_cross = refs[2 * len(share) :]
    rows = video_mixed.shape[0]
    half = audio_mixed.shape[0]
    parts = video_mixed.shape[1] // chips // LANES
    pairs = audio_mixed.shape[1] // chips // LANES
    me = lax.axis_index("seq")
    core, home = me % 2, me // 2
    for u, (zero, one) in enumerate(share):
        for ref, chip in (
            (back[u], home ^ jnp.where(core == 0, zero, one)),
            (other[u], home ^ jnp.where(core == 0, one, zero)),
        ):
            base = pl.multiple_of(core * (ref.shape[0] // 2), 16)

            def piece(at):
                return ref[pl.ds(base + at, rows), :]

            for h in range(parts):
                at = pl.multiple_of((chip * parts + h) * LANES, LANES)
                video_mixed[:, pl.ds(at, LANES)] = piece(h * rows)
            for p in range(pairs):
                at = pl.multiple_of((chip * pairs + p) * LANES, LANES)
                out = (parts + p) * rows
                video_cross[:, pl.ds(at, LANES)] = piece(out)
                both = piece(out + pairs * rows)
                audio_mixed[:, pl.ds(at, LANES)] = both[:half, :]
                audio_cross[:, pl.ds(at, LANES)] = both[half:, :]


def swap(piece, n, step):
    return lax.ppermute(piece, "seq", [(i, i ^ step) for i in range(n)])


def shards_packed(*arrays):
    (
        video_query, video_keys, video_values,
        audio_query, audio_keys, audio_values,
        cross_video_query, cross_video_keys, cross_video_values,
        cross_audio_query, cross_audio_keys, cross_audio_values,
        video_length, audio_length, align_offset,
    ) = arrays
    n = lax.axis_size("seq")
    chips = n // 2
    rows = video_query.shape[0]
    parts = video_query.shape[1] // chips // LANES
    pairs = audio_query.shape[1] // chips // LANES
    vmem = pl.BlockSpec(memory_space=pltpu.VMEM)
    hbm = pl.BlockSpec(memory_space=pltpu.HBM)
    smem = pl.BlockSpec(memory_space=pltpu.SMEM)
    params = pltpu.CompilerParams(vmem_limit_bytes=32 * 1024 * 1024)

    def buffer(*shape):
        return jax.ShapeDtypeStruct(shape, jnp.bfloat16)

    sources = (
        video_query, video_keys, video_values,
        cross_video_query, cross_video_keys, cross_video_values,
        audio_query, audio_keys, audio_values,
        cross_audio_query, cross_audio_keys, cross_audio_values,
    )
    packed = pl.pallas_call(
        functools.partial(pack_kernel, chips),
        out_shape=[pltpu.VMEM(((3 * parts + 6 * pairs) * rows, LANES), jnp.bfloat16)] * chips,
        in_specs=[hbm] * 12,
        out_specs=[vmem] * chips,
        scratch_shapes=[pltpu.VMEM(source.shape, source.dtype) for source in sources]
        + [pltpu.SemaphoreType.DMA((12,))],
        compiler_params=params,
    )(*[pltpu.with_memory_space_constraint(source, pltpu.HBM) for source in sources])
    packed = by_step(packed)
    moved = [swap(packed[j], n, 2 * j) for j in range(1, chips)]
    own = in_order(packed[:1] + moved)
    early = chips // 2
    slab = packed[0].shape
    bounds, first = pl.pallas_call(
        gather_kernel,
        out_shape=(
            pltpu.VMEM((8, LANES), jnp.int32),
            pltpu.VMEM((early,) + slab, jnp.bfloat16),
        ),
        in_specs=[smem] * 3 + [vmem] * early,
        out_specs=(vmem, vmem),
        compiler_params=params,
    )(video_length, audio_length, align_offset, *own[:early])
    second = pl.pallas_call(
        merge_kernel,
        out_shape=pltpu.VMEM((chips - early,) + slab, jnp.bfloat16),
        in_specs=[vmem] * (chips - early),
        out_specs=vmem,
        compiler_params=params,
    )(*own[early:])
    share = shares(chips)
    done = pl.pallas_call(
        functools.partial(attend_kernel, chips, rows, parts, pairs),
        out_shape=[buffer(2 * (parts + 2 * pairs) * rows, LANES)] * len(share),
        in_specs=[vmem] * (3 + chips),
        out_specs=[vmem] * len(share),
        compiler_params=params,
    )(bounds, *own, swap(first, n, 1), swap(second, n, 1))
    back = [
        lax.ppermute(piece, "seq", [(i, i ^ 2 * pair[i % 2]) for i in range(n)])
        for piece, pair in zip(done, share)
    ]
    return pl.pallas_call(
        functools.partial(unpack_kernel, chips),
        out_shape=(
            buffer(*video_query.shape),
            buffer(*audio_query.shape),
            buffer(*cross_video_query.shape),
            buffer(*cross_audio_query.shape),
        ),
        in_specs=[vmem] * (2 * len(share)),
        out_specs=(vmem,) * 4,
        compiler_params=params,
    )(*back, *[swap(piece, n, 1) for piece in back])


def shards(*arrays):
    n = lax.axis_size("seq")
    chips = max(n // 2, 1)
    rows, half = arrays[0].shape[0], arrays[3].shape[0]
    fits = (
        n % 8 == 0
        and n & (n - 1) == 0
        and arrays[0].shape[1] % (chips * LANES) == 0
        and arrays[3].shape[1] % (chips * LANES) == 0
        and HDV == LANES
        and LANES % HDA == 0
        and rows == 2 * half
        and half % 8 == 0
        and half & (half - 1) == 0
    )
    return shards_packed(*arrays) if fits else shards_general(*arrays)


def solution(mesh):
    placed = (
        P(("clip", "seq"), None),
        P(("clip", "seq"), None),
        P(("clip", "seq"), None),
        P(("clip", "seq"), None),
        P(("clip", "seq"), None),
        P(("clip", "seq"), None),
        P(("clip", "seq"), None),
        P(("clip", "seq"), None),
        P(("clip", "seq"), None),
        P(("clip", "seq"), None),
        P(("clip", "seq"), None),
        P(("clip", "seq"), None),
        P("clip"),
        P("clip"),
        P("clip"),
    )
    return jax.shard_map(
        shards,
        mesh=mesh,
        in_specs=placed,
        out_specs=(
            P(("clip", "seq"), None),
            P(("clip", "seq"), None),
            P(("clip", "seq"), None),
            P(("clip", "seq"), None),
        ),
        check_vma=False,
    )
```

```python
import functools
import math

import jax
import jax.numpy as jnp
from jax import lax
from jax.experimental import pallas as pl
from jax.experimental.pallas import tpu as pltpu
from jax.sharding import PartitionSpec as P

HV = 32
HDV = 128
HA = 32
HDA = 64


def block_size(total, limit):
    chosen = min(total, limit)
    while total % chosen:
        chosen -= 1
    return chosen


def split_heads(tokens, heads, depth, copies):
    rows = tokens.shape[0]
    shaped = tokens.reshape(copies, rows // copies, heads, depth).transpose(2, 0, 1, 3)
    return shaped.reshape(heads * copies, rows // copies, depth)


def spread_heads(tokens, heads, depth, copies):
    rows = tokens.shape[0]
    shaped = tokens.reshape(rows, heads, depth).transpose(1, 0, 2)
    shaped = jnp.broadcast_to(shaped[:, None], (heads, copies, rows, depth))
    return shaped.reshape(heads * copies, rows, depth)


def join_heads(owned, heads, depth, copies):
    part_rows = owned.shape[1]
    shaped = owned.reshape(heads, copies, part_rows, depth).transpose(1, 2, 0, 3)
    return shaped.reshape(copies * part_rows, heads * depth)


def owned_positions(rows, copies, devices, index):
    part_rows = rows // copies
    flat = jnp.arange(devices * part_rows, dtype=jnp.int32)
    return flat // part_rows * rows + index % copies * part_rows + flat % part_rows


def online_update(carry, scores, permit, value_tile, value_form):
    running, total, accum = carry
    scores = jnp.where(permit, scores, -1e30)
    newmax = jnp.maximum(running, jnp.max(scores, axis=2))
    weights = jnp.where(permit, jnp.exp(scores - newmax[:, :, None]), 0.0)
    factor = jnp.exp(running - newmax)
    total = total * factor + jnp.sum(weights, axis=2)
    mixed = jnp.einsum(
        value_form, weights.astype(jnp.bfloat16), value_tile, preferred_element_type=jnp.float32
    )
    accum = accum * factor[:, :, None] + mixed
    return (newmax, total, accum)


def fold_initial(rows, heads, depth):
    return (
        jnp.full((heads, rows), -1e30, jnp.float32),
        jnp.zeros((heads, rows), jnp.float32),
        jnp.zeros((heads, rows, depth), jnp.float32),
    )


def fold_piece(carry, local_query, key_rows, value_rows, permit, heads, depth):
    keyed = key_rows.reshape(key_rows.shape[0], heads, depth)
    valued = value_rows.reshape(value_rows.shape[0], heads, depth)
    scores = jnp.einsum("qhd,khd->hqk", local_query, keyed, preferred_element_type=jnp.float32) * (
        1.0 / math.sqrt(depth)
    )
    return online_update(carry, scores, permit[None], valued, "hqk,khd->hqd")


def fold_finish(carry, heads, depth):
    running, total, accum = carry
    result = (accum / total[:, :, None]).astype(jnp.bfloat16)
    return result.transpose(1, 0, 2).reshape(result.shape[1], heads * depth)


def attend_local(queries, keys, values, query_pos, key_pos, allowed):
    heads, q_count, depth = queries.shape
    k_count = keys.shape[1]
    q_block = block_size(q_count, 512)
    k_block = block_size(k_count, 2048)
    scale = 1.0 / math.sqrt(depth)
    q_tiles = queries.reshape(heads, q_count // q_block, q_block, depth).transpose(1, 0, 2, 3)
    k_tiles = keys.reshape(heads, k_count // k_block, k_block, depth).transpose(1, 0, 2, 3)
    v_tiles = values.reshape(heads, k_count // k_block, k_block, depth).transpose(1, 0, 2, 3)
    q_places = query_pos.reshape(q_count // q_block, q_block)
    k_places = key_pos.reshape(k_count // k_block, k_block)

    def one_tile(packed):
        q_tile, q_where = packed

        def absorb(carry, piece):
            k_tile, v_tile, k_where = piece
            scores = (
                jnp.einsum("hqd,hkd->hqk", q_tile, k_tile, preferred_element_type=jnp.float32)
                * scale
            )
            permit = allowed(q_where[:, None], k_where[None, :])[None]
            return (online_update(carry, scores, permit, v_tile, "hqk,hkd->hqd"), None)

        initial = fold_initial(q_block, heads, depth)
        final_state, unused = lax.scan(absorb, initial, (k_tiles, v_tiles, k_places))
        running, total, accum = final_state
        return (accum / total[:, :, None]).astype(jnp.bfloat16)

    tiles = lax.map(one_tile, (q_tiles, q_places))
    return tiles.transpose(1, 0, 2, 3).reshape(heads, q_count, depth)


def shards_general(
    video_query,
    video_keys,
    video_values,
    audio_query,
    audio_keys,
    audio_values,
    cross_video_query,
    cross_video_keys,
    cross_video_values,
    cross_audio_query,
    cross_audio_keys,
    cross_audio_values,
    video_length,
    audio_length,
    align_offset,
):
    devices = lax.axis_size("seq")
    index = lax.axis_index("seq")
    video_rows = video_query.shape[0]
    audio_rows = audio_query.shape[0]
    video_total = video_rows * devices
    audio_total = audio_rows * devices
    video_reach = video_total // 8
    audio_reach = 5 * audio_total // 8
    video_valid = video_length[0]
    audio_valid = audio_length[0]
    align_shift = align_offset[0]
    copies = max(devices // HV, 1)
    video_places = jnp.arange(video_total, dtype=jnp.int32)
    audio_places = jnp.arange(audio_total, dtype=jnp.int32)

    def video_open(q_where, k_where):
        return k_where < video_valid

    def toward_video(q_where, k_where):
        center = jnp.clip(q_where * audio_total // video_total + align_shift, 0, audio_valid - 1)
        return (k_where < audio_valid) & (jnp.abs(k_where - center) <= audio_reach)

    def toward_audio(q_where, k_where):
        center = jnp.clip((q_where - align_shift) * video_total // audio_total, 0, video_valid - 1)
        return (k_where < video_valid) & (jnp.abs(k_where - center) <= video_reach)

    video_owned = (
        lax.all_to_all(
            split_heads(video_query, HV, HDV, copies),
            "seq",
            split_axis=0,
            concat_axis=1,
            tiled=True,
        ),
        lax.all_to_all(
            spread_heads(video_keys, HV, HDV, copies),
            "seq",
            split_axis=0,
            concat_axis=1,
            tiled=True,
        ),
        lax.all_to_all(
            spread_heads(video_values, HV, HDV, copies),
            "seq",
            split_axis=0,
            concat_axis=1,
            tiled=True,
        ),
    )
    video_done = attend_local(
        video_owned[0],
        video_owned[1],
        video_owned[2],
        owned_positions(video_rows, copies, devices, index),
        video_places,
        video_open,
    )
    video_mixed = join_heads(
        lax.all_to_all(video_done, "seq", split_axis=1, concat_axis=0, tiled=True), HV, HDV, copies
    )
    audio_local = audio_query.reshape(audio_rows, HA, HDA)
    piece = (
        lax.all_gather(audio_keys, "seq", axis=0, tiled=True),
        lax.all_gather(audio_values, "seq", axis=0, tiled=True),
    )
    k_where = jnp.arange(piece[0].shape[0], dtype=jnp.int32)
    audio_k_where = k_where[None, :]
    permit = audio_k_where < audio_valid
    audio_state = fold_piece(
        fold_initial(audio_rows, HA, HDA), audio_local, piece[0], piece[1], permit, HA, HDA
    )
    audio_mixed = fold_finish(audio_state, HA, HDA)
    cross_owned = (
        lax.all_to_all(
            split_heads(cross_video_query, HA, HDA, copies),
            "seq",
            split_axis=0,
            concat_axis=1,
            tiled=True,
        ),
        lax.all_to_all(
            spread_heads(cross_audio_keys, HA, HDA, copies),
            "seq",
            split_axis=0,
            concat_axis=1,
            tiled=True,
        ),
        lax.all_to_all(
            spread_heads(cross_audio_values, HA, HDA, copies),
            "seq",
            split_axis=0,
            concat_axis=1,
            tiled=True,
        ),
    )
    cross_done = attend_local(
        cross_owned[0],
        cross_owned[1],
        cross_owned[2],
        owned_positions(video_rows, copies, devices, index),
        audio_places,
        toward_video,
    )
    video_cross = join_heads(
        lax.all_to_all(cross_done, "seq", split_axis=1, concat_axis=0, tiled=True), HA, HDA, copies
    )
    listen_owned = (
        lax.all_to_all(
            split_heads(cross_audio_query, HA, HDA, copies),
            "seq",
            split_axis=0,
            concat_axis=1,
            tiled=True,
        ),
        lax.all_to_all(
            spread_heads(cross_video_keys, HA, HDA, copies),
            "seq",
            split_axis=0,
            concat_axis=1,
            tiled=True,
        ),
        lax.all_to_all(
            spread_heads(cross_video_values, HA, HDA, copies),
            "seq",
            split_axis=0,
            concat_axis=1,
            tiled=True,
        ),
    )
    listen_done = attend_local(
        listen_owned[0],
        listen_owned[1],
        listen_owned[2],
        owned_positions(audio_rows, copies, devices, index),
        video_places,
        toward_audio,
    )
    audio_cross = join_heads(
        lax.all_to_all(listen_done, "seq", split_axis=1, concat_axis=0, tiled=True), HA, HDA, copies
    )
    return (video_mixed, audio_mixed, video_cross, audio_cross)


LANES = 128


def fetch(sources, held, arrived):
    copies = [
        pltpu.make_async_copy(source, slot, arrived.at[i])
        for i, (source, slot) in enumerate(zip(sources, held))
    ]
    for copy in copies:
        copy.start()
    return copies


def step_order(chips):
    far, near = list(range(chips - 1, chips // 2 - 1, -1)), list(range(1, chips // 2))
    return [0] + far[:1] + near[:1] + far[1:2] + near[1:] + far[2:]


def by_step(items):
    order = step_order(len(items))
    return [items[order.index(j)] for j in range(len(items))]


def in_order(items):
    return [items[j] for j in step_order(len(items))]


def pack_kernel(chips, *refs):
    sources, refs = refs[:12], refs[12:]
    packed, held, arrived = by_step(refs[:chips]), refs[chips : chips + 12], refs[chips + 12]
    copies = fetch(sources, held, arrived)
    chip = lax.axis_index("seq") // 2
    video, cross, audio = held[0:3], held[3:6], held[6:12]
    rows = video[0].shape[0]

    def group(ref, j, part):
        width = ref.shape[1] // chips
        at = pl.multiple_of((chip ^ j) * width + part * LANES, LANES)
        return ref[:, pl.ds(at, LANES)]

    at = 0
    for i, ref in enumerate(video + cross):
        copies[i].wait()
        for part in range(ref.shape[1] // chips // LANES):
            for j in range(chips):
                packed[j][at : at + rows, :] = group(ref, j, part)
            at += rows
    for i in range(0, 6, 2):
        copies[6 + i].wait()
        copies[7 + i].wait()
        for part in range(audio[i].shape[1] // chips // LANES):
            for j in range(chips):
                pair = jnp.concatenate(
                    [group(audio[i], j, part), group(audio[i + 1], j, part)], axis=0
                )
                packed[j][at : at + rows, :] = pair
            at += rows


def gather_kernel(video_len, audio_len, shift, *refs):
    slabs, bounds, merged = refs[:-2], refs[-2], refs[-1]
    row = lax.broadcasted_iota(jnp.int32, bounds.shape, 0)
    bounds[...] = jnp.where(row == 0, video_len[0], jnp.where(row == 1, audio_len[0], shift[0]))
    for i, slab in enumerate(slabs):
        merged[i] = slab[...]


def merge_kernel(*refs):
    for i, slab in enumerate(refs[:-1]):
        refs[-1][i] = slab[...]


def mix_all(units):
    scores = [
        lax.dot_general(query, key, (((1,), (1,)), ((), ())), preferred_element_type=jnp.float32)
        for query, key, value, depth, permit in units
    ]
    weights, totals = [], []
    for score, (query, key, value, depth, permit) in zip(scores, units):
        score = jnp.where(permit, score, -1e30)
        peak = jnp.max(score, axis=1, keepdims=True)
        weight = jnp.exp2((score - peak) * (math.log2(math.e) / math.sqrt(depth)))
        totals.append(jnp.sum(weight, axis=1, keepdims=True))
        weights.append(weight.astype(jnp.bfloat16))
    return [
        jnp.dot(weight, unit[2], preferred_element_type=jnp.float32) / total
        for weight, total, unit in zip(weights, totals, units)
    ]


def pair_units(query, key, value, permit):
    lane = lax.broadcasted_iota(jnp.int32, query.shape, 1) // HDA
    zero = jnp.zeros_like(query)
    return [
        (jnp.where(lane == h, query, zero), key, value, HDA, permit) for h in range(LANES // HDA)
    ]


def pair_join(mixed):
    lane = lax.broadcasted_iota(jnp.int32, mixed[0].shape, 1) // HDA
    result = mixed[0]
    for h in range(1, len(mixed)):
        result = jnp.where(lane == h, mixed[h], result)
    return result


def shares(chips):
    quarter = chips // 4
    far = list(zip(range(chips - 1, 3 * quarter - 1, -1), range(3 * quarter - 1, 2 * quarter - 1, -1)))
    near = list(zip(range(quarter - 1, -1, -1), range(2 * quarter - 1, quarter - 1, -1)))
    return far + near


def attend_kernel(chips, rows, parts, pairs, bounds, *refs):
    own, early, late, done = by_step(refs[:chips]), refs[chips], refs[chips + 1], refs[chips + 2 :]
    other = by_step([ref.at[i] for ref in (early, late) for i in range(ref.shape[0])])
    share = shares(chips)
    every = [ref for both in zip(own, other) for ref in both]
    half = rows // 2
    tv, ta = 2 * chips * rows, 2 * chips * half
    bits = (tv // ta).bit_length() - 1
    me = lax.axis_index("seq")
    core, home = me % 2, me // 2 * 2
    video_valid, audio_valid, offset = (bounds[i : i + 1, 0:1] for i in range(3))

    def slab(at):
        return jnp.concatenate([ref[at : at + rows, :] for ref in every], axis=0)

    def asked(at):
        pieces = []
        for zero, one in share:
            for c in range(2):
                low = (own, other)[c][zero][at : at + rows, :]
                high = (other, own)[c][one][at : at + rows, :]
                pieces.append(jnp.where(core == 0, low, high))
        return jnp.concatenate(pieces, axis=0)

    def split(wide):
        wide = wide.astype(jnp.float32).reshape(-1, rows, LANES)
        first = wide[:, :half, :].reshape(-1, LANES).astype(jnp.bfloat16)
        second = wide[:, half:, :].reshape(-1, LANES).astype(jnp.bfloat16)
        return first, second

    def places(q_step, k_step):
        shape = (chips * q_step, 2 * chips * k_step)
        k_at = lax.broadcasted_iota(jnp.int32, shape, 1) ^ (me * k_step)
        starts = []
        for zero, one in share:
            chip = home ^ jnp.where(core == 0, 2 * zero, 2 * one)
            starts.append(lax.broadcasted_iota(jnp.int32, (2 * q_step, 1), 0) + chip * q_step)
        return jnp.concatenate(starts, axis=0), k_at

    def put(at, mixed):
        count = done[0].shape[0] // 2
        for u in range(len(share)):
            for c in range(2):
                piece = mixed[(2 * u + c) * rows : (2 * u + c + 1) * rows]
                done[u][c * count + at : c * count + at + rows, :] = piece.astype(jnp.bfloat16)

    q_at, k_at = places(rows, rows)
    permit = k_at < video_valid
    units = [
        (
            asked(h * rows),
            slab((parts + h) * rows),
            slab((2 * parts + h) * rows),
            HDV,
            permit,
        )
        for h in range(parts)
    ]
    for h, mixed in enumerate(mix_all(units)):
        put(h * rows, mixed)

    cross = 3 * parts * rows
    audio = cross + 3 * pairs * rows
    q_at, k_at = places(rows, half)
    center = jnp.clip((q_at >> bits) + offset, 0, audio_valid - 1)
    toward_video = (k_at < audio_valid) & (jnp.abs(k_at - center) <= 5 * ta // 8)
    q_at, k_at = places(half, half)
    within_audio = k_at < audio_valid
    q_at, k_at = places(half, rows)
    center = jnp.clip((q_at - offset) << bits, 0, video_valid - 1)
    toward_audio = (k_at < video_valid) & (jnp.abs(k_at - center) <= tv // 8)
    units = []
    for p in range(pairs):
        at = cross + p * rows
        cross_query = asked(at)
        cross_keys = slab(at + pairs * rows)
        cross_values = slab(at + 2 * pairs * rows)
        at = audio + p * rows
        audio_query = split(asked(at))[0]
        audio_keys = split(slab(at))[1]
        at += pairs * rows
        audio_values = split(slab(at))[0]
        listen_query = split(asked(at))[1]
        at += pairs * rows
        sound_keys, sound_values = split(slab(at))
        units += pair_units(cross_query, sound_keys, sound_values, toward_video)
        units += pair_units(audio_query, audio_keys, audio_values, within_audio)
        units += pair_units(listen_query, cross_keys, cross_values, toward_audio)
    mixed = mix_all(units)
    heads = LANES // HDA
    for p in range(pairs):
        seen, heard, listened = (
            pair_join(mixed[(3 * p + i) * heads : (3 * p + i + 1) * heads]) for i in range(3)
        )
        out = (parts + p) * rows
        put(out, seen)
        both = jnp.concatenate(
            [heard.reshape(-1, half, LANES), listened.reshape(-1, half, LANES)], axis=1
        )
        put(out + pairs * rows, both.reshape(-1, LANES))


def unpack_kernel(chips, *refs):
    share = shares(chips)
    back, other = refs[: len(share)], refs[len(share) : 2 * len(share)]
    video_mixed, audio_mixed, video_cross, audio_cross = refs[2 * len(share) :]
    rows = video_mixed.shape[0]
    half = audio_mixed.shape[0]
    parts = video_mixed.shape[1] // chips // LANES
    pairs = audio_mixed.shape[1] // chips // LANES
    me = lax.axis_index("seq")
    core, home = me % 2, me // 2
    for u, (zero, one) in enumerate(share):
        for ref, chip in (
            (back[u], home ^ jnp.where(core == 0, zero, one)),
            (other[u], home ^ jnp.where(core == 0, one, zero)),
        ):
            base = pl.multiple_of(core * (ref.shape[0] // 2), 16)

            def piece(at):
                return ref[pl.ds(base + at, rows), :]

            for h in range(parts):
                at = pl.multiple_of((chip * parts + h) * LANES, LANES)
                video_mixed[:, pl.ds(at, LANES)] = piece(h * rows)
            for p in range(pairs):
                at = pl.multiple_of((chip * pairs + p) * LANES, LANES)
                out = (parts + p) * rows
                video_cross[:, pl.ds(at, LANES)] = piece(out)
                both = piece(out + pairs * rows)
                audio_mixed[:, pl.ds(at, LANES)] = both[:half, :]
                audio_cross[:, pl.ds(at, LANES)] = both[half:, :]


def swap(piece, n, step):
    return lax.ppermute(piece, "seq", [(i, i ^ step) for i in range(n)])


def shards_packed(*arrays):
    (
        video_query, video_keys, video_values,
        audio_query, audio_keys, audio_values,
        cross_video_query, cross_video_keys, cross_video_values,
        cross_audio_query, cross_audio_keys, cross_audio_values,
        video_length, audio_length, align_offset,
    ) = arrays
    n = lax.axis_size("seq")
    chips = n // 2
    rows = video_query.shape[0]
    parts = video_query.shape[1] // chips // LANES
    pairs = audio_query.shape[1] // chips // LANES
    vmem = pl.BlockSpec(memory_space=pltpu.VMEM)
    hbm = pl.BlockSpec(memory_space=pltpu.HBM)
    smem = pl.BlockSpec(memory_space=pltpu.SMEM)
    params = pltpu.CompilerParams(vmem_limit_bytes=32 * 1024 * 1024)

    def buffer(*shape):
        return jax.ShapeDtypeStruct(shape, jnp.bfloat16)

    sources = (
        video_query, video_keys, video_values,
        cross_video_query, cross_video_keys, cross_video_values,
        audio_query, audio_keys, audio_values,
        cross_audio_query, cross_audio_keys, cross_audio_values,
    )
    packed = pl.pallas_call(
        functools.partial(pack_kernel, chips),
        out_shape=[pltpu.VMEM(((3 * parts + 6 * pairs) * rows, LANES), jnp.bfloat16)] * chips,
        in_specs=[hbm] * 12,
        out_specs=[vmem] * chips,
        scratch_shapes=[pltpu.VMEM(source.shape, source.dtype) for source in sources]
        + [pltpu.SemaphoreType.DMA((12,))],
        compiler_params=params,
    )(*[pltpu.with_memory_space_constraint(source, pltpu.HBM) for source in sources])
    packed = by_step(packed)
    moved = [swap(packed[j], n, 2 * j) for j in range(1, chips)]
    own = in_order(packed[:1] + moved)
    early = chips // 2
    slab = packed[0].shape
    bounds, first = pl.pallas_call(
        gather_kernel,
        out_shape=(
            pltpu.VMEM((8, LANES), jnp.int32),
            pltpu.VMEM((early,) + slab, jnp.bfloat16),
        ),
        in_specs=[smem] * 3 + [vmem] * early,
        out_specs=(vmem, vmem),
        compiler_params=params,
    )(video_length, audio_length, align_offset, *own[:early])
    second = pl.pallas_call(
        merge_kernel,
        out_shape=pltpu.VMEM((chips - early,) + slab, jnp.bfloat16),
        in_specs=[vmem] * (chips - early),
        out_specs=vmem,
        compiler_params=params,
    )(*own[early:])
    share = shares(chips)
    done = pl.pallas_call(
        functools.partial(attend_kernel, chips, rows, parts, pairs),
        out_shape=[buffer(2 * (parts + 2 * pairs) * rows, LANES)] * len(share),
        in_specs=[vmem] * (3 + chips),
        out_specs=[vmem] * len(share),
        compiler_params=params,
    )(bounds, *own, swap(first, n, 1), swap(second, n, 1))
    back = [
        lax.ppermute(piece, "seq", [(i, i ^ 2 * pair[i % 2]) for i in range(n)])
        for piece, pair in zip(done, share)
    ]
    return pl.pallas_call(
        functools.partial(unpack_kernel, chips),
        out_shape=(
            buffer(*video_query.shape),
            buffer(*audio_query.shape),
            buffer(*cross_video_query.shape),
            buffer(*cross_audio_query.shape),
        ),
        in_specs=[vmem] * (2 * len(share)),
        out_specs=(vmem,) * 4,
        compiler_params=params,
    )(*back, *[swap(piece, n, 1) for piece in back])


def shards(*arrays):
    n = lax.axis_size("seq")
    chips = max(n // 2, 1)
    rows, half = arrays[0].shape[0], arrays[3].shape[0]
    fits = (
        n % 8 == 0
        and n & (n - 1) == 0
        and arrays[0].shape[1] % (chips * LANES) == 0
        and arrays[3].shape[1] % (chips * LANES) == 0
        and HDV == LANES
        and LANES % HDA == 0
        and rows == 2 * half
        and half % 8 == 0
        and half & (half - 1) == 0
    )
    return shards_packed(*arrays) if fits else shards_general(*arrays)


def solution(mesh):
    placed = (
        P(("clip", "seq"), None),
        P(("clip", "seq"), None),
        P(("clip", "seq"), None),
        P(("clip", "seq"), None),
        P(("clip", "seq"), None),
        P(("clip", "seq"), None),
        P(("clip", "seq"), None),
        P(("clip", "seq"), None),
        P(("clip", "seq"), None),
        P(("clip", "seq"), None),
        P(("clip", "seq"), None),
        P(("clip", "seq"), None),
        P("clip"),
        P("clip"),
        P("clip"),
    )
    return jax.shard_map(
        shards,
        mesh=mesh,
        in_specs=placed,
        out_specs=(
            P(("clip", "seq"), None),
            P(("clip", "seq"), None),
            P(("clip", "seq"), None),
            P(("clip", "seq"), None),
        ),
        check_vma=False,
    )
```

```python
import functools
import math

import jax
import jax.numpy as jnp
from jax import lax
from jax.experimental import pallas as pl
from jax.experimental.pallas import tpu as pltpu
from jax.sharding import PartitionSpec as P

HV = 32
HDV = 128
HA = 32
HDA = 64


def block_size(total, limit):
    chosen = min(total, limit)
    while total % chosen:
        chosen -= 1
    return chosen


def split_heads(tokens, heads, depth, copies):
    rows = tokens.shape[0]
    shaped = tokens.reshape(copies, rows // copies, heads, depth).transpose(2, 0, 1, 3)
    return shaped.reshape(heads * copies, rows // copies, depth)


def spread_heads(tokens, heads, depth, copies):
    rows = tokens.shape[0]
    shaped = tokens.reshape(rows, heads, depth).transpose(1, 0, 2)
    shaped = jnp.broadcast_to(shaped[:, None], (heads, copies, rows, depth))
    return shaped.reshape(heads * copies, rows, depth)


def join_heads(owned, heads, depth, copies):
    part_rows = owned.shape[1]
    shaped = owned.reshape(heads, copies, part_rows, depth).transpose(1, 2, 0, 3)
    return shaped.reshape(copies * part_rows, heads * depth)


def owned_positions(rows, copies, devices, index):
    part_rows = rows // copies
    flat = jnp.arange(devices * part_rows, dtype=jnp.int32)
    return flat // part_rows * rows + index % copies * part_rows + flat % part_rows


def online_update(carry, scores, permit, value_tile, value_form):
    running, total, accum = carry
    scores = jnp.where(permit, scores, -1e30)
    newmax = jnp.maximum(running, jnp.max(scores, axis=2))
    weights = jnp.where(permit, jnp.exp(scores - newmax[:, :, None]), 0.0)
    factor = jnp.exp(running - newmax)
    total = total * factor + jnp.sum(weights, axis=2)
    mixed = jnp.einsum(
        value_form, weights.astype(jnp.bfloat16), value_tile, preferred_element_type=jnp.float32
    )
    accum = accum * factor[:, :, None] + mixed
    return (newmax, total, accum)


def fold_initial(rows, heads, depth):
    return (
        jnp.full((heads, rows), -1e30, jnp.float32),
        jnp.zeros((heads, rows), jnp.float32),
        jnp.zeros((heads, rows, depth), jnp.float32),
    )


def fold_piece(carry, local_query, key_rows, value_rows, permit, heads, depth):
    keyed = key_rows.reshape(key_rows.shape[0], heads, depth)
    valued = value_rows.reshape(value_rows.shape[0], heads, depth)
    scores = jnp.einsum("qhd,khd->hqk", local_query, keyed, preferred_element_type=jnp.float32) * (
        1.0 / math.sqrt(depth)
    )
    return online_update(carry, scores, permit[None], valued, "hqk,khd->hqd")


def fold_finish(carry, heads, depth):
    running, total, accum = carry
    result = (accum / total[:, :, None]).astype(jnp.bfloat16)
    return result.transpose(1, 0, 2).reshape(result.shape[1], heads * depth)


def attend_local(queries, keys, values, query_pos, key_pos, allowed):
    heads, q_count, depth = queries.shape
    k_count = keys.shape[1]
    q_block = block_size(q_count, 512)
    k_block = block_size(k_count, 2048)
    scale = 1.0 / math.sqrt(depth)
    q_tiles = queries.reshape(heads, q_count // q_block, q_block, depth).transpose(1, 0, 2, 3)
    k_tiles = keys.reshape(heads, k_count // k_block, k_block, depth).transpose(1, 0, 2, 3)
    v_tiles = values.reshape(heads, k_count // k_block, k_block, depth).transpose(1, 0, 2, 3)
    q_places = query_pos.reshape(q_count // q_block, q_block)
    k_places = key_pos.reshape(k_count // k_block, k_block)

    def one_tile(packed):
        q_tile, q_where = packed

        def absorb(carry, piece):
            k_tile, v_tile, k_where = piece
            scores = (
                jnp.einsum("hqd,hkd->hqk", q_tile, k_tile, preferred_element_type=jnp.float32)
                * scale
            )
            permit = allowed(q_where[:, None], k_where[None, :])[None]
            return (online_update(carry, scores, permit, v_tile, "hqk,hkd->hqd"), None)

        initial = fold_initial(q_block, heads, depth)
        final_state, unused = lax.scan(absorb, initial, (k_tiles, v_tiles, k_places))
        running, total, accum = final_state
        return (accum / total[:, :, None]).astype(jnp.bfloat16)

    tiles = lax.map(one_tile, (q_tiles, q_places))
    return tiles.transpose(1, 0, 2, 3).reshape(heads, q_count, depth)


def shards_general(
    video_query,
    video_keys,
    video_values,
    audio_query,
    audio_keys,
    audio_values,
    cross_video_query,
    cross_video_keys,
    cross_video_values,
    cross_audio_query,
    cross_audio_keys,
    cross_audio_values,
    video_length,
    audio_length,
    align_offset,
):
    devices = lax.axis_size("seq")
    index = lax.axis_index("seq")
    video_rows = video_query.shape[0]
    audio_rows = audio_query.shape[0]
    video_total = video_rows * devices
    audio_total = audio_rows * devices
    video_reach = video_total // 8
    audio_reach = 5 * audio_total // 8
    video_valid = video_length[0]
    audio_valid = audio_length[0]
    align_shift = align_offset[0]
    copies = max(devices // HV, 1)
    video_places = jnp.arange(video_total, dtype=jnp.int32)
    audio_places = jnp.arange(audio_total, dtype=jnp.int32)

    def video_open(q_where, k_where):
        return k_where < video_valid

    def toward_video(q_where, k_where):
        center = jnp.clip(q_where * audio_total // video_total + align_shift, 0, audio_valid - 1)
        return (k_where < audio_valid) & (jnp.abs(k_where - center) <= audio_reach)

    def toward_audio(q_where, k_where):
        center = jnp.clip((q_where - align_shift) * video_total // audio_total, 0, video_valid - 1)
        return (k_where < video_valid) & (jnp.abs(k_where - center) <= video_reach)

    video_owned = (
        lax.all_to_all(
            split_heads(video_query, HV, HDV, copies),
            "seq",
            split_axis=0,
            concat_axis=1,
            tiled=True,
        ),
        lax.all_to_all(
            spread_heads(video_keys, HV, HDV, copies),
            "seq",
            split_axis=0,
            concat_axis=1,
            tiled=True,
        ),
        lax.all_to_all(
            spread_heads(video_values, HV, HDV, copies),
            "seq",
            split_axis=0,
            concat_axis=1,
            tiled=True,
        ),
    )
    video_done = attend_local(
        video_owned[0],
        video_owned[1],
        video_owned[2],
        owned_positions(video_rows, copies, devices, index),
        video_places,
        video_open,
    )
    video_mixed = join_heads(
        lax.all_to_all(video_done, "seq", split_axis=1, concat_axis=0, tiled=True), HV, HDV, copies
    )
    audio_local = audio_query.reshape(audio_rows, HA, HDA)
    piece = (
        lax.all_gather(audio_keys, "seq", axis=0, tiled=True),
        lax.all_gather(audio_values, "seq", axis=0, tiled=True),
    )
    k_where = jnp.arange(piece[0].shape[0], dtype=jnp.int32)
    audio_k_where = k_where[None, :]
    permit = audio_k_where < audio_valid
    audio_state = fold_piece(
        fold_initial(audio_rows, HA, HDA), audio_local, piece[0], piece[1], permit, HA, HDA
    )
    audio_mixed = fold_finish(audio_state, HA, HDA)
    cross_owned = (
        lax.all_to_all(
            split_heads(cross_video_query, HA, HDA, copies),
            "seq",
            split_axis=0,
            concat_axis=1,
            tiled=True,
        ),
        lax.all_to_all(
            spread_heads(cross_audio_keys, HA, HDA, copies),
            "seq",
            split_axis=0,
            concat_axis=1,
            tiled=True,
        ),
        lax.all_to_all(
            spread_heads(cross_audio_values, HA, HDA, copies),
            "seq",
            split_axis=0,
            concat_axis=1,
            tiled=True,
        ),
    )
    cross_done = attend_local(
        cross_owned[0],
        cross_owned[1],
        cross_owned[2],
        owned_positions(video_rows, copies, devices, index),
        audio_places,
        toward_video,
    )
    video_cross = join_heads(
        lax.all_to_all(cross_done, "seq", split_axis=1, concat_axis=0, tiled=True), HA, HDA, copies
    )
    listen_owned = (
        lax.all_to_all(
            split_heads(cross_audio_query, HA, HDA, copies),
            "seq",
            split_axis=0,
            concat_axis=1,
            tiled=True,
        ),
        lax.all_to_all(
            spread_heads(cross_video_keys, HA, HDA, copies),
            "seq",
            split_axis=0,
            concat_axis=1,
            tiled=True,
        ),
        lax.all_to_all(
            spread_heads(cross_video_values, HA, HDA, copies),
            "seq",
            split_axis=0,
            concat_axis=1,
            tiled=True,
        ),
    )
    listen_done = attend_local(
        listen_owned[0],
        listen_owned[1],
        listen_owned[2],
        owned_positions(audio_rows, copies, devices, index),
        video_places,
        toward_audio,
    )
    audio_cross = join_heads(
        lax.all_to_all(listen_done, "seq", split_axis=1, concat_axis=0, tiled=True), HA, HDA, copies
    )
    return (video_mixed, audio_mixed, video_cross, audio_cross)


LANES = 128


def fetch(sources, held, arrived):
    copies = [
        pltpu.make_async_copy(source, slot, arrived.at[i])
        for i, (source, slot) in enumerate(zip(sources, held))
    ]
    for copy in copies:
        copy.start()
    return copies


def step_order(chips):
    far, near = list(range(chips - 1, chips // 2 - 1, -1)), list(range(1, chips // 2))
    return [0] + far[:1] + near[:1] + far[1:2] + near[1:] + far[2:]


def by_step(items):
    order = step_order(len(items))
    return [items[order.index(j)] for j in range(len(items))]


def in_order(items):
    return [items[j] for j in step_order(len(items))]


def pack_kernel(chips, *refs):
    sources, refs = refs[:12], refs[12:]
    packed, held, arrived = by_step(refs[:chips]), refs[chips : chips + 12], refs[chips + 12]
    copies = fetch(sources, held, arrived)
    chip = lax.axis_index("seq") // 2
    video, cross, audio = held[0:3], held[3:6], held[6:12]
    rows = video[0].shape[0]

    def group(ref, j, part):
        width = ref.shape[1] // chips
        at = pl.multiple_of((chip ^ j) * width + part * LANES, LANES)
        return ref[:, pl.ds(at, LANES)]

    at = 0
    for i, ref in enumerate(video + cross):
        copies[i].wait()
        for part in range(ref.shape[1] // chips // LANES):
            for j in range(chips):
                packed[j][at : at + rows, :] = group(ref, j, part)
            at += rows
    for i in range(0, 6, 2):
        copies[6 + i].wait()
        copies[7 + i].wait()
        for part in range(audio[i].shape[1] // chips // LANES):
            for j in range(chips):
                pair = jnp.concatenate(
                    [group(audio[i], j, part), group(audio[i + 1], j, part)], axis=0
                )
                packed[j][at : at + rows, :] = pair
            at += rows


def gather_kernel(video_len, audio_len, shift, *refs):
    slabs, bounds, merged = refs[:-2], refs[-2], refs[-1]
    row = lax.broadcasted_iota(jnp.int32, bounds.shape, 0)
    bounds[...] = jnp.where(row == 0, video_len[0], jnp.where(row == 1, audio_len[0], shift[0]))
    for i, slab in enumerate(slabs):
        merged[i] = slab[...]


def merge_kernel(*refs):
    for i, slab in enumerate(refs[:-1]):
        refs[-1][i] = slab[...]


def mix_all(units):
    scores = [
        lax.dot_general(query, key, (((1,), (1,)), ((), ())), preferred_element_type=jnp.float32)
        for query, key, value, depth, permit in units
    ]
    weights, totals = [], []
    for score, (query, key, value, depth, permit) in zip(scores, units):
        score = jnp.where(permit, score, -1e30)
        peak = jnp.max(score, axis=1, keepdims=True)
        weight = jnp.exp2((score - peak) * (math.log2(math.e) / math.sqrt(depth)))
        totals.append(jnp.sum(weight, axis=1, keepdims=True))
        weights.append(weight.astype(jnp.bfloat16))
    return [
        jnp.dot(weight, unit[2], preferred_element_type=jnp.float32) / total
        for weight, total, unit in zip(weights, totals, units)
    ]


def pair_units(query, key, value, permit):
    lane = lax.broadcasted_iota(jnp.int32, query.shape, 1) // HDA
    zero = jnp.zeros_like(query)
    return [
        (jnp.where(lane == h, query, zero), key, value, HDA, permit) for h in range(LANES // HDA)
    ]


def pair_join(mixed):
    lane = lax.broadcasted_iota(jnp.int32, mixed[0].shape, 1) // HDA
    result = mixed[0]
    for h in range(1, len(mixed)):
        result = jnp.where(lane == h, mixed[h], result)
    return result


def shares(chips):
    quarter = chips // 4
    far = list(zip(range(chips - 1, 3 * quarter - 1, -1), range(3 * quarter - 1, 2 * quarter - 1, -1)))
    near = list(zip(range(quarter - 1, -1, -1), range(2 * quarter - 1, quarter - 1, -1)))
    return far + near


def attend_kernel(chips, rows, parts, pairs, bounds, *refs):
    own, merged, done = by_step(refs[:chips]), refs[chips : 3 * chips // 2], refs[3 * chips // 2 :]
    other = by_step([ref.at[i] for ref in merged for i in range(ref.shape[0])])
    share = shares(chips)
    every = [ref for both in zip(own, other) for ref in both]
    half = rows // 2
    tv, ta = 2 * chips * rows, 2 * chips * half
    bits = (tv // ta).bit_length() - 1
    me = lax.axis_index("seq")
    core, home = me % 2, me // 2 * 2
    video_valid, audio_valid, offset = (bounds[i : i + 1, 0:1] for i in range(3))

    def slab(at):
        return jnp.concatenate([ref[at : at + rows, :] for ref in every], axis=0)

    def asked(at):
        pieces = []
        for zero, one in share:
            for c in range(2):
                low = (own, other)[c][zero][at : at + rows, :]
                high = (other, own)[c][one][at : at + rows, :]
                pieces.append(jnp.where(core == 0, low, high))
        return jnp.concatenate(pieces, axis=0)

    def split(wide):
        wide = wide.astype(jnp.float32).reshape(-1, rows, LANES)
        first = wide[:, :half, :].reshape(-1, LANES).astype(jnp.bfloat16)
        second = wide[:, half:, :].reshape(-1, LANES).astype(jnp.bfloat16)
        return first, second

    def places(q_step, k_step):
        shape = (chips * q_step, 2 * chips * k_step)
        k_at = lax.broadcasted_iota(jnp.int32, shape, 1) ^ (me * k_step)
        starts = []
        for zero, one in share:
            chip = home ^ jnp.where(core == 0, 2 * zero, 2 * one)
            starts.append(lax.broadcasted_iota(jnp.int32, (2 * q_step, 1), 0) + chip * q_step)
        return jnp.concatenate(starts, axis=0), k_at

    def put(at, mixed):
        count = done[0].shape[0] // 2
        for u in range(len(share)):
            for c in range(2):
                piece = mixed[(2 * u + c) * rows : (2 * u + c + 1) * rows]
                done[u][c * count + at : c * count + at + rows, :] = piece.astype(jnp.bfloat16)

    q_at, k_at = places(rows, rows)
    permit = k_at < video_valid
    units = [
        (
            asked(h * rows),
            slab((parts + h) * rows),
            slab((2 * parts + h) * rows),
            HDV,
            permit,
        )
        for h in range(parts)
    ]
    for h, mixed in enumerate(mix_all(units)):
        put(h * rows, mixed)

    cross = 3 * parts * rows
    audio = cross + 3 * pairs * rows
    q_at, k_at = places(rows, half)
    center = jnp.clip((q_at >> bits) + offset, 0, audio_valid - 1)
    toward_video = (k_at < audio_valid) & (jnp.abs(k_at - center) <= 5 * ta // 8)
    q_at, k_at = places(half, half)
    within_audio = k_at < audio_valid
    q_at, k_at = places(half, rows)
    center = jnp.clip((q_at - offset) << bits, 0, video_valid - 1)
    toward_audio = (k_at < video_valid) & (jnp.abs(k_at - center) <= tv // 8)
    units = []
    for p in range(pairs):
        at = cross + p * rows
        cross_query = asked(at)
        cross_keys = slab(at + pairs * rows)
        cross_values = slab(at + 2 * pairs * rows)
        at = audio + p * rows
        audio_query = split(asked(at))[0]
        audio_keys = split(slab(at))[1]
        at += pairs * rows
        audio_values = split(slab(at))[0]
        listen_query = split(asked(at))[1]
        at += pairs * rows
        sound_keys, sound_values = split(slab(at))
        units += pair_units(cross_query, sound_keys, sound_values, toward_video)
        units += pair_units(audio_query, audio_keys, audio_values, within_audio)
        units += pair_units(listen_query, cross_keys, cross_values, toward_audio)
    mixed = mix_all(units)
    heads = LANES // HDA
    for p in range(pairs):
        seen, heard, listened = (
            pair_join(mixed[(3 * p + i) * heads : (3 * p + i + 1) * heads]) for i in range(3)
        )
        out = (parts + p) * rows
        put(out, seen)
        both = jnp.concatenate(
            [heard.reshape(-1, half, LANES), listened.reshape(-1, half, LANES)], axis=1
        )
        put(out + pairs * rows, both.reshape(-1, LANES))


def hand_kernel(*refs):
    core = lax.axis_index("seq") % 2
    for u, ref in enumerate(refs[:-1]):
        count = refs[-1].shape[1]
        refs[-1][u] = ref[pl.ds(pl.multiple_of((1 - core) * count, 16), count), :]


def unpack_kernel(chips, *refs):
    share = shares(chips)
    back, handed = refs[: len(share)], refs[len(share)]
    video_mixed, audio_mixed, video_cross, audio_cross = refs[len(share) + 1 :]
    rows = video_mixed.shape[0]
    half = audio_mixed.shape[0]
    parts = video_mixed.shape[1] // chips // LANES
    pairs = audio_mixed.shape[1] // chips // LANES
    me = lax.axis_index("seq")
    core, home = me % 2, me // 2
    for u, (zero, one) in enumerate(share):
        for ref, base, chip in (
            (back[u], core * handed.shape[1], home ^ jnp.where(core == 0, zero, one)),
            (handed.at[u], 0, home ^ jnp.where(core == 0, one, zero)),
        ):
            base = pl.multiple_of(base, 16)

            def piece(at):
                return ref[pl.ds(base + at, rows), :]

            for h in range(parts):
                at = pl.multiple_of((chip * parts + h) * LANES, LANES)
                video_mixed[:, pl.ds(at, LANES)] = piece(h * rows)
            for p in range(pairs):
                at = pl.multiple_of((chip * pairs + p) * LANES, LANES)
                out = (parts + p) * rows
                video_cross[:, pl.ds(at, LANES)] = piece(out)
                both = piece(out + pairs * rows)
                audio_mixed[:, pl.ds(at, LANES)] = both[:half, :]
                audio_cross[:, pl.ds(at, LANES)] = both[half:, :]


def swap(piece, n, step):
    return lax.ppermute(piece, "seq", [(i, i ^ step) for i in range(n)])


def shards_packed(*arrays):
    (
        video_query, video_keys, video_values,
        audio_query, audio_keys, audio_values,
        cross_video_query, cross_video_keys, cross_video_values,
        cross_audio_query, cross_audio_keys, cross_audio_values,
        video_length, audio_length, align_offset,
    ) = arrays
    n = lax.axis_size("seq")
    chips = n // 2
    rows = video_query.shape[0]
    parts = video_query.shape[1] // chips // LANES
    pairs = audio_query.shape[1] // chips // LANES
    vmem = pl.BlockSpec(memory_space=pltpu.VMEM)
    hbm = pl.BlockSpec(memory_space=pltpu.HBM)
    smem = pl.BlockSpec(memory_space=pltpu.SMEM)
    params = pltpu.CompilerParams(vmem_limit_bytes=32 * 1024 * 1024)

    def buffer(*shape):
        return jax.ShapeDtypeStruct(shape, jnp.bfloat16)

    sources = (
        video_query, video_keys, video_values,
        cross_video_query, cross_video_keys, cross_video_values,
        audio_query, audio_keys, audio_values,
        cross_audio_query, cross_audio_keys, cross_audio_values,
    )
    packed = pl.pallas_call(
        functools.partial(pack_kernel, chips),
        out_shape=[pltpu.VMEM(((3 * parts + 6 * pairs) * rows, LANES), jnp.bfloat16)] * chips,
        in_specs=[hbm] * 12,
        out_specs=[vmem] * chips,
        scratch_shapes=[pltpu.VMEM(source.shape, source.dtype) for source in sources]
        + [pltpu.SemaphoreType.DMA((12,))],
        compiler_params=params,
    )(*[pltpu.with_memory_space_constraint(source, pltpu.HBM) for source in sources])
    packed = by_step(packed)
    moved = [swap(packed[j], n, 2 * j) for j in range(1, chips)]
    own = in_order(packed[:1] + moved)
    joint = pltpu.VMEM((2,) + packed[0].shape, jnp.bfloat16)
    bounds, first = pl.pallas_call(
        gather_kernel,
        out_shape=(pltpu.VMEM((8, LANES), jnp.int32), joint),
        in_specs=[smem] * 3 + [vmem] * 2,
        out_specs=(vmem, vmem),
        compiler_params=params,
    )(video_length, audio_length, align_offset, *own[:2])
    merged = [first] + [
        pl.pallas_call(
            merge_kernel,
            out_shape=joint,
            in_specs=[vmem] * 2,
            out_specs=vmem,
            compiler_params=params,
        )(*own[i : i + 2])
        for i in range(2, chips, 2)
    ]
    share = shares(chips)
    done = pl.pallas_call(
        functools.partial(attend_kernel, chips, rows, parts, pairs),
        out_shape=[buffer(2 * (parts + 2 * pairs) * rows, LANES)] * len(share),
        in_specs=[vmem] * (1 + chips + len(merged)),
        out_specs=[vmem] * len(share),
        compiler_params=params,
    )(bounds, *own, *[swap(piece, n, 1) for piece in merged])
    back = [
        lax.ppermute(piece, "seq", [(i, i ^ 2 * pair[i % 2]) for i in range(n)])
        for piece, pair in zip(done, share)
    ]
    handed = pl.pallas_call(
        hand_kernel,
        out_shape=pltpu.VMEM((len(share), done[0].shape[0] // 2, LANES), jnp.bfloat16),
        in_specs=[vmem] * len(share),
        out_specs=vmem,
        compiler_params=params,
    )(*back)
    return pl.pallas_call(
        functools.partial(unpack_kernel, chips),
        out_shape=(
            buffer(*video_query.shape),
            buffer(*audio_query.shape),
            buffer(*cross_video_query.shape),
            buffer(*cross_audio_query.shape),
        ),
        in_specs=[vmem] * (len(share) + 1),
        out_specs=(vmem,) * 4,
        compiler_params=params,
    )(*back, swap(handed, n, 1))


def shards(*arrays):
    n = lax.axis_size("seq")
    chips = max(n // 2, 1)
    rows, half = arrays[0].shape[0], arrays[3].shape[0]
    fits = (
        n % 8 == 0
        and n & (n - 1) == 0
        and arrays[0].shape[1] % (chips * LANES) == 0
        and arrays[3].shape[1] % (chips * LANES) == 0
        and HDV == LANES
        and LANES % HDA == 0
        and rows == 2 * half
        and half % 8 == 0
        and half & (half - 1) == 0
    )
    return shards_packed(*arrays) if fits else shards_general(*arrays)


def solution(mesh):
    placed = (
        P(("clip", "seq"), None),
        P(("clip", "seq"), None),
        P(("clip", "seq"), None),
        P(("clip", "seq"), None),
        P(("clip", "seq"), None),
        P(("clip", "seq"), None),
        P(("clip", "seq"), None),
        P(("clip", "seq"), None),
        P(("clip", "seq"), None),
        P(("clip", "seq"), None),
        P(("clip", "seq"), None),
        P(("clip", "seq"), None),
        P("clip"),
        P("clip"),
        P("clip"),
    )
    return jax.shard_map(
        shards,
        mesh=mesh,
        in_specs=placed,
        out_specs=(
            P(("clip", "seq"), None),
            P(("clip", "seq"), None),
            P(("clip", "seq"), None),
            P(("clip", "seq"), None),
        ),
        check_vma=False,
    )
```

```python
import functools
import math

import jax
import jax.numpy as jnp
from jax import lax
from jax.experimental import pallas as pl
from jax.experimental.pallas import tpu as pltpu
from jax.sharding import PartitionSpec as P

HV = 32
HDV = 128
HA = 32
HDA = 64


def block_size(total, limit):
    chosen = min(total, limit)
    while total % chosen:
        chosen -= 1
    return chosen


def split_heads(tokens, heads, depth, copies):
    rows = tokens.shape[0]
    shaped = tokens.reshape(copies, rows // copies, heads, depth).transpose(2, 0, 1, 3)
    return shaped.reshape(heads * copies, rows // copies, depth)


def spread_heads(tokens, heads, depth, copies):
    rows = tokens.shape[0]
    shaped = tokens.reshape(rows, heads, depth).transpose(1, 0, 2)
    shaped = jnp.broadcast_to(shaped[:, None], (heads, copies, rows, depth))
    return shaped.reshape(heads * copies, rows, depth)


def join_heads(owned, heads, depth, copies):
    part_rows = owned.shape[1]
    shaped = owned.reshape(heads, copies, part_rows, depth).transpose(1, 2, 0, 3)
    return shaped.reshape(copies * part_rows, heads * depth)


def owned_positions(rows, copies, devices, index):
    part_rows = rows // copies
    flat = jnp.arange(devices * part_rows, dtype=jnp.int32)
    return flat // part_rows * rows + index % copies * part_rows + flat % part_rows


def online_update(carry, scores, permit, value_tile, value_form):
    running, total, accum = carry
    scores = jnp.where(permit, scores, -1e30)
    newmax = jnp.maximum(running, jnp.max(scores, axis=2))
    weights = jnp.where(permit, jnp.exp(scores - newmax[:, :, None]), 0.0)
    factor = jnp.exp(running - newmax)
    total = total * factor + jnp.sum(weights, axis=2)
    mixed = jnp.einsum(
        value_form, weights.astype(jnp.bfloat16), value_tile, preferred_element_type=jnp.float32
    )
    accum = accum * factor[:, :, None] + mixed
    return (newmax, total, accum)


def fold_initial(rows, heads, depth):
    return (
        jnp.full((heads, rows), -1e30, jnp.float32),
        jnp.zeros((heads, rows), jnp.float32),
        jnp.zeros((heads, rows, depth), jnp.float32),
    )


def fold_piece(carry, local_query, key_rows, value_rows, permit, heads, depth):
    keyed = key_rows.reshape(key_rows.shape[0], heads, depth)
    valued = value_rows.reshape(value_rows.shape[0], heads, depth)
    scores = jnp.einsum("qhd,khd->hqk", local_query, keyed, preferred_element_type=jnp.float32) * (
        1.0 / math.sqrt(depth)
    )
    return online_update(carry, scores, permit[None], valued, "hqk,khd->hqd")


def fold_finish(carry, heads, depth):
    running, total, accum = carry
    result = (accum / total[:, :, None]).astype(jnp.bfloat16)
    return result.transpose(1, 0, 2).reshape(result.shape[1], heads * depth)


def attend_local(queries, keys, values, query_pos, key_pos, allowed):
    heads, q_count, depth = queries.shape
    k_count = keys.shape[1]
    q_block = block_size(q_count, 512)
    k_block = block_size(k_count, 2048)
    scale = 1.0 / math.sqrt(depth)
    q_tiles = queries.reshape(heads, q_count // q_block, q_block, depth).transpose(1, 0, 2, 3)
    k_tiles = keys.reshape(heads, k_count // k_block, k_block, depth).transpose(1, 0, 2, 3)
    v_tiles = values.reshape(heads, k_count // k_block, k_block, depth).transpose(1, 0, 2, 3)
    q_places = query_pos.reshape(q_count // q_block, q_block)
    k_places = key_pos.reshape(k_count // k_block, k_block)

    def one_tile(packed):
        q_tile, q_where = packed

        def absorb(carry, piece):
            k_tile, v_tile, k_where = piece
            scores = (
                jnp.einsum("hqd,hkd->hqk", q_tile, k_tile, preferred_element_type=jnp.float32)
                * scale
            )
            permit = allowed(q_where[:, None], k_where[None, :])[None]
            return (online_update(carry, scores, permit, v_tile, "hqk,hkd->hqd"), None)

        initial = fold_initial(q_block, heads, depth)
        final_state, unused = lax.scan(absorb, initial, (k_tiles, v_tiles, k_places))
        running, total, accum = final_state
        return (accum / total[:, :, None]).astype(jnp.bfloat16)

    tiles = lax.map(one_tile, (q_tiles, q_places))
    return tiles.transpose(1, 0, 2, 3).reshape(heads, q_count, depth)


def shards_general(
    video_query,
    video_keys,
    video_values,
    audio_query,
    audio_keys,
    audio_values,
    cross_video_query,
    cross_video_keys,
    cross_video_values,
    cross_audio_query,
    cross_audio_keys,
    cross_audio_values,
    video_length,
    audio_length,
    align_offset,
):
    devices = lax.axis_size("seq")
    index = lax.axis_index("seq")
    video_rows = video_query.shape[0]
    audio_rows = audio_query.shape[0]
    video_total = video_rows * devices
    audio_total = audio_rows * devices
    video_reach = video_total // 8
    audio_reach = 5 * audio_total // 8
    video_valid = video_length[0]
    audio_valid = audio_length[0]
    align_shift = align_offset[0]
    copies = max(devices // HV, 1)
    video_places = jnp.arange(video_total, dtype=jnp.int32)
    audio_places = jnp.arange(audio_total, dtype=jnp.int32)

    def video_open(q_where, k_where):
        return k_where < video_valid

    def toward_video(q_where, k_where):
        center = jnp.clip(q_where * audio_total // video_total + align_shift, 0, audio_valid - 1)
        return (k_where < audio_valid) & (jnp.abs(k_where - center) <= audio_reach)

    def toward_audio(q_where, k_where):
        center = jnp.clip((q_where - align_shift) * video_total // audio_total, 0, video_valid - 1)
        return (k_where < video_valid) & (jnp.abs(k_where - center) <= video_reach)

    video_owned = (
        lax.all_to_all(
            split_heads(video_query, HV, HDV, copies),
            "seq",
            split_axis=0,
            concat_axis=1,
            tiled=True,
        ),
        lax.all_to_all(
            spread_heads(video_keys, HV, HDV, copies),
            "seq",
            split_axis=0,
            concat_axis=1,
            tiled=True,
        ),
        lax.all_to_all(
            spread_heads(video_values, HV, HDV, copies),
            "seq",
            split_axis=0,
            concat_axis=1,
            tiled=True,
        ),
    )
    video_done = attend_local(
        video_owned[0],
        video_owned[1],
        video_owned[2],
        owned_positions(video_rows, copies, devices, index),
        video_places,
        video_open,
    )
    video_mixed = join_heads(
        lax.all_to_all(video_done, "seq", split_axis=1, concat_axis=0, tiled=True), HV, HDV, copies
    )
    audio_local = audio_query.reshape(audio_rows, HA, HDA)
    piece = (
        lax.all_gather(audio_keys, "seq", axis=0, tiled=True),
        lax.all_gather(audio_values, "seq", axis=0, tiled=True),
    )
    k_where = jnp.arange(piece[0].shape[0], dtype=jnp.int32)
    audio_k_where = k_where[None, :]
    permit = audio_k_where < audio_valid
    audio_state = fold_piece(
        fold_initial(audio_rows, HA, HDA), audio_local, piece[0], piece[1], permit, HA, HDA
    )
    audio_mixed = fold_finish(audio_state, HA, HDA)
    cross_owned = (
        lax.all_to_all(
            split_heads(cross_video_query, HA, HDA, copies),
            "seq",
            split_axis=0,
            concat_axis=1,
            tiled=True,
        ),
        lax.all_to_all(
            spread_heads(cross_audio_keys, HA, HDA, copies),
            "seq",
            split_axis=0,
            concat_axis=1,
            tiled=True,
        ),
        lax.all_to_all(
            spread_heads(cross_audio_values, HA, HDA, copies),
            "seq",
            split_axis=0,
            concat_axis=1,
            tiled=True,
        ),
    )
    cross_done = attend_local(
        cross_owned[0],
        cross_owned[1],
        cross_owned[2],
        owned_positions(video_rows, copies, devices, index),
        audio_places,
        toward_video,
    )
    video_cross = join_heads(
        lax.all_to_all(cross_done, "seq", split_axis=1, concat_axis=0, tiled=True), HA, HDA, copies
    )
    listen_owned = (
        lax.all_to_all(
            split_heads(cross_audio_query, HA, HDA, copies),
            "seq",
            split_axis=0,
            concat_axis=1,
            tiled=True,
        ),
        lax.all_to_all(
            spread_heads(cross_video_keys, HA, HDA, copies),
            "seq",
            split_axis=0,
            concat_axis=1,
            tiled=True,
        ),
        lax.all_to_all(
            spread_heads(cross_video_values, HA, HDA, copies),
            "seq",
            split_axis=0,
            concat_axis=1,
            tiled=True,
        ),
    )
    listen_done = attend_local(
        listen_owned[0],
        listen_owned[1],
        listen_owned[2],
        owned_positions(audio_rows, copies, devices, index),
        video_places,
        toward_audio,
    )
    audio_cross = join_heads(
        lax.all_to_all(listen_done, "seq", split_axis=1, concat_axis=0, tiled=True), HA, HDA, copies
    )
    return (video_mixed, audio_mixed, video_cross, audio_cross)


LANES = 128


def fetch(sources, held, arrived):
    copies = [
        pltpu.make_async_copy(source, slot, arrived.at[i])
        for i, (source, slot) in enumerate(zip(sources, held))
    ]
    for copy in copies:
        copy.start()
    return copies


def step_order(chips):
    far, near = list(range(chips - 1, chips // 2 - 1, -1)), list(range(1, chips // 2))
    return [0] + far[:1] + near[:1] + far[1:2] + near[1:] + far[2:]


def by_step(items):
    order = step_order(len(items))
    return [items[order.index(j)] for j in range(len(items))]


def in_order(items):
    return [items[j] for j in step_order(len(items))]


def pack_kernel(chips, steps, *refs):
    sources, packed, held, arrived = refs[:12], refs[13:-13], refs[-13:-1], refs[-1]
    copies = fetch(sources, held, arrived)
    chip = lax.axis_index("seq") // 2
    video, cross, audio = held[0:3], held[3:6], held[6:12]
    rows = video[0].shape[0]

    def group(ref, j, part):
        width = ref.shape[1] // chips
        at = pl.multiple_of((chip ^ j) * width + part * LANES, LANES)
        return ref[:, pl.ds(at, LANES)]

    at = 0
    for i, ref in enumerate(video + cross):
        copies[i].wait()
        for part in range(ref.shape[1] // chips // LANES):
            for slab, j in zip(packed, steps):
                slab[at : at + rows, :] = group(ref, j, part)
            at += rows
    for i in range(0, 6, 2):
        copies[6 + i].wait()
        copies[7 + i].wait()
        for part in range(audio[i].shape[1] // chips // LANES):
            for slab, j in zip(packed, steps):
                pair = jnp.concatenate(
                    [group(audio[i], j, part), group(audio[i + 1], j, part)], axis=0
                )
                slab[at : at + rows, :] = pair
            at += rows


def gather_kernel(video_len, audio_len, shift, *refs):
    slabs, bounds, merged = refs[:-2], refs[-2], refs[-1]
    row = lax.broadcasted_iota(jnp.int32, bounds.shape, 0)
    bounds[...] = jnp.where(row == 0, video_len[0], jnp.where(row == 1, audio_len[0], shift[0]))
    for i, slab in enumerate(slabs):
        merged[i] = slab[...]


def merge_kernel(*refs):
    for i, slab in enumerate(refs[:-1]):
        refs[-1][i] = slab[...]


def mix_all(units):
    scores = [
        lax.dot_general(query, key, (((1,), (1,)), ((), ())), preferred_element_type=jnp.float32)
        for query, key, value, depth, permit in units
    ]
    weights, totals = [], []
    for score, (query, key, value, depth, permit) in zip(scores, units):
        score = jnp.where(permit, score, -1e30)
        peak = jnp.max(score, axis=1, keepdims=True)
        weight = jnp.exp2((score - peak) * (math.log2(math.e) / math.sqrt(depth)))
        totals.append(jnp.sum(weight, axis=1, keepdims=True))
        weights.append(weight.astype(jnp.bfloat16))
    return [
        jnp.dot(weight, unit[2], preferred_element_type=jnp.float32) / total
        for weight, total, unit in zip(weights, totals, units)
    ]


def pair_units(query, key, value, permit):
    lane = lax.broadcasted_iota(jnp.int32, query.shape, 1) // HDA
    zero = jnp.zeros_like(query)
    return [
        (jnp.where(lane == h, query, zero), key, value, HDA, permit) for h in range(LANES // HDA)
    ]


def pair_join(mixed):
    lane = lax.broadcasted_iota(jnp.int32, mixed[0].shape, 1) // HDA
    result = mixed[0]
    for h in range(1, len(mixed)):
        result = jnp.where(lane == h, mixed[h], result)
    return result


def shares(chips):
    quarter = chips // 4
    far = list(zip(range(chips - 1, 3 * quarter - 1, -1), range(3 * quarter - 1, 2 * quarter - 1, -1)))
    near = list(zip(range(quarter - 1, -1, -1), range(2 * quarter - 1, quarter - 1, -1)))
    return far + near


def attend_kernel(chips, rows, parts, pairs, bounds, *refs):
    own, merged, done = by_step(refs[:chips]), refs[chips : 3 * chips // 2], refs[3 * chips // 2 :]
    other = by_step([ref.at[i] for ref in merged for i in range(ref.shape[0])])
    share = shares(chips)
    every = [ref for both in zip(own, other) for ref in both]
    half = rows // 2
    tv, ta = 2 * chips * rows, 2 * chips * half
    bits = (tv // ta).bit_length() - 1
    me = lax.axis_index("seq")
    core, home = me % 2, me // 2 * 2
    video_valid, audio_valid, offset = (bounds[i : i + 1, 0:1] for i in range(3))

    def slab(at):
        return jnp.concatenate([ref[at : at + rows, :] for ref in every], axis=0)

    def asked(at):
        pieces = []
        for zero, one in share:
            for c in range(2):
                low = (own, other)[c][zero][at : at + rows, :]
                high = (other, own)[c][one][at : at + rows, :]
                pieces.append(jnp.where(core == 0, low, high))
        return jnp.concatenate(pieces, axis=0)

    def split(wide):
        wide = wide.astype(jnp.float32).reshape(-1, rows, LANES)
        first = wide[:, :half, :].reshape(-1, LANES).astype(jnp.bfloat16)
        second = wide[:, half:, :].reshape(-1, LANES).astype(jnp.bfloat16)
        return first, second

    def places(q_step, k_step):
        shape = (chips * q_step, 2 * chips * k_step)
        k_at = lax.broadcasted_iota(jnp.int32, shape, 1) ^ (me * k_step)
        starts = []
        for zero, one in share:
            chip = home ^ jnp.where(core == 0, 2 * zero, 2 * one)
            starts.append(lax.broadcasted_iota(jnp.int32, (2 * q_step, 1), 0) + chip * q_step)
        return jnp.concatenate(starts, axis=0), k_at

    def put(at, mixed):
        count = done[0].shape[0] // 2
        for u in range(len(share)):
            for c in range(2):
                piece = mixed[(2 * u + c) * rows : (2 * u + c + 1) * rows]
                done[u][c * count + at : c * count + at + rows, :] = piece.astype(jnp.bfloat16)

    q_at, k_at = places(rows, rows)
    permit = k_at < video_valid
    units = [
        (
            asked(h * rows),
            slab((parts + h) * rows),
            slab((2 * parts + h) * rows),
            HDV,
            permit,
        )
        for h in range(parts)
    ]
    for h, mixed in enumerate(mix_all(units)):
        put(h * rows, mixed)

    cross = 3 * parts * rows
    audio = cross + 3 * pairs * rows
    q_at, k_at = places(rows, half)
    center = jnp.clip((q_at >> bits) + offset, 0, audio_valid - 1)
    toward_video = (k_at < audio_valid) & (jnp.abs(k_at - center) <= 5 * ta // 8)
    q_at, k_at = places(half, half)
    within_audio = k_at < audio_valid
    q_at, k_at = places(half, rows)
    center = jnp.clip((q_at - offset) << bits, 0, video_valid - 1)
    toward_audio = (k_at < video_valid) & (jnp.abs(k_at - center) <= tv // 8)
    units = []
    for p in range(pairs):
        at = cross + p * rows
        cross_query = asked(at)
        cross_keys = slab(at + pairs * rows)
        cross_values = slab(at + 2 * pairs * rows)
        at = audio + p * rows
        audio_query = split(asked(at))[0]
        audio_keys = split(slab(at))[1]
        at += pairs * rows
        audio_values = split(slab(at))[0]
        listen_query = split(asked(at))[1]
        at += pairs * rows
        sound_keys, sound_values = split(slab(at))
        units += pair_units(cross_query, sound_keys, sound_values, toward_video)
        units += pair_units(audio_query, audio_keys, audio_values, within_audio)
        units += pair_units(listen_query, cross_keys, cross_values, toward_audio)
    mixed = mix_all(units)
    heads = LANES // HDA
    for p in range(pairs):
        seen, heard, listened = (
            pair_join(mixed[(3 * p + i) * heads : (3 * p + i + 1) * heads]) for i in range(3)
        )
        out = (parts + p) * rows
        put(out, seen)
        both = jnp.concatenate(
            [heard.reshape(-1, half, LANES), listened.reshape(-1, half, LANES)], axis=1
        )
        put(out + pairs * rows, both.reshape(-1, LANES))


def hand_kernel(*refs):
    core = lax.axis_index("seq") % 2
    for u, ref in enumerate(refs[:-1]):
        count = refs[-1].shape[1]
        refs[-1][u] = ref[pl.ds(pl.multiple_of((1 - core) * count, 16), count), :]


def unpack_kernel(chips, *refs):
    share = shares(chips)
    back, handed = refs[: len(share)], refs[len(share)]
    video_mixed, audio_mixed, video_cross, audio_cross = refs[len(share) + 1 :]
    rows = video_mixed.shape[0]
    half = audio_mixed.shape[0]
    parts = video_mixed.shape[1] // chips // LANES
    pairs = audio_mixed.shape[1] // chips // LANES
    me = lax.axis_index("seq")
    core, home = me % 2, me // 2
    for u, (zero, one) in enumerate(share):
        for ref, base, chip in (
            (back[u], core * handed.shape[1], home ^ jnp.where(core == 0, zero, one)),
            (handed.at[u], 0, home ^ jnp.where(core == 0, one, zero)),
        ):
            base = pl.multiple_of(base, 16)

            def piece(at):
                return ref[pl.ds(base + at, rows), :]

            for h in range(parts):
                at = pl.multiple_of((chip * parts + h) * LANES, LANES)
                video_mixed[:, pl.ds(at, LANES)] = piece(h * rows)
            for p in range(pairs):
                at = pl.multiple_of((chip * pairs + p) * LANES, LANES)
                out = (parts + p) * rows
                video_cross[:, pl.ds(at, LANES)] = piece(out)
                both = piece(out + pairs * rows)
                audio_mixed[:, pl.ds(at, LANES)] = both[:half, :]
                audio_cross[:, pl.ds(at, LANES)] = both[half:, :]


def swap(piece, n, step):
    return lax.ppermute(piece, "seq", [(i, i ^ step) for i in range(n)])


def shards_packed(*arrays):
    (
        video_query, video_keys, video_values,
        audio_query, audio_keys, audio_values,
        cross_video_query, cross_video_keys, cross_video_values,
        cross_audio_query, cross_audio_keys, cross_audio_values,
        video_length, audio_length, align_offset,
    ) = arrays
    n = lax.axis_size("seq")
    chips = n // 2
    rows = video_query.shape[0]
    parts = video_query.shape[1] // chips // LANES
    pairs = audio_query.shape[1] // chips // LANES
    vmem = pl.BlockSpec(memory_space=pltpu.VMEM)
    hbm = pl.BlockSpec(memory_space=pltpu.HBM)
    smem = pl.BlockSpec(memory_space=pltpu.SMEM)
    params = pltpu.CompilerParams(vmem_limit_bytes=32 * 1024 * 1024)

    def buffer(*shape):
        return jax.ShapeDtypeStruct(shape, jnp.bfloat16)

    sources = (
        video_query, video_keys, video_values,
        cross_video_query, cross_video_keys, cross_video_values,
        audio_query, audio_keys, audio_values,
        cross_audio_query, cross_audio_keys, cross_audio_values,
    )
    sources = [pltpu.with_memory_space_constraint(source, pltpu.HBM) for source in sources]
    slab = pltpu.VMEM(((3 * parts + 6 * pairs) * rows, LANES), jnp.bfloat16)

    def pack(steps, after):
        return pl.pallas_call(
            functools.partial(pack_kernel, chips, steps),
            out_shape=[slab] * len(steps),
            in_specs=[hbm] * 12 + [pl.BlockSpec(memory_space=pl.ANY)],
            out_specs=[vmem] * len(steps),
            scratch_shapes=[pltpu.VMEM(source.shape, source.dtype) for source in sources]
            + [pltpu.SemaphoreType.DMA((12,))],
            compiler_params=params,
        )(*sources, after)

    order = step_order(chips)
    (ahead,) = pack(order[1:2], sources[0])
    rest = pack(order[:1] + order[2:], ahead)
    packed = by_step([rest[0], ahead, *rest[1:]])
    moved = [swap(packed[j], n, 2 * j) for j in range(1, chips)]
    own = in_order(packed[:1] + moved)
    joint = pltpu.VMEM((2,) + packed[0].shape, jnp.bfloat16)
    bounds, first = pl.pallas_call(
        gather_kernel,
        out_shape=(pltpu.VMEM((8, LANES), jnp.int32), joint),
        in_specs=[smem] * 3 + [vmem] * 2,
        out_specs=(vmem, vmem),
        compiler_params=params,
    )(video_length, audio_length, align_offset, *own[:2])
    merged = [first] + [
        pl.pallas_call(
            merge_kernel,
            out_shape=joint,
            in_specs=[vmem] * 2,
            out_specs=vmem,
            compiler_params=params,
        )(*own[i : i + 2])
        for i in range(2, chips, 2)
    ]
    share = shares(chips)
    done = pl.pallas_call(
        functools.partial(attend_kernel, chips, rows, parts, pairs),
        out_shape=[buffer(2 * (parts + 2 * pairs) * rows, LANES)] * len(share),
        in_specs=[vmem] * (1 + chips + len(merged)),
        out_specs=[vmem] * len(share),
        compiler_params=params,
    )(bounds, *own, *[swap(piece, n, 1) for piece in merged])
    back = [
        lax.ppermute(piece, "seq", [(i, i ^ 2 * pair[i % 2]) for i in range(n)])
        for piece, pair in zip(done, share)
    ]
    handed = pl.pallas_call(
        hand_kernel,
        out_shape=pltpu.VMEM((len(share), done[0].shape[0] // 2, LANES), jnp.bfloat16),
        in_specs=[vmem] * len(share),
        out_specs=vmem,
        compiler_params=params,
    )(*back)
    return pl.pallas_call(
        functools.partial(unpack_kernel, chips),
        out_shape=(
            buffer(*video_query.shape),
            buffer(*audio_query.shape),
            buffer(*cross_video_query.shape),
            buffer(*cross_audio_query.shape),
        ),
        in_specs=[vmem] * (len(share) + 1),
        out_specs=(vmem,) * 4,
        compiler_params=params,
    )(*back, swap(handed, n, 1))


def shards(*arrays):
    n = lax.axis_size("seq")
    chips = max(n // 2, 1)
    rows, half = arrays[0].shape[0], arrays[3].shape[0]
    fits = (
        n % 8 == 0
        and n & (n - 1) == 0
        and arrays[0].shape[1] % (chips * LANES) == 0
        and arrays[3].shape[1] % (chips * LANES) == 0
        and HDV == LANES
        and LANES % HDA == 0
        and rows == 2 * half
        and half % 8 == 0
        and half & (half - 1) == 0
    )
    return shards_packed(*arrays) if fits else shards_general(*arrays)


def solution(mesh):
    placed = (
        P(("clip", "seq"), None),
        P(("clip", "seq"), None),
        P(("clip", "seq"), None),
        P(("clip", "seq"), None),
        P(("clip", "seq"), None),
        P(("clip", "seq"), None),
        P(("clip", "seq"), None),
        P(("clip", "seq"), None),
        P(("clip", "seq"), None),
        P(("clip", "seq"), None),
        P(("clip", "seq"), None),
        P(("clip", "seq"), None),
        P("clip"),
        P("clip"),
        P("clip"),
    )
    return jax.shard_map(
        shards,
        mesh=mesh,
        in_specs=placed,
        out_specs=(
            P(("clip", "seq"), None),
            P(("clip", "seq"), None),
            P(("clip", "seq"), None),
            P(("clip", "seq"), None),
        ),
        check_vma=False,
    )
```

```python
import functools
import math

import jax
import jax.numpy as jnp
from jax import lax
from jax.experimental import pallas as pl
from jax.experimental.pallas import tpu as pltpu
from jax.sharding import PartitionSpec as P

HV = 32
HDV = 128
HA = 32
HDA = 64


def block_size(total, limit):
    chosen = min(total, limit)
    while total % chosen:
        chosen -= 1
    return chosen


def split_heads(tokens, heads, depth, copies):
    rows = tokens.shape[0]
    shaped = tokens.reshape(copies, rows // copies, heads, depth).transpose(2, 0, 1, 3)
    return shaped.reshape(heads * copies, rows // copies, depth)


def spread_heads(tokens, heads, depth, copies):
    rows = tokens.shape[0]
    shaped = tokens.reshape(rows, heads, depth).transpose(1, 0, 2)
    shaped = jnp.broadcast_to(shaped[:, None], (heads, copies, rows, depth))
    return shaped.reshape(heads * copies, rows, depth)


def join_heads(owned, heads, depth, copies):
    part_rows = owned.shape[1]
    shaped = owned.reshape(heads, copies, part_rows, depth).transpose(1, 2, 0, 3)
    return shaped.reshape(copies * part_rows, heads * depth)


def owned_positions(rows, copies, devices, index):
    part_rows = rows // copies
    flat = jnp.arange(devices * part_rows, dtype=jnp.int32)
    return flat // part_rows * rows + index % copies * part_rows + flat % part_rows


def online_update(carry, scores, permit, value_tile, value_form):
    running, total, accum = carry
    scores = jnp.where(permit, scores, -1e30)
    newmax = jnp.maximum(running, jnp.max(scores, axis=2))
    weights = jnp.where(permit, jnp.exp(scores - newmax[:, :, None]), 0.0)
    factor = jnp.exp(running - newmax)
    total = total * factor + jnp.sum(weights, axis=2)
    mixed = jnp.einsum(
        value_form, weights.astype(jnp.bfloat16), value_tile, preferred_element_type=jnp.float32
    )
    accum = accum * factor[:, :, None] + mixed
    return (newmax, total, accum)


def fold_initial(rows, heads, depth):
    return (
        jnp.full((heads, rows), -1e30, jnp.float32),
        jnp.zeros((heads, rows), jnp.float32),
        jnp.zeros((heads, rows, depth), jnp.float32),
    )


def fold_piece(carry, local_query, key_rows, value_rows, permit, heads, depth):
    keyed = key_rows.reshape(key_rows.shape[0], heads, depth)
    valued = value_rows.reshape(value_rows.shape[0], heads, depth)
    scores = jnp.einsum("qhd,khd->hqk", local_query, keyed, preferred_element_type=jnp.float32) * (
        1.0 / math.sqrt(depth)
    )
    return online_update(carry, scores, permit[None], valued, "hqk,khd->hqd")


def fold_finish(carry, heads, depth):
    running, total, accum = carry
    result = (accum / total[:, :, None]).astype(jnp.bfloat16)
    return result.transpose(1, 0, 2).reshape(result.shape[1], heads * depth)


def attend_local(queries, keys, values, query_pos, key_pos, allowed):
    heads, q_count, depth = queries.shape
    k_count = keys.shape[1]
    q_block = block_size(q_count, 512)
    k_block = block_size(k_count, 2048)
    scale = 1.0 / math.sqrt(depth)
    q_tiles = queries.reshape(heads, q_count // q_block, q_block, depth).transpose(1, 0, 2, 3)
    k_tiles = keys.reshape(heads, k_count // k_block, k_block, depth).transpose(1, 0, 2, 3)
    v_tiles = values.reshape(heads, k_count // k_block, k_block, depth).transpose(1, 0, 2, 3)
    q_places = query_pos.reshape(q_count // q_block, q_block)
    k_places = key_pos.reshape(k_count // k_block, k_block)

    def one_tile(packed):
        q_tile, q_where = packed

        def absorb(carry, piece):
            k_tile, v_tile, k_where = piece
            scores = (
                jnp.einsum("hqd,hkd->hqk", q_tile, k_tile, preferred_element_type=jnp.float32)
                * scale
            )
            permit = allowed(q_where[:, None], k_where[None, :])[None]
            return (online_update(carry, scores, permit, v_tile, "hqk,hkd->hqd"), None)

        initial = fold_initial(q_block, heads, depth)
        final_state, unused = lax.scan(absorb, initial, (k_tiles, v_tiles, k_places))
        running, total, accum = final_state
        return (accum / total[:, :, None]).astype(jnp.bfloat16)

    tiles = lax.map(one_tile, (q_tiles, q_places))
    return tiles.transpose(1, 0, 2, 3).reshape(heads, q_count, depth)


def shards_general(
    video_query,
    video_keys,
    video_values,
    audio_query,
    audio_keys,
    audio_values,
    cross_video_query,
    cross_video_keys,
    cross_video_values,
    cross_audio_query,
    cross_audio_keys,
    cross_audio_values,
    video_length,
    audio_length,
    align_offset,
):
    devices = lax.axis_size("seq")
    index = lax.axis_index("seq")
    video_rows = video_query.shape[0]
    audio_rows = audio_query.shape[0]
    video_total = video_rows * devices
    audio_total = audio_rows * devices
    video_reach = video_total // 8
    audio_reach = 5 * audio_total // 8
    video_valid = video_length[0]
    audio_valid = audio_length[0]
    align_shift = align_offset[0]
    copies = max(devices // HV, 1)
    video_places = jnp.arange(video_total, dtype=jnp.int32)
    audio_places = jnp.arange(audio_total, dtype=jnp.int32)

    def video_open(q_where, k_where):
        return k_where < video_valid

    def toward_video(q_where, k_where):
        center = jnp.clip(q_where * audio_total // video_total + align_shift, 0, audio_valid - 1)
        return (k_where < audio_valid) & (jnp.abs(k_where - center) <= audio_reach)

    def toward_audio(q_where, k_where):
        center = jnp.clip((q_where - align_shift) * video_total // audio_total, 0, video_valid - 1)
        return (k_where < video_valid) & (jnp.abs(k_where - center) <= video_reach)

    video_owned = (
        lax.all_to_all(
            split_heads(video_query, HV, HDV, copies),
            "seq",
            split_axis=0,
            concat_axis=1,
            tiled=True,
        ),
        lax.all_to_all(
            spread_heads(video_keys, HV, HDV, copies),
            "seq",
            split_axis=0,
            concat_axis=1,
            tiled=True,
        ),
        lax.all_to_all(
            spread_heads(video_values, HV, HDV, copies),
            "seq",
            split_axis=0,
            concat_axis=1,
            tiled=True,
        ),
    )
    video_done = attend_local(
        video_owned[0],
        video_owned[1],
        video_owned[2],
        owned_positions(video_rows, copies, devices, index),
        video_places,
        video_open,
    )
    video_mixed = join_heads(
        lax.all_to_all(video_done, "seq", split_axis=1, concat_axis=0, tiled=True), HV, HDV, copies
    )
    audio_local = audio_query.reshape(audio_rows, HA, HDA)
    piece = (
        lax.all_gather(audio_keys, "seq", axis=0, tiled=True),
        lax.all_gather(audio_values, "seq", axis=0, tiled=True),
    )
    k_where = jnp.arange(piece[0].shape[0], dtype=jnp.int32)
    audio_k_where = k_where[None, :]
    permit = audio_k_where < audio_valid
    audio_state = fold_piece(
        fold_initial(audio_rows, HA, HDA), audio_local, piece[0], piece[1], permit, HA, HDA
    )
    audio_mixed = fold_finish(audio_state, HA, HDA)
    cross_owned = (
        lax.all_to_all(
            split_heads(cross_video_query, HA, HDA, copies),
            "seq",
            split_axis=0,
            concat_axis=1,
            tiled=True,
        ),
        lax.all_to_all(
            spread_heads(cross_audio_keys, HA, HDA, copies),
            "seq",
            split_axis=0,
            concat_axis=1,
            tiled=True,
        ),
        lax.all_to_all(
            spread_heads(cross_audio_values, HA, HDA, copies),
            "seq",
            split_axis=0,
            concat_axis=1,
            tiled=True,
        ),
    )
    cross_done = attend_local(
        cross_owned[0],
        cross_owned[1],
        cross_owned[2],
        owned_positions(video_rows, copies, devices, index),
        audio_places,
        toward_video,
    )
    video_cross = join_heads(
        lax.all_to_all(cross_done, "seq", split_axis=1, concat_axis=0, tiled=True), HA, HDA, copies
    )
    listen_owned = (
        lax.all_to_all(
            split_heads(cross_audio_query, HA, HDA, copies),
            "seq",
            split_axis=0,
            concat_axis=1,
            tiled=True,
        ),
        lax.all_to_all(
            spread_heads(cross_video_keys, HA, HDA, copies),
            "seq",
            split_axis=0,
            concat_axis=1,
            tiled=True,
        ),
        lax.all_to_all(
            spread_heads(cross_video_values, HA, HDA, copies),
            "seq",
            split_axis=0,
            concat_axis=1,
            tiled=True,
        ),
    )
    listen_done = attend_local(
        listen_owned[0],
        listen_owned[1],
        listen_owned[2],
        owned_positions(audio_rows, copies, devices, index),
        video_places,
        toward_audio,
    )
    audio_cross = join_heads(
        lax.all_to_all(listen_done, "seq", split_axis=1, concat_axis=0, tiled=True), HA, HDA, copies
    )
    return (video_mixed, audio_mixed, video_cross, audio_cross)


LANES = 128


def fetch(sources, held, arrived):
    copies = [
        pltpu.make_async_copy(source, slot, arrived.at[i])
        for i, (source, slot) in enumerate(zip(sources, held))
    ]
    for copy in copies:
        copy.start()
    return copies


def step_order(chips):
    far, near = list(range(chips - 1, chips // 2 - 1, -1)), list(range(1, chips // 2))
    return [0] + far[:2] + near + far[2:]


def by_step(items):
    order = step_order(len(items))
    return [items[order.index(j)] for j in range(len(items))]


def in_order(items):
    return [items[j] for j in step_order(len(items))]


def pack_kernel(chips, *refs):
    sources, refs = refs[:12], refs[12:]
    packed, held, arrived = by_step(refs[:chips]), refs[chips : chips + 12], refs[chips + 12]
    copies = fetch(sources, held, arrived)
    chip = lax.axis_index("seq") // 2
    video, cross, audio = held[0:3], held[3:6], held[6:12]
    rows = video[0].shape[0]

    def group(ref, j, part):
        width = ref.shape[1] // chips
        at = pl.multiple_of((chip ^ j) * width + part * LANES, LANES)
        return ref[:, pl.ds(at, LANES)]

    at = 0
    for i, ref in enumerate(video + cross):
        copies[i].wait()
        for part in range(ref.shape[1] // chips // LANES):
            for j in range(chips):
                packed[j][at : at + rows, :] = group(ref, j, part)
            at += rows
    for i in range(0, 6, 2):
        copies[6 + i].wait()
        copies[7 + i].wait()
        for part in range(audio[i].shape[1] // chips // LANES):
            for j in range(chips):
                pair = jnp.concatenate(
                    [group(audio[i], j, part), group(audio[i + 1], j, part)], axis=0
                )
                packed[j][at : at + rows, :] = pair
            at += rows


def gather_kernel(video_len, audio_len, shift, *refs):
    slabs, bounds, merged = refs[:-2], refs[-2], refs[-1]
    row = lax.broadcasted_iota(jnp.int32, bounds.shape, 0)
    bounds[...] = jnp.where(row == 0, video_len[0], jnp.where(row == 1, audio_len[0], shift[0]))
    for i, slab in enumerate(slabs):
        merged[i] = slab[...]


def merge_kernel(*refs):
    for i, slab in enumerate(refs[:-1]):
        refs[-1][i] = slab[...]


def mix_all(units):
    scores = [
        lax.dot_general(query, key, (((1,), (1,)), ((), ())), preferred_element_type=jnp.float32)
        for query, key, value, depth, permit in units
    ]
    weights, totals = [], []
    for score, (query, key, value, depth, permit) in zip(scores, units):
        score = jnp.where(permit, score, -1e30)
        peak = jnp.max(score, axis=1, keepdims=True)
        weight = jnp.exp2((score - peak) * (math.log2(math.e) / math.sqrt(depth)))
        totals.append(jnp.sum(weight, axis=1, keepdims=True))
        weights.append(weight.astype(jnp.bfloat16))
    return [
        jnp.dot(weight, unit[2], preferred_element_type=jnp.float32) / total
        for weight, total, unit in zip(weights, totals, units)
    ]


def pair_units(query, key, value, permit):
    lane = lax.broadcasted_iota(jnp.int32, query.shape, 1) // HDA
    zero = jnp.zeros_like(query)
    return [
        (jnp.where(lane == h, query, zero), key, value, HDA, permit) for h in range(LANES // HDA)
    ]


def pair_join(mixed):
    lane = lax.broadcasted_iota(jnp.int32, mixed[0].shape, 1) // HDA
    result = mixed[0]
    for h in range(1, len(mixed)):
        result = jnp.where(lane == h, mixed[h], result)
    return result


def shares(chips):
    quarter = chips // 4
    far = list(zip(range(chips - 1, 3 * quarter - 1, -1), range(3 * quarter - 1, 2 * quarter - 1, -1)))
    near = list(zip(range(quarter - 1, -1, -1), range(2 * quarter - 1, quarter - 1, -1)))
    return far + near


def attend_kernel(chips, rows, parts, pairs, bounds, *refs):
    own, merged, done = by_step(refs[:chips]), refs[chips : 3 * chips // 2], refs[3 * chips // 2 :]
    other = by_step([ref.at[i] for ref in merged for i in range(ref.shape[0])])
    share = shares(chips)
    every = [ref for both in zip(own, other) for ref in both]
    half = rows // 2
    tv, ta = 2 * chips * rows, 2 * chips * half
    bits = (tv // ta).bit_length() - 1
    me = lax.axis_index("seq")
    core, home = me % 2, me // 2 * 2
    video_valid, audio_valid, offset = (bounds[i : i + 1, 0:1] for i in range(3))

    def slab(at):
        return jnp.concatenate([ref[at : at + rows, :] for ref in every], axis=0)

    def asked(at):
        pieces = []
        for zero, one in share:
            for c in range(2):
                low = (own, other)[c][zero][at : at + rows, :]
                high = (other, own)[c][one][at : at + rows, :]
                pieces.append(jnp.where(core == 0, low, high))
        return jnp.concatenate(pieces, axis=0)

    def split(wide):
        wide = wide.astype(jnp.float32).reshape(-1, rows, LANES)
        first = wide[:, :half, :].reshape(-1, LANES).astype(jnp.bfloat16)
        second = wide[:, half:, :].reshape(-1, LANES).astype(jnp.bfloat16)
        return first, second

    def places(q_step, k_step):
        shape = (chips * q_step, 2 * chips * k_step)
        k_at = lax.broadcasted_iota(jnp.int32, shape, 1) ^ (me * k_step)
        starts = []
        for zero, one in share:
            chip = home ^ jnp.where(core == 0, 2 * zero, 2 * one)
            starts.append(lax.broadcasted_iota(jnp.int32, (2 * q_step, 1), 0) + chip * q_step)
        return jnp.concatenate(starts, axis=0), k_at

    def put(at, mixed):
        count = done[0].shape[0] // 2
        for u in range(len(share)):
            for c in range(2):
                piece = mixed[(2 * u + c) * rows : (2 * u + c + 1) * rows]
                done[u][c * count + at : c * count + at + rows, :] = piece.astype(jnp.bfloat16)

    q_at, k_at = places(rows, rows)
    permit = k_at < video_valid
    units = [
        (
            asked(h * rows),
            slab((parts + h) * rows),
            slab((2 * parts + h) * rows),
            HDV,
            permit,
        )
        for h in range(parts)
    ]
    for h, mixed in enumerate(mix_all(units)):
        put(h * rows, mixed)

    cross = 3 * parts * rows
    audio = cross + 3 * pairs * rows
    q_at, k_at = places(rows, half)
    center = jnp.clip((q_at >> bits) + offset, 0, audio_valid - 1)
    toward_video = (k_at < audio_valid) & (jnp.abs(k_at - center) <= 5 * ta // 8)
    q_at, k_at = places(half, half)
    within_audio = k_at < audio_valid
    q_at, k_at = places(half, rows)
    center = jnp.clip((q_at - offset) << bits, 0, video_valid - 1)
    toward_audio = (k_at < video_valid) & (jnp.abs(k_at - center) <= tv // 8)
    units = []
    for p in range(pairs):
        at = cross + p * rows
        cross_query = asked(at)
        cross_keys = slab(at + pairs * rows)
        cross_values = slab(at + 2 * pairs * rows)
        at = audio + p * rows
        audio_query = split(asked(at))[0]
        audio_keys = split(slab(at))[1]
        at += pairs * rows
        audio_values = split(slab(at))[0]
        listen_query = split(asked(at))[1]
        at += pairs * rows
        sound_keys, sound_values = split(slab(at))
        units += pair_units(cross_query, sound_keys, sound_values, toward_video)
        units += pair_units(audio_query, audio_keys, audio_values, within_audio)
        units += pair_units(listen_query, cross_keys, cross_values, toward_audio)
    mixed = mix_all(units)
    heads = LANES // HDA
    for p in range(pairs):
        seen, heard, listened = (
            pair_join(mixed[(3 * p + i) * heads : (3 * p + i + 1) * heads]) for i in range(3)
        )
        out = (parts + p) * rows
        put(out, seen)
        both = jnp.concatenate(
            [heard.reshape(-1, half, LANES), listened.reshape(-1, half, LANES)], axis=1
        )
        put(out + pairs * rows, both.reshape(-1, LANES))


def hand_kernel(*refs):
    core = lax.axis_index("seq") % 2
    for u, ref in enumerate(refs[:-1]):
        count = refs[-1].shape[1]
        refs[-1][u] = ref[pl.ds(pl.multiple_of((1 - core) * count, 16), count), :]


def unpack_kernel(chips, *refs):
    share = shares(chips)
    back, handed = refs[: len(share)], refs[len(share)]
    video_mixed, audio_mixed, video_cross, audio_cross = refs[len(share) + 1 :]
    rows = video_mixed.shape[0]
    half = audio_mixed.shape[0]
    parts = video_mixed.shape[1] // chips // LANES
    pairs = audio_mixed.shape[1] // chips // LANES
    me = lax.axis_index("seq")
    core, home = me % 2, me // 2
    for u, (zero, one) in enumerate(share):
        for ref, base, chip in (
            (back[u], core * handed.shape[1], home ^ jnp.where(core == 0, zero, one)),
            (handed.at[u], 0, home ^ jnp.where(core == 0, one, zero)),
        ):
            base = pl.multiple_of(base, 16)

            def piece(at):
                return ref[pl.ds(base + at, rows), :]

            for h in range(parts):
                at = pl.multiple_of((chip * parts + h) * LANES, LANES)
                video_mixed[:, pl.ds(at, LANES)] = piece(h * rows)
            for p in range(pairs):
                at = pl.multiple_of((chip * pairs + p) * LANES, LANES)
                out = (parts + p) * rows
                video_cross[:, pl.ds(at, LANES)] = piece(out)
                both = piece(out + pairs * rows)
                audio_mixed[:, pl.ds(at, LANES)] = both[:half, :]
                audio_cross[:, pl.ds(at, LANES)] = both[half:, :]


def swap(piece, n, step):
    return lax.ppermute(piece, "seq", [(i, i ^ step) for i in range(n)])


def shards_packed(*arrays):
    (
        video_query, video_keys, video_values,
        audio_query, audio_keys, audio_values,
        cross_video_query, cross_video_keys, cross_video_values,
        cross_audio_query, cross_audio_keys, cross_audio_values,
        video_length, audio_length, align_offset,
    ) = arrays
    n = lax.axis_size("seq")
    chips = n // 2
    rows = video_query.shape[0]
    parts = video_query.shape[1] // chips // LANES
    pairs = audio_query.shape[1] // chips // LANES
    vmem = pl.BlockSpec(memory_space=pltpu.VMEM)
    hbm = pl.BlockSpec(memory_space=pltpu.HBM)
    smem = pl.BlockSpec(memory_space=pltpu.SMEM)
    params = pltpu.CompilerParams(vmem_limit_bytes=32 * 1024 * 1024)

    def buffer(*shape):
        return jax.ShapeDtypeStruct(shape, jnp.bfloat16)

    sources = (
        video_query, video_keys, video_values,
        cross_video_query, cross_video_keys, cross_video_values,
        audio_query, audio_keys, audio_values,
        cross_audio_query, cross_audio_keys, cross_audio_values,
    )
    packed = pl.pallas_call(
        functools.partial(pack_kernel, chips),
        out_shape=[pltpu.VMEM(((3 * parts + 6 * pairs) * rows, LANES), jnp.bfloat16)] * chips,
        in_specs=[hbm] * 12,
        out_specs=[vmem] * chips,
        scratch_shapes=[pltpu.VMEM(source.shape, source.dtype) for source in sources]
        + [pltpu.SemaphoreType.DMA((12,))],
        compiler_params=params,
    )(*[pltpu.with_memory_space_constraint(source, pltpu.HBM) for source in sources])
    packed = by_step(packed)
    moved = [swap(packed[j], n, 2 * j) for j in range(1, chips)]
    own = in_order(packed[:1] + moved)
    joint = pltpu.VMEM((2,) + packed[0].shape, jnp.bfloat16)
    bounds, first = pl.pallas_call(
        gather_kernel,
        out_shape=(pltpu.VMEM((8, LANES), jnp.int32), joint),
        in_specs=[smem] * 3 + [vmem] * 2,
        out_specs=(vmem, vmem),
        compiler_params=params,
    )(video_length, audio_length, align_offset, *own[:2])
    merged = [first] + [
        pl.pallas_call(
            merge_kernel,
            out_shape=joint,
            in_specs=[vmem] * 2,
            out_specs=vmem,
            compiler_params=params,
        )(*own[i : i + 2])
        for i in range(2, chips, 2)
    ]
    share = shares(chips)
    done = pl.pallas_call(
        functools.partial(attend_kernel, chips, rows, parts, pairs),
        out_shape=[buffer(2 * (parts + 2 * pairs) * rows, LANES)] * len(share),
        in_specs=[vmem] * (1 + chips + len(merged)),
        out_specs=[vmem] * len(share),
        compiler_params=params,
    )(bounds, *own, *[swap(piece, n, 1) for piece in merged])
    back = [
        lax.ppermute(piece, "seq", [(i, i ^ 2 * pair[i % 2]) for i in range(n)])
        for piece, pair in zip(done, share)
    ]
    handed = pl.pallas_call(
        hand_kernel,
        out_shape=pltpu.VMEM((len(share), done[0].shape[0] // 2, LANES), jnp.bfloat16),
        in_specs=[vmem] * len(share),
        out_specs=vmem,
        compiler_params=params,
    )(*back)
    return pl.pallas_call(
        functools.partial(unpack_kernel, chips),
        out_shape=(
            buffer(*video_query.shape),
            buffer(*audio_query.shape),
            buffer(*cross_video_query.shape),
            buffer(*cross_audio_query.shape),
        ),
        in_specs=[vmem] * (len(share) + 1),
        out_specs=(vmem,) * 4,
        compiler_params=params,
    )(*back, swap(handed, n, 1))


def shards(*arrays):
    n = lax.axis_size("seq")
    chips = max(n // 2, 1)
    rows, half = arrays[0].shape[0], arrays[3].shape[0]
    fits = (
        n % 8 == 0
        and n & (n - 1) == 0
        and arrays[0].shape[1] % (chips * LANES) == 0
        and arrays[3].shape[1] % (chips * LANES) == 0
        and HDV == LANES
        and LANES % HDA == 0
        and rows == 2 * half
        and half % 8 == 0
        and half & (half - 1) == 0
    )
    return shards_packed(*arrays) if fits else shards_general(*arrays)


def solution(mesh):
    placed = (
        P(("clip", "seq"), None),
        P(("clip", "seq"), None),
        P(("clip", "seq"), None),
        P(("clip", "seq"), None),
        P(("clip", "seq"), None),
        P(("clip", "seq"), None),
        P(("clip", "seq"), None),
        P(("clip", "seq"), None),
        P(("clip", "seq"), None),
        P(("clip", "seq"), None),
        P(("clip", "seq"), None),
        P(("clip", "seq"), None),
        P("clip"),
        P("clip"),
        P("clip"),
    )
    return jax.shard_map(
        shards,
        mesh=mesh,
        in_specs=placed,
        out_specs=(
            P(("clip", "seq"), None),
            P(("clip", "seq"), None),
            P(("clip", "seq"), None),
            P(("clip", "seq"), None),
        ),
        check_vma=False,
    )
```

```python
import functools
import math

import jax
import jax.numpy as jnp
from jax import lax
from jax.experimental import pallas as pl
from jax.experimental.pallas import tpu as pltpu
from jax.sharding import PartitionSpec as P

HV = 32
HDV = 128
HA = 32
HDA = 64


def block_size(total, limit):
    chosen = min(total, limit)
    while total % chosen:
        chosen -= 1
    return chosen


def split_heads(tokens, heads, depth, copies):
    rows = tokens.shape[0]
    shaped = tokens.reshape(copies, rows // copies, heads, depth).transpose(2, 0, 1, 3)
    return shaped.reshape(heads * copies, rows // copies, depth)


def spread_heads(tokens, heads, depth, copies):
    rows = tokens.shape[0]
    shaped = tokens.reshape(rows, heads, depth).transpose(1, 0, 2)
    shaped = jnp.broadcast_to(shaped[:, None], (heads, copies, rows, depth))
    return shaped.reshape(heads * copies, rows, depth)


def join_heads(owned, heads, depth, copies):
    part_rows = owned.shape[1]
    shaped = owned.reshape(heads, copies, part_rows, depth).transpose(1, 2, 0, 3)
    return shaped.reshape(copies * part_rows, heads * depth)


def owned_positions(rows, copies, devices, index):
    part_rows = rows // copies
    flat = jnp.arange(devices * part_rows, dtype=jnp.int32)
    return flat // part_rows * rows + index % copies * part_rows + flat % part_rows


def online_update(carry, scores, permit, value_tile, value_form):
    running, total, accum = carry
    scores = jnp.where(permit, scores, -1e30)
    newmax = jnp.maximum(running, jnp.max(scores, axis=2))
    weights = jnp.where(permit, jnp.exp(scores - newmax[:, :, None]), 0.0)
    factor = jnp.exp(running - newmax)
    total = total * factor + jnp.sum(weights, axis=2)
    mixed = jnp.einsum(
        value_form, weights.astype(jnp.bfloat16), value_tile, preferred_element_type=jnp.float32
    )
    accum = accum * factor[:, :, None] + mixed
    return (newmax, total, accum)


def fold_initial(rows, heads, depth):
    return (
        jnp.full((heads, rows), -1e30, jnp.float32),
        jnp.zeros((heads, rows), jnp.float32),
        jnp.zeros((heads, rows, depth), jnp.float32),
    )


def fold_piece(carry, local_query, key_rows, value_rows, permit, heads, depth):
    keyed = key_rows.reshape(key_rows.shape[0], heads, depth)
    valued = value_rows.reshape(value_rows.shape[0], heads, depth)
    scores = jnp.einsum("qhd,khd->hqk", local_query, keyed, preferred_element_type=jnp.float32) * (
        1.0 / math.sqrt(depth)
    )
    return online_update(carry, scores, permit[None], valued, "hqk,khd->hqd")


def fold_finish(carry, heads, depth):
    running, total, accum = carry
    result = (accum / total[:, :, None]).astype(jnp.bfloat16)
    return result.transpose(1, 0, 2).reshape(result.shape[1], heads * depth)


def attend_local(queries, keys, values, query_pos, key_pos, allowed):
    heads, q_count, depth = queries.shape
    k_count = keys.shape[1]
    q_block = block_size(q_count, 512)
    k_block = block_size(k_count, 2048)
    scale = 1.0 / math.sqrt(depth)
    q_tiles = queries.reshape(heads, q_count // q_block, q_block, depth).transpose(1, 0, 2, 3)
    k_tiles = keys.reshape(heads, k_count // k_block, k_block, depth).transpose(1, 0, 2, 3)
    v_tiles = values.reshape(heads, k_count // k_block, k_block, depth).transpose(1, 0, 2, 3)
    q_places = query_pos.reshape(q_count // q_block, q_block)
    k_places = key_pos.reshape(k_count // k_block, k_block)

    def one_tile(packed):
        q_tile, q_where = packed

        def absorb(carry, piece):
            k_tile, v_tile, k_where = piece
            scores = (
                jnp.einsum("hqd,hkd->hqk", q_tile, k_tile, preferred_element_type=jnp.float32)
                * scale
            )
            permit = allowed(q_where[:, None], k_where[None, :])[None]
            return (online_update(carry, scores, permit, v_tile, "hqk,hkd->hqd"), None)

        initial = fold_initial(q_block, heads, depth)
        final_state, unused = lax.scan(absorb, initial, (k_tiles, v_tiles, k_places))
        running, total, accum = final_state
        return (accum / total[:, :, None]).astype(jnp.bfloat16)

    tiles = lax.map(one_tile, (q_tiles, q_places))
    return tiles.transpose(1, 0, 2, 3).reshape(heads, q_count, depth)


def shards_general(
    video_query,
    video_keys,
    video_values,
    audio_query,
    audio_keys,
    audio_values,
    cross_video_query,
    cross_video_keys,
    cross_video_values,
    cross_audio_query,
    cross_audio_keys,
    cross_audio_values,
    video_length,
    audio_length,
    align_offset,
):
    devices = lax.axis_size("seq")
    index = lax.axis_index("seq")
    video_rows = video_query.shape[0]
    audio_rows = audio_query.shape[0]
    video_total = video_rows * devices
    audio_total = audio_rows * devices
    video_reach = video_total // 8
    audio_reach = 5 * audio_total // 8
    video_valid = video_length[0]
    audio_valid = audio_length[0]
    align_shift = align_offset[0]
    copies = max(devices // HV, 1)
    video_places = jnp.arange(video_total, dtype=jnp.int32)
    audio_places = jnp.arange(audio_total, dtype=jnp.int32)

    def video_open(q_where, k_where):
        return k_where < video_valid

    def toward_video(q_where, k_where):
        center = jnp.clip(q_where * audio_total // video_total + align_shift, 0, audio_valid - 1)
        return (k_where < audio_valid) & (jnp.abs(k_where - center) <= audio_reach)

    def toward_audio(q_where, k_where):
        center = jnp.clip((q_where - align_shift) * video_total // audio_total, 0, video_valid - 1)
        return (k_where < video_valid) & (jnp.abs(k_where - center) <= video_reach)

    video_owned = (
        lax.all_to_all(
            split_heads(video_query, HV, HDV, copies),
            "seq",
            split_axis=0,
            concat_axis=1,
            tiled=True,
        ),
        lax.all_to_all(
            spread_heads(video_keys, HV, HDV, copies),
            "seq",
            split_axis=0,
            concat_axis=1,
            tiled=True,
        ),
        lax.all_to_all(
            spread_heads(video_values, HV, HDV, copies),
            "seq",
            split_axis=0,
            concat_axis=1,
            tiled=True,
        ),
    )
    video_done = attend_local(
        video_owned[0],
        video_owned[1],
        video_owned[2],
        owned_positions(video_rows, copies, devices, index),
        video_places,
        video_open,
    )
    video_mixed = join_heads(
        lax.all_to_all(video_done, "seq", split_axis=1, concat_axis=0, tiled=True), HV, HDV, copies
    )
    audio_local = audio_query.reshape(audio_rows, HA, HDA)
    piece = (
        lax.all_gather(audio_keys, "seq", axis=0, tiled=True),
        lax.all_gather(audio_values, "seq", axis=0, tiled=True),
    )
    k_where = jnp.arange(piece[0].shape[0], dtype=jnp.int32)
    audio_k_where = k_where[None, :]
    permit = audio_k_where < audio_valid
    audio_state = fold_piece(
        fold_initial(audio_rows, HA, HDA), audio_local, piece[0], piece[1], permit, HA, HDA
    )
    audio_mixed = fold_finish(audio_state, HA, HDA)
    cross_owned = (
        lax.all_to_all(
            split_heads(cross_video_query, HA, HDA, copies),
            "seq",
            split_axis=0,
            concat_axis=1,
            tiled=True,
        ),
        lax.all_to_all(
            spread_heads(cross_audio_keys, HA, HDA, copies),
            "seq",
            split_axis=0,
            concat_axis=1,
            tiled=True,
        ),
        lax.all_to_all(
            spread_heads(cross_audio_values, HA, HDA, copies),
            "seq",
            split_axis=0,
            concat_axis=1,
            tiled=True,
        ),
    )
    cross_done = attend_local(
        cross_owned[0],
        cross_owned[1],
        cross_owned[2],
        owned_positions(video_rows, copies, devices, index),
        audio_places,
        toward_video,
    )
    video_cross = join_heads(
        lax.all_to_all(cross_done, "seq", split_axis=1, concat_axis=0, tiled=True), HA, HDA, copies
    )
    listen_owned = (
        lax.all_to_all(
            split_heads(cross_audio_query, HA, HDA, copies),
            "seq",
            split_axis=0,
            concat_axis=1,
            tiled=True,
        ),
        lax.all_to_all(
            spread_heads(cross_video_keys, HA, HDA, copies),
            "seq",
            split_axis=0,
            concat_axis=1,
            tiled=True,
        ),
        lax.all_to_all(
            spread_heads(cross_video_values, HA, HDA, copies),
            "seq",
            split_axis=0,
            concat_axis=1,
            tiled=True,
        ),
    )
    listen_done = attend_local(
        listen_owned[0],
        listen_owned[1],
        listen_owned[2],
        owned_positions(audio_rows, copies, devices, index),
        video_places,
        toward_audio,
    )
    audio_cross = join_heads(
        lax.all_to_all(listen_done, "seq", split_axis=1, concat_axis=0, tiled=True), HA, HDA, copies
    )
    return (video_mixed, audio_mixed, video_cross, audio_cross)


LANES = 128


def fetch(sources, held, arrived):
    copies = [
        pltpu.make_async_copy(source, slot, arrived.at[i])
        for i, (source, slot) in enumerate(zip(sources, held))
    ]
    for copy in copies:
        copy.start()
    return copies


def step_order(chips):
    far, near = list(range(chips - 1, chips // 2 - 1, -1)), list(range(1, chips // 2))
    return [0] + far[:2] + near + far[2:]


def by_step(items):
    order = step_order(len(items))
    return [items[order.index(j)] for j in range(len(items))]


def in_order(items):
    return [items[j] for j in step_order(len(items))]


def pack_kernel(chips, *refs):
    sources, refs = refs[:12], refs[12:]
    packed, held, arrived = by_step(refs[:chips]), refs[chips : chips + 12], refs[chips + 12]
    copies = fetch(sources, held, arrived)
    chip = lax.axis_index("seq") // 2
    video, cross, audio = held[0:3], held[3:6], held[6:12]
    rows = video[0].shape[0]

    def group(ref, j, part):
        width = ref.shape[1] // chips
        at = pl.multiple_of((chip ^ j) * width + part * LANES, LANES)
        return ref[:, pl.ds(at, LANES)]

    at = 0
    for i, ref in enumerate(video + cross):
        copies[i].wait()
        for part in range(ref.shape[1] // chips // LANES):
            for j in range(chips):
                packed[j][at : at + rows, :] = group(ref, j, part)
            at += rows
    for i in range(0, 6, 2):
        copies[6 + i].wait()
        copies[7 + i].wait()
        for part in range(audio[i].shape[1] // chips // LANES):
            for j in range(chips):
                pair = jnp.concatenate(
                    [group(audio[i], j, part), group(audio[i + 1], j, part)], axis=0
                )
                packed[j][at : at + rows, :] = pair
            at += rows


def gather_kernel(video_len, audio_len, shift, *refs):
    slabs, bounds, merged = refs[:-2], refs[-2], refs[-1]
    row = lax.broadcasted_iota(jnp.int32, bounds.shape, 0)
    bounds[...] = jnp.where(row == 0, video_len[0], jnp.where(row == 1, audio_len[0], shift[0]))
    for i, slab in enumerate(slabs):
        merged[i] = slab[...]


def merge_kernel(*refs):
    for i, slab in enumerate(refs[:-1]):
        refs[-1][i] = slab[...]


def mix_all(units):
    scores = [
        lax.dot_general(query, key, (((1,), (1,)), ((), ())), preferred_element_type=jnp.float32)
        for query, key, value, depth, permit in units
    ]
    weights, totals = [], []
    for score, (query, key, value, depth, permit) in zip(scores, units):
        score = jnp.where(permit, score, -1e30)
        peak = jnp.max(score, axis=1, keepdims=True)
        weight = jnp.exp2((score - peak) * (math.log2(math.e) / math.sqrt(depth)))
        totals.append(jnp.sum(weight, axis=1, keepdims=True))
        weights.append(weight.astype(jnp.bfloat16))
    return [
        jnp.dot(weight, unit[2], preferred_element_type=jnp.float32) / total
        for weight, total, unit in zip(weights, totals, units)
    ]


def pair_units(query, key, value, permit):
    lane = lax.broadcasted_iota(jnp.int32, query.shape, 1) // HDA
    zero = jnp.zeros_like(query)
    return [
        (jnp.where(lane == h, query, zero), key, value, HDA, permit) for h in range(LANES // HDA)
    ]


def pair_join(mixed):
    lane = lax.broadcasted_iota(jnp.int32, mixed[0].shape, 1) // HDA
    result = mixed[0]
    for h in range(1, len(mixed)):
        result = jnp.where(lane == h, mixed[h], result)
    return result


def shares(chips):
    quarter = chips // 4
    far = list(zip(range(chips - 1, 3 * quarter - 1, -1), range(3 * quarter - 1, 2 * quarter - 1, -1)))
    near = list(zip(range(quarter - 1, -1, -1), range(2 * quarter - 1, quarter - 1, -1)))
    return far + near


def attend_kernel(chips, rows, parts, pairs, bounds, *refs):
    own, merged, done = by_step(refs[:chips]), refs[chips : 3 * chips // 2], refs[3 * chips // 2 :]
    other = by_step([ref.at[i] for ref in merged for i in range(ref.shape[0])])
    share = shares(chips)
    every = [ref for both in zip(own, other) for ref in both]
    half = rows // 2
    tv, ta = 2 * chips * rows, 2 * chips * half
    bits = (tv // ta).bit_length() - 1
    me = lax.axis_index("seq")
    core, home = me % 2, me // 2 * 2
    video_valid, audio_valid, offset = (bounds[i : i + 1, 0:1] for i in range(3))

    def slab(at):
        return jnp.concatenate([ref[at : at + rows, :] for ref in every], axis=0)

    def asked(at):
        pieces = []
        for zero, one in share:
            for c in range(2):
                low = (own, other)[c][zero][at : at + rows, :]
                high = (other, own)[c][one][at : at + rows, :]
                pieces.append(jnp.where(core == 0, low, high))
        return jnp.concatenate(pieces, axis=0)

    def split(wide):
        wide = wide.astype(jnp.float32).reshape(-1, rows, LANES)
        first = wide[:, :half, :].reshape(-1, LANES).astype(jnp.bfloat16)
        second = wide[:, half:, :].reshape(-1, LANES).astype(jnp.bfloat16)
        return first, second

    def places(q_step, k_step):
        shape = (chips * q_step, 2 * chips * k_step)
        k_at = lax.broadcasted_iota(jnp.int32, shape, 1) ^ (me * k_step)
        starts = []
        for zero, one in share:
            chip = home ^ jnp.where(core == 0, 2 * zero, 2 * one)
            starts.append(lax.broadcasted_iota(jnp.int32, (2 * q_step, 1), 0) + chip * q_step)
        return jnp.concatenate(starts, axis=0), k_at

    def put(at, mixed):
        count = done[0].shape[0] // 2
        for u in range(len(share)):
            for c in range(2):
                piece = mixed[(2 * u + c) * rows : (2 * u + c + 1) * rows]
                done[u][c * count + at : c * count + at + rows, :] = piece.astype(jnp.bfloat16)

    q_at, k_at = places(rows, rows)
    permit = k_at < video_valid
    units = [
        (
            asked(h * rows),
            slab((parts + h) * rows),
            slab((2 * parts + h) * rows),
            HDV,
            permit,
        )
        for h in range(parts)
    ]

    cross = 3 * parts * rows
    audio = cross + 3 * pairs * rows
    q_at, k_at = places(rows, half)
    center = jnp.clip((q_at >> bits) + offset, 0, audio_valid - 1)
    toward_video = (k_at < audio_valid) & (jnp.abs(k_at - center) <= 5 * ta // 8)
    q_at, k_at = places(half, half)
    within_audio = k_at < audio_valid
    q_at, k_at = places(half, rows)
    center = jnp.clip((q_at - offset) << bits, 0, video_valid - 1)
    toward_audio = (k_at < video_valid) & (jnp.abs(k_at - center) <= tv // 8)
    for p in range(pairs):
        at = cross + p * rows
        cross_query = asked(at)
        cross_keys = slab(at + pairs * rows)
        cross_values = slab(at + 2 * pairs * rows)
        at = audio + p * rows
        audio_query = split(asked(at))[0]
        audio_keys = split(slab(at))[1]
        at += pairs * rows
        audio_values = split(slab(at))[0]
        listen_query = split(asked(at))[1]
        at += pairs * rows
        sound_keys, sound_values = split(slab(at))
        units += pair_units(cross_query, sound_keys, sound_values, toward_video)
        units += pair_units(audio_query, audio_keys, audio_values, within_audio)
        units += pair_units(listen_query, cross_keys, cross_values, toward_audio)
    mixed = mix_all(units)
    for h in range(parts):
        put(h * rows, mixed[h])
    mixed = mixed[parts:]
    heads = LANES // HDA
    for p in range(pairs):
        seen, heard, listened = (
            pair_join(mixed[(3 * p + i) * heads : (3 * p + i + 1) * heads]) for i in range(3)
        )
        out = (parts + p) * rows
        put(out, seen)
        both = jnp.concatenate(
            [heard.reshape(-1, half, LANES), listened.reshape(-1, half, LANES)], axis=1
        )
        put(out + pairs * rows, both.reshape(-1, LANES))


def hand_kernel(*refs):
    core = lax.axis_index("seq") % 2
    for u, ref in enumerate(refs[:-1]):
        count = refs[-1].shape[1]
        refs[-1][u] = ref[pl.ds(pl.multiple_of((1 - core) * count, 16), count), :]


def unpack_kernel(chips, *refs):
    share = shares(chips)
    back, handed = refs[: len(share)], refs[len(share)]
    video_mixed, audio_mixed, video_cross, audio_cross = refs[len(share) + 1 :]
    rows = video_mixed.shape[0]
    half = audio_mixed.shape[0]
    parts = video_mixed.shape[1] // chips // LANES
    pairs = audio_mixed.shape[1] // chips // LANES
    me = lax.axis_index("seq")
    core, home = me % 2, me // 2
    for u, (zero, one) in enumerate(share):
        for ref, base, chip in (
            (back[u], core * handed.shape[1], home ^ jnp.where(core == 0, zero, one)),
            (handed.at[u], 0, home ^ jnp.where(core == 0, one, zero)),
        ):
            base = pl.multiple_of(base, 16)

            def piece(at):
                return ref[pl.ds(base + at, rows), :]

            for h in range(parts):
                at = pl.multiple_of((chip * parts + h) * LANES, LANES)
                video_mixed[:, pl.ds(at, LANES)] = piece(h * rows)
            for p in range(pairs):
                at = pl.multiple_of((chip * pairs + p) * LANES, LANES)
                out = (parts + p) * rows
                video_cross[:, pl.ds(at, LANES)] = piece(out)
                both = piece(out + pairs * rows)
                audio_mixed[:, pl.ds(at, LANES)] = both[:half, :]
                audio_cross[:, pl.ds(at, LANES)] = both[half:, :]


def swap(piece, n, step):
    return lax.ppermute(piece, "seq", [(i, i ^ step) for i in range(n)])


def shards_packed(*arrays):
    (
        video_query, video_keys, video_values,
        audio_query, audio_keys, audio_values,
        cross_video_query, cross_video_keys, cross_video_values,
        cross_audio_query, cross_audio_keys, cross_audio_values,
        video_length, audio_length, align_offset,
    ) = arrays
    n = lax.axis_size("seq")
    chips = n // 2
    rows = video_query.shape[0]
    parts = video_query.shape[1] // chips // LANES
    pairs = audio_query.shape[1] // chips // LANES
    vmem = pl.BlockSpec(memory_space=pltpu.VMEM)
    hbm = pl.BlockSpec(memory_space=pltpu.HBM)
    smem = pl.BlockSpec(memory_space=pltpu.SMEM)
    params = pltpu.CompilerParams(vmem_limit_bytes=32 * 1024 * 1024)

    def buffer(*shape):
        return jax.ShapeDtypeStruct(shape, jnp.bfloat16)

    sources = (
        video_query, video_keys, video_values,
        cross_video_query, cross_video_keys, cross_video_values,
        audio_query, audio_keys, audio_values,
        cross_audio_query, cross_audio_keys, cross_audio_values,
    )
    packed = pl.pallas_call(
        functools.partial(pack_kernel, chips),
        out_shape=[pltpu.VMEM(((3 * parts + 6 * pairs) * rows, LANES), jnp.bfloat16)] * chips,
        in_specs=[hbm] * 12,
        out_specs=[vmem] * chips,
        scratch_shapes=[pltpu.VMEM(source.shape, source.dtype) for source in sources]
        + [pltpu.SemaphoreType.DMA((12,))],
        compiler_params=params,
    )(*[pltpu.with_memory_space_constraint(source, pltpu.HBM) for source in sources])
    packed = by_step(packed)
    moved = [swap(packed[j], n, 2 * j) for j in range(1, chips)]
    own = in_order(packed[:1] + moved)
    joint = pltpu.VMEM((2,) + packed[0].shape, jnp.bfloat16)
    bounds, first = pl.pallas_call(
        gather_kernel,
        out_shape=(pltpu.VMEM((8, LANES), jnp.int32), joint),
        in_specs=[smem] * 3 + [vmem] * 2,
        out_specs=(vmem, vmem),
        compiler_params=params,
    )(video_length, audio_length, align_offset, *own[:2])
    merged = [first] + [
        pl.pallas_call(
            merge_kernel,
            out_shape=joint,
            in_specs=[vmem] * 2,
            out_specs=vmem,
            compiler_params=params,
        )(*own[i : i + 2])
        for i in range(2, chips, 2)
    ]
    share = shares(chips)
    done = pl.pallas_call(
        functools.partial(attend_kernel, chips, rows, parts, pairs),
        out_shape=[buffer(2 * (parts + 2 * pairs) * rows, LANES)] * len(share),
        in_specs=[vmem] * (1 + chips + len(merged)),
        out_specs=[vmem] * len(share),
        compiler_params=params,
    )(bounds, *own, *[swap(piece, n, 1) for piece in merged])
    back = [
        lax.ppermute(piece, "seq", [(i, i ^ 2 * pair[i % 2]) for i in range(n)])
        for piece, pair in zip(done, share)
    ]
    handed = pl.pallas_call(
        hand_kernel,
        out_shape=pltpu.VMEM((len(share), done[0].shape[0] // 2, LANES), jnp.bfloat16),
        in_specs=[vmem] * len(share),
        out_specs=vmem,
        compiler_params=params,
    )(*back)
    return pl.pallas_call(
        functools.partial(unpack_kernel, chips),
        out_shape=(
            buffer(*video_query.shape),
            buffer(*audio_query.shape),
            buffer(*cross_video_query.shape),
            buffer(*cross_audio_query.shape),
        ),
        in_specs=[vmem] * (len(share) + 1),
        out_specs=(vmem,) * 4,
        compiler_params=params,
    )(*back, swap(handed, n, 1))


def shards(*arrays):
    n = lax.axis_size("seq")
    chips = max(n // 2, 1)
    rows, half = arrays[0].shape[0], arrays[3].shape[0]
    fits = (
        n % 8 == 0
        and n & (n - 1) == 0
        and arrays[0].shape[1] % (chips * LANES) == 0
        and arrays[3].shape[1] % (chips * LANES) == 0
        and HDV == LANES
        and LANES % HDA == 0
        and rows == 2 * half
        and half % 8 == 0
        and half & (half - 1) == 0
    )
    return shards_packed(*arrays) if fits else shards_general(*arrays)


def solution(mesh):
    placed = (
        P(("clip", "seq"), None),
        P(("clip", "seq"), None),
        P(("clip", "seq"), None),
        P(("clip", "seq"), None),
        P(("clip", "seq"), None),
        P(("clip", "seq"), None),
        P(("clip", "seq"), None),
        P(("clip", "seq"), None),
        P(("clip", "seq"), None),
        P(("clip", "seq"), None),
        P(("clip", "seq"), None),
        P(("clip", "seq"), None),
        P("clip"),
        P("clip"),
        P("clip"),
    )
    return jax.shard_map(
        shards,
        mesh=mesh,
        in_specs=placed,
        out_specs=(
            P(("clip", "seq"), None),
            P(("clip", "seq"), None),
            P(("clip", "seq"), None),
            P(("clip", "seq"), None),
        ),
        check_vma=False,
    )
```

```python
import functools
import math

import jax
import jax.numpy as jnp
from jax import lax
from jax.experimental import pallas as pl
from jax.experimental.pallas import tpu as pltpu
from jax.sharding import PartitionSpec as P

HV = 32
HDV = 128
HA = 32
HDA = 64


def block_size(total, limit):
    chosen = min(total, limit)
    while total % chosen:
        chosen -= 1
    return chosen


def split_heads(tokens, heads, depth, copies):
    rows = tokens.shape[0]
    shaped = tokens.reshape(copies, rows // copies, heads, depth).transpose(2, 0, 1, 3)
    return shaped.reshape(heads * copies, rows // copies, depth)


def spread_heads(tokens, heads, depth, copies):
    rows = tokens.shape[0]
    shaped = tokens.reshape(rows, heads, depth).transpose(1, 0, 2)
    shaped = jnp.broadcast_to(shaped[:, None], (heads, copies, rows, depth))
    return shaped.reshape(heads * copies, rows, depth)


def join_heads(owned, heads, depth, copies):
    part_rows = owned.shape[1]
    shaped = owned.reshape(heads, copies, part_rows, depth).transpose(1, 2, 0, 3)
    return shaped.reshape(copies * part_rows, heads * depth)


def owned_positions(rows, copies, devices, index):
    part_rows = rows // copies
    flat = jnp.arange(devices * part_rows, dtype=jnp.int32)
    return flat // part_rows * rows + index % copies * part_rows + flat % part_rows


def online_update(carry, scores, permit, value_tile, value_form):
    running, total, accum = carry
    scores = jnp.where(permit, scores, -1e30)
    newmax = jnp.maximum(running, jnp.max(scores, axis=2))
    weights = jnp.where(permit, jnp.exp(scores - newmax[:, :, None]), 0.0)
    factor = jnp.exp(running - newmax)
    total = total * factor + jnp.sum(weights, axis=2)
    mixed = jnp.einsum(
        value_form, weights.astype(jnp.bfloat16), value_tile, preferred_element_type=jnp.float32
    )
    accum = accum * factor[:, :, None] + mixed
    return (newmax, total, accum)


def fold_initial(rows, heads, depth):
    return (
        jnp.full((heads, rows), -1e30, jnp.float32),
        jnp.zeros((heads, rows), jnp.float32),
        jnp.zeros((heads, rows, depth), jnp.float32),
    )


def fold_piece(carry, local_query, key_rows, value_rows, permit, heads, depth):
    keyed = key_rows.reshape(key_rows.shape[0], heads, depth)
    valued = value_rows.reshape(value_rows.shape[0], heads, depth)
    scores = jnp.einsum("qhd,khd->hqk", local_query, keyed, preferred_element_type=jnp.float32) * (
        1.0 / math.sqrt(depth)
    )
    return online_update(carry, scores, permit[None], valued, "hqk,khd->hqd")


def fold_finish(carry, heads, depth):
    running, total, accum = carry
    result = (accum / total[:, :, None]).astype(jnp.bfloat16)
    return result.transpose(1, 0, 2).reshape(result.shape[1], heads * depth)


def attend_local(queries, keys, values, query_pos, key_pos, allowed):
    heads, q_count, depth = queries.shape
    k_count = keys.shape[1]
    q_block = block_size(q_count, 512)
    k_block = block_size(k_count, 2048)
    scale = 1.0 / math.sqrt(depth)
    q_tiles = queries.reshape(heads, q_count // q_block, q_block, depth).transpose(1, 0, 2, 3)
    k_tiles = keys.reshape(heads, k_count // k_block, k_block, depth).transpose(1, 0, 2, 3)
    v_tiles = values.reshape(heads, k_count // k_block, k_block, depth).transpose(1, 0, 2, 3)
    q_places = query_pos.reshape(q_count // q_block, q_block)
    k_places = key_pos.reshape(k_count // k_block, k_block)

    def one_tile(packed):
        q_tile, q_where = packed

        def absorb(carry, piece):
            k_tile, v_tile, k_where = piece
            scores = (
                jnp.einsum("hqd,hkd->hqk", q_tile, k_tile, preferred_element_type=jnp.float32)
                * scale
            )
            permit = allowed(q_where[:, None], k_where[None, :])[None]
            return (online_update(carry, scores, permit, v_tile, "hqk,hkd->hqd"), None)

        initial = fold_initial(q_block, heads, depth)
        final_state, unused = lax.scan(absorb, initial, (k_tiles, v_tiles, k_places))
        running, total, accum = final_state
        return (accum / total[:, :, None]).astype(jnp.bfloat16)

    tiles = lax.map(one_tile, (q_tiles, q_places))
    return tiles.transpose(1, 0, 2, 3).reshape(heads, q_count, depth)


def shards_general(
    video_query,
    video_keys,
    video_values,
    audio_query,
    audio_keys,
    audio_values,
    cross_video_query,
    cross_video_keys,
    cross_video_values,
    cross_audio_query,
    cross_audio_keys,
    cross_audio_values,
    video_length,
    audio_length,
    align_offset,
):
    devices = lax.axis_size("seq")
    index = lax.axis_index("seq")
    video_rows = video_query.shape[0]
    audio_rows = audio_query.shape[0]
    video_total = video_rows * devices
    audio_total = audio_rows * devices
    video_reach = video_total // 8
    audio_reach = 5 * audio_total // 8
    video_valid = video_length[0]
    audio_valid = audio_length[0]
    align_shift = align_offset[0]
    copies = max(devices // HV, 1)
    video_places = jnp.arange(video_total, dtype=jnp.int32)
    audio_places = jnp.arange(audio_total, dtype=jnp.int32)

    def video_open(q_where, k_where):
        return k_where < video_valid

    def toward_video(q_where, k_where):
        center = jnp.clip(q_where * audio_total // video_total + align_shift, 0, audio_valid - 1)
        return (k_where < audio_valid) & (jnp.abs(k_where - center) <= audio_reach)

    def toward_audio(q_where, k_where):
        center = jnp.clip((q_where - align_shift) * video_total // audio_total, 0, video_valid - 1)
        return (k_where < video_valid) & (jnp.abs(k_where - center) <= video_reach)

    video_owned = (
        lax.all_to_all(
            split_heads(video_query, HV, HDV, copies),
            "seq",
            split_axis=0,
            concat_axis=1,
            tiled=True,
        ),
        lax.all_to_all(
            spread_heads(video_keys, HV, HDV, copies),
            "seq",
            split_axis=0,
            concat_axis=1,
            tiled=True,
        ),
        lax.all_to_all(
            spread_heads(video_values, HV, HDV, copies),
            "seq",
            split_axis=0,
            concat_axis=1,
            tiled=True,
        ),
    )
    video_done = attend_local(
        video_owned[0],
        video_owned[1],
        video_owned[2],
        owned_positions(video_rows, copies, devices, index),
        video_places,
        video_open,
    )
    video_mixed = join_heads(
        lax.all_to_all(video_done, "seq", split_axis=1, concat_axis=0, tiled=True), HV, HDV, copies
    )
    audio_local = audio_query.reshape(audio_rows, HA, HDA)
    piece = (
        lax.all_gather(audio_keys, "seq", axis=0, tiled=True),
        lax.all_gather(audio_values, "seq", axis=0, tiled=True),
    )
    k_where = jnp.arange(piece[0].shape[0], dtype=jnp.int32)
    audio_k_where = k_where[None, :]
    permit = audio_k_where < audio_valid
    audio_state = fold_piece(
        fold_initial(audio_rows, HA, HDA), audio_local, piece[0], piece[1], permit, HA, HDA
    )
    audio_mixed = fold_finish(audio_state, HA, HDA)
    cross_owned = (
        lax.all_to_all(
            split_heads(cross_video_query, HA, HDA, copies),
            "seq",
            split_axis=0,
            concat_axis=1,
            tiled=True,
        ),
        lax.all_to_all(
            spread_heads(cross_audio_keys, HA, HDA, copies),
            "seq",
            split_axis=0,
            concat_axis=1,
            tiled=True,
        ),
        lax.all_to_all(
            spread_heads(cross_audio_values, HA, HDA, copies),
            "seq",
            split_axis=0,
            concat_axis=1,
            tiled=True,
        ),
    )
    cross_done = attend_local(
        cross_owned[0],
        cross_owned[1],
        cross_owned[2],
        owned_positions(video_rows, copies, devices, index),
        audio_places,
        toward_video,
    )
    video_cross = join_heads(
        lax.all_to_all(cross_done, "seq", split_axis=1, concat_axis=0, tiled=True), HA, HDA, copies
    )
    listen_owned = (
        lax.all_to_all(
            split_heads(cross_audio_query, HA, HDA, copies),
            "seq",
            split_axis=0,
            concat_axis=1,
            tiled=True,
        ),
        lax.all_to_all(
            spread_heads(cross_video_keys, HA, HDA, copies),
            "seq",
            split_axis=0,
            concat_axis=1,
            tiled=True,
        ),
        lax.all_to_all(
            spread_heads(cross_video_values, HA, HDA, copies),
            "seq",
            split_axis=0,
            concat_axis=1,
            tiled=True,
        ),
    )
    listen_done = attend_local(
        listen_owned[0],
        listen_owned[1],
        listen_owned[2],
        owned_positions(audio_rows, copies, devices, index),
        video_places,
        toward_audio,
    )
    audio_cross = join_heads(
        lax.all_to_all(listen_done, "seq", split_axis=1, concat_axis=0, tiled=True), HA, HDA, copies
    )
    return (video_mixed, audio_mixed, video_cross, audio_cross)


LANES = 128


def fetch(sources, held, arrived):
    copies = [
        pltpu.make_async_copy(source, slot, arrived.at[i])
        for i, (source, slot) in enumerate(zip(sources, held))
    ]
    for copy in copies:
        copy.start()
    return copies


def step_order(chips):
    far, near = list(range(chips - 1, chips // 2 - 1, -1)), list(range(1, chips // 2))
    return [0] + far[:2] + near + far[2:]


def by_step(items):
    order = step_order(len(items))
    return [items[order.index(j)] for j in range(len(items))]


def in_order(items):
    return [items[j] for j in step_order(len(items))]


def pack_kernel(chips, *refs):
    sources, refs = refs[:12], refs[12:]
    packed, held, arrived = by_step(refs[:chips]), refs[chips : chips + 12], refs[chips + 12]
    copies = fetch(sources, held, arrived)
    chip = lax.axis_index("seq") // 2
    video, cross, audio = held[0:3], held[3:6], held[6:12]
    rows = video[0].shape[0]

    def group(ref, j, part):
        width = ref.shape[1] // chips
        at = pl.multiple_of((chip ^ j) * width + part * LANES, LANES)
        return ref[:, pl.ds(at, LANES)]

    at = 0
    for i, ref in enumerate(video + cross):
        copies[i].wait()
        for part in range(ref.shape[1] // chips // LANES):
            for j in range(chips):
                packed[j][at : at + rows, :] = group(ref, j, part)
            at += rows
    for i in range(0, 6, 2):
        copies[6 + i].wait()
        copies[7 + i].wait()
        for part in range(audio[i].shape[1] // chips // LANES):
            for j in range(chips):
                pair = jnp.concatenate(
                    [group(audio[i], j, part), group(audio[i + 1], j, part)], axis=0
                )
                packed[j][at : at + rows, :] = pair
            at += rows


def gather_kernel(video_len, audio_len, shift, *refs):
    slabs, bounds, merged = refs[:-2], refs[-2], refs[-1]
    row = lax.broadcasted_iota(jnp.int32, bounds.shape, 0)
    bounds[...] = jnp.where(row == 0, video_len[0], jnp.where(row == 1, audio_len[0], shift[0]))
    for i, slab in enumerate(slabs):
        merged[i] = slab[...]


def merge_kernel(*refs):
    for i, slab in enumerate(refs[:-1]):
        refs[-1][i] = slab[...]


def mix_all(units):
    scores = [
        lax.dot_general(query, key, (((1,), (1,)), ((), ())), preferred_element_type=jnp.float32)
        for query, key, value, depth, permit in units
    ]
    weights, totals = [], []
    for score, (query, key, value, depth, permit) in zip(scores, units):
        score = jnp.where(permit, score, -1e30)
        peak = jnp.max(score, axis=1, keepdims=True)
        weight = jnp.exp2((score - peak) * (math.log2(math.e) / math.sqrt(depth)))
        totals.append(jnp.sum(weight, axis=1, keepdims=True))
        weights.append(weight.astype(jnp.bfloat16))
    return [
        jnp.dot(weight, unit[2], preferred_element_type=jnp.float32) / total
        for weight, total, unit in zip(weights, totals, units)
    ]


def pair_units(query, key, value, permit):
    lane = lax.broadcasted_iota(jnp.int32, query.shape, 1) // HDA
    zero = jnp.zeros_like(query)
    return [
        (jnp.where(lane == h, query, zero), key, value, HDA, permit) for h in range(LANES // HDA)
    ]


def pair_join(mixed):
    lane = lax.broadcasted_iota(jnp.int32, mixed[0].shape, 1) // HDA
    result = mixed[0]
    for h in range(1, len(mixed)):
        result = jnp.where(lane == h, mixed[h], result)
    return result


def shares(chips):
    quarter = chips // 4
    far = list(zip(range(chips - 1, 3 * quarter - 1, -1), range(3 * quarter - 1, 2 * quarter - 1, -1)))
    near = list(zip(range(quarter - 1, -1, -1), range(quarter, 2 * quarter)))
    return far + near


def attend_kernel(chips, rows, parts, pairs, bounds, *refs):
    own, merged, done = by_step(refs[:chips]), refs[chips : 3 * chips // 2], refs[3 * chips // 2 :]
    other = by_step([ref.at[i] for ref in merged for i in range(ref.shape[0])])
    share = shares(chips)
    every = [ref for both in zip(own, other) for ref in both]
    half = rows // 2
    tv, ta = 2 * chips * rows, 2 * chips * half
    bits = (tv // ta).bit_length() - 1
    me = lax.axis_index("seq")
    core, home = me % 2, me // 2 * 2
    video_valid, audio_valid, offset = (bounds[i : i + 1, 0:1] for i in range(3))

    def slab(at):
        return jnp.concatenate([ref[at : at + rows, :] for ref in every], axis=0)

    def asked(at):
        pieces = []
        for zero, one in share:
            for c in range(2):
                low = (own, other)[c][zero][at : at + rows, :]
                high = (other, own)[c][one][at : at + rows, :]
                pieces.append(jnp.where(core == 0, low, high))
        return jnp.concatenate(pieces, axis=0)

    def split(wide):
        wide = wide.astype(jnp.float32).reshape(-1, rows, LANES)
        first = wide[:, :half, :].reshape(-1, LANES).astype(jnp.bfloat16)
        second = wide[:, half:, :].reshape(-1, LANES).astype(jnp.bfloat16)
        return first, second

    def places(q_step, k_step):
        shape = (chips * q_step, 2 * chips * k_step)
        k_at = lax.broadcasted_iota(jnp.int32, shape, 1) ^ (me * k_step)
        starts = []
        for zero, one in share:
            chip = home ^ jnp.where(core == 0, 2 * zero, 2 * one)
            starts.append(lax.broadcasted_iota(jnp.int32, (2 * q_step, 1), 0) + chip * q_step)
        return jnp.concatenate(starts, axis=0), k_at

    def put(at, mixed):
        count = done[0].shape[0] // 2
        for u in range(len(share)):
            for c in range(2):
                piece = mixed[(2 * u + c) * rows : (2 * u + c + 1) * rows]
                done[u][c * count + at : c * count + at + rows, :] = piece.astype(jnp.bfloat16)

    q_at, k_at = places(rows, rows)
    permit = k_at < video_valid
    units = [
        (
            asked(h * rows),
            slab((parts + h) * rows),
            slab((2 * parts + h) * rows),
            HDV,
            permit,
        )
        for h in range(parts)
    ]

    cross = 3 * parts * rows
    audio = cross + 3 * pairs * rows
    q_at, k_at = places(rows, half)
    center = jnp.clip((q_at >> bits) + offset, 0, audio_valid - 1)
    toward_video = (k_at < audio_valid) & (jnp.abs(k_at - center) <= 5 * ta // 8)
    q_at, k_at = places(half, half)
    within_audio = k_at < audio_valid
    q_at, k_at = places(half, rows)
    center = jnp.clip((q_at - offset) << bits, 0, video_valid - 1)
    toward_audio = (k_at < video_valid) & (jnp.abs(k_at - center) <= tv // 8)
    for p in range(pairs):
        at = cross + p * rows
        cross_query = asked(at)
        cross_keys = slab(at + pairs * rows)
        cross_values = slab(at + 2 * pairs * rows)
        at = audio + p * rows
        audio_query = split(asked(at))[0]
        audio_keys = split(slab(at))[1]
        at += pairs * rows
        audio_values = split(slab(at))[0]
        listen_query = split(asked(at))[1]
        at += pairs * rows
        sound_keys, sound_values = split(slab(at))
        units += pair_units(cross_query, sound_keys, sound_values, toward_video)
        units += pair_units(audio_query, audio_keys, audio_values, within_audio)
        units += pair_units(listen_query, cross_keys, cross_values, toward_audio)
    mixed = mix_all(units)
    for h in range(parts):
        put(h * rows, mixed[h])
    mixed = mixed[parts:]
    heads = LANES // HDA
    for p in range(pairs):
        seen, heard, listened = (
            pair_join(mixed[(3 * p + i) * heads : (3 * p + i + 1) * heads]) for i in range(3)
        )
        out = (parts + p) * rows
        put(out, seen)
        both = jnp.concatenate(
            [heard.reshape(-1, half, LANES), listened.reshape(-1, half, LANES)], axis=1
        )
        put(out + pairs * rows, both.reshape(-1, LANES))


def hand_kernel(*refs):
    core = lax.axis_index("seq") % 2
    for u, ref in enumerate(refs[:-1]):
        count = refs[-1].shape[1]
        refs[-1][u] = ref[pl.ds(pl.multiple_of((1 - core) * count, 16), count), :]


def unpack_kernel(chips, *refs):
    share = shares(chips)
    back, handed = refs[: len(share)], refs[len(share)]
    video_mixed, audio_mixed, video_cross, audio_cross = refs[len(share) + 1 :]
    rows = video_mixed.shape[0]
    half = audio_mixed.shape[0]
    parts = video_mixed.shape[1] // chips // LANES
    pairs = audio_mixed.shape[1] // chips // LANES
    me = lax.axis_index("seq")
    core, home = me % 2, me // 2
    for u, (zero, one) in enumerate(share):
        for ref, base, chip in (
            (back[u], core * handed.shape[1], home ^ jnp.where(core == 0, zero, one)),
            (handed.at[u], 0, home ^ jnp.where(core == 0, one, zero)),
        ):
            base = pl.multiple_of(base, 16)

            def piece(at):
                return ref[pl.ds(base + at, rows), :]

            for h in range(parts):
                at = pl.multiple_of((chip * parts + h) * LANES, LANES)
                video_mixed[:, pl.ds(at, LANES)] = piece(h * rows)
            for p in range(pairs):
                at = pl.multiple_of((chip * pairs + p) * LANES, LANES)
                out = (parts + p) * rows
                video_cross[:, pl.ds(at, LANES)] = piece(out)
                both = piece(out + pairs * rows)
                audio_mixed[:, pl.ds(at, LANES)] = both[:half, :]
                audio_cross[:, pl.ds(at, LANES)] = both[half:, :]


def swap(piece, n, step):
    return lax.ppermute(piece, "seq", [(i, i ^ step) for i in range(n)])


def shards_packed(*arrays):
    (
        video_query, video_keys, video_values,
        audio_query, audio_keys, audio_values,
        cross_video_query, cross_video_keys, cross_video_values,
        cross_audio_query, cross_audio_keys, cross_audio_values,
        video_length, audio_length, align_offset,
    ) = arrays
    n = lax.axis_size("seq")
    chips = n // 2
    rows = video_query.shape[0]
    parts = video_query.shape[1] // chips // LANES
    pairs = audio_query.shape[1] // chips // LANES
    vmem = pl.BlockSpec(memory_space=pltpu.VMEM)
    hbm = pl.BlockSpec(memory_space=pltpu.HBM)
    smem = pl.BlockSpec(memory_space=pltpu.SMEM)
    params = pltpu.CompilerParams(vmem_limit_bytes=32 * 1024 * 1024)

    def buffer(*shape):
        return jax.ShapeDtypeStruct(shape, jnp.bfloat16)

    sources = (
        video_query, video_keys, video_values,
        cross_video_query, cross_video_keys, cross_video_values,
        audio_query, audio_keys, audio_values,
        cross_audio_query, cross_audio_keys, cross_audio_values,
    )
    packed = pl.pallas_call(
        functools.partial(pack_kernel, chips),
        out_shape=[pltpu.VMEM(((3 * parts + 6 * pairs) * rows, LANES), jnp.bfloat16)] * chips,
        in_specs=[hbm] * 12,
        out_specs=[vmem] * chips,
        scratch_shapes=[pltpu.VMEM(source.shape, source.dtype) for source in sources]
        + [pltpu.SemaphoreType.DMA((12,))],
        compiler_params=params,
    )(*[pltpu.with_memory_space_constraint(source, pltpu.HBM) for source in sources])
    packed = by_step(packed)
    moved = [swap(packed[j], n, 2 * j) for j in range(1, chips)]
    own = in_order(packed[:1] + moved)
    joint = pltpu.VMEM((2,) + packed[0].shape, jnp.bfloat16)
    bounds, first = pl.pallas_call(
        gather_kernel,
        out_shape=(pltpu.VMEM((8, LANES), jnp.int32), joint),
        in_specs=[smem] * 3 + [vmem] * 2,
        out_specs=(vmem, vmem),
        compiler_params=params,
    )(video_length, audio_length, align_offset, *own[:2])
    merged = [first] + [
        pl.pallas_call(
            merge_kernel,
            out_shape=joint,
            in_specs=[vmem] * 2,
            out_specs=vmem,
            compiler_params=params,
        )(*own[i : i + 2])
        for i in range(2, chips, 2)
    ]
    share = shares(chips)
    done = pl.pallas_call(
        functools.partial(attend_kernel, chips, rows, parts, pairs),
        out_shape=[buffer(2 * (parts + 2 * pairs) * rows, LANES)] * len(share),
        in_specs=[vmem] * (1 + chips + len(merged)),
        out_specs=[vmem] * len(share),
        compiler_params=params,
    )(bounds, *own, *[swap(piece, n, 1) for piece in merged])
    back = [
        lax.ppermute(piece, "seq", [(i, i ^ 2 * pair[i % 2]) for i in range(n)])
        for piece, pair in zip(done, share)
    ]
    handed = pl.pallas_call(
        hand_kernel,
        out_shape=pltpu.VMEM((len(share), done[0].shape[0] // 2, LANES), jnp.bfloat16),
        in_specs=[vmem] * len(share),
        out_specs=vmem,
        compiler_params=params,
    )(*back)
    return pl.pallas_call(
        functools.partial(unpack_kernel, chips),
        out_shape=(
            buffer(*video_query.shape),
            buffer(*audio_query.shape),
            buffer(*cross_video_query.shape),
            buffer(*cross_audio_query.shape),
        ),
        in_specs=[vmem] * (len(share) + 1),
        out_specs=(vmem,) * 4,
        compiler_params=params,
    )(*back, swap(handed, n, 1))


def shards(*arrays):
    n = lax.axis_size("seq")
    chips = max(n // 2, 1)
    rows, half = arrays[0].shape[0], arrays[3].shape[0]
    fits = (
        n % 8 == 0
        and n & (n - 1) == 0
        and arrays[0].shape[1] % (chips * LANES) == 0
        and arrays[3].shape[1] % (chips * LANES) == 0
        and HDV == LANES
        and LANES % HDA == 0
        and rows == 2 * half
        and half % 8 == 0
        and half & (half - 1) == 0
    )
    return shards_packed(*arrays) if fits else shards_general(*arrays)


def solution(mesh):
    placed = (
        P(("clip", "seq"), None),
        P(("clip", "seq"), None),
        P(("clip", "seq"), None),
        P(("clip", "seq"), None),
        P(("clip", "seq"), None),
        P(("clip", "seq"), None),
        P(("clip", "seq"), None),
        P(("clip", "seq"), None),
        P(("clip", "seq"), None),
        P(("clip", "seq"), None),
        P(("clip", "seq"), None),
        P(("clip", "seq"), None),
        P("clip"),
        P("clip"),
        P("clip"),
    )
    return jax.shard_map(
        shards,
        mesh=mesh,
        in_specs=placed,
        out_specs=(
            P(("clip", "seq"), None),
            P(("clip", "seq"), None),
            P(("clip", "seq"), None),
            P(("clip", "seq"), None),
        ),
        check_vma=False,
    )
```
